32 devices in a mesh: dp: 8 (over z, core), tensor: 4 (over y, x).
Axes of the slice: x: 2, y: 2, z: 4, core: 2. Of those that a mesh axis runs over, the one named last changes fastest.
Arguments:
- tokens: bfloat16 [16384, 2048], P(('dp', 'tensor')), may hold values from -6 to 6
- out_grad: bfloat16 [16384, 2048], P(('dp', 'tensor')), may hold values from -6 to 6
- lengths: int32 [8, 16], P('dp'), may hold values from 0 to 1024, as said below
- norm_gain: float32 [2, 2048], P(None, 'dp'), may hold values from 0.5 to 1.5
- norm_bias: float32 [2, 2048], P(None, 'dp'), may hold values from -1.2 to 1.2
- qkv_weight: float32 [3, 2048, 2048], P(None, 'dp', 'tensor'), may hold values from -0.125 to 0.125
- qkv_bias: float32 [3, 2048], P(None, 'dp'), may hold values from -1.2 to 1.2
- out_weight: float32 [2048, 2048], P('tensor', 'dp'), may hold values from -0.5 to 0.5
- gate_up_weight: float32 [2, 2048, 5632], P(None, 'dp', 'tensor'), may hold values from -0.125 to 0.125
- down_weight: float32 [5632, 2048], P('tensor', 'dp'), may hold values from -0.15625 to 0.15625
- first_norm_gain: float32 [2, 2048], P(None, 'dp'), may hold values from -100 to 100
- first_norm_bias: float32 [2, 2048], P(None, 'dp'), may hold values from -100 to 100
- first_qkv_weight: float32 [3, 2048, 2048], P(None, 'dp', 'tensor'), may hold values from -42 to 42
- first_qkv_bias: float32 [3, 2048], P(None, 'dp'), may hold values from -42 to 42
- first_out_weight: float32 [2048, 2048], P('tensor', 'dp'), may hold values from -30 to 30
- first_gate_up_weight: float32 [2, 2048, 5632], P(None, 'dp', 'tensor'), may hold values from -60 to 60
- first_down_weight: float32 [5632, 2048], P('tensor', 'dp'), may hold values from -54 to 54
- second_norm_gain: float32 [2, 2048], P(None, 'dp'), may hold values from 600 to 1800
- second_norm_bias: float32 [2, 2048], P(None, 'dp'), may hold values from 600 to 1800
- second_qkv_weight: float32 [3, 2048, 2048], P(None, 'dp', 'tensor'), may hold values from 100 to 300
- second_qkv_bias: float32 [3, 2048], P(None, 'dp'), may hold values from 100 to 300
- second_out_weight: float32 [2048, 2048], P('tensor', 'dp'), may hold values from 50 to 150
- second_gate_up_weight: float32 [2, 2048, 5632], P(None, 'dp', 'tensor'), may hold values from 250 to 750
- second_down_weight: float32 [5632, 2048], P('tensor', 'dp'), may hold values from 200 to 600
Outputs:
- layer_out: bfloat16 [16384, 2048], P(('dp', 'tensor'))
- input_grad: bfloat16 [16384, 2048], P(('dp', 'tensor'))
- grad_norm_gain: float32 [2, 2048], P(None, 'dp')
- grad_norm_bias: float32 [2, 2048], P(None, 'dp')
- grad_qkv_weight: float32 [3, 2048, 2048], P(None, 'dp', 'tensor')
- grad_qkv_bias: float32 [3, 2048], P(None, 'dp')
- grad_out_weight: float32 [2048, 2048], P('tensor', 'dp')
- grad_gate_up_weight: float32 [2, 2048, 5632], P(None, 'dp', 'tensor')
- grad_down_weight: float32 [5632, 2048], P('tensor', 'dp')
- update_norm_gain: float32 [2, 2048], P(None, 'dp')
- update_norm_bias: float32 [2, 2048], P(None, 'dp')
- update_qkv_weight: float32 [3, 2048, 2048], P(None, 'dp', 'tensor')
- update_qkv_bias: float32 [3, 2048], P(None, 'dp')
- update_out_weight: float32 [2048, 2048], P('tensor', 'dp')
- update_gate_up_weight: float32 [2, 2048, 5632], P(None, 'dp', 'tensor')
- update_down_weight: float32 [5632, 2048], P('tensor', 'dp')
- new_first_norm_gain: float32 [2, 2048], P(None, 'dp')
- new_first_norm_bias: float32 [2, 2048], P(None, 'dp')
- new_first_qkv_weight: float32 [3, 2048, 2048], P(None, 'dp', 'tensor')
- new_first_qkv_bias: float32 [3, 2048], P(None, 'dp')
- new_first_out_weight: float32 [2048, 2048], P('tensor', 'dp')
- new_first_gate_up_weight: float32 [2, 2048, 5632], P(None, 'dp', 'tensor')
- new_first_down_weight: float32 [5632, 2048], P('tensor', 'dp')
- new_second_norm_gain: float32 [2, 2048], P(None, 'dp')
- new_second_norm_bias: float32 [2, 2048], P(None, 'dp')
- new_second_qkv_weight: float32 [3, 2048, 2048], P(None, 'dp', 'tensor')
- new_second_qkv_bias: float32 [3, 2048], P(None, 'dp')
- new_second_out_weight: float32 [2048, 2048], P('tensor', 'dp')
- new_second_gate_up_weight: float32 [2, 2048, 5632], P(None, 'dp', 'tensor')
- new_second_down_weight: float32 [5632, 2048], P('tensor', 'dp')
The draws below stay inside these ranges and needn't reach their ends.
Inputs may be any that keep to these rules, and one draw needn't show every extreme that they name: Row g of lengths lists the sequences of data group g in order; a zero is followed only by zeros. Each group's lengths sum to between 512 and 2048; some group sums to exactly 2048, and some sequence has exactly 1024 tokens.
All inputs are finite; a program needn't handle non-finite values.
Results may differ from the reference program's by a relative error of at most 0.02.
Values may be sent and summed in bfloat16 or wider, within the bound.
A program may use at most 384 MiB of HBM per device.

```python
import math
import jax
import jax.numpy as jnp
from jax import lax

D = 2048
HEADS = 32
HEAD_DIM = 64
FF = 5632
ROT = 16
GROUP_TOK = 2048
SEQ_MAX = 1024
SLOTS = 16
TOKENS = 16384
N_DP = 8


def draw_lengths(key, part):
    key_pick, key_total, key_length = jax.random.split(key, 3)
    full_group = jax.random.randint(key_pick, (), 0, N_DP)
    group_ids = jnp.arange(N_DP)
    group_totals = jax.random.randint(key_total, (N_DP,), GROUP_TOK // 4, GROUP_TOK + 1)
    group_totals = jnp.where(group_ids == full_group, GROUP_TOK, group_totals)
    drawn = jax.random.randint(key_length, (N_DP, SLOTS), SEQ_MAX // 8, SEQ_MAX + 1)
    leading = jnp.where(group_ids == full_group, SEQ_MAX, drawn[:, 0])
    drawn = jnp.concatenate([leading[:, None], drawn[:, 1:]], axis=1)
    preceding = jnp.cumsum(drawn, axis=1) - drawn
    remaining = jnp.maximum(group_totals[:, None] - preceding, 0)
    return jnp.minimum(drawn, remaining).astype(jnp.int32)


def shard_levels(stream_key, shape, cuts, least, largest):
    level, own = 1.0, jax.random.fold_in(stream_key, 6)
    for axis_at, shards_of in cuts:
        draws = jnp.exp(jax.random.uniform(jax.random.fold_in(own, axis_at), (shards_of,), jnp.float32, least / len(cuts), largest / len(cuts)))
        level = level * jnp.repeat(draws, shape[axis_at] // shards_of).reshape([-1 if axis == axis_at else 1 for axis in range(len(shape))])
    return level


def centred(rng, shape, scale, reach, pieces=(), held_as=jnp.bfloat16):
    loudness = shard_levels(rng, shape, pieces, -0.22, 0.18) if pieces else 1.0
    values = jax.random.normal(rng, shape, jnp.float32) * scale * loudness
    return jnp.minimum(jnp.maximum(values, -reach), reach).astype(held_as)


def setup_inputs(seed: int = 0) -> dict:
    seeds = jax.random.split(jax.random.key(seed), 25)
    tokens = centred(seeds[0], (TOKENS, D), 1.0, 6.0, ((0, 32),))
    out_grad = centred(seeds[1], (TOKENS, D), 1.0, 6.0, ((0, 32),))
    lengths = draw_lengths(jax.random.fold_in(seeds[24], 71), 0)
    norm_gain = jnp.clip(1.0 + 0.1 * jax.random.normal(seeds[3], (2, D), jnp.float32), 0.5, 1.5)
    norm_bias = centred(seeds[4], (2, D), 0.2, 1.2, ((1, 8),), jnp.float32)
    qkv_weight = centred(seeds[5], (3, D, D), D ** -0.5, 0.125, ((1, 8), (2, 4)), jnp.float32)
    qkv_bias = centred(seeds[6], (3, D), 0.2, 1.2, ((1, 8),), jnp.float32)
    out_weight = centred(seeds[7], (D, D), (D // 16) ** -0.5, 0.5, ((0, 4), (1, 8)), jnp.float32)
    gate_up_weight = centred(seeds[8], (2, D, FF), D ** -0.5, 0.125, ((1, 8), (2, 4)), jnp.float32)
    down_weight = centred(seeds[9], (FF, D), (FF // 4) ** -0.5, 0.15625, ((0, 4), (1, 8)), jnp.float32)
    first_norm_gain = centred(seeds[10], (2, D), 17.0, 100.0, ((1, 8),), jnp.float32)
    first_norm_bias = centred(seeds[11], (2, D), 17.0, 100.0, ((1, 8),), jnp.float32)
    first_qkv_weight = centred(seeds[12], (3, D, D), 7.0, 42.0, ((1, 8), (2, 4)), jnp.float32)
    first_qkv_bias = centred(seeds[13], (3, D), 7.0, 42.0, ((1, 8),), jnp.float32)
    first_out_weight = centred(seeds[14], (D, D), 5.0, 30.0, ((0, 4), (1, 8)), jnp.float32)
    first_gate_up_weight = centred(seeds[15], (2, D, FF), 10.0, 60.0, ((1, 8), (2, 4)), jnp.float32)
    first_down_weight = centred(seeds[16], (FF, D), 9.0, 54.0, ((0, 4), (1, 8)), jnp.float32)
    second_norm_gain = jnp.clip(jnp.exp(math.log(1800.0) - 1.0986123 * jax.random.uniform(seeds[17], (2, D), jnp.float32) ** shard_levels(seeds[17], (2, D), ((1, 8),), -0.2, 0.2)), 600.0, 1800.0)
    second_norm_bias = jnp.clip(jnp.exp(math.log(1800.0) - 1.0986123 * jax.random.uniform(seeds[18], (2, D), jnp.float32) ** shard_levels(seeds[18], (2, D), ((1, 8),), -0.2, 0.2)), 600.0, 1800.0)
    second_qkv_weight = jnp.clip(jnp.exp(math.log(300.0) - 1.0986123 * jax.random.uniform(seeds[19], (3, D, D), jnp.float32) ** shard_levels(seeds[19], (3, D, D), ((1, 8), (2, 4)), -0.2, 0.2)), 100.0, 300.0)
    second_qkv_bias = jnp.clip(jnp.exp(math.log(300.0) - 1.0986123 * jax.random.uniform(seeds[20], (3, D), jnp.float32) ** shard_levels(seeds[20], (3, D), ((1, 8),), -0.2, 0.2)), 100.0, 300.0)
    second_out_weight = jnp.clip(jnp.exp(math.log(150.0) - 1.0986123 * jax.random.uniform(seeds[21], (D, D), jnp.float32) ** shard_levels(seeds[21], (D, D), ((0, 4), (1, 8)), -0.2, 0.2)), 50.0, 150.0)
    second_gate_up_weight = jnp.clip(jnp.exp(math.log(750.0) - 1.0986123 * jax.random.uniform(seeds[22], (2, D, FF), jnp.float32) ** shard_levels(seeds[22], (2, D, FF), ((1, 8), (2, 4)), -0.2, 0.2)), 250.0, 750.0)
    second_down_weight = jnp.clip(jnp.exp(math.log(600.0) - 1.0986123 * jax.random.uniform(seeds[23], (FF, D), jnp.float32) ** shard_levels(seeds[23], (FF, D), ((0, 4), (1, 8)), -0.2, 0.2)), 200.0, 600.0)
    return {"tokens": tokens, "out_grad": out_grad, "lengths": lengths, "norm_gain": norm_gain, "norm_bias": norm_bias, "qkv_weight": qkv_weight, "qkv_bias": qkv_bias, "out_weight": out_weight, "gate_up_weight": gate_up_weight, "down_weight": down_weight, "first_norm_gain": first_norm_gain, "first_norm_bias": first_norm_bias, "first_qkv_weight": first_qkv_weight, "first_qkv_bias": first_qkv_bias, "first_out_weight": first_out_weight, "first_gate_up_weight": first_gate_up_weight, "first_down_weight": first_down_weight, "second_norm_gain": second_norm_gain, "second_norm_bias": second_norm_bias, "second_qkv_weight": second_qkv_weight, "second_qkv_bias": second_qkv_bias, "second_out_weight": second_out_weight, "second_gate_up_weight": second_gate_up_weight, "second_down_weight": second_down_weight}


norm_eps = 1e-05
rope_base = 10000.0
beta_one = 0.9
beta_two = 0.95
adam_eps = 1e-08
learn_rate = 0.01
weight_decay = 0.1
step_count = 10.0
masked_score = -1e+30
highest = lax.Precision.HIGHEST

@jax.custom_vjp
def low(v):
    return lax.optimization_barrier(v.astype(jnp.bfloat16)).astype(jnp.float32)

@jax.custom_vjp
def low_back(v):
    return v

def low_keep(v):
    return (low(v), None)

def low_pass(kept, grad):
    return (grad,)

def back_keep(v):
    return (v, None)

def back_low(kept, grad):
    return (low(grad),)
low.defvjp(low_keep, low_pass)
low_back.defvjp(back_keep, back_low)

def layout(seq_lengths, row_index):
    seq_ends = jnp.cumsum(seq_lengths).astype(jnp.int32)
    passed = row_index[:, None] >= seq_ends[None, :]
    segment = lax.optimization_barrier(jnp.sum(passed.astype(jnp.int32), axis=1)).astype(jnp.int32)
    seq_start = lax.optimization_barrier(jnp.sum(jnp.where(passed, seq_lengths[None, :], 0), axis=1)).astype(jnp.int32)
    live_total = jnp.sum(seq_lengths).astype(jnp.int32)
    live_rows = (row_index < live_total).astype(jnp.float32)
    return (segment, row_index - seq_start, live_rows)

def rotary_tables(position):
    half_rot = ROT // 2
    powers = jnp.arange(half_rot, dtype=jnp.float32) * (2.0 / ROT)
    inverse = jnp.power(rope_base, -powers)
    angles = position.astype(jnp.float32)[:, None] * inverse[None, :]
    return (jnp.cos(angles), jnp.sin(angles))

def rotate(values, cos_table, sine_table):
    half_rot = ROT // 2
    leading = values[..., :half_rot]
    trailing = values[..., half_rot:ROT]
    cos_part = cos_table[:, None, :]
    sine_part = sine_table[:, None, :]
    return jnp.concatenate([leading * cos_part - trailing * sine_part, trailing * cos_part + leading * sine_part, values[..., ROT:]], axis=-1)

def layer_norm(values, gain_row, shift_row):
    center = values - lax.optimization_barrier(jnp.mean(values, axis=-1, keepdims=True))
    spread = lax.optimization_barrier(jnp.mean(center * center, axis=-1, keepdims=True))
    return center * lax.rsqrt(spread + norm_eps) * gain_row + shift_row

def swiglu(gate_in, up_in):
    return jax.nn.silu(gate_in) * up_in

def adamw_update(weight_now, gradient, moment_one, moment_two, decay_rate):
    moment_one = beta_one * moment_one + (1.0 - beta_one) * gradient
    moment_two = beta_two * moment_two + (1.0 - beta_two) * gradient * gradient
    scaled_one = moment_one / (1.0 - beta_one ** step_count)
    scaled_two = moment_two / (1.0 - beta_two ** step_count)
    change = scaled_one / (jnp.sqrt(scaled_two) + adam_eps) + decay_rate * weight_now
    return (-learn_rate * change, moment_one, moment_two)

def group_forward(param_set, rows_in, seq_lengths):
    gain_pair = low(param_set[0])
    shift_pair = low(param_set[1])
    qkv_mats = low(param_set[2])
    qkv_shift = low(param_set[3])
    out_mat = low(param_set[4])
    gate_up_mats = low(param_set[5])
    down_mat = low(param_set[6])
    group_rows = rows_in.shape[0]
    row_index = jnp.arange(group_rows, dtype=jnp.int32)
    segment, position, live_rows = layout(seq_lengths, row_index)
    live_col = live_rows[:, None]
    cos_table, sine_table = rotary_tables(position)
    head_shape = (group_rows, HEADS, HEAD_DIM)
    normed_one = low(layer_norm(rows_in, gain_pair[0], shift_pair[0]))
    lin_query = low_back(jnp.dot(normed_one, qkv_mats[0], preferred_element_type=jnp.float32, precision=highest) + qkv_shift[0])
    lin_key = low_back(jnp.dot(normed_one, qkv_mats[1], preferred_element_type=jnp.float32, precision=highest) + qkv_shift[1])
    lin_value = low_back(jnp.dot(normed_one, qkv_mats[2], preferred_element_type=jnp.float32, precision=highest) + qkv_shift[2])
    query_heads = low(rotate(lin_query.reshape(head_shape), cos_table, sine_table))
    key_heads = low(rotate(lin_key.reshape(head_shape), cos_table, sine_table))
    value_heads = low(lin_value).reshape(head_shape)
    block_rows = min(512, group_rows)
    block_count = group_rows // block_rows
    score_scale = HEAD_DIM ** (-0.5)

    def attend(block_in):
        query_block, seg_block, idx_block = block_in
        scores = low_back(jnp.einsum('qhd,khd->hqk', query_block, key_heads, precision=highest) * score_scale)
        allowed = (seg_block[:, None] == segment[None, :]) & (row_index[None, :] <= idx_block[:, None])
        scores = jnp.where(allowed[None], scores, masked_score)
        row_peak = lax.optimization_barrier(jnp.max(scores, axis=-1, keepdims=True))
        weights = jnp.exp(scores - row_peak)
        prob_low = low(weights / lax.optimization_barrier(jnp.sum(weights, axis=-1, keepdims=True)))
        return jnp.einsum('hqk,khd->qhd', prob_low, value_heads, precision=highest)
    mixed_blocks = lax.map(jax.checkpoint(attend), (query_heads.reshape(block_count, block_rows, HEADS, HEAD_DIM), segment.reshape(block_count, block_rows), row_index.reshape(block_count, block_rows)))
    attended = low(low_back(mixed_blocks.reshape(group_rows, D)))
    attn_out = low_back(jnp.dot(attended, out_mat, preferred_element_type=jnp.float32, precision=highest))
    resid_one = rows_in + live_col * attn_out
    normed_two = low(layer_norm(resid_one, gain_pair[1], shift_pair[1]))
    gate_lin = low_back(jnp.dot(normed_two, gate_up_mats[0], preferred_element_type=jnp.float32, precision=highest))
    up_lin = low_back(jnp.dot(normed_two, gate_up_mats[1], preferred_element_type=jnp.float32, precision=highest))
    activated = low(swiglu(gate_lin, up_lin))
    mlp_out = low_back(jnp.dot(activated, down_mat, preferred_element_type=jnp.float32, precision=highest))
    return resid_one + live_col * mlp_out

def reference(tokens, out_grad, lengths, norm_gain, norm_bias, qkv_weight, qkv_bias, out_weight, gate_up_weight, down_weight, first_norm_gain, first_norm_bias, first_qkv_weight, first_qkv_bias, first_out_weight, first_gate_up_weight, first_down_weight, second_norm_gain, second_norm_bias, second_qkv_weight, second_qkv_bias, second_out_weight, second_gate_up_weight, second_down_weight):
    params = (norm_gain, norm_bias, qkv_weight, qkv_bias, out_weight, gate_up_weight, down_weight)
    rows_all = tokens.astype(jnp.float32).reshape(-1, GROUP_TOK, D)
    cotangent_all = out_grad.astype(jnp.float32).reshape(-1, GROUP_TOK, D)

    def one_group(grad_carry, group_in):
        rows_in, cotangent_in, seq_lengths = group_in

        def forward(param_set, rows_value):
            return group_forward(param_set, rows_value, seq_lengths)
        layer_value, pull_back = jax.vjp(forward, params, rows_in)
        grad_params, grad_rows = pull_back(cotangent_in)
        grad_carry = jax.tree.map(jnp.add, grad_carry, grad_params)
        return (grad_carry, (layer_value.astype(jnp.bfloat16), grad_rows.astype(jnp.bfloat16)))
    zero_grads = jax.tree.map(jnp.zeros_like, params)
    grad_sums, outputs = lax.scan(one_group, zero_grads, (rows_all, cotangent_all, lengths))
    layer_out = outputs[0].reshape(-1, D)
    input_grad = outputs[1].reshape(-1, D)
    firsts = (first_norm_gain, first_norm_bias, first_qkv_weight, first_qkv_bias, first_out_weight, first_gate_up_weight, first_down_weight)
    seconds = (second_norm_gain, second_norm_bias, second_qkv_weight, second_qkv_bias, second_out_weight, second_gate_up_weight, second_down_weight)
    decays = (0.0, 0.0, weight_decay, 0.0, weight_decay, weight_decay, weight_decay)
    new_change = []
    new_first = []
    new_second = []
    for weight_now, gradient, moment_one, moment_two, decay_rate in zip(params, grad_sums, firsts, seconds, decays):
        change, moment_next, square_next = adamw_update(weight_now, gradient, moment_one, moment_two, decay_rate)
        new_change.append(change)
        new_first.append(moment_next)
        new_second.append(square_next)
    return (layer_out, input_grad, grad_sums[0], grad_sums[1], grad_sums[2], grad_sums[3], grad_sums[4], grad_sums[5], grad_sums[6], new_change[0], new_change[1], new_change[2], new_change[3], new_change[4], new_change[5], new_change[6], new_first[0], new_first[1], new_first[2], new_first[3], new_first[4], new_first[5], new_first[6], new_second[0], new_second[1], new_second[2], new_second[3], new_second[4], new_second[5], new_second[6])
```

```python
import functools

import jax
import jax.numpy as jnp
from jax import lax
from jax.experimental import pallas as pl
from jax.experimental.pallas import tpu as pltpu
from jax.sharding import PartitionSpec as P

HEAD_DIM = 64
ROT = 16


norm_eps = 1e-05
rope_base = 10000.0
beta_one = 0.9
beta_two = 0.95
adam_eps = 1e-08
learn_rate = 0.01
weight_decay = 0.1
step_count = 10.0
masked_score = -1e30
contract_last = (((1,), (1,)), ((), ()))
contract_first = (((0,), (0,)), ((), ()))


def layout(seq_lengths, row_index):
    slot = jnp.arange(seq_lengths.shape[0])
    seq_ends = jnp.sum(jnp.where(slot[:, None] <= slot[None, :], seq_lengths[:, None], 0), axis=0)
    passed = row_index[:, None] >= seq_ends[None, :]
    segment = jnp.sum(passed.astype(jnp.int32), axis=1)
    seq_start = jnp.sum(jnp.where(passed, seq_lengths[None, :], 0), axis=1)
    live_total = jnp.sum(seq_lengths)
    live_rows = (row_index < live_total).astype(jnp.float32)
    return (seq_start, row_index - seq_start, live_rows)


def rotary_tables(position):
    half_rot = ROT // 2
    powers = jnp.arange(half_rot, dtype=jnp.float32) * (2.0 / ROT)
    inverse = jnp.power(rope_base, -powers)
    angles = position.astype(jnp.float32)[:, None] * inverse[None, :]
    return (jnp.cos(angles), jnp.sin(angles))


def rotate(values, cos_table, sine_table):
    half_rot = ROT // 2
    leading = values[..., :half_rot]
    trailing = values[..., half_rot:ROT]
    cos_part = cos_table[:, None, :]
    sine_part = sine_table[:, None, :]
    return jnp.concatenate(
        [
            leading * cos_part - trailing * sine_part,
            trailing * cos_part + leading * sine_part,
            values[..., ROT:],
        ],
        axis=-1,
    )


def layer_norm(values, gain_row, shift_row):
    center = values - jnp.mean(values, axis=-1, keepdims=True)
    spread = jnp.mean(center * center, axis=-1, keepdims=True)
    return center * lax.rsqrt(spread + norm_eps) * gain_row + shift_row


def swiglu(gate_in, up_in):
    return jax.nn.silu(gate_in) * up_in


def adamw_update(weight_now, gradient, moment_one, moment_two, decay_rate):
    moment_one = beta_one * moment_one + (1.0 - beta_one) * gradient
    moment_two = beta_two * moment_two + (1.0 - beta_two) * gradient * gradient
    scaled_one = moment_one / (1.0 - beta_one**step_count)
    scaled_two = moment_two / (1.0 - beta_two**step_count)
    change = scaled_one / (jnp.sqrt(scaled_two) + adam_eps) + decay_rate * weight_now
    return (-learn_rate * change, moment_one, moment_two)


HD=64
BQ=256
BK=256
NT=(((1,),(1,)),((),()))
def dotf(a,b,dims=None):
    if dims is None: return jnp.dot(a,b,preferred_element_type=jnp.float32)
    return lax.dot_general(a,b,dims,preferred_element_type=jnp.float32)

def place(block, rank, per):
    return (jnp.bitwise_xor(block // per, rank)) * per + block % per

def attn_fwd_kernel(per, sc_ref, q_ref, k_ref, vt_ref, start_ref, o_ref, lse_ref, m_s, l_s, acc_s, bias_s):
    i = pl.program_id(0)
    rank = sc_ref[0]
    heads = q_ref.shape[1] // HD
    low = lax.broadcasted_iota(jnp.int32, (BQ, 2*HD), 1) < HD
    qm = []
    for h in range(heads):
        pair = q_ref[:, (h//2)*2*HD:(h//2+1)*2*HD]
        keep = low if h % 2 == 0 else jnp.logical_not(low)
        qm.append(jnp.where(keep, pair, jnp.zeros_like(pair)))
    m_s[...] = jnp.full_like(m_s, -jnp.inf)
    l_s[...] = jnp.zeros_like(l_s)
    acc_s[...] = jnp.zeros_like(acc_s)
    start = start_ref[...]
    row = i*BQ + lax.broadcasted_iota(jnp.int32, (BK, BQ), 1)

    def step(kb, carry):
        col = kb*BK + lax.broadcasted_iota(jnp.int32, (BK, BQ), 0)
        bias_s[...] = jnp.where((col >= start) & (col <= row), 0.0, -1e30)
        at = pl.multiple_of(place(kb, rank, per)*BK, BK)
        for h in range(heads):
            kp = k_ref[pl.ds(at, BK), (h//2)*2*HD:(h//2+1)*2*HD]
            s = dotf(kp, qm[h], NT) + bias_s[...]
            m_old = m_s[h:h+1, :]
            m_new = jnp.maximum(m_old, jnp.max(s, axis=0, keepdims=True))
            alpha = jnp.exp(m_old - m_new)
            p = jnp.exp(s - m_new)
            l_s[h:h+1, :] = l_s[h:h+1, :]*alpha + jnp.sum(p, axis=0, keepdims=True)
            m_s[h:h+1, :] = m_new
            pv = dotf(vt_ref[h*HD:(h+1)*HD, pl.ds(at, BK)], p.astype(jnp.bfloat16))
            acc_s[h*HD:(h+1)*HD, :] = acc_s[h*HD:(h+1)*HD, :]*alpha + pv
        return carry
    lax.fori_loop(sc_ref[1+i], i*BQ//BK + BQ//BK if BQ>=BK else (i*BQ+BQ-1)//BK+1, step, 0)
    for h in range(heads):
        acc_s[h*HD:(h+1)*HD, :] = acc_s[h*HD:(h+1)*HD, :] / l_s[h:h+1, :]
    o_ref[...] = acc_s[...].T.astype(jnp.bfloat16)
    lse_ref[...] = m_s[...] + jnp.log(l_s[...])

def attn_fwd(sc, q, k, vt, start):
    rows, width = q.shape
    heads = width//HD
    nq = rows//BQ
    per = rows//4//BK
    perq = rows//4//BQ
    qmap = lambda i, sc: (place(i, sc[0], perq), 0)
    return pl.pallas_call(
        functools.partial(attn_fwd_kernel, per),
        grid_spec=pltpu.PrefetchScalarGridSpec(
            num_scalar_prefetch=1, grid=(nq,),
            in_specs=[pl.BlockSpec((BQ,width), qmap),
                      pl.BlockSpec((rows,width), lambda i, sc:(0,0)),
                      pl.BlockSpec((width,rows), lambda i, sc:(0,0)),
                      pl.BlockSpec((1,BQ), lambda i, sc:(0,i))],
            out_specs=[pl.BlockSpec((BQ,width), qmap),
                       pl.BlockSpec((heads,BQ), lambda i, sc:(0,i))],
            scratch_shapes=[pltpu.VMEM((heads,BQ),jnp.float32),pltpu.VMEM((heads,BQ),jnp.float32),
                            pltpu.VMEM((width,BQ),jnp.float32),pltpu.VMEM((BK,BQ),jnp.float32)]),
        out_shape=[jax.ShapeDtypeStruct((rows,width),jnp.bfloat16),jax.ShapeDtypeStruct((heads,rows),jnp.float32)],
        cost_estimate=pl.CostEstimate(flops=8*10**9,bytes_accessed=10*2**20,transcendentals=10**7),
        compiler_params=pltpu.CompilerParams(vmem_limit_bytes=40*2**20),
        name="attn_fwd",
    )(sc, q, k, vt, start)

def attn_bwd_kernel(per, nq, sc_ref, q_ref, do_ref, o_ref, k_ref, v_ref, kt_ref, start_ref, lse_ref, dq_ref, dk_ref, dv_ref, dq_s, bias_s):
    i = pl.program_id(0)
    rank = sc_ref[0]
    heads = q_ref.shape[1] // HD
    low = lax.broadcasted_iota(jnp.int32, (BQ, 2*HD), 1) < HD

    @pl.when(i == 0)
    def _():
        dk_ref[...] = jnp.zeros_like(dk_ref)
        dv_ref[...] = jnp.zeros_like(dv_ref)
    dq_s[...] = jnp.zeros_like(dq_s)
    qm, dm, delta = [], [], []
    for h in range(heads):
        cols = slice((h//2)*2*HD,(h//2+1)*2*HD)
        keep = low if h % 2 == 0 else jnp.logical_not(low)
        pair = q_ref[:, cols]
        qm.append(jnp.where(keep, pair, jnp.zeros_like(pair)))
        pair = do_ref[:, cols]
        pair = jnp.where(keep, pair, jnp.zeros_like(pair))
        dm.append(pair)
    prod = (do_ref[...].astype(jnp.float32) * o_ref[...].astype(jnp.float32)).T
    for h in range(heads):
        delta.append(jnp.sum(prod[h*HD:(h+1)*HD, :], axis=0, keepdims=True))
    start = start_ref[...]
    row = i*BQ + lax.broadcasted_iota(jnp.int32, (BK, BQ), 1)

    def step(kb, carry):
        col = kb*BK + lax.broadcasted_iota(jnp.int32, (BK, BQ), 0)
        bias_s[...] = jnp.where((col >= start) & (col <= row), 0.0, -1e30)
        at = pl.multiple_of(place(kb, rank, per)*BK, BK)
        for hp in range(heads//2):
            cols = slice(hp*2*HD,(hp+1)*2*HD)
            kp = k_ref[pl.ds(at, BK), cols]
            vp = v_ref[pl.ds(at, BK), cols]
            ps, dss = [], []
            for h in (2*hp, 2*hp+1):
                s = dotf(kp, qm[h], NT) + bias_s[...]
                p = jnp.exp(s - lse_ref[h:h+1, :])
                dp = dotf(vp, dm[h], NT)
                ds = (p * (dp - delta[h])).astype(jnp.bfloat16)
                ps.append(p.astype(jnp.bfloat16))
                dss.append(ds)
                dq_s[h*HD:(h+1)*HD, :] += dotf(kt_ref[h*HD:(h+1)*HD, pl.ds(at, BK)], ds)
            dv_ref[pl.ds(at, BK), cols] += dotf(ps[0], dm[2*hp]) + dotf(ps[1], dm[2*hp+1])
            dk_ref[pl.ds(at, BK), cols] += dotf(dss[0], qm[2*hp]) + dotf(dss[1], qm[2*hp+1])
        return carry
    lax.fori_loop(sc_ref[1+i], i*BQ//BK + BQ//BK if BQ>=BK else (i*BQ+BQ-1)//BK+1, step, 0)
    dq_ref[...] = dq_s[...].T

def attn_bwd(sc, q, do, o, k, v, kt, start, lse):
    rows, width = q.shape
    heads = width//HD
    nq = rows//BQ
    per = rows//4//BK
    perq = rows//4//BQ
    qmap = lambda i, sc: (place(i, sc[0], perq), 0)
    whole = lambda i, sc: (0, 0)
    return pl.pallas_call(
        functools.partial(attn_bwd_kernel, per, nq),
        grid_spec=pltpu.PrefetchScalarGridSpec(
            num_scalar_prefetch=1, grid=(nq,),
            in_specs=[pl.BlockSpec((BQ,width), qmap)]*3 + [pl.BlockSpec((rows,width), whole)]*2 + [
                      pl.BlockSpec((width,rows), whole),
                      pl.BlockSpec((1,BQ), lambda i, sc:(0,i)),
                      pl.BlockSpec((heads,BQ), lambda i, sc:(0,i))],
            out_specs=[pl.BlockSpec((BQ,width), qmap), pl.BlockSpec((rows,width), whole), pl.BlockSpec((rows,width), whole)],
            scratch_shapes=[pltpu.VMEM((width,BQ),jnp.float32),pltpu.VMEM((BK,BQ),jnp.float32)]),
        out_shape=[jax.ShapeDtypeStruct((rows,width),jnp.float32)]*3,
        cost_estimate=pl.CostEstimate(flops=20*10**9,bytes_accessed=20*2**20,transcendentals=10**7),
        compiler_params=pltpu.CompilerParams(vmem_limit_bytes=56*2**20),
        name="attn_bwd",
    )(sc, q, do, o, k, v, kt, start, lse)


def body(
    tokens,
    out_grad,
    lengths,
    norm_gain,
    norm_bias,
    qkv_weight,
    qkv_bias,
    out_weight,
    gate_up_weight,
    down_weight,
    first_norm_gain,
    first_norm_bias,
    first_qkv_weight,
    first_qkv_bias,
    first_out_weight,
    first_gate_up_weight,
    first_down_weight,
    second_norm_gain,
    second_norm_bias,
    second_qkv_weight,
    second_qkv_bias,
    second_out_weight,
    second_gate_up_weight,
    second_down_weight,
):
    low_type = jnp.bfloat16
    tensor_count = lax.axis_size("tensor")
    tensor_rank = lax.axis_index("tensor")
    row_count = tokens.shape[0]
    group_rows = row_count * tensor_count
    local_width = out_weight.shape[0]
    local_heads = local_width // HEAD_DIM
    score_scale = HEAD_DIM ** (-0.5)
    row_index = jnp.arange(group_rows, dtype=jnp.int32)
    segment, position, live_all = layout(lengths[0], row_index)
    own_start = tensor_rank * row_count
    live_own = lax.dynamic_slice_in_dim(live_all, own_start, row_count)[:, None]
    cos_table, sine_table = rotary_tables(position)
    column_start = tensor_rank * local_width
    head_shape = (group_rows, local_heads, HEAD_DIM)
    small_low = jnp.concatenate([norm_gain, norm_bias, qkv_bias], axis=0).astype(low_type)
    small_full = lax.all_gather(small_low, "dp", axis=1, tiled=True)
    qkv_full = lax.all_gather(qkv_weight.astype(low_type), "dp", axis=1, tiled=True)
    out_full = lax.all_gather(out_weight.astype(low_type), "dp", axis=1, tiled=True)
    gate_up_full = lax.all_gather(gate_up_weight.astype(low_type), "dp", axis=1, tiled=True)
    down_full = lax.all_gather(down_weight.astype(low_type), "dp", axis=1, tiled=True)
    norm_full = small_full[:4].astype(jnp.float32)
    gain_one, gain_two, shift_one, shift_two = norm_full[0], norm_full[1], norm_full[2], norm_full[3]
    bias_full = small_full[4:7]
    input_rows = tokens.astype(jnp.float32)
    normed_one = layer_norm(input_rows, gain_one, shift_one).astype(low_type)
    normed_all = lax.all_gather(normed_one, "tensor", axis=0, tiled=True)
    bias_local = lax.dynamic_slice_in_dim(bias_full, column_start, local_width, 1).astype(
        jnp.float32
    )
    lin_query = jnp.dot(normed_all, qkv_full[0], preferred_element_type=jnp.float32) + bias_local[0]
    lin_key = jnp.dot(normed_all, qkv_full[1], preferred_element_type=jnp.float32) + bias_local[1]
    lin_value = jnp.dot(normed_all, qkv_full[2], preferred_element_type=jnp.float32) + bias_local[2]
    query_heads = rotate(lin_query.reshape(head_shape), cos_table, sine_table).astype(low_type)
    key_heads = rotate(lin_key.reshape(head_shape), cos_table, sine_table).astype(low_type)
    value_heads = lin_value.reshape(head_shape).astype(low_type)
    flat = (group_rows, local_width)
    query_flat = query_heads.reshape(flat) * jnp.asarray(score_scale, low_type)
    key_flat = key_heads.reshape(flat)
    value_flat = value_heads.reshape(flat)
    starts = segment[None, :]
    table = jnp.concatenate([jnp.zeros((1,), jnp.int32), segment[::BQ] // BK])
    attended, lse = attn_fwd(table, query_flat, key_flat, value_flat.T, starts)
    attn_rows = lax.psum_scatter(
        jnp.dot(attended, out_full, preferred_element_type=jnp.float32).astype(low_type),
        "tensor",
        scatter_dimension=0,
        tiled=True,
    )
    resid_one = input_rows + live_own * attn_rows
    normed_two = layer_norm(resid_one, gain_two, shift_two).astype(low_type)
    normed_mlp = lax.all_gather(normed_two, "tensor", axis=0, tiled=True)
    gate_lin = jnp.dot(normed_mlp, gate_up_full[0], preferred_element_type=jnp.float32)
    up_lin = jnp.dot(normed_mlp, gate_up_full[1], preferred_element_type=jnp.float32)
    activated = swiglu(gate_lin, up_lin).astype(low_type)
    mlp_rows = lax.psum_scatter(
        jnp.dot(activated, down_full, preferred_element_type=jnp.float32).astype(low_type),
        "tensor",
        scatter_dimension=0,
        tiled=True,
    )
    layer_out = (resid_one + live_own * mlp_rows).astype(low_type)
    cotangent_rows = out_grad.astype(jnp.float32)
    grad_mlp_rows = (cotangent_rows * live_own).astype(low_type)
    grad_mlp_all = lax.all_gather(grad_mlp_rows, "tensor", axis=0, tiled=True)
    grad_hidden = lax.dot_general(
        grad_mlp_all, down_full, contract_last, preferred_element_type=jnp.float32
    )
    grad_down = lax.dot_general(
        activated, grad_mlp_all, contract_first, preferred_element_type=jnp.float32
    )
    unused_value, swiglu_pull = jax.vjp(swiglu, gate_lin, up_lin)
    grad_gate, grad_up = swiglu_pull(grad_hidden)
    grad_gate = grad_gate.astype(low_type)
    grad_up = grad_up.astype(low_type)
    grad_gate_up = jnp.stack(
        [
            lax.dot_general(
                normed_mlp, grad_gate, contract_first, preferred_element_type=jnp.float32
            ),
            lax.dot_general(
                normed_mlp, grad_up, contract_first, preferred_element_type=jnp.float32
            ),
        ]
    )
    grad_normed_two = lax.psum_scatter(
        (lax.dot_general(
            grad_gate, gate_up_full[0], contract_last, preferred_element_type=jnp.float32
        )
        + lax.dot_general(
            grad_up, gate_up_full[1], contract_last, preferred_element_type=jnp.float32
        )).astype(low_type),
        "tensor",
        scatter_dimension=0,
        tiled=True,
    )
    unused_norm, norm_pull_two = jax.vjp(layer_norm, resid_one, gain_two, shift_two)
    grad_resid_norm, grad_gain_two, grad_shift_two = norm_pull_two(grad_normed_two.astype(jnp.float32))
    grad_resid_one = cotangent_rows + grad_resid_norm
    grad_gate_up_own, grad_down_own = (
        lax.psum_scatter(grad_gate_up.astype(low_type), "dp", scatter_dimension=1, tiled=True).astype(jnp.float32),
        lax.psum_scatter(grad_down.astype(low_type), "dp", scatter_dimension=1, tiled=True).astype(jnp.float32),
    )
    grad_attn_rows = (grad_resid_one * live_own).astype(low_type)
    grad_attn_all = lax.all_gather(grad_attn_rows, "tensor", axis=0, tiled=True)
    grad_out = lax.dot_general(
        attended, grad_attn_all, contract_first, preferred_element_type=jnp.float32
    )
    grad_attended = lax.dot_general(
        grad_attn_all, out_full, contract_last, preferred_element_type=jnp.float32
    ).astype(low_type)
    grad_query_rot, grad_key_rot, grad_value = attn_bwd(
        table, query_flat, grad_attended, attended, key_flat, value_flat, key_flat.T, starts, lse
    )
    grad_query_rot = (grad_query_rot * score_scale).reshape(head_shape)
    grad_key_rot = grad_key_rot.reshape(head_shape)
    grad_lin_query = (
        rotate(grad_query_rot, cos_table, -sine_table)
        .reshape(group_rows, local_width)
        .astype(low_type)
    )
    grad_lin_key = (
        rotate(grad_key_rot, cos_table, -sine_table)
        .reshape(group_rows, local_width)
        .astype(low_type)
    )
    grad_lin_value = grad_value.reshape(group_rows, local_width).astype(low_type)
    grad_qkv = jnp.stack(
        [
            lax.dot_general(
                normed_all, grad_lin_query, contract_first, preferred_element_type=jnp.float32
            ),
            lax.dot_general(
                normed_all, grad_lin_key, contract_first, preferred_element_type=jnp.float32
            ),
            lax.dot_general(
                normed_all, grad_lin_value, contract_first, preferred_element_type=jnp.float32
            ),
        ]
    )
    grad_bias_local = jnp.stack(
        [
            jnp.sum(grad_lin_query, axis=0, dtype=jnp.float32),
            jnp.sum(grad_lin_key, axis=0, dtype=jnp.float32),
            jnp.sum(grad_lin_value, axis=0, dtype=jnp.float32),
        ]
    )
    summed = lax.dot_general(
        grad_lin_query, qkv_full[0], contract_last, preferred_element_type=jnp.float32
    )
    summed = summed + lax.dot_general(
        grad_lin_key, qkv_full[1], contract_last, preferred_element_type=jnp.float32
    )
    grad_normed_one = lax.psum_scatter(
        (
            summed
            + lax.dot_general(
                grad_lin_value, qkv_full[2], contract_last, preferred_element_type=jnp.float32
            )
        ).astype(low_type),
        "tensor",
        scatter_dimension=0,
        tiled=True,
    )
    unused_first, norm_pull_one = jax.vjp(layer_norm, input_rows, gain_one, shift_one)
    grad_input_norm, grad_gain_one, grad_shift_one = norm_pull_one(grad_normed_one.astype(jnp.float32))
    input_grad = (grad_resid_one + grad_input_norm).astype(low_type)
    bias_placed = lax.dynamic_update_slice(
        jnp.zeros((3, qkv_full.shape[1]), jnp.float32),
        grad_bias_local,
        (jnp.int32(0), column_start),
    )
    small_local = jnp.concatenate(
        [
            jnp.stack([grad_gain_one, grad_gain_two]),
            jnp.stack([grad_shift_one, grad_shift_two]),
            bias_placed,
        ],
        axis=0,
    )
    small_sum = lax.psum(small_local, "tensor")
    grad_qkv_own, grad_out_own, small_own = (
        lax.psum_scatter(grad_qkv.astype(low_type), "dp", scatter_dimension=1, tiled=True).astype(jnp.float32),
        lax.psum_scatter(grad_out.astype(low_type), "dp", scatter_dimension=1, tiled=True).astype(jnp.float32),
        lax.psum_scatter(small_sum, "dp", scatter_dimension=1, tiled=True),
    )
    own_grads = (
        small_own[0:2],
        small_own[2:4],
        grad_qkv_own,
        small_own[4:7],
        grad_out_own,
        grad_gate_up_own,
        grad_down_own,
    )
    masters = (norm_gain, norm_bias, qkv_weight, qkv_bias, out_weight, gate_up_weight, down_weight)
    firsts = (
        first_norm_gain,
        first_norm_bias,
        first_qkv_weight,
        first_qkv_bias,
        first_out_weight,
        first_gate_up_weight,
        first_down_weight,
    )
    seconds = (
        second_norm_gain,
        second_norm_bias,
        second_qkv_weight,
        second_qkv_bias,
        second_out_weight,
        second_gate_up_weight,
        second_down_weight,
    )
    decays = (0.0, 0.0, weight_decay, 0.0, weight_decay, weight_decay, weight_decay)
    new_change = []
    new_first = []
    new_second = []
    for weight_now, gradient, moment_one, moment_two, decay_rate in zip(
        masters, own_grads, firsts, seconds, decays
    ):
        change, moment_next, square_next = adamw_update(
            weight_now, gradient, moment_one, moment_two, decay_rate
        )
        new_change.append(change)
        new_first.append(moment_next)
        new_second.append(square_next)
    return (
        (layer_out, input_grad)
        + own_grads
        + tuple(new_change)
        + tuple(new_first)
        + tuple(new_second)
    )


def solution(mesh):
    return jax.shard_map(
        body,
        mesh=mesh,
        in_specs=(
            P(("dp", "tensor"), None),
            P(("dp", "tensor"), None),
            P("dp", None),
            P(None, "dp"),
            P(None, "dp"),
            P(None, "dp", "tensor"),
            P(None, "dp"),
            P("tensor", "dp"),
            P(None, "dp", "tensor"),
            P("tensor", "dp"),
            P(None, "dp"),
            P(None, "dp"),
            P(None, "dp", "tensor"),
            P(None, "dp"),
            P("tensor", "dp"),
            P(None, "dp", "tensor"),
            P("tensor", "dp"),
            P(None, "dp"),
            P(None, "dp"),
            P(None, "dp", "tensor"),
            P(None, "dp"),
            P("tensor", "dp"),
            P(None, "dp", "tensor"),
            P("tensor", "dp"),
        ),
        out_specs=(
            P(("dp", "tensor"), None),
            P(("dp", "tensor"), None),
            P(None, "dp"),
            P(None, "dp"),
            P(None, "dp", "tensor"),
            P(None, "dp"),
            P("tensor", "dp"),
            P(None, "dp", "tensor"),
            P("tensor", "dp"),
            P(None, "dp"),
            P(None, "dp"),
            P(None, "dp", "tensor"),
            P(None, "dp"),
            P("tensor", "dp"),
            P(None, "dp", "tensor"),
            P("tensor", "dp"),
            P(None, "dp"),
            P(None, "dp"),
            P(None, "dp", "tensor"),
            P(None, "dp"),
            P("tensor", "dp"),
            P(None, "dp", "tensor"),
            P("tensor", "dp"),
            P(None, "dp"),
            P(None, "dp"),
            P(None, "dp", "tensor"),
            P(None, "dp"),
            P("tensor", "dp"),
            P(None, "dp", "tensor"),
            P("tensor", "dp"),
        ),
        check_vma=False,
    )
```

```python
import functools

import jax
import jax.numpy as jnp
from jax import lax
from jax.experimental import pallas as pl
from jax.experimental.pallas import tpu as pltpu
from jax.sharding import PartitionSpec as P

HEAD_DIM = 64
ROT = 16
PAIR = 2 * HEAD_DIM
BLOCK = 256

norm_eps = 1e-05
rope_base = 10000.0
beta_one = 0.9
beta_two = 0.95
adam_eps = 1e-08
learn_rate = 0.01
weight_decay = 0.1
step_count = 10.0
masked_score = -1e30
contract_last = (((1,), (1,)), ((), ()))
contract_first = (((0,), (0,)), ((), ()))
low_type = jnp.bfloat16
MIB = 2**20


def layout(seq_lengths, row_index):
    slot = jnp.arange(seq_lengths.shape[0])
    seq_ends = jnp.sum(
        jnp.where(slot[:, None] <= slot[None, :], seq_lengths[:, None], 0), axis=0
    )
    passed = row_index[:, None] >= seq_ends[None, :]
    seq_start = jnp.sum(jnp.where(passed, seq_lengths[None, :], 0), axis=1)
    live_rows = (row_index < jnp.sum(seq_lengths)).astype(jnp.float32)
    return (seq_start, live_rows)


def rotary_tables(position):
    half_rot = ROT // 2
    lane = jnp.arange(PAIR, dtype=jnp.int32) % HEAD_DIM
    powers = (lane % half_rot).astype(jnp.float32) * (2.0 / ROT)
    inverse = jnp.power(rope_base, -powers)
    angles = position.astype(jnp.float32)[:, None] * inverse[None, :]
    cos_part, sine_part = jnp.cos(angles), jnp.sin(angles)
    lane = lane[None, :]
    keep = jnp.where(lane < ROT, cos_part, 1.0)
    above = jnp.where(lane < half_rot, -sine_part, 0.0)
    below = jnp.where((lane >= half_rot) & (lane < ROT), sine_part, 0.0)
    return (keep, above, below)


def dot32(a, b, dims=None):
    if dims is None:
        return jnp.dot(a, b, preferred_element_type=jnp.float32)
    return lax.dot_general(a, b, dims, preferred_element_type=jnp.float32)


def turn(values, keep, above, below):
    up = pltpu.roll(values, PAIR - ROT // 2, 1)
    down = pltpu.roll(values, ROT // 2, 1)
    return values * keep + up * above + down * below


def turn_back(values, keep, above, below):
    up = pltpu.roll(values, PAIR - ROT // 2, 1)
    down = pltpu.roll(values, ROT // 2, 1)
    return values * keep - up * above - down * below


def adamw_update(weight_now, gradient, moment_one, moment_two, decay_rate):
    moment_one = beta_one * moment_one + (1.0 - beta_one) * gradient
    moment_two = beta_two * moment_two + (1.0 - beta_two) * gradient * gradient
    scaled_one = moment_one / (1.0 - beta_one**step_count)
    scaled_two = moment_two / (1.0 - beta_two**step_count)
    change = scaled_one / (jnp.sqrt(scaled_two) + adam_eps) + decay_rate * weight_now
    return (-learn_rate * change, moment_one, moment_two)


def cost(flops, moved, exps=0):
    return pl.CostEstimate(flops=int(flops) // 16, bytes_accessed=int(moved) // 16, transcendentals=int(exps) // 16)


def params(limit):
    return pltpu.CompilerParams(vmem_limit_bytes=limit * MIB)


ANY = pl.BlockSpec(memory_space=pl.ANY)


def stream(refs, buf, sem):
    step = pl.program_id(0)

    def fetch(j, slot):
        pltpu.make_async_copy(refs[j], buf.at[slot], sem.at[slot]).start()

    @pl.when(step == 0)
    def _():
        fetch(0, 0)

    for j in range(1, len(refs)):

        @pl.when(step == j - 1)
        def _(j=j):
            fetch(j, j % 2)

    now = step % 2
    pltpu.make_async_copy(refs[0], buf.at[now], sem.at[now]).wait()
    return now


def norm_one_kernel(x_ref, norm_ref, h_ref):
    x = x_ref[...].astype(jnp.float32)
    c = x - jnp.mean(x, axis=-1, keepdims=True)
    s = lax.rsqrt(jnp.mean(c * c, axis=-1, keepdims=True) + norm_eps)
    h_ref[...] = (c * s * norm_ref[0:1, :] + norm_ref[2:3, :]).astype(low_type)


def norm_one(x, norm):
    rows, model = x.shape
    block = 64
    row = pl.BlockSpec((block, model), lambda r: (r, 0))
    return pl.pallas_call(
        norm_one_kernel,
        grid=(rows // block,),
        in_specs=[row, pl.BlockSpec(norm.shape, lambda r: (0, 0))],
        out_specs=row,
        out_shape=jax.ShapeDtypeStruct((rows, model), low_type),
        cost_estimate=cost(10 * rows * model, 4 * rows * model),
        compiler_params=params(16),
        name="norm_one",
    )(x, norm)


def qkv_kernel(scale, count, w_ref, bias_ref, keep_ref, above_ref, below_ref, *rest):
    h_ref, q_ref, k_ref, v_ref, kt_ref, vt_ref, buf, sem = rest[count:]
    now = stream(rest[:count], buf, sem)
    h = buf[now]
    h_ref[...] = h
    keep, above, below = keep_ref[...], above_ref[...], below_ref[...]
    width = q_ref.shape[1]
    lin = dot32(h, w_ref[0]) + bias_ref[0]
    for c in range(0, width, PAIR):
        u = turn(lin[:, c : c + PAIR], keep, above, below)
        q_ref[:, c : c + PAIR] = (u.astype(low_type) * scale).astype(low_type)
    lin = dot32(h, w_ref[1]) + bias_ref[1]
    for c in range(0, width, PAIR):
        u = turn(lin[:, c : c + PAIR], keep, above, below)
        k_ref[:, c : c + PAIR] = u.astype(low_type)
        kt_ref[c : c + PAIR, :] = u.T.astype(low_type)
    lin = dot32(h, w_ref[2]) + bias_ref[2]
    v_ref[...] = lin.astype(low_type)
    vt_ref[...] = lin.T.astype(low_type)


def qkv_all(blocks, w, bias, tables):
    count = len(blocks)
    rows, model = blocks[0].shape
    width = w.shape[2]
    total = rows * count
    row = lambda n: pl.BlockSpec((rows, n), lambda i: (i, 0))
    col = pl.BlockSpec((width, rows), lambda i: (0, i))
    once = pl.Buffered(1)
    flat = jax.ShapeDtypeStruct((total, width), low_type)
    turned = jax.ShapeDtypeStruct((width, total), low_type)
    return pl.pallas_call(
        functools.partial(qkv_kernel, HEAD_DIM ** (-0.5), count),
        grid=(count,),
        in_specs=[
            pl.BlockSpec(w.shape, lambda i: (0, 0, 0), pipeline_mode=once),
            pl.BlockSpec(bias.shape, lambda i: (0, 0, 0)),
            row(PAIR),
            row(PAIR),
            row(PAIR),
        ]
        + [ANY] * count,
        out_specs=[row(model), row(width), row(width), row(width), col, col],
        out_shape=[jax.ShapeDtypeStruct((total, model), low_type), flat, flat, flat, turned, turned],
        scratch_shapes=[pltpu.VMEM((2, rows, model), low_type), pltpu.SemaphoreType.DMA((2,))],
        cost_estimate=cost(6 * total * model * width, 6 * model * width + 10 * total * model),
        compiler_params=params(48),
        name="qkv",
    )(w, bias, *tables, *blocks)


def place(block, rank, per):
    return jnp.bitwise_xor(block // per, rank) * per + block % per


def attn_fwd_kernel(per, table_ref, q_ref, k_ref, vt_ref, start_ref, o_ref, lse_ref, m_s, l_s, acc_s, bias_s):
    i = pl.program_id(0)
    rank = table_ref[0]
    heads = q_ref.shape[1] // HEAD_DIM
    first = lax.broadcasted_iota(jnp.int32, (BLOCK, PAIR), 1) < HEAD_DIM
    queries = []
    for h in range(heads):
        pair = q_ref[:, (h // 2) * PAIR : (h // 2 + 1) * PAIR]
        keep = first if h % 2 == 0 else jnp.logical_not(first)
        queries.append(jnp.where(keep, pair, jnp.zeros_like(pair)))
    m_s[...] = jnp.full_like(m_s, -jnp.inf)
    l_s[...] = jnp.zeros_like(l_s)
    acc_s[...] = jnp.zeros_like(acc_s)
    start = start_ref[...]
    row = i * BLOCK + lax.broadcasted_iota(jnp.int32, (BLOCK, BLOCK), 1)

    def step(kb, carry):
        col = kb * BLOCK + lax.broadcasted_iota(jnp.int32, (BLOCK, BLOCK), 0)
        bias_s[...] = jnp.where((col >= start) & (col <= row), 0.0, masked_score)
        at = pl.ds(pl.multiple_of(place(kb, rank, per) * BLOCK, BLOCK), BLOCK)
        for h in range(heads):
            own = slice(h * HEAD_DIM, (h + 1) * HEAD_DIM)
            keys = k_ref[at, (h // 2) * PAIR : (h // 2 + 1) * PAIR]
            s = dot32(keys, queries[h], contract_last) + bias_s[...]
            m_old = m_s[h : h + 1, :]
            m_new = jnp.maximum(m_old, jnp.max(s, axis=0, keepdims=True))
            alpha = jnp.exp(m_old - m_new)
            p = jnp.exp(s - m_new)
            l_s[h : h + 1, :] = l_s[h : h + 1, :] * alpha + jnp.sum(p, axis=0, keepdims=True)
            m_s[h : h + 1, :] = m_new
            mixed = dot32(vt_ref[own, at], p.astype(low_type))
            acc_s[own, :] = acc_s[own, :] * alpha + mixed
        return carry

    lax.fori_loop(table_ref[1 + i], i + 1, step, 0)
    for h in range(heads):
        own = slice(h * HEAD_DIM, (h + 1) * HEAD_DIM)
        acc_s[own, :] = acc_s[own, :] / l_s[h : h + 1, :]
    o_ref[...] = acc_s[...].T.astype(low_type)
    lse_ref[0] = m_s[...] + jnp.log(l_s[...])


def attn_fwd(half, slots, table, q, k, vt, start):
    rows, width = q.shape
    part = width // 2
    heads = part // HEAD_DIM
    count = rows // BLOCK
    per = rows // slots // BLOCK
    at = lambda i, t: place(i, t[0], per)
    return pl.pallas_call(
        functools.partial(attn_fwd_kernel, per),
        grid_spec=pltpu.PrefetchScalarGridSpec(
            num_scalar_prefetch=1,
            grid=(count,),
            in_specs=[
                pl.BlockSpec((BLOCK, part), lambda i, t: (at(i, t), half)),
                pl.BlockSpec((rows, part), lambda i, t: (0, half)),
                pl.BlockSpec((part, rows), lambda i, t: (half, 0)),
                pl.BlockSpec((1, BLOCK), lambda i, t: (0, at(i, t))),
            ],
            out_specs=[
                pl.BlockSpec((BLOCK, part), lambda i, t: (at(i, t), 0)),
                pl.BlockSpec((1, heads, BLOCK), lambda i, t: (at(i, t), 0, 0)),
            ],
            scratch_shapes=[
                pltpu.VMEM((heads, BLOCK), jnp.float32),
                pltpu.VMEM((heads, BLOCK), jnp.float32),
                pltpu.VMEM((part, BLOCK), jnp.float32),
                pltpu.VMEM((BLOCK, BLOCK), jnp.float32),
            ],
        ),
        out_shape=[
            jax.ShapeDtypeStruct((rows, part), low_type),
            jax.ShapeDtypeStruct((count, heads, BLOCK), jnp.float32),
        ],
        cost_estimate=cost(20 * rows * rows * part // 2, 8 * rows * part, 8 * rows * rows // 4),
        compiler_params=params(40),
        name="attn_fwd",
    )(table, q, k, vt, start)


def attn_bwd_kernel(per, slots, table_ref, q_ref, do_ref, o_ref, k_ref, v_ref, kt_ref, start_ref, lse_ref,
                    keep_ref, above_ref, below_ref, dq_ref, dk_ref, dv_ref, dq_s, dk_s, dv_s, bias_s):
    i = pl.program_id(0)
    rank = table_ref[0]
    width = q_ref.shape[1]
    heads = width // HEAD_DIM
    first = lax.broadcasted_iota(jnp.int32, (BLOCK, PAIR), 1) < HEAD_DIM

    @pl.when(i == 0)
    def _():
        dk_s[...] = jnp.zeros_like(dk_s)
        dv_s[...] = jnp.zeros_like(dv_s)

    dq_s[...] = jnp.zeros_like(dq_s)
    queries, cotangents, inner = [], [], []
    product = (do_ref[...].astype(jnp.float32) * o_ref[...].astype(jnp.float32)).T
    for h in range(heads):
        cols = slice((h // 2) * PAIR, (h // 2 + 1) * PAIR)
        keep = first if h % 2 == 0 else jnp.logical_not(first)
        pair = q_ref[:, cols]
        queries.append(jnp.where(keep, pair, jnp.zeros_like(pair)))
        pair = do_ref[:, cols]
        cotangents.append(jnp.where(keep, pair, jnp.zeros_like(pair)))
        inner.append(jnp.sum(product[h * HEAD_DIM : (h + 1) * HEAD_DIM, :], axis=0, keepdims=True))
    start = start_ref[...]
    row = i * BLOCK + lax.broadcasted_iota(jnp.int32, (BLOCK, BLOCK), 1)

    def step(kb, carry):
        col = kb * BLOCK + lax.broadcasted_iota(jnp.int32, (BLOCK, BLOCK), 0)
        bias_s[...] = jnp.where((col >= start) & (col <= row), 0.0, masked_score)
        at = pl.ds(pl.multiple_of(place(kb, rank, per) * BLOCK, BLOCK), BLOCK)
        for pair in range(heads // 2):
            cols = slice(pair * PAIR, (pair + 1) * PAIR)
            keys, values = k_ref[at, cols], v_ref[at, cols]
            probs, scores = [], []
            for h in (2 * pair, 2 * pair + 1):
                own = slice(h * HEAD_DIM, (h + 1) * HEAD_DIM)
                s = dot32(keys, queries[h], contract_last) + bias_s[...]
                p = jnp.exp(s - lse_ref[0, h : h + 1, :])
                dp = dot32(values, cotangents[h], contract_last)
                ds = (p * (dp - inner[h])).astype(low_type)
                probs.append(p.astype(low_type))
                scores.append(ds)
                dq_s[own, :] += dot32(kt_ref[own, at], ds)
            dv_s[at, cols] += dot32(probs[0], cotangents[2 * pair]) + dot32(probs[1], cotangents[2 * pair + 1])
            dk_s[at, cols] += dot32(scores[0], queries[2 * pair]) + dot32(scores[1], queries[2 * pair + 1])
        return carry

    lax.fori_loop(table_ref[1 + i], i + 1, step, 0)
    dq = dq_s[...].T * (HEAD_DIM ** (-0.5))
    here = pl.ds(pl.multiple_of(place(i, rank, per) * BLOCK, BLOCK), BLOCK)
    for c in range(0, width, PAIR):
        dq_ref[:, c : c + PAIR] = turn_back(
            dq[:, c : c + PAIR], keep_ref[here, :], above_ref[here, :], below_ref[here, :]
        ).astype(low_type)

    @pl.when(i == pl.num_programs(0) - 1)
    def _():
        @pl.loop(0, dk_s.shape[0] // BLOCK)
        def _(b):
            at = pl.ds(pl.multiple_of(b * BLOCK, BLOCK), BLOCK)
            for c in range(0, width, PAIR):
                cols = slice(c, c + PAIR)
                dk_ref[at, cols] = turn_back(
                    dk_s[at, cols], keep_ref[at, :], above_ref[at, :], below_ref[at, :]
                ).astype(low_type)
                dv_ref[at, cols] = dv_s[at, cols].astype(low_type)


def attn_bwd(half, slots, table, q, do, o, k, v, kt, start, lse, tables):
    rows, width = q.shape
    part = width // 2
    heads = part // HEAD_DIM
    count = rows // BLOCK
    per = rows // slots // BLOCK
    at = lambda i, t: place(i, t[0], per)
    whole = pl.BlockSpec((rows, part), lambda i, t: (0, half))
    turns = pl.BlockSpec((rows, PAIR), lambda i, t: (0, 0))
    result = pl.BlockSpec((rows, part), lambda i, t: (0, 0))
    return pl.pallas_call(
        functools.partial(attn_bwd_kernel, per, slots),
        grid_spec=pltpu.PrefetchScalarGridSpec(
            num_scalar_prefetch=1,
            grid=(count,),
            in_specs=[
                pl.BlockSpec((BLOCK, part), lambda i, t: (at(i, t), half)),
                pl.BlockSpec((BLOCK, part), lambda i, t: (at(i, t), half)),
                pl.BlockSpec((BLOCK, part), lambda i, t: (at(i, t), 0)),
                whole,
                whole,
                pl.BlockSpec((part, rows), lambda i, t: (half, 0)),
                pl.BlockSpec((1, BLOCK), lambda i, t: (0, at(i, t))),
                pl.BlockSpec((1, heads, BLOCK), lambda i, t: (at(i, t), 0, 0)),
                turns,
                turns,
                turns,
            ],
            out_specs=[pl.BlockSpec((BLOCK, part), lambda i, t: (at(i, t), 0)), result, result],
            scratch_shapes=[
                pltpu.VMEM((part, BLOCK), jnp.float32),
                pltpu.VMEM((rows, part), jnp.float32),
                pltpu.VMEM((rows, part), jnp.float32),
                pltpu.VMEM((BLOCK, BLOCK), jnp.float32),
            ],
        ),
        out_shape=[jax.ShapeDtypeStruct((rows, part), low_type)] * 3,
        cost_estimate=cost(25 * rows * rows * part // 2, 16 * rows * part, 8 * rows * rows // 4),
        compiler_params=params(48),
        name="attn_bwd",
    )(table, q, do, o, k, v, kt, start, lse, *tables)


def sum_nt_kernel(count, *refs):
    w_ref, out_ref = refs[count:]
    total = None
    for n in range(count):
        depth = refs[n].shape[1]
        per = w_ref.shape[2] // depth
        cols = slice((n % per) * depth, (n % per + 1) * depth)
        term = dot32(refs[n][...], w_ref[n // per, :, cols], contract_last)
        total = term if total is None else total + term
    out_ref[...] = total.astype(out_ref.dtype)


def sum_nt(lefts, w, slot, rows):
    stacked, model, depth = w.shape
    tile = 512
    return pl.pallas_call(
        functools.partial(sum_nt_kernel, len(lefts)),
        grid=(model // tile,),
        in_specs=[pl.BlockSpec((rows, left.shape[1]), lambda n: (slot, 0)) for left in lefts]
        + [pl.BlockSpec((stacked, tile, depth), lambda n: (0, n, 0))],
        out_specs=pl.BlockSpec((rows, tile), lambda n: (0, n)),
        out_shape=jax.ShapeDtypeStruct((rows, model), low_type),
        cost_estimate=cost(2 * stacked * rows * model * depth, 2 * stacked * model * depth + 2 * rows * model),
        compiler_params=params(48),
        name="sum_nt",
    )(*lefts, w)


def weight_grad_kernel(left_ref, right_ref, *rest):
    rest[-1][0] = dot32(left_ref[...], right_ref[...], contract_first).astype(low_type)


def weight_grad(left, right, index, count, held=None):
    rows, model = left.shape
    depth = right.shape[1]
    tile = 512
    extra = [] if held is None else [held]
    return pl.pallas_call(
        weight_grad_kernel,
        grid=(model // tile,),
        in_specs=[
            pl.BlockSpec((rows, tile), lambda n: (0, n)),
            pl.BlockSpec((rows, depth), lambda n: (0, 0), pipeline_mode=pl.Buffered(1)),
        ]
        + [ANY] * len(extra),
        out_specs=pl.BlockSpec((1, tile, depth), lambda n: (index, n, 0)),
        out_shape=jax.ShapeDtypeStruct((count, model, depth), low_type),
        input_output_aliases={2: 0} if extra else {},
        cost_estimate=cost(2 * rows * model * depth, 2 * rows * (model + depth) + 2 * model * depth),
        compiler_params=params(48),
        name="weight_grad",
    )(left, right, *extra)


def qkv_grad_kernel(*refs):
    left_ref, rights, (out_ref, sum_ref) = refs[0], refs[1:-2], refs[-2:]
    part = rights[0].shape[1]

    @pl.when(pl.program_id(0) == 0)
    def _():
        for n, right in enumerate(rights):
            sum_ref[n // 2 : n // 2 + 1, (n % 2) * part : (n % 2 + 1) * part] = jnp.sum(
                right[...].astype(jnp.float32), axis=0, keepdims=True
            )

    left = left_ref[...]
    for n, right in enumerate(rights):
        out_ref[n // 2, :, (n % 2) * part : (n % 2 + 1) * part] = dot32(left, right[...], contract_first).astype(low_type)


def qkv_grad(left, rights):
    rows, model = left.shape
    part = rights[0].shape[1]
    count = len(rights) // 2
    tile = 512
    return pl.pallas_call(
        qkv_grad_kernel,
        grid=(model // tile,),
        in_specs=[pl.BlockSpec((rows, tile), lambda n: (0, n))]
        + [pl.BlockSpec((rows, part), lambda n: (0, 0), pipeline_mode=pl.Buffered(1))] * len(rights),
        out_specs=[
            pl.BlockSpec((count, tile, 2 * part), lambda n: (0, n, 0)),
            pl.BlockSpec((count, 2 * part), lambda n: (0, 0)),
        ],
        out_shape=[
            jax.ShapeDtypeStruct((count, model, 2 * part), low_type),
            jax.ShapeDtypeStruct((count, 2 * part), jnp.float32),
        ],
        cost_estimate=cost(4 * count * rows * model * part, 4 * rows * model),
        compiler_params=params(48),
        name="qkv_grad",
    )(left, *rights)


def out_grad_kernel(a_ref, b_ref, right_ref, out_ref):
    part = a_ref.shape[1]
    right = right_ref[...]
    out_ref[:part, :] = dot32(a_ref[...], right, contract_first).astype(low_type)
    out_ref[part:, :] = dot32(b_ref[...], right, contract_first).astype(low_type)


def out_weight_grad(a, b, right):
    rows, part = a.shape
    model = right.shape[1]
    tile = 512
    return pl.pallas_call(
        out_grad_kernel,
        grid=(model // tile,),
        in_specs=[pl.BlockSpec((rows, part), lambda n: (0, 0), pipeline_mode=pl.Buffered(1))] * 2
        + [pl.BlockSpec((rows, tile), lambda n: (0, n))],
        out_specs=pl.BlockSpec((2 * part, tile), lambda n: (0, n)),
        out_shape=jax.ShapeDtypeStruct((2 * part, model), low_type),
        cost_estimate=cost(4 * rows * model * part, 4 * rows * model),
        compiler_params=params(48),
        name="out_grad",
    )(a, b, right)


def out_kernel(a_ref, b_ref, w_ref, out_ref):
    part = a_ref.shape[1]
    out_ref[...] = (dot32(a_ref[...], w_ref[:part, :]) + dot32(b_ref[...], w_ref[part:, :])).astype(low_type)


def out_slot(a, b, w, slot, rows):
    depth, model = w.shape
    part = a.shape[1]
    tile = 512
    return pl.pallas_call(
        out_kernel,
        grid=(model // tile,),
        in_specs=[pl.BlockSpec((rows, part), lambda n: (slot, 0))] * 2
        + [pl.BlockSpec((depth, tile), lambda n: (0, n))],
        out_specs=pl.BlockSpec((rows, tile), lambda n: (0, n)),
        out_shape=jax.ShapeDtypeStruct((rows, model), low_type),
        cost_estimate=cost(2 * rows * model * depth, 2 * model * depth + 2 * rows * model),
        compiler_params=params(32),
        name="out_proj",
    )(a, b, w)


def gate_up_kernel(h_ref, w_ref, *rest):
    all_ref, act_ref, one_ref, two_ref = rest[-4:]
    h = h_ref[...]
    all_ref[...] = h
    gate = dot32(h, w_ref[0])
    up = dot32(h, w_ref[1])
    sig = 1.0 / (1.0 + jnp.exp(-gate))
    silu = gate * sig
    act_ref[...] = (silu * up).astype(low_type)
    two_ref[...] = silu.astype(low_type)
    one_ref[...] = (up * sig * (1.0 + gate * (1.0 - sig))).astype(low_type)


def gate_up_slot(slot, slots, h, w, held):
    rows, model = h.shape
    depth = w.shape[2]
    total = rows * slots
    block = min(256, rows)
    per = rows // block
    at = lambda r: (slot * per + r, 0)
    extra = [] if held is None else list(held)
    outs = [model, depth, depth, depth]
    return pl.pallas_call(
        gate_up_kernel,
        grid=(per,),
        in_specs=[
            pl.BlockSpec((block, model), lambda r: (r, 0)),
            pl.BlockSpec(w.shape, lambda r: (0, 0, 0), pipeline_mode=pl.Buffered(1)),
        ]
        + [ANY] * len(extra),
        out_specs=[pl.BlockSpec((block, n), at) for n in outs],
        out_shape=[jax.ShapeDtypeStruct((total, n), low_type) for n in outs],
        input_output_aliases={2 + i: i for i in range(len(extra))},
        cost_estimate=cost(4 * rows * model * depth, 4 * model * depth + 4 * rows * model + 6 * rows * depth),
        compiler_params=params(56),
        name="gate_up",
    )(h, w, *extra)


def down_kernel(count, act_ref, one_ref, two_ref, w_ref, *rest):
    out_ref, dgate_ref, dup_ref, all_ref, buf, sem = rest[count:]
    now = stream(rest[:count], buf, sem)
    w = w_ref[...]
    out_ref[...] = dot32(act_ref[...], w).astype(low_type)
    dm = buf[now]
    all_ref[...] = dm
    da = dot32(dm, w, contract_last)
    dgate_ref[...] = (da * one_ref[...].astype(jnp.float32)).astype(low_type)
    dup_ref[...] = (da * two_ref[...].astype(jnp.float32)).astype(low_type)


def down_and_back(act, dm_blocks, one, two, w):
    depth, model = w.shape
    count = len(dm_blocks)
    block = dm_blocks[0].shape[0]
    rows = block * count
    row = lambda n: pl.BlockSpec((block, n), lambda r: (r, 0))
    wide = jax.ShapeDtypeStruct((rows, model), low_type)
    deep = jax.ShapeDtypeStruct((rows, depth), low_type)
    return pl.pallas_call(
        functools.partial(down_kernel, count),
        grid=(count,),
        in_specs=[
            row(depth),
            row(depth),
            row(depth),
            pl.BlockSpec(w.shape, lambda r: (0, 0), pipeline_mode=pl.Buffered(1)),
        ]
        + [ANY] * count,
        out_specs=[row(model), row(depth), row(depth), row(model)],
        out_shape=[wide, deep, deep, wide],
        scratch_shapes=[pltpu.VMEM((2, block, model), low_type), pltpu.SemaphoreType.DMA((2,))],
        cost_estimate=cost(4 * rows * model * depth, 2 * model * depth + 6 * rows * model + 10 * rows * depth),
        compiler_params=params(56),
        name="down_back",
    )(act, one, two, w, *dm_blocks)


def do_kernel(count, w_ref, *rest):
    do_ref, all_ref, buf, sem = rest[count:]
    now = stream(rest[:count], buf, sem)
    dattn = buf[now]
    all_ref[...] = dattn
    do_ref[...] = dot32(dattn, w_ref[...], contract_last).astype(low_type)


def back_through_out(blocks, w):
    depth, model = w.shape
    count = len(blocks)
    block = blocks[0].shape[0]
    rows = block * count
    row = lambda n: pl.BlockSpec((block, n), lambda r: (r, 0))
    return pl.pallas_call(
        functools.partial(do_kernel, count),
        grid=(count,),
        in_specs=[pl.BlockSpec(w.shape, lambda r: (0, 0), pipeline_mode=pl.Buffered(1))] + [ANY] * count,
        out_specs=[row(depth), row(model)],
        out_shape=[jax.ShapeDtypeStruct((rows, depth), low_type), jax.ShapeDtypeStruct((rows, model), low_type)],
        scratch_shapes=[pltpu.VMEM((2, block, model), low_type), pltpu.SemaphoreType.DMA((2,))],
        cost_estimate=cost(2 * rows * model * depth, 2 * model * depth + 4 * rows * model),
        compiler_params=params(32),
        name="do",
    )(w, *blocks)


def norm_two_kernel(x_ref, a_ref, live_ref, norm_ref, *rest):
    parts, (x1_ref, h_ref) = rest[:-2], rest[-2:]
    attn = a_ref[...].astype(jnp.float32)
    for part in parts:
        attn += part[...].astype(jnp.float32)
    x1 = x_ref[...].astype(jnp.float32) + live_ref[...] * attn
    x1_ref[...] = x1
    c = x1 - jnp.mean(x1, axis=-1, keepdims=True)
    s = lax.rsqrt(jnp.mean(c * c, axis=-1, keepdims=True) + norm_eps)
    h_ref[...] = (c * s * norm_ref[1:2, :] + norm_ref[3:4, :]).astype(low_type)


def norm_two(x, parts, live, norm):
    rows, model = x.shape
    block = 64
    row = pl.BlockSpec((block, model), lambda r: (r, 0))
    return pl.pallas_call(
        norm_two_kernel,
        grid=(rows // block,),
        in_specs=[row, row, pl.BlockSpec((block, 1), lambda r: (r, 0)), pl.BlockSpec(norm.shape, lambda r: (0, 0))]
        + [row] * (len(parts) - 1),
        out_specs=[row, row],
        out_shape=[jax.ShapeDtypeStruct((rows, model), jnp.float32), jax.ShapeDtypeStruct((rows, model), low_type)],
        cost_estimate=cost(20 * rows * model, 14 * rows * model),
        compiler_params=params(32),
        name="norm_two",
    )(x, parts[0], live, norm, *parts[1:])


def norm_back_kernel(gain_row, second, v_ref, base_ref, live_ref, norm_ref, *rest):
    held = 5 if second else 3
    parts, outs = rest[:-held], rest[-held:]
    i = pl.program_id(0)
    e = parts[0][...].astype(jnp.float32)
    for part in parts[1:]:
        e += part[...].astype(jnp.float32)
    v = v_ref[...].astype(jnp.float32)
    c = v - jnp.mean(v, axis=-1, keepdims=True)
    s = lax.rsqrt(jnp.mean(c * c, axis=-1, keepdims=True) + norm_eps)
    xh = c * s
    w = e * norm_ref[gain_row : gain_row + 1, :]
    back = s * (w - jnp.mean(w, axis=-1, keepdims=True) - xh * jnp.mean(w * xh, axis=-1, keepdims=True))
    dx = base_ref[...].astype(jnp.float32) + back
    outs[0][...] = dx.astype(outs[0].dtype)
    if second:
        half = pl.num_programs(0) // 2

        @pl.when(i < half)
        def _():
            outs[1][...] = (dx * live_ref[...]).astype(low_type)

        @pl.when(i >= half)
        def _():
            outs[2][...] = (dx * live_ref[...]).astype(low_type)

    @pl.when(i == 0)
    def _():
        outs[-2][...] = jnp.zeros_like(outs[-2])
        outs[-1][...] = jnp.zeros_like(outs[-1])

    outs[-2][...] += jnp.sum(e * xh, axis=0, keepdims=True)
    outs[-1][...] += jnp.sum(e, axis=0, keepdims=True)


def norm_back(v, parts, base, live, norm, second):
    rows, model = v.shape
    block = 64
    half = rows // block // 2
    row = pl.BlockSpec((block, model), lambda r: (r, 0))
    top = pl.BlockSpec((block, model), lambda r: (jnp.minimum(r, half - 1), 0))
    end = pl.BlockSpec((block, model), lambda r: (jnp.maximum(r, half) - half, 0))
    total = pl.BlockSpec((1, model), lambda r: (0, 0))
    if second:
        specs, shapes = [row, top, end], [(rows, jnp.float32), (rows // 2, low_type), (rows // 2, low_type)]
    else:
        specs, shapes = [row], [(rows, low_type)]
    return pl.pallas_call(
        functools.partial(norm_back_kernel, 1 if second else 0, second),
        grid=(rows // block,),
        in_specs=[row, row, pl.BlockSpec((block, 1), lambda r: (r, 0)), pl.BlockSpec(norm.shape, lambda r: (0, 0))]
        + [row] * len(parts),
        out_specs=specs + [total, total],
        out_shape=[jax.ShapeDtypeStruct((n, model), t) for n, t in shapes]
        + [jax.ShapeDtypeStruct((1, model), jnp.float32)] * 2,
        cost_estimate=cost(30 * rows * model, 18 * rows * model),
        compiler_params=params(32),
        name="norm_back",
    )(v, base, live, norm, *parts)


swap_x = [(0, 1), (1, 0), (2, 3), (3, 2)]
swap_y = [(0, 2), (2, 0), (1, 3), (3, 1)]


def square(count):
    return count == 4


def gather_rows(top, end, count, between=()):
    if not square(count):
        whole = lax.all_gather(jnp.concatenate([top, end], axis=0), "tensor", axis=0, tiled=True)
        half = top.shape[0]
        return [whole[j * half : (j + 1) * half] for j in range(2 * count)]
    x_top = lax.ppermute(top, "tensor", swap_x)
    y_end = lax.ppermute(end, "tensor", swap_y)
    x_end = lax.ppermute(end, "tensor", swap_x)
    y_top = lax.ppermute(top, "tensor", swap_y)
    far_top = lax.ppermute(after(x_top, *between), "tensor", swap_y)
    far_end = lax.ppermute(after(y_end, *between), "tensor", swap_x)
    return [top, end, x_top, x_end, y_top, y_end, far_top, far_end]


def after(value, *others):
    return lax.optimization_barrier((value,) + others)[0]


def halves(value):
    half = value.shape[0] // 2
    return value[:half], value[half:]


def add_low(a, b):
    return (a.astype(jnp.float32) + b.astype(jnp.float32)).astype(low_type)


def scatter_first(partial, count, own):
    if not square(count):
        return [jnp.concatenate([own()] + [partial(j) for j in range(1, count)], axis=0)]
    far = partial(3)
    half = far.shape[0] // 2
    top = lax.ppermute(far[:half], "tensor", swap_x)
    end = lax.ppermute(far[half:], "tensor", swap_y)
    return [top, end]


def scatter_middle(partial, first, count):
    if not square(count):
        return first
    top, end = first
    half = top.shape[0]
    for_x, for_y = partial(1), partial(2)
    for_y = jnp.concatenate([add_low(for_y[:half], top), for_y[half:]], axis=0)
    for_x = jnp.concatenate([for_x[:half], add_low(for_x[half:], end)], axis=0)
    return [for_x, for_y]


def scatter_last(own, middle, count):
    if not square(count):
        return [lax.psum_scatter(middle[0], "tensor", scatter_dimension=0, tiled=True)]
    from_x = lax.ppermute(middle[0], "tensor", swap_x)
    from_y = lax.ppermute(middle[1], "tensor", swap_y)
    return [own, from_x, from_y]


MESH = pl.DeviceIdType.MESH


def greet(near_x, near_y):
    barrier = pltpu.get_barrier_semaphore()
    for near in (near_x, near_y):
        pl.semaphore_signal(barrier, inc=1, device_id={"tensor": near}, device_id_type=MESH)
    pl.semaphore_wait(barrier, 2)


def neighbours():
    rank = lax.axis_index("tensor")
    return jnp.bitwise_xor(rank, 1), jnp.bitwise_xor(rank, 2)


def out_scatter_kernel(a_ref, b_ref, w_ref, x_ref, live_ref, norm_ref, x1_ref, h_ref, far_s, for_x, for_y, top_s, end_s, from_x, from_y, send, recv):
    near_x, near_y = neighbours()
    rows = x_ref.shape[0]
    half = rows // 2
    part = a_ref.shape[1]
    model = w_ref.shape[1]
    tile = 512
    greet(near_x, near_y)

    def partial(slot, which, store):
        at = pl.ds(slot * rows + which * half, half)

        @pl.loop(0, model // tile)
        def _(n):
            cols = pl.ds(pl.multiple_of(n * tile, tile), tile)
            store(cols, dot32(a_ref[at, :], w_ref[:part, cols]) + dot32(b_ref[at, :], w_ref[part:, cols]))

    def copy(index, source, target, near):
        return pltpu.make_async_remote_copy(
            src_ref=source,
            dst_ref=target,
            send_sem=send.at[index],
            recv_sem=recv.at[index],
            device_id={"tensor": near},
            device_id_type=MESH,
        )

    def into(ref, which):
        def store(cols, value):
            ref[pl.ds(which * half, half), cols] = value.astype(low_type)

        return store

    def added(ref, which, other):
        def store(cols, value):
            ref[pl.ds(which * half, half), cols] = (value + other[:, cols].astype(jnp.float32)).astype(low_type)

        return store

    t, e = pl.ds(0, half), pl.ds(half, half)
    copies = [
        copy(0, far_s.at[t], top_s, near_x),
        copy(1, far_s.at[e], end_s, near_y),
        copy(2, for_x.at[t], from_x.at[t], near_x),
        copy(3, for_y.at[e], from_y.at[e], near_y),
        copy(4, for_x.at[e], from_x.at[e], near_x),
        copy(5, for_y.at[t], from_y.at[t], near_y),
    ]
    partial(3, 0, into(far_s, 0))
    copies[0].start()
    partial(3, 1, into(far_s, 1))
    copies[1].start()
    partial(1, 0, into(for_x, 0))
    copies[2].start()
    partial(2, 1, into(for_y, 1))
    copies[3].start()
    copies[0].wait_recv()
    partial(2, 0, added(for_y, 0, top_s))
    copies[5].start()
    copies[1].wait_recv()
    partial(1, 1, added(for_x, 1, end_s))
    copies[4].start()

    def own(which):
        def store(cols, value):
            x1_ref[pl.ds(which * half, half), cols] = value

        return store

    partial(0, 0, own(0))
    partial(0, 1, own(1))
    step = 32

    def finish(which):
        @pl.loop(0, half // step)
        def _(r):
            at = pl.ds(pl.multiple_of(which * half + r * step, step), step)
            attn = x1_ref[at, :] + from_x[at, :].astype(jnp.float32) + from_y[at, :].astype(jnp.float32)
            x1 = x_ref[at, :].astype(jnp.float32) + live_ref[at, :] * attn
            x1_ref[at, :] = x1
            c = x1 - jnp.mean(x1, axis=-1, keepdims=True)
            s = lax.rsqrt(jnp.mean(c * c, axis=-1, keepdims=True) + norm_eps)
            h_ref[at, :] = (c * s * norm_ref[1:2, :] + norm_ref[3:4, :]).astype(low_type)

    copies[2].wait_recv()
    copies[5].wait_recv()
    finish(0)
    copies[3].wait_recv()
    copies[4].wait_recv()
    finish(1)
    for c in copies:
        c.wait_send()


def out_scatter(a, b, w, x, live, norm):
    rows, model = x.shape
    half = rows // 2
    big = pltpu.VMEM((rows, model), low_type)
    small = pltpu.VMEM((half, model), low_type)
    vmem = pl.BlockSpec(memory_space=pltpu.VMEM)
    total = a.shape[0]
    return pl.pallas_call(
        out_scatter_kernel,
        in_specs=[vmem] * 6,
        out_specs=[vmem] * 2,
        out_shape=[jax.ShapeDtypeStruct((rows, model), jnp.float32), jax.ShapeDtypeStruct((rows, model), low_type)],
        scratch_shapes=[
            big,
            big,
            big,
            small,
            small,
            big,
            big,
            pltpu.SemaphoreType.DMA((6,)),
            pltpu.SemaphoreType.DMA((6,)),
        ],
        cost_estimate=cost(2 * total * model * w.shape[0], 20 * rows * model),
        compiler_params=pltpu.CompilerParams(vmem_limit_bytes=48 * MIB, collective_id=0, has_side_effects=True),
        name="out_scatter",
    )(a, b, w, x, live, norm)


def gather_gate_up_kernel(h_ref, w_hbm, all_ref, act_ref, one_ref, two_ref, w_s, all_s, stage, send, recv, local, h_sem, out_sem):
    near_x, near_y = neighbours()
    half = h_ref.shape[0] // 2
    own = pltpu.make_async_copy(h_ref, all_s.at[pl.ds(0, 2 * half)], local.at[0])
    own.start()
    weights = pltpu.make_async_copy(w_hbm, w_s, local.at[1])
    weights.start()
    greet(near_x, near_y)
    own.wait()

    def copy(index, source, target, near):
        return pltpu.make_async_remote_copy(
            src_ref=all_s.at[pl.ds(source * half, half)],
            dst_ref=all_s.at[pl.ds(target * half, half)],
            send_sem=send.at[index],
            recv_sem=recv.at[index],
            device_id={"tensor": near},
            device_id_type=MESH,
        )

    x_top = copy(0, 0, 2, near_x)
    y_end = copy(1, 1, 5, near_y)
    x_end = copy(2, 1, 3, near_x)
    y_top = copy(3, 0, 4, near_y)
    far_top = copy(4, 2, 6, near_y)
    far_end = copy(5, 5, 7, near_x)
    for c in (x_top, y_end, x_end, y_top):
        c.start()
    weights.wait()

    def outs(buf, row):
        return [
            pltpu.make_async_copy(stage.at[buf, n], ref.at[pl.ds(row, half)], out_sem.at[buf, n])
            for n, ref in enumerate((act_ref, one_ref, two_ref))
        ]

    def keep(i, row):
        return pltpu.make_async_copy(all_s.at[pl.ds(row, half)], all_ref.at[pl.ds(row, half)], h_sem.at[i])

    def step(i, carry):
        slot = jnp.where(i == 3, 5, jnp.where(i == 4, 3, jnp.where(i == 5, 4, i)))

        @pl.when(i == 2)
        def _():
            x_top.wait_recv()
            far_top.start()
            y_end.wait_recv()
            far_end.start()

        @pl.when(i == 4)
        def _():
            x_end.wait_recv()

        @pl.when(i == 5)
        def _():
            y_top.wait_recv()

        @pl.when(i == 6)
        def _():
            far_top.wait_recv()

        @pl.when(i == 7)
        def _():
            far_end.wait_recv()

        row = pl.multiple_of(slot * half, half)
        buf = i % 2
        keep(i, row).start()

        @pl.when(i >= 2)
        def _():
            for c in outs(buf, row):
                c.wait()

        h = all_s[pl.ds(row, half), :]
        gate = dot32(h, w_s[0])
        up = dot32(h, w_s[1])
        sig = 1.0 / (1.0 + jnp.exp(-gate))
        silu = gate * sig
        stage[buf, 0] = (silu * up).astype(low_type)
        stage[buf, 1] = (up * sig * (1.0 + gate * (1.0 - sig))).astype(low_type)
        stage[buf, 2] = silu.astype(low_type)
        for c in outs(buf, row):
            c.start()
        return carry

    lax.fori_loop(0, 8, step, 0)
    for buf in (0, 1):
        for c in outs(buf, 0):
            c.wait()
    for i in range(8):
        keep(i, 0).wait()
    for c in (x_top, y_end, x_end, y_top, far_top, far_end):
        c.wait_send()


def gather_gate_up(h, w):
    rows, model = h.shape
    depth = w.shape[2]
    total = 4 * rows
    deep = jax.ShapeDtypeStruct((total, depth), low_type)
    return pl.pallas_call(
        gather_gate_up_kernel,
        in_specs=[ANY] * 2,
        out_specs=[ANY] * 4,
        out_shape=[jax.ShapeDtypeStruct((total, model), low_type), deep, deep, deep],
        scratch_shapes=[
            pltpu.VMEM(w.shape, low_type),
            pltpu.VMEM((total, model), low_type),
            pltpu.VMEM((2, 3, rows // 2, depth), low_type),
            pltpu.SemaphoreType.DMA((6,)),
            pltpu.SemaphoreType.DMA((6,)),
            pltpu.SemaphoreType.DMA((2,)),
            pltpu.SemaphoreType.DMA((8,)),
            pltpu.SemaphoreType.DMA((2, 3)),
        ],
        cost_estimate=cost(4 * total * model * depth, 4 * model * depth + 4 * total * model + 6 * total * depth),
        compiler_params=pltpu.CompilerParams(vmem_limit_bytes=56 * MIB, collective_id=1, has_side_effects=True),
        name="gather_gate_up",
    )(h, w)


def small_kernel(nd, nt, x_ref, o_ref, groups, partial, shares, send, recv, send_t, recv_t):
    d, t = lax.axis_index("dp"), lax.axis_index("tensor")
    width = o_ref.shape[1]
    barrier = pltpu.get_barrier_semaphore()
    for k in range(1, nd):
        pl.semaphore_signal(barrier, inc=1, device_id={"dp": lax.rem(d + k, nd)}, device_id_type=MESH)
    for k in range(1, nt):
        pl.semaphore_signal(barrier, inc=1, device_id={"tensor": lax.rem(t + k, nt)}, device_id_type=MESH)
    pl.semaphore_wait(barrier, nd + nt - 2)
    copies = []
    for k in range(1, nd):
        peer = lax.rem(d + k, nd)
        c = pltpu.make_async_remote_copy(
            src_ref=x_ref.at[:, pl.ds(pl.multiple_of(peer * width, width), width)],
            dst_ref=groups.at[k],
            send_sem=send.at[k],
            recv_sem=recv.at[k],
            device_id={"dp": peer},
            device_id_type=MESH,
        )
        c.start()
        copies.append(c)
    total = x_ref[:, pl.ds(pl.multiple_of(d * width, width), width)]
    for k in range(1, nd):
        copies[k - 1].wait_recv()
        total += groups[k]
    partial[...] = total
    shares[t] = total
    for k in range(1, nt):
        c = pltpu.make_async_remote_copy(
            src_ref=partial,
            dst_ref=shares.at[t],
            send_sem=send_t.at[k],
            recv_sem=recv_t.at[k],
            device_id={"tensor": lax.rem(t + k, nt)},
            device_id_type=MESH,
        )
        c.start()
        copies.append(c)
    for k in range(1, nt):
        copies[nd - 2 + k].wait_recv()
    total = shares[0]
    for k in range(1, nt):
        total += shares[k]
    o_ref[...] = total
    for c in copies:
        c.wait_send()


def sum_small(x):
    nd, nt = lax.axis_size("dp"), lax.axis_size("tensor")
    rows, model = x.shape
    width = model // nd
    vmem = pl.BlockSpec(memory_space=pltpu.VMEM)
    return pl.pallas_call(
        functools.partial(small_kernel, nd, nt),
        in_specs=[vmem],
        out_specs=vmem,
        out_shape=jax.ShapeDtypeStruct((rows, width), jnp.float32),
        scratch_shapes=[
            pltpu.VMEM((nd, rows, width), jnp.float32),
            pltpu.VMEM((rows, width), jnp.float32),
            pltpu.VMEM((nt, rows, width), jnp.float32),
            pltpu.SemaphoreType.DMA((nd,)),
            pltpu.SemaphoreType.DMA((nd,)),
            pltpu.SemaphoreType.DMA((nt,)),
            pltpu.SemaphoreType.DMA((nt,)),
        ],
        cost_estimate=cost(rows * model, 8 * rows * model),
        compiler_params=pltpu.CompilerParams(collective_id=2, has_side_effects=True),
        name="sum_small",
    )(x)


def body(
    tokens,
    out_grad,
    lengths,
    norm_gain,
    norm_bias,
    qkv_weight,
    qkv_bias,
    out_weight,
    gate_up_weight,
    down_weight,
    first_norm_gain,
    first_norm_bias,
    first_qkv_weight,
    first_qkv_bias,
    first_out_weight,
    first_gate_up_weight,
    first_down_weight,
    second_norm_gain,
    second_norm_bias,
    second_qkv_weight,
    second_qkv_bias,
    second_out_weight,
    second_gate_up_weight,
    second_down_weight,
):
    slots = lax.axis_size("tensor")
    rank = lax.axis_index("tensor")
    own_rows = tokens.shape[0]
    group_rows = own_rows * slots
    width = out_weight.shape[0]
    order = rank if square(slots) else jnp.zeros_like(rank)

    chunk = jnp.bitwise_xor(jnp.arange(slots, dtype=jnp.int32), order)
    row_index = (chunk[:, None] * own_rows + jnp.arange(own_rows, dtype=jnp.int32)[None, :]).reshape(-1)
    seq_start, _ = layout(lengths[0], row_index)
    tables = rotary_tables(row_index - seq_start)
    own_index = rank * own_rows + jnp.arange(own_rows, dtype=jnp.int32)
    live = layout(lengths[0], own_index)[1][:, None]
    block_start, _ = layout(lengths[0], jnp.arange(group_rows // BLOCK, dtype=jnp.int32) * BLOCK)
    table = jnp.concatenate([order.reshape(1).astype(jnp.int32), block_start // BLOCK])
    starts = seq_start[None, :]

    small_low = jnp.concatenate([norm_gain, norm_bias, qkv_bias], axis=0).astype(low_type)
    small_full = lax.all_gather(small_low, "dp", axis=1, tiled=True)
    norm = small_full[:4].astype(jnp.float32)
    bias = lax.dynamic_slice_in_dim(small_full[4:7], rank * width, width, 1).astype(jnp.float32)[:, None, :]
    x_own = halves(tokens)
    h_own = [norm_one(b, norm) for b in x_own]
    x_blocks = gather_rows(*x_own, slots, h_own)
    if square(slots):
        h_blocks = h_own + [norm_one(b, norm) for b in x_blocks[2:]]
    else:
        h_blocks = [norm_one(b, norm) for b in x_blocks]

    qkv_full = lax.all_gather(qkv_weight.astype(low_type), "dp", axis=1, tiled=True)
    out_low = after(out_weight.astype(low_type), qkv_full, *x_blocks)
    out_full = lax.all_gather(out_low, "dp", axis=1, tiled=True)

    h1, q, k, v, kt, vt = qkv_all(h_blocks, qkv_full, bias, tables)

    gate_up_low = after(gate_up_weight.astype(low_type), out_full, q)
    gate_up_full = lax.all_gather(gate_up_low, "dp", axis=1, tiled=True)

    dm_own = (after(out_grad, *x_blocks).astype(jnp.float32) * live).astype(low_type)
    dm_blocks = gather_rows(*halves(dm_own), slots)

    o_a, lse_a = attn_fwd(0, slots, table, q, k, vt, starts)
    o_b, lse_b = attn_fwd(1, slots, table, after(q, o_a, *dm_blocks[2:6]), k, vt, starts)
    o_b = after(o_b, *dm_blocks[6:])

    if square(slots):
        x1, h2_own = out_scatter(o_a, o_b, out_full, tokens, live, norm)
    else:
        attn_slot = lambda j: out_slot(o_a, o_b, out_full, j, own_rows)
        attn_first = scatter_first(attn_slot, slots, lambda: attn_slot(0))
        attn_parts = scatter_last(None, attn_first, slots)
        x1, h2_own = norm_two(tokens, attn_parts, live, norm)
    down_low = after(down_weight.astype(low_type), gate_up_full, h2_own)
    down_full = lax.all_gather(down_low, "dp", axis=1, tiled=True)
    if square(slots):
        h2, act, slope_gate, slope_up = gather_gate_up(h2_own, gate_up_full)
    else:
        held = None
        for j, h in enumerate(gather_rows(*halves(h2_own), slots)):
            held = gate_up_slot(j, 2 * slots, h, gate_up_full, held)
        h2, act, slope_gate, slope_up = held

    mlp, dgate, dup, dm = down_and_back(act, dm_blocks, slope_gate, slope_up, down_full)

    dh2 = [sum_nt((dgate, dup), gate_up_full, j, own_rows) for j in range(1, slots)]
    dh2_first = scatter_first(lambda j: dh2[j - 1], slots, lambda: sum_nt((dgate, dup), gate_up_full, 0, own_rows))
    dh2_middle = scatter_middle(lambda j: dh2[j - 1], dh2_first, slots)
    dh2_own = sum_nt((after(dgate, *dh2_middle), dup), gate_up_full, 0, own_rows)
    dh2_parts = scatter_last(dh2_own, dh2_middle, slots)
    grad_down = weight_grad(after(dm, dh2_own), act, 0, 1)
    grad_down_turned = lax.psum_scatter(grad_down[0], "dp", scatter_dimension=0, tiled=True)
    grad_gate = weight_grad(after(h2, grad_down), dgate, 0, 2)
    dh2_parts[-1] = after(dh2_parts[-1], grad_gate)
    dx1, dattn_top, dattn_end, gain_two, shift_two = norm_back(x1, dh2_parts, out_grad, live, norm, True)

    dattn_blocks = gather_rows(dattn_top, dattn_end, slots, [grad_down_turned])
    grad_gate_up = weight_grad(after(h2, dattn_blocks[2], dattn_blocks[5]), dup, 1, 2, grad_gate)
    dattn_blocks[-1] = after(dattn_blocks[-1], grad_gate_up)
    grad_gate_up = after(grad_gate_up, grad_down_turned)
    grad_gate_up_own = lax.psum_scatter(grad_gate_up, "dp", scatter_dimension=1, tiled=True)

    mlp_late = after(mlp, *dattn_blocks[2:])
    mlp_slot = lambda j: mlp_late[j * own_rows : (j + 1) * own_rows]
    mlp_first = scatter_first(mlp_slot, slots, lambda: mlp_slot(0))
    do, dattn = back_through_out(dattn_blocks, out_full)
    grad_out = out_weight_grad(o_a, o_b, dattn)
    back_a = attn_bwd(0, slots, table, q, do, o_a, k, v, kt, starts, lse_a, tables)
    mlp_first = [after(part, do, grad_out) for part in mlp_first]
    mlp_middle = scatter_middle(mlp_slot, mlp_first, slots)
    mlp_parts = scatter_last(mlp_slot(0), mlp_middle, slots)
    back_b = attn_bwd(1, slots, table, q, after(do, back_a[0], *mlp_middle), o_b, k, v, kt, starts, lse_b, tables)
    mlp_rows = mlp_parts[0].astype(jnp.float32)
    for part in mlp_parts[1:]:
        mlp_rows += part.astype(jnp.float32)
    layer_out = (x1 + live * mlp_rows).astype(low_type)

    grad_out = after(grad_out, grad_gate_up_own, back_a[0])
    grad_out_own = lax.psum_scatter(grad_out, "dp", scatter_dimension=1, tiled=True)

    dlin = [side for pair in zip(back_a, back_b) for side in pair]
    dlin[0] = after(dlin[0], *mlp_parts)
    dh1_far = sum_nt(dlin, qkv_full, slots - 1, own_rows)
    grad_qkv, bias_local = qkv_grad(after(h1, dh1_far), dlin)
    late = [after(dlin[0], grad_qkv)] + dlin[1:]
    dh1 = [sum_nt(late, qkv_full, j, own_rows) for j in range(1, slots - 1)] + [dh1_far]
    dh1_own = sum_nt(late, qkv_full, 0, own_rows)
    dh1_first = scatter_first(lambda j: dh1[j - 1], slots, lambda: dh1_own)
    dh1_middle = scatter_middle(lambda j: dh1[j - 1], dh1_first, slots)
    dh1_parts = scatter_last(dh1_own, dh1_middle, slots)
    grad_qkv = after(grad_qkv, grad_out_own)
    grad_qkv_own = lax.psum_scatter(grad_qkv, "dp", scatter_dimension=1, tiled=True)
    input_grad, gain_one, shift_one = norm_back(tokens, dh1_parts, dx1, live, norm, False)

    bias_placed = lax.dynamic_update_slice(
        jnp.zeros((3, small_full.shape[1]), jnp.float32), bias_local, (jnp.int32(0), rank * width)
    )
    small_local = jnp.concatenate([gain_one, gain_two, shift_one, shift_two, bias_placed, bias_placed[:1]], axis=0)
    small_own = sum_small(small_local)

    own_grads = (
        small_own[0:2],
        small_own[2:4],
        grad_qkv_own.astype(jnp.float32),
        small_own[4:7],
        grad_out_own.astype(jnp.float32),
        grad_gate_up_own.astype(jnp.float32),
        grad_down_turned.T.astype(jnp.float32),
    )
    masters = (norm_gain, norm_bias, qkv_weight, qkv_bias, out_weight, gate_up_weight, down_weight)
    firsts = (
        first_norm_gain,
        first_norm_bias,
        first_qkv_weight,
        first_qkv_bias,
        first_out_weight,
        first_gate_up_weight,
        first_down_weight,
    )
    seconds = (
        second_norm_gain,
        second_norm_bias,
        second_qkv_weight,
        second_qkv_bias,
        second_out_weight,
        second_gate_up_weight,
        second_down_weight,
    )
    decays = (0.0, 0.0, weight_decay, 0.0, weight_decay, weight_decay, weight_decay)
    new_change = []
    new_first = []
    new_second = []
    for weight_now, gradient, moment_one, moment_two, decay_rate in zip(
        masters, own_grads, firsts, seconds, decays
    ):
        change, moment_next, square_next = adamw_update(
            weight_now, gradient, moment_one, moment_two, decay_rate
        )
        new_change.append(change)
        new_first.append(moment_next)
        new_second.append(square_next)
    return (
        (layer_out, input_grad)
        + own_grads
        + tuple(new_change)
        + tuple(new_first)
        + tuple(new_second)
    )


def solution(mesh):
    return jax.shard_map(
        body,
        mesh=mesh,
        in_specs=(
            P(("dp", "tensor"), None),
            P(("dp", "tensor"), None),
            P("dp", None),
            P(None, "dp"),
            P(None, "dp"),
            P(None, "dp", "tensor"),
            P(None, "dp"),
            P("tensor", "dp"),
            P(None, "dp", "tensor"),
            P("tensor", "dp"),
            P(None, "dp"),
            P(None, "dp"),
            P(None, "dp", "tensor"),
            P(None, "dp"),
            P("tensor", "dp"),
            P(None, "dp", "tensor"),
            P("tensor", "dp"),
            P(None, "dp"),
            P(None, "dp"),
            P(None, "dp", "tensor"),
            P(None, "dp"),
            P("tensor", "dp"),
            P(None, "dp", "tensor"),
            P("tensor", "dp"),
        ),
        out_specs=(
            P(("dp", "tensor"), None),
            P(("dp", "tensor"), None),
            P(None, "dp"),
            P(None, "dp"),
            P(None, "dp", "tensor"),
            P(None, "dp"),
            P("tensor", "dp"),
            P(None, "dp", "tensor"),
            P("tensor", "dp"),
            P(None, "dp"),
            P(None, "dp"),
            P(None, "dp", "tensor"),
            P(None, "dp"),
            P("tensor", "dp"),
            P(None, "dp", "tensor"),
            P("tensor", "dp"),
            P(None, "dp"),
            P(None, "dp"),
            P(None, "dp", "tensor"),
            P(None, "dp"),
            P("tensor", "dp"),
            P(None, "dp", "tensor"),
            P("tensor", "dp"),
            P(None, "dp"),
            P(None, "dp"),
            P(None, "dp", "tensor"),
            P(None, "dp"),
            P("tensor", "dp"),
            P(None, "dp", "tensor"),
            P("tensor", "dp"),
        ),
        check_vma=False,
    )
```

```python
import functools

import jax
import jax.numpy as jnp
from jax import lax
from jax.experimental import pallas as pl
from jax.experimental.pallas import tpu as pltpu
from jax.sharding import PartitionSpec as P

HEAD_DIM = 64
ROT = 16
PAIR = 2 * HEAD_DIM
BLOCK = 256

norm_eps = 1e-05
rope_base = 10000.0
beta_one = 0.9
beta_two = 0.95
adam_eps = 1e-08
learn_rate = 0.01
weight_decay = 0.1
step_count = 10.0
masked_score = -1e30
contract_last = (((1,), (1,)), ((), ()))
contract_first = (((0,), (0,)), ((), ()))
low_type = jnp.bfloat16
MIB = 2**20


def layout(seq_lengths, row_index):
    slot = jnp.arange(seq_lengths.shape[0])
    seq_ends = jnp.sum(
        jnp.where(slot[:, None] <= slot[None, :], seq_lengths[:, None], 0), axis=0
    )
    passed = row_index[:, None] >= seq_ends[None, :]
    seq_start = jnp.sum(jnp.where(passed, seq_lengths[None, :], 0), axis=1)
    live_rows = (row_index < jnp.sum(seq_lengths)).astype(jnp.float32)
    return (seq_start, live_rows)


def rotary_tables(position):
    half_rot = ROT // 2
    lane = jnp.arange(PAIR, dtype=jnp.int32) % HEAD_DIM
    powers = (lane % half_rot).astype(jnp.float32) * (2.0 / ROT)
    inverse = jnp.power(rope_base, -powers)
    angles = position.astype(jnp.float32)[:, None] * inverse[None, :]
    cos_part, sine_part = jnp.cos(angles), jnp.sin(angles)
    lane = lane[None, :]
    keep = jnp.where(lane < ROT, cos_part, 1.0)
    above = jnp.where(lane < half_rot, -sine_part, 0.0)
    below = jnp.where((lane >= half_rot) & (lane < ROT), sine_part, 0.0)
    return (keep, above, below)


def dot32(a, b, dims=None):
    if dims is None:
        return jnp.dot(a, b, preferred_element_type=jnp.float32)
    return lax.dot_general(a, b, dims, preferred_element_type=jnp.float32)


def turn(values, keep, above, below):
    up = pltpu.roll(values, PAIR - ROT // 2, 1)
    down = pltpu.roll(values, ROT // 2, 1)
    return values * keep + up * above + down * below


def turn_back(values, keep, above, below):
    up = pltpu.roll(values, PAIR - ROT // 2, 1)
    down = pltpu.roll(values, ROT // 2, 1)
    return values * keep - up * above - down * below


def adamw_update(weight_now, gradient, moment_one, moment_two, decay_rate):
    moment_one = beta_one * moment_one + (1.0 - beta_one) * gradient
    moment_two = beta_two * moment_two + (1.0 - beta_two) * gradient * gradient
    scaled_one = moment_one / (1.0 - beta_one**step_count)
    scaled_two = moment_two / (1.0 - beta_two**step_count)
    change = scaled_one / (jnp.sqrt(scaled_two) + adam_eps) + decay_rate * weight_now
    return (-learn_rate * change, moment_one, moment_two)


def cost(flops, moved, exps=0):
    return pl.CostEstimate(flops=int(flops) // 16, bytes_accessed=int(moved) // 16, transcendentals=int(exps) // 16)


def params(limit):
    return pltpu.CompilerParams(vmem_limit_bytes=limit * MIB)


ANY = pl.BlockSpec(memory_space=pl.ANY)


def stream(refs, buf, sem):
    step = pl.program_id(0)

    def fetch(j, slot):
        pltpu.make_async_copy(refs[j], buf.at[slot], sem.at[slot]).start()

    @pl.when(step == 0)
    def _():
        fetch(0, 0)

    for j in range(1, len(refs)):

        @pl.when(step == j - 1)
        def _(j=j):
            fetch(j, j % 2)

    now = step % 2
    pltpu.make_async_copy(refs[0], buf.at[now], sem.at[now]).wait()
    return now


def layer_norm(values, gain_row, shift_row):
    center = values - jnp.mean(values, axis=-1, keepdims=True)
    spread = jnp.mean(center * center, axis=-1, keepdims=True)
    return center * lax.rsqrt(spread + norm_eps) * gain_row + shift_row


def qkv_kernel(scale, h_ref, w_ref, bias_ref, keep_ref, above_ref, below_ref, q_ref, k_ref, v_ref, kt_ref, vt_ref):
    h = h_ref[...]
    keep, above, below = keep_ref[...], above_ref[...], below_ref[...]
    width = q_ref.shape[1]
    lin = dot32(h, w_ref[0]) + bias_ref[0]
    for c in range(0, width, PAIR):
        u = turn(lin[:, c : c + PAIR], keep, above, below)
        q_ref[:, c : c + PAIR] = (u.astype(low_type) * scale).astype(low_type)
    lin = dot32(h, w_ref[1]) + bias_ref[1]
    for c in range(0, width, PAIR):
        u = turn(lin[:, c : c + PAIR], keep, above, below)
        k_ref[:, c : c + PAIR] = u.astype(low_type)
        kt_ref[c : c + PAIR, :] = u.T.astype(low_type)
    lin = dot32(h, w_ref[2]) + bias_ref[2]
    v_ref[...] = lin.astype(low_type)
    vt_ref[...] = lin.T.astype(low_type)


def qkv_all(h, w, bias, tables):
    total, model = h.shape
    rows = 256
    width = w.shape[2]
    row = lambda n: pl.BlockSpec((rows, n), lambda i: (i, 0))
    col = pl.BlockSpec((width, rows), lambda i: (0, i))
    flat = jax.ShapeDtypeStruct((total, width), low_type)
    turned = jax.ShapeDtypeStruct((width, total), low_type)
    return pl.pallas_call(
        functools.partial(qkv_kernel, HEAD_DIM ** (-0.5)),
        grid=(total // rows,),
        in_specs=[
            row(model),
            pl.BlockSpec(w.shape, lambda i: (0, 0, 0), pipeline_mode=pl.Buffered(1)),
            pl.BlockSpec(bias.shape, lambda i: (0, 0, 0)),
            row(PAIR),
            row(PAIR),
            row(PAIR),
        ],
        out_specs=[row(width), row(width), row(width), col, col],
        out_shape=[flat, flat, flat, turned, turned],
        cost_estimate=cost(6 * total * model * width, 6 * model * width + 10 * total * model),
        compiler_params=params(48),
        name="qkv",
    )(h, w, bias, *tables)


def place(block, rank, per):
    return jnp.bitwise_xor(block // per, rank) * per + block % per


def attn_fwd_kernel(per, table_ref, q_ref, k_ref, vt_ref, start_ref, o_ref, lse_ref, m_s, l_s, acc_s, bias_s):
    i = pl.program_id(0)
    rank = table_ref[0]
    heads = q_ref.shape[1] // HEAD_DIM
    first = lax.broadcasted_iota(jnp.int32, (BLOCK, PAIR), 1) < HEAD_DIM
    queries = []
    for h in range(heads):
        pair = q_ref[:, (h // 2) * PAIR : (h // 2 + 1) * PAIR]
        keep = first if h % 2 == 0 else jnp.logical_not(first)
        queries.append(jnp.where(keep, pair, jnp.zeros_like(pair)))
    m_s[...] = jnp.full_like(m_s, -jnp.inf)
    l_s[...] = jnp.zeros_like(l_s)
    acc_s[...] = jnp.zeros_like(acc_s)
    start = start_ref[...]
    row = i * BLOCK + lax.broadcasted_iota(jnp.int32, (BLOCK, BLOCK), 1)

    def step(kb, carry):
        col = kb * BLOCK + lax.broadcasted_iota(jnp.int32, (BLOCK, BLOCK), 0)
        bias_s[...] = jnp.where((col >= start) & (col <= row), 0.0, masked_score)
        at = pl.ds(pl.multiple_of(place(kb, rank, per) * BLOCK, BLOCK), BLOCK)
        for h in range(heads):
            own = slice(h * HEAD_DIM, (h + 1) * HEAD_DIM)
            keys = k_ref[at, (h // 2) * PAIR : (h // 2 + 1) * PAIR]
            s = dot32(keys, queries[h], contract_last) + bias_s[...]
            m_old = m_s[h : h + 1, :]
            m_new = jnp.maximum(m_old, jnp.max(s, axis=0, keepdims=True))
            alpha = jnp.exp(m_old - m_new)
            p = jnp.exp(s - m_new)
            l_s[h : h + 1, :] = l_s[h : h + 1, :] * alpha + jnp.sum(p, axis=0, keepdims=True)
            m_s[h : h + 1, :] = m_new
            mixed = dot32(vt_ref[own, at], p.astype(low_type))
            acc_s[own, :] = acc_s[own, :] * alpha + mixed
        return carry

    lax.fori_loop(table_ref[1 + i], i + 1, step, 0)
    for h in range(heads):
        own = slice(h * HEAD_DIM, (h + 1) * HEAD_DIM)
        acc_s[own, :] = acc_s[own, :] / l_s[h : h + 1, :]
    o_ref[...] = acc_s[...].T.astype(low_type)
    lse_ref[0] = m_s[...] + jnp.log(l_s[...])


def attn_fwd(half, slots, table, q, k, vt, start):
    rows, width = q.shape
    part = width // 2
    heads = part // HEAD_DIM
    count = rows // BLOCK
    per = rows // slots // BLOCK
    at = lambda i, t: place(i, t[0], per)
    return pl.pallas_call(
        functools.partial(attn_fwd_kernel, per),
        grid_spec=pltpu.PrefetchScalarGridSpec(
            num_scalar_prefetch=1,
            grid=(count,),
            in_specs=[
                pl.BlockSpec((BLOCK, part), lambda i, t: (at(i, t), half)),
                pl.BlockSpec((rows, part), lambda i, t: (0, half)),
                pl.BlockSpec((part, rows), lambda i, t: (half, 0)),
                pl.BlockSpec((1, BLOCK), lambda i, t: (0, at(i, t))),
            ],
            out_specs=[
                pl.BlockSpec((BLOCK, part), lambda i, t: (at(i, t), 0)),
                pl.BlockSpec((1, heads, BLOCK), lambda i, t: (at(i, t), 0, 0)),
            ],
            scratch_shapes=[
                pltpu.VMEM((heads, BLOCK), jnp.float32),
                pltpu.VMEM((heads, BLOCK), jnp.float32),
                pltpu.VMEM((part, BLOCK), jnp.float32),
                pltpu.VMEM((BLOCK, BLOCK), jnp.float32),
            ],
        ),
        out_shape=[
            jax.ShapeDtypeStruct((rows, part), low_type),
            jax.ShapeDtypeStruct((count, heads, BLOCK), jnp.float32),
        ],
        cost_estimate=cost(20 * rows * rows * part // 2, 8 * rows * part, 8 * rows * rows // 4),
        compiler_params=params(40),
        name="attn_fwd",
    )(table, q, k, vt, start)


def attn_bwd_kernel(per, slots, table_ref, q_ref, do_ref, o_ref, k_ref, v_ref, kt_ref, start_ref, lse_ref,
                    keep_ref, above_ref, below_ref, dq_ref, dk_ref, dv_ref, dq_s, dk_s, dv_s, bias_s):
    i = pl.program_id(0)
    rank = table_ref[0]
    width = q_ref.shape[1]
    heads = width // HEAD_DIM
    first = lax.broadcasted_iota(jnp.int32, (BLOCK, PAIR), 1) < HEAD_DIM

    @pl.when(i == 0)
    def _():
        dk_s[...] = jnp.zeros_like(dk_s)
        dv_s[...] = jnp.zeros_like(dv_s)

    dq_s[...] = jnp.zeros_like(dq_s)
    queries, cotangents, inner = [], [], []
    product = (do_ref[...].astype(jnp.float32) * o_ref[...].astype(jnp.float32)).T
    for h in range(heads):
        cols = slice((h // 2) * PAIR, (h // 2 + 1) * PAIR)
        keep = first if h % 2 == 0 else jnp.logical_not(first)
        pair = q_ref[:, cols]
        queries.append(jnp.where(keep, pair, jnp.zeros_like(pair)))
        pair = do_ref[:, cols]
        cotangents.append(jnp.where(keep, pair, jnp.zeros_like(pair)))
        inner.append(jnp.sum(product[h * HEAD_DIM : (h + 1) * HEAD_DIM, :], axis=0, keepdims=True))
    start = start_ref[...]
    row = i * BLOCK + lax.broadcasted_iota(jnp.int32, (BLOCK, BLOCK), 1)

    def step(kb, carry):
        col = kb * BLOCK + lax.broadcasted_iota(jnp.int32, (BLOCK, BLOCK), 0)
        bias_s[...] = jnp.where((col >= start) & (col <= row), 0.0, masked_score)
        at = pl.ds(pl.multiple_of(place(kb, rank, per) * BLOCK, BLOCK), BLOCK)
        for pair in range(heads // 2):
            cols = slice(pair * PAIR, (pair + 1) * PAIR)
            keys, values = k_ref[at, cols], v_ref[at, cols]
            probs, scores = [], []
            for h in (2 * pair, 2 * pair + 1):
                own = slice(h * HEAD_DIM, (h + 1) * HEAD_DIM)
                s = dot32(keys, queries[h], contract_last) + bias_s[...]
                p = jnp.exp(s - lse_ref[0, h : h + 1, :])
                dp = dot32(values, cotangents[h], contract_last)
                ds = (p * (dp - inner[h])).astype(low_type)
                probs.append(p.astype(low_type))
                scores.append(ds)
                dq_s[own, :] += dot32(kt_ref[own, at], ds)
            dv_s[at, cols] += dot32(probs[0], cotangents[2 * pair]) + dot32(probs[1], cotangents[2 * pair + 1])
            dk_s[at, cols] += dot32(scores[0], queries[2 * pair]) + dot32(scores[1], queries[2 * pair + 1])
        return carry

    lax.fori_loop(table_ref[1 + i], i + 1, step, 0)
    dq = dq_s[...].T * (HEAD_DIM ** (-0.5))
    here = pl.ds(pl.multiple_of(place(i, rank, per) * BLOCK, BLOCK), BLOCK)
    for c in range(0, width, PAIR):
        dq_ref[:, c : c + PAIR] = turn_back(
            dq[:, c : c + PAIR], keep_ref[here, :], above_ref[here, :], below_ref[here, :]
        ).astype(low_type)

    @pl.when(i == pl.num_programs(0) - 1)
    def _():
        @pl.loop(0, dk_s.shape[0] // BLOCK)
        def _(b):
            at = pl.ds(pl.multiple_of(b * BLOCK, BLOCK), BLOCK)
            for c in range(0, width, PAIR):
                cols = slice(c, c + PAIR)
                dk_ref[at, cols] = turn_back(
                    dk_s[at, cols], keep_ref[at, :], above_ref[at, :], below_ref[at, :]
                ).astype(low_type)
                dv_ref[at, cols] = dv_s[at, cols].astype(low_type)


def attn_bwd(half, slots, table, q, do, o, k, v, kt, start, lse, tables):
    rows, width = q.shape
    part = width // 2
    heads = part // HEAD_DIM
    count = rows // BLOCK
    per = rows // slots // BLOCK
    at = lambda i, t: place(i, t[0], per)
    whole = pl.BlockSpec((rows, part), lambda i, t: (0, half))
    turns = pl.BlockSpec((rows, PAIR), lambda i, t: (0, 0))
    result = pl.BlockSpec((rows, part), lambda i, t: (0, 0))
    return pl.pallas_call(
        functools.partial(attn_bwd_kernel, per, slots),
        grid_spec=pltpu.PrefetchScalarGridSpec(
            num_scalar_prefetch=1,
            grid=(count,),
            in_specs=[
                pl.BlockSpec((BLOCK, part), lambda i, t: (at(i, t), half)),
                pl.BlockSpec((BLOCK, part), lambda i, t: (at(i, t), half)),
                pl.BlockSpec((BLOCK, part), lambda i, t: (at(i, t), 0)),
                whole,
                whole,
                pl.BlockSpec((part, rows), lambda i, t: (half, 0)),
                pl.BlockSpec((1, BLOCK), lambda i, t: (0, at(i, t))),
                pl.BlockSpec((1, heads, BLOCK), lambda i, t: (at(i, t), 0, 0)),
                turns,
                turns,
                turns,
            ],
            out_specs=[pl.BlockSpec((BLOCK, part), lambda i, t: (at(i, t), 0)), result, result],
            scratch_shapes=[
                pltpu.VMEM((part, BLOCK), jnp.float32),
                pltpu.VMEM((rows, part), jnp.float32),
                pltpu.VMEM((rows, part), jnp.float32),
                pltpu.VMEM((BLOCK, BLOCK), jnp.float32),
            ],
        ),
        out_shape=[jax.ShapeDtypeStruct((rows, part), low_type)] * 3,
        cost_estimate=cost(25 * rows * rows * part // 2, 16 * rows * part, 8 * rows * rows // 4),
        compiler_params=params(48),
        name="attn_bwd",
    )(table, q, do, o, k, v, kt, start, lse, *tables)


def qkv_grad_kernel(*refs):
    left_ref, other_ref, rights, (out_ref, sum_ref) = refs[0], refs[1], refs[2:-2], refs[-2:]
    part = rights[0].shape[1]

    @pl.when(pl.program_id(0) == 0)
    def _():
        for n, right in enumerate(rights):
            sum_ref[n // 2 : n // 2 + 1, (n % 2) * part : (n % 2 + 1) * part] = jnp.sum(
                right[...].astype(jnp.float32), axis=0, keepdims=True
            )

    left = left_ref[...]
    for n, right in enumerate(rights):
        out_ref[n // 2, :, (n % 2) * part : (n % 2 + 1) * part] = dot32(left, right[...], contract_first).astype(low_type)
    out_ref[len(rights) // 2] = other_ref[...]


def qkv_grad(left, rights, other):
    rows, model = left.shape
    part = rights[0].shape[1]
    count = len(rights) // 2
    tile = 512
    return pl.pallas_call(
        qkv_grad_kernel,
        grid=(model // tile,),
        in_specs=[pl.BlockSpec((rows, tile), lambda n: (0, n)), pl.BlockSpec((tile, 2 * part), lambda n: (n, 0))]
        + [pl.BlockSpec((rows, part), lambda n: (0, 0), pipeline_mode=pl.Buffered(1))] * len(rights),
        out_specs=[
            pl.BlockSpec((count + 1, tile, 2 * part), lambda n: (0, n, 0)),
            pl.BlockSpec((count, 2 * part), lambda n: (0, 0)),
        ],
        out_shape=[
            jax.ShapeDtypeStruct((count + 1, model, 2 * part), low_type),
            jax.ShapeDtypeStruct((count, 2 * part), jnp.float32),
        ],
        cost_estimate=cost(4 * count * rows * model * part, 4 * rows * model),
        compiler_params=params(48),
        name="qkv_grad",
    )(left, other, *rights)


def stream(refs, buf, sem):
    step = pl.program_id(0)
    fetch_next(step, refs, buf, sem)
    return step % 2


def back_kernel(count, one_ref, two_ref, w_ref, *rest):
    dgate_ref, dup_ref, buf, sem = rest[count:]
    now = stream(rest[:count], buf, sem)
    da = dot32(buf[now], w_ref[...], contract_last)
    dgate_ref[...] = (da * one_ref[...].astype(jnp.float32)).astype(low_type)
    dup_ref[...] = (da * two_ref[...].astype(jnp.float32)).astype(low_type)


def back_through_down(dm_blocks, one, two, w):
    depth, model = w.shape
    count = len(dm_blocks)
    block = dm_blocks[0].shape[0]
    rows = block * count
    row = pl.BlockSpec((block, depth), lambda r: (r, 0))
    deep = jax.ShapeDtypeStruct((rows, depth), low_type)
    return pl.pallas_call(
        functools.partial(back_kernel, count),
        grid=(count,),
        in_specs=[row, row, pl.BlockSpec(w.shape, lambda r: (0, 0), pipeline_mode=pl.Buffered(1))] + [ANY] * count,
        out_specs=[row, row],
        out_shape=[deep, deep],
        scratch_shapes=[pltpu.VMEM((2, block, model), low_type), pltpu.SemaphoreType.DMA((2,))],
        cost_estimate=cost(2 * rows * model * depth, 2 * model * depth + 2 * rows * model + 8 * rows * depth),
        compiler_params=params(56),
        name="back_down",
    )(one, two, w, *dm_blocks)


swap_x = [(0, 1), (1, 0), (2, 3), (3, 2)]
swap_y = [(0, 2), (2, 0), (1, 3), (3, 1)]


def square(count):
    return count == 4


def gather_rows(top, end):
    x_top = lax.ppermute(top, "tensor", swap_x)
    y_end = lax.ppermute(end, "tensor", swap_y)
    x_end = lax.ppermute(end, "tensor", swap_x)
    y_top = lax.ppermute(top, "tensor", swap_y)
    first = [top, end, x_top, x_end, y_top, y_end]

    def rest(*between):
        far_top = lax.ppermute(after(x_top, *between), "tensor", swap_y)
        far_end = lax.ppermute(after(y_end, *between), "tensor", swap_x)
        return [far_top, far_end]

    return first, rest


def after(value, *others):
    return lax.optimization_barrier((value,) + others)[0]


def halves(value):
    half = value.shape[0] // 2
    return value[:half], value[half:]


def add_low(a, b):
    return (a.astype(jnp.float32) + b.astype(jnp.float32)).astype(low_type)


def scatter_first(values):
    far, half = values[3], values[3].shape[0] // 2
    top = lax.ppermute(far[:half], "tensor", swap_x)
    end = lax.ppermute(far[half:], "tensor", swap_y)
    return [top, end]


def scatter_last(values, first):
    top, end = first
    half = top.shape[0]
    for_x, for_y = values[1], values[2]
    for_y = jnp.concatenate([add_low(for_y[:half], top), for_y[half:]], axis=0)
    for_x = jnp.concatenate([for_x[:half], add_low(for_x[half:], end)], axis=0)
    from_x = lax.ppermute(for_x, "tensor", swap_x)
    from_y = lax.ppermute(for_y, "tensor", swap_y)
    return [values[0], from_x, from_y]


MESH = pl.DeviceIdType.MESH


def greet(near_x, near_y):
    barrier = pltpu.get_barrier_semaphore()
    for near in (near_x, near_y):
        pl.semaphore_signal(barrier, inc=1, device_id={"tensor": near}, device_id_type=MESH)
    pl.semaphore_wait(barrier, 2)


def neighbours():
    rank = lax.axis_index("tensor")
    return jnp.bitwise_xor(rank, 1), jnp.bitwise_xor(rank, 2)


def out_scatter_kernel(a_ref, b_ref, w_ref, x_ref, live_ref, norm_ref, x1_ref, h_ref, far_s, for_x, for_y, top_s, end_s, from_x, from_y, send, recv):
    near_x, near_y = neighbours()
    rows = x_ref.shape[0]
    half = rows // 2
    part = a_ref.shape[1]
    model = w_ref.shape[1]
    tile = 512
    greet(near_x, near_y)

    def partial(slot, which, store):
        at = pl.ds(slot * rows + which * half, half)

        @pl.loop(0, model // tile)
        def _(n):
            cols = pl.ds(pl.multiple_of(n * tile, tile), tile)
            store(cols, dot32(a_ref[at, :], w_ref[:part, cols]) + dot32(b_ref[at, :], w_ref[part:, cols]))

    def copy(index, source, target, near):
        return pltpu.make_async_remote_copy(
            src_ref=source,
            dst_ref=target,
            send_sem=send.at[index],
            recv_sem=recv.at[index],
            device_id={"tensor": near},
            device_id_type=MESH,
        )

    def into(ref, which):
        def store(cols, value):
            ref[pl.ds(which * half, half), cols] = value.astype(low_type)

        return store

    def added(ref, which, other):
        def store(cols, value):
            ref[pl.ds(which * half, half), cols] = (value + other[:, cols].astype(jnp.float32)).astype(low_type)

        return store

    t, e = pl.ds(0, half), pl.ds(half, half)
    copies = [
        copy(0, far_s.at[t], top_s, near_x),
        copy(1, far_s.at[e], end_s, near_y),
        copy(2, for_x.at[t], from_x.at[t], near_x),
        copy(3, for_y.at[e], from_y.at[e], near_y),
        copy(4, for_x.at[e], from_x.at[e], near_x),
        copy(5, for_y.at[t], from_y.at[t], near_y),
    ]
    partial(3, 0, into(far_s, 0))
    copies[0].start()
    partial(3, 1, into(far_s, 1))
    copies[1].start()
    partial(1, 0, into(for_x, 0))
    copies[2].start()
    partial(2, 1, into(for_y, 1))
    copies[3].start()
    copies[0].wait_recv()
    partial(2, 0, added(for_y, 0, top_s))
    copies[5].start()
    copies[1].wait_recv()
    partial(1, 1, added(for_x, 1, end_s))
    copies[4].start()

    def own(which):
        def store(cols, value):
            x1_ref[pl.ds(which * half, half), cols] = value

        return store

    partial(0, 0, own(0))
    partial(0, 1, own(1))
    step = 32

    def finish(which):
        @pl.loop(0, half // step)
        def _(r):
            at = pl.ds(pl.multiple_of(which * half + r * step, step), step)
            attn = x1_ref[at, :] + from_x[at, :].astype(jnp.float32) + from_y[at, :].astype(jnp.float32)
            x1 = x_ref[at, :].astype(jnp.float32) + live_ref[at, :] * attn
            x1_ref[at, :] = x1
            c = x1 - jnp.mean(x1, axis=-1, keepdims=True)
            s = lax.rsqrt(jnp.mean(c * c, axis=-1, keepdims=True) + norm_eps)
            h_ref[at, :] = (c * s * norm_ref[1:2, :] + norm_ref[3:4, :]).astype(low_type)

    copies[2].wait_recv()
    copies[5].wait_recv()
    finish(0)
    copies[3].wait_recv()
    copies[4].wait_recv()
    finish(1)
    for c in copies:
        c.wait_send()


def out_scatter(a, b, w, x, live, norm):
    rows, model = x.shape
    half = rows // 2
    big = pltpu.VMEM((rows, model), low_type)
    small = pltpu.VMEM((half, model), low_type)
    vmem = pl.BlockSpec(memory_space=pltpu.VMEM)
    total = a.shape[0]
    return pl.pallas_call(
        out_scatter_kernel,
        in_specs=[vmem] * 6,
        out_specs=[vmem] * 2,
        out_shape=[jax.ShapeDtypeStruct((rows, model), jnp.float32), jax.ShapeDtypeStruct((rows, model), low_type)],
        scratch_shapes=[
            big,
            big,
            big,
            small,
            small,
            big,
            big,
            pltpu.SemaphoreType.DMA((6,)),
            pltpu.SemaphoreType.DMA((6,)),
        ],
        cost_estimate=cost(2 * total * model * w.shape[0], 20 * rows * model),
        compiler_params=pltpu.CompilerParams(vmem_limit_bytes=48 * MIB, collective_id=0, has_side_effects=True),
        name="out_scatter",
    )(a, b, w, x, live, norm)


def remote(index, source, target, near, send, recv):
    return pltpu.make_async_remote_copy(
        src_ref=source,
        dst_ref=target,
        send_sem=send.at[index],
        recv_sem=recv.at[index],
        device_id={"tensor": near},
        device_id_type=MESH,
    )


arrival = (0, 1, 2, 5, 3, 4, 6, 7)


def arrival_slot(i):
    return jnp.where(i == 3, 5, jnp.where(i == 4, 3, jnp.where(i == 5, 4, i)))


def square_copies(all_s, half, send, recv):
    near_x, near_y = neighbours()
    at = lambda n: all_s.at[pl.ds(n * half, half)]
    return (
        remote(0, at(0), at(2), near_x, send, recv),
        remote(1, at(1), at(5), near_y, send, recv),
        remote(2, at(1), at(3), near_x, send, recv),
        remote(3, at(0), at(4), near_y, send, recv),
        remote(4, at(2), at(6), near_y, send, recv),
        remote(5, at(5), at(7), near_x, send, recv),
    )


def await_slot(i, copies):
    x_top, y_end, x_end, y_top, far_top, far_end = copies

    @pl.when(i == 2)
    def _():
        x_top.wait_recv()
        far_top.start()
        y_end.wait_recv()
        far_end.start()

    for n, c in ((4, x_end), (5, y_top), (6, far_top), (7, far_end)):

        @pl.when(i == n)
        def _(c=c):
            c.wait_recv()


def fetch_next(i, refs, buf, sem):
    def fetch(j):
        pltpu.make_async_copy(refs[j], buf.at[j % 2], sem.at[j % 2]).start()

    for j in range(len(refs)):

        @pl.when(i == max(j - 1, 0) if j else i == 0)
        def _(j=j):
            fetch(j)

    pltpu.make_async_copy(refs[0], buf.at[i % 2], sem.at[i % 2]).wait()


def gather_norm_kernel(nd, x_ref, small_ref, pos_ref, inv_ref, h_ref, full_ref, keep_ref, above_ref, below_ref,
                       all_s, full_s, stage, send, recv, local, small_send, small_recv, out_sem):
    d = lax.axis_index("dp")
    near_x, near_y = neighbours()
    half = x_ref.shape[0] // 2
    width = small_ref.shape[1]
    own = pltpu.make_async_copy(x_ref, all_s.at[pl.ds(0, 2 * half)], local)
    own.start()
    barrier = pltpu.get_barrier_semaphore()
    for near in (near_x, near_y):
        pl.semaphore_signal(barrier, inc=1, device_id={"tensor": near}, device_id_type=MESH)
    for k in range(1, nd):
        pl.semaphore_signal(barrier, inc=1, device_id={"dp": lax.rem(d + k, nd)}, device_id_type=MESH)
    pl.semaphore_wait(barrier, nd + 1)
    own.wait()
    copies = square_copies(all_s, half, send, recv)
    for c in copies[:4]:
        c.start()
    small = []
    for k in range(1, nd):
        c = pltpu.make_async_remote_copy(
            src_ref=small_ref,
            dst_ref=full_s.at[d],
            send_sem=small_send.at[k],
            recv_sem=small_recv.at[k],
            device_id={"dp": lax.rem(d + k, nd)},
            device_id_type=MESH,
        )
        c.start()
        small.append(c)
    full_s[d] = small_ref[...]
    for c in small:
        c.wait_recv()
    for n in range(nd):
        full_ref[:, n * width : (n + 1) * width] = full_s[n]
    step = 32
    lane = lax.broadcasted_iota(jnp.int32, (256, PAIR), 1) % HEAD_DIM

    def turns(at):
        angles = pos_ref[at, :] * inv_ref[...]
        cos_part, sine_part = jnp.cos(angles), jnp.sin(angles)
        keep_ref[at, :] = jnp.where(lane < ROT, cos_part, 1.0)
        above_ref[at, :] = jnp.where(lane < ROT // 2, -sine_part, 0.0)
        below_ref[at, :] = jnp.where((lane >= ROT // 2) & (lane < ROT), sine_part, 0.0)

    def out(buf, row):
        return pltpu.make_async_copy(stage.at[buf], h_ref.at[pl.ds(row, half)], out_sem.at[buf])

    def body_step(i, carry):
        await_slot(i, copies)
        row = pl.multiple_of(arrival_slot(i) * half, half)
        buf = i % 2

        @pl.when(i >= 2)
        def _():
            out(buf, row).wait()

        @pl.loop(0, half // step)
        def _(r):
            at = pl.ds(pl.multiple_of(r * step, step), step)
            x = all_s[pl.ds(pl.multiple_of(row + r * step, step), step), :].astype(jnp.float32)
            c = x - jnp.mean(x, axis=-1, keepdims=True)
            s = lax.rsqrt(jnp.mean(c * c, axis=-1, keepdims=True) + norm_eps)
            stage[buf, at, :] = (c * s * full_ref[0:1, :] + full_ref[2:3, :]).astype(low_type)

        out(buf, row).start()

        @pl.when(i < 4)
        def _():
            turns(pl.ds(pl.multiple_of(i * 512, 256), 256))
            turns(pl.ds(pl.multiple_of(i * 512 + 256, 256), 256))

        return carry

    lax.fori_loop(0, 8, body_step, 0)
    for buf in (0, 1):
        out(buf, 0).wait()
    for c in copies:
        c.wait_send()
    for c in small:
        c.wait_send()


def gather_norm(x, small, pos, inverse):
    nd = lax.axis_size("dp")
    rows, model = x.shape
    total = 4 * rows
    count, width = small.shape
    vmem = pl.BlockSpec(memory_space=pltpu.VMEM)
    table = jax.ShapeDtypeStruct((total, PAIR), jnp.float32)
    return pl.pallas_call(
        functools.partial(gather_norm_kernel, nd),
        in_specs=[ANY, vmem, vmem, vmem],
        out_specs=[ANY, vmem, vmem, vmem, vmem],
        out_shape=[
            jax.ShapeDtypeStruct((total, model), low_type),
            jax.ShapeDtypeStruct((count, width * nd), jnp.float32),
            table,
            table,
            table,
        ],
        scratch_shapes=[
            pltpu.VMEM((total, model), low_type),
            pltpu.VMEM((nd, count, width), jnp.float32),
            pltpu.VMEM((2, rows // 2, model), low_type),
            pltpu.SemaphoreType.DMA((6,)),
            pltpu.SemaphoreType.DMA((6,)),
            pltpu.SemaphoreType.DMA,
            pltpu.SemaphoreType.DMA((nd,)),
            pltpu.SemaphoreType.DMA((nd,)),
            pltpu.SemaphoreType.DMA((2,)),
        ],
        cost_estimate=cost(20 * total * model, 4 * total * model),
        compiler_params=pltpu.CompilerParams(vmem_limit_bytes=40 * MIB, collective_id=3, has_side_effects=True),
        name="gather_norm",
    )(x, small, pos, inverse)


def gather_do_kernel(d_ref, act_ref, o_a_ref, o_b_ref, wo_ref, wd_hbm, do_ref, grad_ref, mlp_ref,
                     all_s, wd_s, acc, act_s, stage, send, recv, local, act_sem, out_sem):
    near_x, near_y = neighbours()
    half = d_ref.shape[0] // 2
    model = d_ref.shape[1]
    part = o_a_ref.shape[1]
    tile = 512
    own = pltpu.make_async_copy(d_ref, all_s.at[pl.ds(0, 2 * half)], local.at[0])
    own.start()
    weights = pltpu.make_async_copy(wd_hbm, wd_s, local.at[1])
    weights.start()
    greet(near_x, near_y)
    own.wait()
    copies = square_copies(all_s, half, send, recv)
    for c in copies[:4]:
        c.start()
    acc[...] = jnp.zeros_like(acc)
    weights.wait()

    def load(i):
        return pltpu.make_async_copy(act_ref.at[pl.ds(pl.multiple_of(i * half, half), half)], act_s.at[i % 2], act_sem.at[i % 2])

    def out(i):
        return pltpu.make_async_copy(stage.at[i % 2], mlp_ref.at[pl.ds(pl.multiple_of(i * half, half), half)], out_sem.at[i % 2])

    load(0).start()

    def step(i, carry):
        @pl.when(i < 7)
        def _():
            load(i + 1).start()

        load(i).wait()

        @pl.when(i >= 2)
        def _():
            out(i - 2).wait()

        stage[i % 2] = dot32(act_s[i % 2], wd_s[...]).astype(low_type)
        out(i).start()
        await_slot(i, copies)
        at = pl.ds(pl.multiple_of(arrival_slot(i) * half, half), half)
        dattn = all_s[at, :]
        do_ref[at, :] = dot32(dattn, wo_ref[...], contract_last).astype(low_type)
        acc[:part, :] += dot32(o_a_ref[at, :], dattn, contract_first)
        acc[part:, :] += dot32(o_b_ref[at, :], dattn, contract_first)
        return carry

    lax.fori_loop(0, 8, step, 0)

    @pl.loop(0, model // tile)
    def _(n):
        cols = pl.ds(pl.multiple_of(n * tile, tile), tile)
        grad_ref[cols, :] = acc[:, cols].T.astype(low_type)

    out(6).wait()
    out(7).wait()
    for c in copies:
        c.wait_send()


def gather_do(dattn, act, o_a, o_b, wo, wd):
    rows, model = dattn.shape
    total = 4 * rows
    depth = act.shape[1]
    width = wo.shape[0]
    vmem = pl.BlockSpec(memory_space=pltpu.VMEM)
    return pl.pallas_call(
        gather_do_kernel,
        in_specs=[ANY, ANY, vmem, vmem, vmem, ANY],
        out_specs=[vmem, vmem, ANY],
        out_shape=[
            jax.ShapeDtypeStruct((total, width), low_type),
            jax.ShapeDtypeStruct((model, width), low_type),
            jax.ShapeDtypeStruct((total, model), low_type),
        ],
        scratch_shapes=[
            pltpu.VMEM((total, model), low_type),
            pltpu.VMEM(wd.shape, low_type),
            pltpu.VMEM((width, model), jnp.float32),
            pltpu.VMEM((2, rows // 2, depth), low_type),
            pltpu.VMEM((2, rows // 2, model), low_type),
            pltpu.SemaphoreType.DMA((6,)),
            pltpu.SemaphoreType.DMA((6,)),
            pltpu.SemaphoreType.DMA((2,)),
            pltpu.SemaphoreType.DMA((2,)),
            pltpu.SemaphoreType.DMA((2,)),
        ],
        cost_estimate=cost(2 * total * model * (depth + 2 * width), 6 * total * model),
        compiler_params=pltpu.CompilerParams(vmem_limit_bytes=56 * MIB, collective_id=4, has_side_effects=True),
        name="gather_do",
    )(dattn, act, o_a, o_b, wo, wd)


def exchange(rows, partial, bufs, send, recv, fill_one, fill_two):
    far_s, for_x, for_y, top_s, end_s, from_x, from_y = bufs
    near_x, near_y = neighbours()
    half = rows // 2
    t, e = pl.ds(0, half), pl.ds(half, half)
    copies = [
        remote(0, far_s.at[t], top_s, near_x, send, recv),
        remote(1, far_s.at[e], end_s, near_y, send, recv),
        remote(2, for_x.at[t], from_x.at[t], near_x, send, recv),
        remote(3, for_y.at[e], from_y.at[e], near_y, send, recv),
        remote(4, for_x.at[e], from_x.at[e], near_x, send, recv),
        remote(5, for_y.at[t], from_y.at[t], near_y, send, recv),
    ]

    def into(ref, which):
        def store(cols, value):
            ref[pl.ds(which * half, half), cols] = value.astype(low_type)

        return store

    def added(ref, which, other):
        def store(cols, value):
            ref[pl.ds(which * half, half), cols] = (value + other[:, cols].astype(jnp.float32)).astype(low_type)

        return store

    partial(3, 0, into(far_s, 0))
    copies[0].start()
    partial(3, 1, into(far_s, 1))
    copies[1].start()
    partial(1, 0, into(for_x, 0))
    copies[2].start()
    partial(2, 1, into(for_y, 1))
    copies[3].start()
    fill_one()
    copies[0].wait_recv()
    partial(2, 0, added(for_y, 0, top_s))
    copies[5].start()
    copies[1].wait_recv()
    partial(1, 1, added(for_x, 1, end_s))
    copies[4].start()
    fill_two()
    return copies


def finish_back(copies, rows, gain_row, v_ref, base_ref, own_ref, live_ref, norm_ref, from_x, from_y, dx_ref, low_ref, gain_ref, shift_ref):
    half = rows // 2
    step = 16
    gain_ref[...] = jnp.zeros_like(gain_ref)
    shift_ref[...] = jnp.zeros_like(shift_ref)

    def finish(which):
        @pl.loop(0, half // step)
        def _(r):
            at = pl.ds(pl.multiple_of(which * half + r * step, step), step)
            e = own_ref[at, :].astype(jnp.float32) + from_x[at, :].astype(jnp.float32) + from_y[at, :].astype(jnp.float32)
            v = v_ref[at, :].astype(jnp.float32)
            c = v - jnp.mean(v, axis=-1, keepdims=True)
            s = lax.rsqrt(jnp.mean(c * c, axis=-1, keepdims=True) + norm_eps)
            xh = c * s
            w = e * norm_ref[gain_row : gain_row + 1, :]
            back = s * (w - jnp.mean(w, axis=-1, keepdims=True) - xh * jnp.mean(w * xh, axis=-1, keepdims=True))
            dx = base_ref[at, :].astype(jnp.float32) + back
            dx_ref[at, :] = dx.astype(dx_ref.dtype)
            if low_ref is not None:
                low_ref[at, :] = (dx * live_ref[at, :]).astype(low_type)
            gain_ref[...] += jnp.sum(e * xh, axis=0, keepdims=True)
            shift_ref[...] += jnp.sum(e, axis=0, keepdims=True)

    copies[2].wait_recv()
    copies[5].wait_recv()
    finish(0)
    copies[3].wait_recv()
    copies[4].wait_recv()
    finish(1)
    for c in copies:
        c.wait_send()


def exchange_scratch(rows, model):
    big = pltpu.VMEM((rows, model), low_type)
    small = pltpu.VMEM((rows // 2, model), low_type)
    return [big, big, big, small, small, big, big, pltpu.SemaphoreType.DMA((6,)), pltpu.SemaphoreType.DMA((6,))]


def hidden_scatter_kernel(dgate_hbm, dup_hbm, w_hbm, h_hbm, x1_ref, og_ref, live_ref, norm_ref,
                          grad_ref, dx_ref, low_ref, gain_ref, shift_ref,
                          *scratch):
    bufs, (send, recv, g_s, w_s, h_s, stage, local, h_sem, out_sem) = scratch[:7], scratch[7:]
    rows, model = x1_ref.shape
    half = rows // 2
    near_x, near_y = neighbours()
    loads = [
        pltpu.make_async_copy(dgate_hbm, g_s.at[0], local.at[0]),
        pltpu.make_async_copy(dup_hbm, g_s.at[1], local.at[1]),
        pltpu.make_async_copy(w_hbm, w_s, local.at[2]),
    ]
    for c in loads:
        c.start()
    greet(near_x, near_y)
    for c in loads:
        c.wait()
    tile = 512

    def partial(slot, which, store):
        at = pl.ds(slot * rows + which * half, half)

        @pl.loop(0, model // tile)
        def _(n):
            cols = pl.ds(pl.multiple_of(n * tile, tile), tile)
            value = dot32(g_s[0, at, :], w_s[0, cols, :], contract_last)
            store(cols, value + dot32(g_s[1, at, :], w_s[1, cols, :], contract_last))

    def own(which):
        def store(cols, value):
            dx_ref[pl.ds(which * half, half), cols] = value

        return store

    strip = 256

    def load(i):
        return pltpu.make_async_copy(h_hbm.at[:, pl.ds(pl.multiple_of(i * strip, strip), strip)], h_s.at[i % 2], h_sem.at[i % 2])

    def outs(i):
        at = pl.ds(pl.multiple_of(i * strip, strip), strip)
        return [pltpu.make_async_copy(stage.at[i % 2, s], grad_ref.at[s, at], out_sem.at[i % 2, s]) for s in (0, 1)]

    strips = model // strip
    load(0).start()

    def strip_step(i, carry):
        @pl.when(i < strips - 1)
        def _():
            load(i + 1).start()

        load(i).wait()

        @pl.when(i >= 2)
        def _():
            for c in outs(i - 2):
                c.wait()

        turned = h_s[i % 2].T
        for s in (0, 1):
            stage[i % 2, s] = dot32(turned, g_s[s]).astype(low_type)
        for c in outs(i):
            c.start()
        return carry

    def fill_one():
        partial(0, 0, own(0))
        partial(0, 1, own(1))
        lax.fori_loop(0, 2, strip_step, 0)

    def fill_two():
        lax.fori_loop(2, strips, strip_step, 0)

    copies = exchange(rows, partial, bufs, send, recv, fill_one, fill_two)
    finish_back(copies, rows, 1, x1_ref, og_ref, dx_ref, live_ref, norm_ref, bufs[5], bufs[6], dx_ref, low_ref, gain_ref, shift_ref)
    for i in (strips - 2, strips - 1):
        for c in outs(i):
            c.wait()


def hidden_scatter(dgate, dup, w, h, x1, out_grad, live, norm):
    rows, model = x1.shape
    total, depth = dgate.shape
    vmem = pl.BlockSpec(memory_space=pltpu.VMEM)
    line = jax.ShapeDtypeStruct((1, model), jnp.float32)
    return pl.pallas_call(
        hidden_scatter_kernel,
        in_specs=[ANY, ANY, ANY, ANY, vmem, vmem, vmem, vmem],
        out_specs=[ANY, vmem, vmem, vmem, vmem],
        out_shape=[
            jax.ShapeDtypeStruct((2, model, depth), low_type),
            jax.ShapeDtypeStruct((rows, model), jnp.float32),
            jax.ShapeDtypeStruct((rows, model), low_type),
            line,
            line,
        ],
        scratch_shapes=exchange_scratch(rows, model)
        + [
            pltpu.VMEM((2, total, depth), low_type),
            pltpu.VMEM(w.shape, low_type),
            pltpu.VMEM((2, total, 256), low_type),
            pltpu.VMEM((2, 2, 256, depth), low_type),
            pltpu.SemaphoreType.DMA((3,)),
            pltpu.SemaphoreType.DMA((2,)),
            pltpu.SemaphoreType.DMA((2, 2)),
        ],
        cost_estimate=cost(8 * total * model * depth, 16 * total * model),
        compiler_params=pltpu.CompilerParams(vmem_limit_bytes=62 * MIB, collective_id=5, has_side_effects=True),
        name="hidden_scatter",
    )(dgate, dup, w, h, x1, out_grad, live, norm)


def first_scatter_kernel(count, *refs):
    lefts = refs[:count]
    w_ref, x_ref, base_ref, norm_ref, dx_ref, gain_ref, shift_ref = refs[count : count + 7]
    scratch = refs[count + 7 :]
    bufs, (send, recv, own_s) = scratch[:7], scratch[7:]
    rows, model = x_ref.shape
    half = rows // 2
    tile = 512
    near_x, near_y = neighbours()
    greet(near_x, near_y)

    def partial(slot, which, store):
        at = pl.ds(slot * rows + which * half, half)

        @pl.loop(0, model // tile)
        def _(n):
            cols = pl.ds(pl.multiple_of(n * tile, tile), tile)
            value = None
            for m, left in enumerate(lefts):
                depth = left.shape[1]
                per = w_ref.shape[2] // depth
                side = slice((m % per) * depth, (m % per + 1) * depth)
                term = dot32(left[at, :], w_ref[m // per, cols, side], contract_last)
                value = term if value is None else value + term
            store(cols, value)

    def own(which):
        def store(cols, value):
            own_s[pl.ds(which * half, half), cols] = value

        return store

    def fill_one():
        partial(0, 0, own(0))
        partial(0, 1, own(1))

    copies = exchange(rows, partial, bufs, send, recv, fill_one, lambda: None)
    finish_back(copies, rows, 0, x_ref, base_ref, own_s, None, norm_ref, bufs[5], bufs[6], dx_ref, None, gain_ref, shift_ref)


def first_scatter(lefts, w, x, base, norm):
    rows, model = x.shape
    vmem = pl.BlockSpec(memory_space=pltpu.VMEM)
    line = jax.ShapeDtypeStruct((1, model), jnp.float32)
    return pl.pallas_call(
        functools.partial(first_scatter_kernel, len(lefts)),
        in_specs=[vmem] * (len(lefts) + 4),
        out_specs=[vmem] * 3,
        out_shape=[jax.ShapeDtypeStruct((rows, model), low_type), line, line],
        scratch_shapes=exchange_scratch(rows, model) + [pltpu.VMEM((rows, model), jnp.float32)],
        cost_estimate=cost(24 * rows * model * w.shape[2], 30 * rows * model),
        compiler_params=pltpu.CompilerParams(vmem_limit_bytes=56 * MIB, collective_id=6, has_side_effects=True),
        name="first_scatter",
    )(*lefts, w, x, base, norm)

def gather_gate_up_kernel(count, h_ref, w_hbm, *rest):
    blocks, (all_ref, act_ref, one_ref, two_ref, grad_ref) = rest[:count], rest[count : count + 5]
    w_s, all_s, stage, acc, turned, dm_s, send, recv, local, h_sem, out_sem, dm_sem = rest[count + 5 :]
    near_x, near_y = neighbours()
    half = h_ref.shape[0] // 2
    own = pltpu.make_async_copy(h_ref, all_s.at[pl.ds(0, 2 * half)], local.at[0])
    own.start()
    weights = pltpu.make_async_copy(w_hbm, w_s, local.at[1])
    weights.start()
    greet(near_x, near_y)
    own.wait()
    copies = square_copies(all_s, half, send, recv)
    for c in copies[:4]:
        c.start()
    acc[...] = jnp.zeros_like(acc)
    weights.wait()
    in_order = [blocks[n] for n in arrival]
    tile = 512

    def outs(buf, row):
        return [
            pltpu.make_async_copy(stage.at[buf, n], ref.at[pl.ds(row, half)], out_sem.at[buf, n])
            for n, ref in enumerate((act_ref, one_ref, two_ref))
        ]

    def keep(i, row):
        return pltpu.make_async_copy(all_s.at[pl.ds(row, half)], all_ref.at[pl.ds(row, half)], h_sem.at[i])

    def step(i, carry):
        await_slot(i, copies)
        row = pl.multiple_of(arrival_slot(i) * half, half)
        buf = i % 2
        keep(i, row).start()

        @pl.when(i >= 2)
        def _():
            for c in outs(buf, row):
                c.wait()

        h = all_s[pl.ds(row, half), :]
        gate = dot32(h, w_s[0])
        up = dot32(h, w_s[1])
        sig = 1.0 / (1.0 + jnp.exp(-gate))
        silu = gate * sig
        act = (silu * up).astype(low_type)
        stage[buf, 0] = act
        stage[buf, 1] = (up * sig * (1.0 + gate * (1.0 - sig))).astype(low_type)
        stage[buf, 2] = silu.astype(low_type)
        for c in outs(buf, row):
            c.start()
        turned[...] = act.T
        fetch_next(i, in_order, dm_s, dm_sem)

        @pl.loop(0, acc.shape[1] // tile)
        def _(n):
            cols = pl.ds(pl.multiple_of(n * tile, tile), tile)
            acc[:, cols] += dot32(turned[...], dm_s[buf, :, cols])

        return carry

    lax.fori_loop(0, 8, step, 0)
    for buf in (0, 1):
        for c in outs(buf, 0):
            c.wait()
    for i in range(8):
        keep(i, 0).wait()
    for c in copies:
        c.wait_send()
    depth = acc.shape[0]
    strip = depth // 8

    @pl.loop(0, 8)
    def _(n):
        at = pl.ds(pl.multiple_of(n * strip, strip), strip)
        all_s[at, :] = acc[at, :].astype(low_type)

    last = pltpu.make_async_copy(all_s.at[pl.ds(0, depth)], grad_ref, local.at[0])
    last.start()
    last.wait()


def gather_gate_up(h, w, dm_blocks):
    rows, model = h.shape
    depth = w.shape[2]
    total = 4 * rows
    half = rows // 2
    deep = jax.ShapeDtypeStruct((total, depth), low_type)
    return pl.pallas_call(
        functools.partial(gather_gate_up_kernel, len(dm_blocks)),
        in_specs=[ANY] * (2 + len(dm_blocks)),
        out_specs=[ANY] * 5,
        out_shape=[
            jax.ShapeDtypeStruct((total, model), low_type),
            deep,
            deep,
            deep,
            jax.ShapeDtypeStruct((depth, model), low_type),
        ],
        scratch_shapes=[
            pltpu.VMEM(w.shape, low_type),
            pltpu.VMEM((total, model), low_type),
            pltpu.VMEM((2, 3, half, depth), low_type),
            pltpu.VMEM((depth, model), jnp.float32),
            pltpu.VMEM((depth, half), low_type),
            pltpu.VMEM((2, half, model), low_type),
            pltpu.SemaphoreType.DMA((6,)),
            pltpu.SemaphoreType.DMA((6,)),
            pltpu.SemaphoreType.DMA((2,)),
            pltpu.SemaphoreType.DMA((8,)),
            pltpu.SemaphoreType.DMA((2, 3)),
            pltpu.SemaphoreType.DMA((2,)),
        ],
        cost_estimate=cost(6 * total * model * depth, 4 * model * depth + 4 * total * model + 6 * total * depth),
        compiler_params=pltpu.CompilerParams(vmem_limit_bytes=60 * MIB, collective_id=1, has_side_effects=True),
        name="gather_gate_up",
    )(h, w, *dm_blocks)


def small_kernel(nd, nt, x_ref, o_ref, groups, partial, shares, send, recv, send_t, recv_t):
    d, t = lax.axis_index("dp"), lax.axis_index("tensor")
    width = o_ref.shape[1]
    barrier = pltpu.get_barrier_semaphore()
    for k in range(1, nd):
        pl.semaphore_signal(barrier, inc=1, device_id={"dp": lax.rem(d + k, nd)}, device_id_type=MESH)
    for k in range(1, nt):
        pl.semaphore_signal(barrier, inc=1, device_id={"tensor": lax.rem(t + k, nt)}, device_id_type=MESH)
    pl.semaphore_wait(barrier, nd + nt - 2)
    copies = []
    for k in range(1, nd):
        peer = lax.rem(d + k, nd)
        c = pltpu.make_async_remote_copy(
            src_ref=x_ref.at[:, pl.ds(pl.multiple_of(peer * width, width), width)],
            dst_ref=groups.at[k],
            send_sem=send.at[k],
            recv_sem=recv.at[k],
            device_id={"dp": peer},
            device_id_type=MESH,
        )
        c.start()
        copies.append(c)
    total = x_ref[:, pl.ds(pl.multiple_of(d * width, width), width)]
    for k in range(1, nd):
        copies[k - 1].wait_recv()
        total += groups[k]
    partial[...] = total
    shares[t] = total
    for k in range(1, nt):
        c = pltpu.make_async_remote_copy(
            src_ref=partial,
            dst_ref=shares.at[t],
            send_sem=send_t.at[k],
            recv_sem=recv_t.at[k],
            device_id={"tensor": lax.rem(t + k, nt)},
            device_id_type=MESH,
        )
        c.start()
        copies.append(c)
    for k in range(1, nt):
        copies[nd - 2 + k].wait_recv()
    total = shares[0]
    for k in range(1, nt):
        total += shares[k]
    o_ref[...] = total
    for c in copies:
        c.wait_send()


def sum_small(x):
    nd, nt = lax.axis_size("dp"), lax.axis_size("tensor")
    rows, model = x.shape
    width = model // nd
    vmem = pl.BlockSpec(memory_space=pltpu.VMEM)
    return pl.pallas_call(
        functools.partial(small_kernel, nd, nt),
        in_specs=[vmem],
        out_specs=vmem,
        out_shape=jax.ShapeDtypeStruct((rows, width), jnp.float32),
        scratch_shapes=[
            pltpu.VMEM((nd, rows, width), jnp.float32),
            pltpu.VMEM((rows, width), jnp.float32),
            pltpu.VMEM((nt, rows, width), jnp.float32),
            pltpu.SemaphoreType.DMA((nd,)),
            pltpu.SemaphoreType.DMA((nd,)),
            pltpu.SemaphoreType.DMA((nt,)),
            pltpu.SemaphoreType.DMA((nt,)),
        ],
        cost_estimate=cost(rows * model, 8 * rows * model),
        compiler_params=pltpu.CompilerParams(collective_id=2, has_side_effects=True),
        name="sum_small",
    )(x)


def body(
    tokens,
    out_grad,
    lengths,
    norm_gain,
    norm_bias,
    qkv_weight,
    qkv_bias,
    out_weight,
    gate_up_weight,
    down_weight,
    first_norm_gain,
    first_norm_bias,
    first_qkv_weight,
    first_qkv_bias,
    first_out_weight,
    first_gate_up_weight,
    first_down_weight,
    second_norm_gain,
    second_norm_bias,
    second_qkv_weight,
    second_qkv_bias,
    second_out_weight,
    second_gate_up_weight,
    second_down_weight,
):
    slots = lax.axis_size("tensor")
    rank = lax.axis_index("tensor")
    own_rows = tokens.shape[0]
    group_rows = own_rows * slots
    width = out_weight.shape[0]
    order = rank if square(slots) else jnp.zeros_like(rank)

    chunk = jnp.bitwise_xor(jnp.arange(slots, dtype=jnp.int32), order)
    row_index = (chunk[:, None] * own_rows + jnp.arange(own_rows, dtype=jnp.int32)[None, :]).reshape(-1)
    seq_start, _ = layout(lengths[0], row_index)
    position = row_index - seq_start
    own_index = rank * own_rows + jnp.arange(own_rows, dtype=jnp.int32)
    live = layout(lengths[0], own_index)[1][:, None]
    block_start, _ = layout(lengths[0], jnp.arange(group_rows // BLOCK, dtype=jnp.int32) * BLOCK)
    table = jnp.concatenate([order.reshape(1).astype(jnp.int32), block_start // BLOCK])
    starts = seq_start[None, :]
    small_low = jnp.concatenate([norm_gain, norm_bias, qkv_bias, qkv_bias[:1]], axis=0).astype(low_type)
    own_bias = lambda full: lax.dynamic_slice_in_dim(full[4:7], rank * width, width, 1)[:, None, :]

    if square(slots):
        qkv_full = lax.all_gather(qkv_weight.astype(low_type), "dp", axis=1, tiled=True)
        lane = jnp.arange(PAIR, dtype=jnp.int32) % (ROT // 2)
        inverse = jnp.power(rope_base, -lane.astype(jnp.float32) * (2.0 / ROT))[None, :]
        h1, small_full, *tables = gather_norm(
            tokens, small_low.astype(jnp.float32), position.astype(jnp.float32)[:, None], inverse
        )
        norm = small_full[:4]
        out_low = after(out_weight.astype(low_type), qkv_full, h1)
        out_full = lax.all_gather(out_low, "dp", axis=1, tiled=True)
        dm_own = (after(out_grad, h1).astype(jnp.float32) * live).astype(low_type)
        dm_first, dm_rest = gather_rows(*halves(dm_own))
        q, k, v, kt, vt = qkv_all(h1, qkv_full, own_bias(small_full), tables)
        gate_up_low = after(gate_up_weight.astype(low_type), out_full, q)
        gate_up_full = lax.all_gather(gate_up_low, "dp", axis=1, tiled=True)

        o_a, lse_a = attn_fwd(0, slots, table, q, k, vt, starts)
        dm_far = dm_rest(o_a)
        o_b, lse_b = attn_fwd(1, slots, table, after(q, o_a, *dm_first), k, vt, starts)
        o_b = after(o_b, *dm_far)
        dm_blocks = dm_first + dm_far

        x1, h2_own = out_scatter(o_a, o_b, out_full, tokens, live, norm)
        down_low = after(down_weight.astype(low_type), gate_up_full, h2_own)
        down_full = lax.all_gather(down_low, "dp", axis=1, tiled=True)
        h2, act, slope_gate, slope_up, grad_down = gather_gate_up(h2_own, gate_up_full, dm_blocks)
        grad_down_own = lax.psum_scatter(after(grad_down, down_full), "dp", scatter_dimension=1, tiled=True)

        dgate, dup = back_through_down(dm_blocks, slope_gate, slope_up, down_full)
        grad_gate_up, dx1, dattn_own, gain_two, shift_two = hidden_scatter(
            dgate, dup, gate_up_full, h2, x1, out_grad, live, norm
        )
        grad_gate_up = after(grad_gate_up, grad_down_own)
        grad_gate_up_own = lax.psum_scatter(grad_gate_up, "dp", scatter_dimension=1, tiled=True)

        do, grad_out, mlp = gather_do(dattn_own, act, o_a, o_b, out_full, down_full)
        mlp = [mlp[j * own_rows : (j + 1) * own_rows] for j in range(slots)]
        mlp_first = scatter_first(mlp)
        back_a = attn_bwd(0, slots, table, q, do, o_a, k, v, kt, starts, lse_a, tables)
        mlp_parts = scatter_last(mlp, [after(part, back_a[0]) for part in mlp_first])
        back_b = attn_bwd(1, slots, table, q, after(do, back_a[0], *mlp_first), o_b, k, v, kt, starts, lse_b, tables)
        dlin = [side for pair in zip(back_a, back_b) for side in pair]
        grad_rest, bias_local = qkv_grad(h1, [after(dlin[0], *mlp_parts)] + dlin[1:], grad_out)
        late = [after(dlin[0], grad_rest)] + dlin[1:]
        input_grad, gain_one, shift_one = first_scatter(late, qkv_full, tokens, dx1, norm)
        grad_rest = after(grad_rest, grad_gate_up_own)
        grad_rest_own = lax.psum_scatter(grad_rest, "dp", scatter_dimension=1, tiled=True)
        grad_qkv_own = grad_rest_own[:3]
        grad_out_own = lax.optimization_barrier(grad_rest_own[3].T)
        layer_out = (x1 + live * sum(part.astype(jnp.float32) for part in mlp_parts)).astype(low_type)
    else:
        everyone = lambda value: lax.all_gather(value, "tensor", axis=0, tiled=True)
        scatter = lambda value, axis, at: lax.psum_scatter(value.astype(low_type), axis, scatter_dimension=at, tiled=True)
        small_full = lax.all_gather(small_low, "dp", axis=1, tiled=True).astype(jnp.float32)
        qkv_full, out_full, gate_up_full, down_full = (
            lax.all_gather(w.astype(low_type), "dp", axis=1, tiled=True)
            for w in (qkv_weight, out_weight, gate_up_weight, down_weight)
        )
        gain_rows, shift_rows = small_full[0:2], small_full[2:4]
        rows_in, cotangent = tokens.astype(jnp.float32), out_grad.astype(jnp.float32)
        tables = rotary_tables(position)
        h1 = everyone(layer_norm(rows_in, gain_rows[0], shift_rows[0]).astype(low_type))
        q, k, v, kt, vt = qkv_all(h1, qkv_full, own_bias(small_full), tables)
        o_a, lse_a = attn_fwd(0, slots, table, q, k, vt, starts)
        o_b, lse_b = attn_fwd(1, slots, table, q, k, vt, starts)
        o = jnp.concatenate([o_a, o_b], axis=1)
        x1 = rows_in + live * scatter(dot32(o, out_full), "tensor", 0).astype(jnp.float32)
        h2 = everyone(layer_norm(x1, gain_rows[1], shift_rows[1]).astype(low_type))
        gate, up = dot32(h2, gate_up_full[0]), dot32(h2, gate_up_full[1])
        sig = 1.0 / (1.0 + jnp.exp(-gate))
        act = (gate * sig * up).astype(low_type)
        mlp_rows = scatter(dot32(act, down_full), "tensor", 0).astype(jnp.float32)
        layer_out = (x1 + live * mlp_rows).astype(low_type)
        dm = everyone((cotangent * live).astype(low_type))
        da = dot32(dm, down_full, contract_last)
        dgate = (da * up * sig * (1.0 + gate * (1.0 - sig))).astype(low_type)
        dup = (da * gate * sig).astype(low_type)
        grad_down_own = scatter(dot32(act, dm, contract_first), "dp", 1)
        grad_gate_up = jnp.stack([dot32(h2, dgate, contract_first), dot32(h2, dup, contract_first)])
        grad_gate_up_own = scatter(grad_gate_up, "dp", 1)
        dh2 = dot32(dgate, gate_up_full[0], contract_last) + dot32(dup, gate_up_full[1], contract_last)
        dh2 = scatter(dh2, "tensor", 0).astype(jnp.float32)
        back, gain_two, shift_two = jax.vjp(layer_norm, x1, gain_rows[1], shift_rows[1])[1](dh2)
        dx1 = cotangent + back
        dattn = everyone((dx1 * live).astype(low_type))
        do = dot32(dattn, out_full, contract_last).astype(low_type)
        grad_out = dot32(dattn, o, contract_first).astype(low_type)
        back_a = attn_bwd(0, slots, table, q, do, o_a, k, v, kt, starts, lse_a, tables)
        back_b = attn_bwd(1, slots, table, q, do, o_b, k, v, kt, starts, lse_b, tables)
        dlin = [side for pair in zip(back_a, back_b) for side in pair]
        grad_rest, bias_local = qkv_grad(h1, dlin, grad_out)
        grad_rest_own = scatter(grad_rest, "dp", 1)
        grad_qkv_own, grad_out_own = grad_rest_own[:3], grad_rest_own[3].T
        dh1 = sum(
            dot32(jnp.concatenate(dlin[2 * n : 2 * n + 2], axis=1), qkv_full[n], contract_last) for n in range(3)
        )
        dh1 = scatter(dh1, "tensor", 0).astype(jnp.float32)
        back, gain_one, shift_one = jax.vjp(layer_norm, rows_in, gain_rows[0], shift_rows[0])[1](dh1)
        input_grad = (dx1 + back).astype(low_type)
        gain_one, gain_two, shift_one, shift_two = (
            value[None, :] for value in (gain_one, gain_two, shift_one, shift_two)
        )

    bias_placed = lax.dynamic_update_slice(
        jnp.zeros((3, small_full.shape[1]), jnp.float32), bias_local, (jnp.int32(0), rank * width)
    )
    small_local = jnp.concatenate([gain_one, gain_two, shift_one, shift_two, bias_placed, bias_placed[:1]], axis=0)
    small_own = sum_small(small_local)

    own_grads = (
        small_own[0:2],
        small_own[2:4],
        grad_qkv_own.astype(jnp.float32),
        small_own[4:7],
        grad_out_own.astype(jnp.float32),
        grad_gate_up_own.astype(jnp.float32),
        grad_down_own.astype(jnp.float32),
    )
    masters = (norm_gain, norm_bias, qkv_weight, qkv_bias, out_weight, gate_up_weight, down_weight)
    firsts = (
        first_norm_gain,
        first_norm_bias,
        first_qkv_weight,
        first_qkv_bias,
        first_out_weight,
        first_gate_up_weight,
        first_down_weight,
    )
    seconds = (
        second_norm_gain,
        second_norm_bias,
        second_qkv_weight,
        second_qkv_bias,
        second_out_weight,
        second_gate_up_weight,
        second_down_weight,
    )
    decays = (0.0, 0.0, weight_decay, 0.0, weight_decay, weight_decay, weight_decay)
    new_change = []
    new_first = []
    new_second = []
    for weight_now, gradient, moment_one, moment_two, decay_rate in zip(
        masters, own_grads, firsts, seconds, decays
    ):
        change, moment_next, square_next = adamw_update(
            weight_now, gradient, moment_one, moment_two, decay_rate
        )
        new_change.append(change)
        new_first.append(moment_next)
        new_second.append(square_next)
    return (
        (layer_out, input_grad)
        + own_grads
        + tuple(new_change)
        + tuple(new_first)
        + tuple(new_second)
    )


def solution(mesh):
    return jax.shard_map(
        body,
        mesh=mesh,
        in_specs=(
            P(("dp", "tensor"), None),
            P(("dp", "tensor"), None),
            P("dp", None),
            P(None, "dp"),
            P(None, "dp"),
            P(None, "dp", "tensor"),
            P(None, "dp"),
            P("tensor", "dp"),
            P(None, "dp", "tensor"),
            P("tensor", "dp"),
            P(None, "dp"),
            P(None, "dp"),
            P(None, "dp", "tensor"),
            P(None, "dp"),
            P("tensor", "dp"),
            P(None, "dp", "tensor"),
            P("tensor", "dp"),
            P(None, "dp"),
            P(None, "dp"),
            P(None, "dp", "tensor"),
            P(None, "dp"),
            P("tensor", "dp"),
            P(None, "dp", "tensor"),
            P("tensor", "dp"),
        ),
        out_specs=(
            P(("dp", "tensor"), None),
            P(("dp", "tensor"), None),
            P(None, "dp"),
            P(None, "dp"),
            P(None, "dp", "tensor"),
            P(None, "dp"),
            P("tensor", "dp"),
            P(None, "dp", "tensor"),
            P("tensor", "dp"),
            P(None, "dp"),
            P(None, "dp"),
            P(None, "dp", "tensor"),
            P(None, "dp"),
            P("tensor", "dp"),
            P(None, "dp", "tensor"),
            P("tensor", "dp"),
            P(None, "dp"),
            P(None, "dp"),
            P(None, "dp", "tensor"),
            P(None, "dp"),
            P("tensor", "dp"),
            P(None, "dp", "tensor"),
            P("tensor", "dp"),
            P(None, "dp"),
            P(None, "dp"),
            P(None, "dp", "tensor"),
            P(None, "dp"),
            P("tensor", "dp"),
            P(None, "dp", "tensor"),
            P("tensor", "dp"),
        ),
        check_vma=False,
    )
```

```python
import functools

import jax
import jax.numpy as jnp
from jax import lax
from jax.experimental import pallas as pl
from jax.experimental.pallas import tpu as pltpu
from jax.sharding import PartitionSpec as P

HEAD_DIM = 64
ROT = 16
PAIR = 2 * HEAD_DIM
BLOCK = 256

norm_eps = 1e-05
rope_base = 10000.0
beta_one = 0.9
beta_two = 0.95
adam_eps = 1e-08
learn_rate = 0.01
weight_decay = 0.1
step_count = 10.0
masked_score = -1e30
contract_last = (((1,), (1,)), ((), ()))
contract_first = (((0,), (0,)), ((), ()))
low_type = jnp.bfloat16
MIB = 2**20


def layout(seq_lengths, row_index):
    slot = jnp.arange(seq_lengths.shape[0])
    seq_ends = jnp.sum(
        jnp.where(slot[:, None] <= slot[None, :], seq_lengths[:, None], 0), axis=0
    )
    passed = row_index[:, None] >= seq_ends[None, :]
    seq_start = jnp.sum(jnp.where(passed, seq_lengths[None, :], 0), axis=1)
    live_rows = (row_index < jnp.sum(seq_lengths)).astype(jnp.float32)
    return (seq_start, live_rows)


def rotary_tables(position):
    half_rot = ROT // 2
    lane = jnp.arange(PAIR, dtype=jnp.int32) % HEAD_DIM
    powers = (lane % half_rot).astype(jnp.float32) * (2.0 / ROT)
    inverse = jnp.power(rope_base, -powers)
    angles = position.astype(jnp.float32)[:, None] * inverse[None, :]
    cos_part, sine_part = jnp.cos(angles), jnp.sin(angles)
    lane = lane[None, :]
    keep = jnp.where(lane < ROT, cos_part, 1.0)
    above = jnp.where(lane < half_rot, -sine_part, 0.0)
    below = jnp.where((lane >= half_rot) & (lane < ROT), sine_part, 0.0)
    return (keep, above, below)


def dot32(a, b, dims=None):
    if dims is None:
        return jnp.dot(a, b, preferred_element_type=jnp.float32)
    return lax.dot_general(a, b, dims, preferred_element_type=jnp.float32)


def turn(values, keep, above, below):
    up = pltpu.roll(values, PAIR - ROT // 2, 1)
    down = pltpu.roll(values, ROT // 2, 1)
    return values * keep + up * above + down * below


def turn_back(values, keep, above, below):
    up = pltpu.roll(values, PAIR - ROT // 2, 1)
    down = pltpu.roll(values, ROT // 2, 1)
    return values * keep - up * above - down * below


def adamw_update(weight_now, gradient, moment_one, moment_two, decay_rate):
    moment_one = beta_one * moment_one + (1.0 - beta_one) * gradient
    moment_two = beta_two * moment_two + (1.0 - beta_two) * gradient * gradient
    scaled_one = moment_one / (1.0 - beta_one**step_count)
    scaled_two = moment_two / (1.0 - beta_two**step_count)
    change = scaled_one / (jnp.sqrt(scaled_two) + adam_eps) + decay_rate * weight_now
    return (-learn_rate * change, moment_one, moment_two)


def cost(flops, moved, exps=0):
    return pl.CostEstimate(flops=int(flops) // 16, bytes_accessed=int(moved) // 16, transcendentals=int(exps) // 16)


def params(limit):
    return pltpu.CompilerParams(vmem_limit_bytes=limit * MIB)


ANY = pl.BlockSpec(memory_space=pl.ANY)


def stream(refs, buf, sem):
    step = pl.program_id(0)

    def fetch(j, slot):
        pltpu.make_async_copy(refs[j], buf.at[slot], sem.at[slot]).start()

    @pl.when(step == 0)
    def _():
        fetch(0, 0)

    for j in range(1, len(refs)):

        @pl.when(step == j - 1)
        def _(j=j):
            fetch(j, j % 2)

    now = step % 2
    pltpu.make_async_copy(refs[0], buf.at[now], sem.at[now]).wait()
    return now


def layer_norm(values, gain_row, shift_row):
    center = values - jnp.mean(values, axis=-1, keepdims=True)
    spread = jnp.mean(center * center, axis=-1, keepdims=True)
    return center * lax.rsqrt(spread + norm_eps) * gain_row + shift_row


def qkv_kernel(scale, h_ref, w_ref, bias_ref, keep_ref, above_ref, below_ref, q_ref, k_ref, v_ref, kt_ref, vt_ref):
    h = h_ref[...]
    keep, above, below = keep_ref[...], above_ref[...], below_ref[...]
    width = q_ref.shape[1]
    lin = dot32(h, w_ref[0]) + bias_ref[0]
    for c in range(0, width, PAIR):
        u = turn(lin[:, c : c + PAIR], keep, above, below)
        q_ref[:, c : c + PAIR] = (u.astype(low_type) * scale).astype(low_type)
    lin = dot32(h, w_ref[1]) + bias_ref[1]
    for c in range(0, width, PAIR):
        u = turn(lin[:, c : c + PAIR], keep, above, below)
        k_ref[:, c : c + PAIR] = u.astype(low_type)
        kt_ref[c : c + PAIR, :] = u.T.astype(low_type)
    lin = dot32(h, w_ref[2]) + bias_ref[2]
    v_ref[...] = lin.astype(low_type)
    vt_ref[...] = lin.T.astype(low_type)


def qkv_all(h, w, bias, tables):
    total, model = h.shape
    rows = 256
    width = w.shape[2]
    row = lambda n: pl.BlockSpec((rows, n), lambda i: (i, 0))
    col = pl.BlockSpec((width, rows), lambda i: (0, i))
    flat = jax.ShapeDtypeStruct((total, width), low_type)
    turned = jax.ShapeDtypeStruct((width, total), low_type)
    return pl.pallas_call(
        functools.partial(qkv_kernel, HEAD_DIM ** (-0.5)),
        grid=(total // rows,),
        in_specs=[
            row(model),
            pl.BlockSpec(w.shape, lambda i: (0, 0, 0), pipeline_mode=pl.Buffered(1)),
            pl.BlockSpec(bias.shape, lambda i: (0, 0, 0)),
            row(PAIR),
            row(PAIR),
            row(PAIR),
        ],
        out_specs=[row(width), row(width), row(width), col, col],
        out_shape=[flat, flat, flat, turned, turned],
        cost_estimate=cost(6 * total * model * width, 6 * model * width + 10 * total * model),
        compiler_params=params(48),
        name="qkv",
    )(h, w, bias, *tables)


def place(block, rank, per):
    return jnp.bitwise_xor(block // per, rank) * per + block % per


def attn_fwd_kernel(per, table_ref, q_ref, k_ref, vt_ref, start_ref, o_ref, lse_ref, m_s, l_s, acc_s):
    i = pl.program_id(0)
    rank = table_ref[0]
    heads = q_ref.shape[1] // HEAD_DIM
    first = lax.broadcasted_iota(jnp.int32, (BLOCK, PAIR), 1) < HEAD_DIM
    queries = []
    for h in range(heads):
        pair = q_ref[:, (h // 2) * PAIR : (h // 2 + 1) * PAIR]
        keep = first if h % 2 == 0 else jnp.logical_not(first)
        queries.append(jnp.where(keep, pair, jnp.zeros_like(pair)))
    m_s[...] = jnp.full_like(m_s, -jnp.inf)
    l_s[...] = jnp.zeros_like(l_s)
    acc_s[...] = jnp.zeros_like(acc_s)
    start = start_ref[...]
    row = i * BLOCK + lax.broadcasted_iota(jnp.int32, (BLOCK, BLOCK), 1)

    def step(kb, carry):
        col = kb * BLOCK + lax.broadcasted_iota(jnp.int32, (BLOCK, BLOCK), 0)
        bias = jnp.where((col >= start) & (col <= row), 0.0, masked_score)
        at = pl.ds(pl.multiple_of(place(kb, rank, per) * BLOCK, BLOCK), BLOCK)
        scores = [
            dot32(k_ref[at, (h // 2) * PAIR : (h // 2 + 1) * PAIR], queries[h], contract_last) for h in range(heads)
        ]
        probs, alphas = [], []
        for h in range(heads):
            s = scores[h] + bias
            m_old = m_s[h : h + 1, :]
            m_new = jnp.maximum(m_old, jnp.max(s, axis=0, keepdims=True))
            alpha = jnp.exp(m_old - m_new)
            p = jnp.exp(s - m_new)
            l_s[h : h + 1, :] = l_s[h : h + 1, :] * alpha + jnp.sum(p, axis=0, keepdims=True)
            m_s[h : h + 1, :] = m_new
            probs.append(p.astype(low_type))
            alphas.append(alpha)
        for h in range(heads):
            own = slice(h * HEAD_DIM, (h + 1) * HEAD_DIM)
            acc_s[own, :] = acc_s[own, :] * alphas[h] + dot32(vt_ref[own, at], probs[h])
        return carry

    lax.fori_loop(table_ref[1 + i], i + 1, step, 0)
    for h in range(heads):
        own = slice(h * HEAD_DIM, (h + 1) * HEAD_DIM)
        acc_s[own, :] = acc_s[own, :] / l_s[h : h + 1, :]
    o_ref[...] = acc_s[...].T.astype(low_type)
    lse_ref[0] = m_s[...] + jnp.log(l_s[...])


def attn_fwd(half, slots, table, q, k, vt, start):
    rows, width = q.shape
    part = width // 2
    heads = part // HEAD_DIM
    count = rows // BLOCK
    per = rows // slots // BLOCK
    at = lambda i, t: place(i, t[0], per)
    return pl.pallas_call(
        functools.partial(attn_fwd_kernel, per),
        grid_spec=pltpu.PrefetchScalarGridSpec(
            num_scalar_prefetch=1,
            grid=(count,),
            in_specs=[
                pl.BlockSpec((BLOCK, part), lambda i, t: (at(i, t), half)),
                pl.BlockSpec((rows, part), lambda i, t: (0, half)),
                pl.BlockSpec((part, rows), lambda i, t: (half, 0)),
                pl.BlockSpec((1, BLOCK), lambda i, t: (0, at(i, t))),
            ],
            out_specs=[
                pl.BlockSpec((BLOCK, part), lambda i, t: (at(i, t), 0)),
                pl.BlockSpec((1, heads, BLOCK), lambda i, t: (at(i, t), 0, 0)),
            ],
            scratch_shapes=[
                pltpu.VMEM((heads, BLOCK), jnp.float32),
                pltpu.VMEM((heads, BLOCK), jnp.float32),
                pltpu.VMEM((part, BLOCK), jnp.float32),
            ],
        ),
        out_shape=[
            jax.ShapeDtypeStruct((rows, part), low_type),
            jax.ShapeDtypeStruct((count, heads, BLOCK), jnp.float32),
        ],
        cost_estimate=cost(half * 10**13, rows * part, 0),
        compiler_params=params(40),
        name="attn_fwd",
    )(table, q, k, vt, start)


def attn_bwd_kernel(per, slots, table_ref, q_ref, do_ref, o_ref, k_ref, v_ref, kt_ref, start_ref, lse_ref,
                    keep_ref, above_ref, below_ref, dq_ref, dk_ref, dv_ref, dq_s, dk_s, dv_s):
    i = pl.program_id(0)
    rank = table_ref[0]
    width = q_ref.shape[1]
    heads = width // HEAD_DIM
    first = lax.broadcasted_iota(jnp.int32, (BLOCK, PAIR), 1) < HEAD_DIM

    @pl.when(i == 0)
    def _():
        dk_s[...] = jnp.zeros_like(dk_s)
        dv_s[...] = jnp.zeros_like(dv_s)

    dq_s[...] = jnp.zeros_like(dq_s)
    queries, cotangents, inner = [], [], []
    product = (do_ref[...].astype(jnp.float32) * o_ref[...].astype(jnp.float32)).T
    for h in range(heads):
        cols = slice((h // 2) * PAIR, (h // 2 + 1) * PAIR)
        keep = first if h % 2 == 0 else jnp.logical_not(first)
        pair = q_ref[:, cols]
        queries.append(jnp.where(keep, pair, jnp.zeros_like(pair)))
        pair = do_ref[:, cols]
        cotangents.append(jnp.where(keep, pair, jnp.zeros_like(pair)))
        inner.append(jnp.sum(product[h * HEAD_DIM : (h + 1) * HEAD_DIM, :], axis=0, keepdims=True))
    start = start_ref[...]
    row = i * BLOCK + lax.broadcasted_iota(jnp.int32, (BLOCK, BLOCK), 1)

    def step(kb, carry):
        col = kb * BLOCK + lax.broadcasted_iota(jnp.int32, (BLOCK, BLOCK), 0)
        bias = jnp.where((col >= start) & (col <= row), 0.0, masked_score)
        at = pl.ds(pl.multiple_of(place(kb, rank, per) * BLOCK, BLOCK), BLOCK)
        raw, grads = [], []
        for h in range(heads):
            cols = slice((h // 2) * PAIR, (h // 2 + 1) * PAIR)
            raw.append(dot32(k_ref[at, cols], queries[h], contract_last))
            grads.append(dot32(v_ref[at, cols], cotangents[h], contract_last))
        probs, scores = [], []
        for h in range(heads):
            p = jnp.exp(raw[h] + bias - lse_ref[0, h : h + 1, :])
            scores.append((p * (grads[h] - inner[h])).astype(low_type))
            probs.append(p.astype(low_type))
        for h in range(heads):
            own = slice(h * HEAD_DIM, (h + 1) * HEAD_DIM)
            dq_s[own, :] += dot32(kt_ref[own, at], scores[h])
        for one in range(0, heads, 2):
            cols = slice(one * HEAD_DIM, one * HEAD_DIM + PAIR)
            dv_s[at, cols] += dot32(probs[one], cotangents[one]) + dot32(probs[one + 1], cotangents[one + 1])
            dk_s[at, cols] += dot32(scores[one], queries[one]) + dot32(scores[one + 1], queries[one + 1])
        return carry

    lax.fori_loop(table_ref[1 + i], i + 1, step, 0)
    dq = dq_s[...].T * (HEAD_DIM ** (-0.5))
    here = pl.ds(pl.multiple_of(place(i, rank, per) * BLOCK, BLOCK), BLOCK)
    for c in range(0, width, PAIR):
        dq_ref[:, c : c + PAIR] = turn_back(
            dq[:, c : c + PAIR], keep_ref[here, :], above_ref[here, :], below_ref[here, :]
        ).astype(low_type)

    @pl.when(i == pl.num_programs(0) - 1)
    def _():
        @pl.loop(0, dk_s.shape[0] // BLOCK)
        def _(b):
            at = pl.ds(pl.multiple_of(b * BLOCK, BLOCK), BLOCK)
            for c in range(0, width, PAIR):
                cols = slice(c, c + PAIR)
                dk_ref[at, cols] = turn_back(
                    dk_s[at, cols], keep_ref[at, :], above_ref[at, :], below_ref[at, :]
                ).astype(low_type)
                dv_ref[at, cols] = dv_s[at, cols].astype(low_type)


def attn_bwd(half, slots, table, q, do, o, k, v, kt, start, lse, tables):
    rows, width = q.shape
    part = width // 2
    heads = part // HEAD_DIM
    count = rows // BLOCK
    per = rows // slots // BLOCK
    at = lambda i, t: place(i, t[0], per)
    whole = pl.BlockSpec((rows, part), lambda i, t: (0, half))
    turns = pl.BlockSpec((rows, PAIR), lambda i, t: (0, 0))
    result = pl.BlockSpec((rows, part), lambda i, t: (0, 0))
    return pl.pallas_call(
        functools.partial(attn_bwd_kernel, per, slots),
        grid_spec=pltpu.PrefetchScalarGridSpec(
            num_scalar_prefetch=1,
            grid=(count,),
            in_specs=[
                pl.BlockSpec((BLOCK, part), lambda i, t: (at(i, t), half)),
                pl.BlockSpec((BLOCK, part), lambda i, t: (at(i, t), half)),
                pl.BlockSpec((BLOCK, part), lambda i, t: (at(i, t), 0)),
                whole,
                whole,
                pl.BlockSpec((part, rows), lambda i, t: (half, 0)),
                pl.BlockSpec((1, BLOCK), lambda i, t: (0, at(i, t))),
                pl.BlockSpec((1, heads, BLOCK), lambda i, t: (at(i, t), 0, 0)),
                turns,
                turns,
                turns,
            ],
            out_specs=[pl.BlockSpec((BLOCK, part), lambda i, t: (at(i, t), 0)), result, result],
            scratch_shapes=[
                pltpu.VMEM((part, BLOCK), jnp.float32),
                pltpu.VMEM((rows, part), jnp.float32),
                pltpu.VMEM((rows, part), jnp.float32),
            ],
        ),
        out_shape=[jax.ShapeDtypeStruct((rows, part), low_type)] * 3,
        cost_estimate=cost(25 * rows * rows * part // 2, 16 * rows * part, 8 * rows * rows // 4),
        compiler_params=params(48),
        name="attn_bwd",
    )(table, q, do, o, k, v, kt, start, lse, *tables)


def qkv_grad_kernel(*refs):
    left_ref, other_ref, rights, (out_ref, sum_ref) = refs[0], refs[1], refs[2:-2], refs[-2:]
    part = rights[0].shape[1]

    @pl.when(pl.program_id(0) == 0)
    def _():
        for n, right in enumerate(rights):
            sum_ref[n // 2 : n // 2 + 1, (n % 2) * part : (n % 2 + 1) * part] = jnp.sum(
                right[...].astype(jnp.float32), axis=0, keepdims=True
            )

    left = left_ref[...]
    for n, right in enumerate(rights):
        out_ref[n // 2, :, (n % 2) * part : (n % 2 + 1) * part] = dot32(left, right[...], contract_first).astype(low_type)
    out_ref[len(rights) // 2] = other_ref[...]


def qkv_grad(left, rights, other):
    rows, model = left.shape
    part = rights[0].shape[1]
    count = len(rights) // 2
    tile = 512
    return pl.pallas_call(
        qkv_grad_kernel,
        grid=(model // tile,),
        in_specs=[pl.BlockSpec((rows, tile), lambda n: (0, n)), pl.BlockSpec((tile, 2 * part), lambda n: (n, 0))]
        + [pl.BlockSpec((rows, part), lambda n: (0, 0), pipeline_mode=pl.Buffered(1))] * len(rights),
        out_specs=[
            pl.BlockSpec((count + 1, tile, 2 * part), lambda n: (0, n, 0)),
            pl.BlockSpec((count, 2 * part), lambda n: (0, 0)),
        ],
        out_shape=[
            jax.ShapeDtypeStruct((count + 1, model, 2 * part), low_type),
            jax.ShapeDtypeStruct((count, 2 * part), jnp.float32),
        ],
        cost_estimate=cost(4 * count * rows * model * part, 4 * rows * model),
        compiler_params=params(48),
        name="qkv_grad",
    )(left, other, *rights)


def stream(refs, buf, sem):
    step = pl.program_id(0)
    fetch_next(step, refs, buf, sem)
    return step % 2


def back_kernel(count, one_ref, two_ref, w_ref, *rest):
    dgate_ref, dup_ref, buf, sem = rest[count:]
    now = stream(rest[:count], buf, sem)
    da = dot32(buf[now], w_ref[...], contract_last)
    dgate_ref[...] = (da * one_ref[...].astype(jnp.float32)).astype(low_type)
    dup_ref[...] = (da * two_ref[...].astype(jnp.float32)).astype(low_type)


def back_through_down(dm_blocks, one, two, w):
    depth, model = w.shape
    count = len(dm_blocks)
    block = dm_blocks[0].shape[0]
    rows = block * count
    row = pl.BlockSpec((block, depth), lambda r: (r, 0))
    deep = jax.ShapeDtypeStruct((rows, depth), low_type)
    return pl.pallas_call(
        functools.partial(back_kernel, count),
        grid=(count,),
        in_specs=[row, row, pl.BlockSpec(w.shape, lambda r: (0, 0), pipeline_mode=pl.Buffered(1))] + [ANY] * count,
        out_specs=[row, row],
        out_shape=[deep, deep],
        scratch_shapes=[pltpu.VMEM((2, block, model), low_type), pltpu.SemaphoreType.DMA((2,))],
        cost_estimate=cost(2 * rows * model * depth, 2 * model * depth + 2 * rows * model + 8 * rows * depth),
        compiler_params=params(56),
        name="back_down",
    )(one, two, w, *dm_blocks)


swap_x = [(0, 1), (1, 0), (2, 3), (3, 2)]
swap_y = [(0, 2), (2, 0), (1, 3), (3, 1)]


def square(count):
    return count == 4


def gather_rows(top, end):
    x_top = lax.ppermute(top, "tensor", swap_x)
    y_end = lax.ppermute(end, "tensor", swap_y)
    x_end = lax.ppermute(end, "tensor", swap_x)
    y_top = lax.ppermute(top, "tensor", swap_y)
    first = [top, end, x_top, x_end, y_top, y_end]

    def rest(*between):
        far_top = lax.ppermute(after(x_top, *between), "tensor", swap_y)
        far_end = lax.ppermute(after(y_end, *between), "tensor", swap_x)
        return [far_top, far_end]

    return first, rest


def after(value, *others):
    return lax.optimization_barrier((value,) + others)[0]


def halves(value):
    half = value.shape[0] // 2
    return value[:half], value[half:]


def add_low(a, b):
    return (a.astype(jnp.float32) + b.astype(jnp.float32)).astype(low_type)


def scatter_first(values):
    far, half = values[3], values[3].shape[0] // 2
    top = lax.ppermute(far[:half], "tensor", swap_x)
    end = lax.ppermute(far[half:], "tensor", swap_y)
    return [top, end]


def scatter_last(values, first):
    top, end = first
    half = top.shape[0]
    for_x, for_y = values[1], values[2]
    for_y = jnp.concatenate([add_low(for_y[:half], top), for_y[half:]], axis=0)
    for_x = jnp.concatenate([for_x[:half], add_low(for_x[half:], end)], axis=0)
    from_x = lax.ppermute(for_x, "tensor", swap_x)
    from_y = lax.ppermute(for_y, "tensor", swap_y)
    return [values[0], from_x, from_y]


MESH = pl.DeviceIdType.MESH


def greet(near_x, near_y):
    barrier = pltpu.get_barrier_semaphore()
    for near in (near_x, near_y):
        pl.semaphore_signal(barrier, inc=1, device_id={"tensor": near}, device_id_type=MESH)
    pl.semaphore_wait(barrier, 2)


def neighbours():
    rank = lax.axis_index("tensor")
    return jnp.bitwise_xor(rank, 1), jnp.bitwise_xor(rank, 2)


def out_scatter_kernel(a_ref, b_ref, w_ref, x_ref, live_ref, norm_ref, x1_ref, h_ref, far_s, for_x, for_y, top_s, end_s, from_x, from_y, send, recv):
    near_x, near_y = neighbours()
    rows = x_ref.shape[0]
    half = rows // 2
    part = a_ref.shape[1]
    model = w_ref.shape[1]
    tile = 512
    greet(near_x, near_y)

    def partial(slot, which, store):
        at = pl.ds(slot * rows + which * half, half)

        @pl.loop(0, model // tile)
        def _(n):
            cols = pl.ds(pl.multiple_of(n * tile, tile), tile)
            store(cols, dot32(a_ref[at, :], w_ref[:part, cols]) + dot32(b_ref[at, :], w_ref[part:, cols]))

    def copy(index, source, target, near):
        return pltpu.make_async_remote_copy(
            src_ref=source,
            dst_ref=target,
            send_sem=send.at[index],
            recv_sem=recv.at[index],
            device_id={"tensor": near},
            device_id_type=MESH,
        )

    def into(ref, which):
        def store(cols, value):
            ref[pl.ds(which * half, half), cols] = value.astype(low_type)

        return store

    def added(ref, which, other):
        def store(cols, value):
            ref[pl.ds(which * half, half), cols] = (value + other[:, cols].astype(jnp.float32)).astype(low_type)

        return store

    t, e = pl.ds(0, half), pl.ds(half, half)
    copies = [
        copy(0, far_s.at[t], top_s, near_x),
        copy(1, far_s.at[e], end_s, near_y),
        copy(2, for_x.at[t], from_x.at[t], near_x),
        copy(3, for_y.at[e], from_y.at[e], near_y),
        copy(4, for_x.at[e], from_x.at[e], near_x),
        copy(5, for_y.at[t], from_y.at[t], near_y),
    ]
    partial(3, 0, into(far_s, 0))
    copies[0].start()
    partial(3, 1, into(far_s, 1))
    copies[1].start()
    partial(1, 0, into(for_x, 0))
    copies[2].start()
    partial(2, 1, into(for_y, 1))
    copies[3].start()
    copies[0].wait_recv()
    partial(2, 0, added(for_y, 0, top_s))
    copies[5].start()
    copies[1].wait_recv()
    partial(1, 1, added(for_x, 1, end_s))
    copies[4].start()

    def own(which):
        def store(cols, value):
            x1_ref[pl.ds(which * half, half), cols] = value

        return store

    partial(0, 0, own(0))
    partial(0, 1, own(1))
    step = 32

    def finish(which):
        @pl.loop(0, half // step)
        def _(r):
            at = pl.ds(pl.multiple_of(which * half + r * step, step), step)
            attn = x1_ref[at, :] + from_x[at, :].astype(jnp.float32) + from_y[at, :].astype(jnp.float32)
            x1 = x_ref[at, :].astype(jnp.float32) + live_ref[at, :] * attn
            x1_ref[at, :] = x1
            c = x1 - jnp.mean(x1, axis=-1, keepdims=True)
            s = lax.rsqrt(jnp.mean(c * c, axis=-1, keepdims=True) + norm_eps)
            h_ref[at, :] = (c * s * norm_ref[1:2, :] + norm_ref[3:4, :]).astype(low_type)

    copies[2].wait_recv()
    copies[5].wait_recv()
    finish(0)
    copies[3].wait_recv()
    copies[4].wait_recv()
    finish(1)
    for c in copies:
        c.wait_send()


def out_scatter(a, b, w, x, live, norm):
    rows, model = x.shape
    half = rows // 2
    big = pltpu.VMEM((rows, model), low_type)
    small = pltpu.VMEM((half, model), low_type)
    vmem = pl.BlockSpec(memory_space=pltpu.VMEM)
    total = a.shape[0]
    return pl.pallas_call(
        out_scatter_kernel,
        in_specs=[vmem] * 6,
        out_specs=[vmem] * 2,
        out_shape=[jax.ShapeDtypeStruct((rows, model), jnp.float32), jax.ShapeDtypeStruct((rows, model), low_type)],
        scratch_shapes=[
            big,
            big,
            big,
            small,
            small,
            big,
            big,
            pltpu.SemaphoreType.DMA((6,)),
            pltpu.SemaphoreType.DMA((6,)),
        ],
        cost_estimate=cost(2 * total * model * w.shape[0], 20 * rows * model),
        compiler_params=pltpu.CompilerParams(vmem_limit_bytes=48 * MIB, collective_id=0, has_side_effects=True),
        name="out_scatter",
    )(a, b, w, x, live, norm)


def remote(index, source, target, near, send, recv):
    return pltpu.make_async_remote_copy(
        src_ref=source,
        dst_ref=target,
        send_sem=send.at[index],
        recv_sem=recv.at[index],
        device_id={"tensor": near},
        device_id_type=MESH,
    )


arrival = (0, 1, 2, 5, 3, 4, 6, 7)


def arrival_slot(i):
    return jnp.where(i == 3, 5, jnp.where(i == 4, 3, jnp.where(i == 5, 4, i)))


def square_copies(all_s, half, send, recv):
    near_x, near_y = neighbours()
    at = lambda n: all_s.at[pl.ds(n * half, half)]
    return (
        remote(0, at(0), at(2), near_x, send, recv),
        remote(1, at(1), at(5), near_y, send, recv),
        remote(2, at(1), at(3), near_x, send, recv),
        remote(3, at(0), at(4), near_y, send, recv),
        remote(4, at(2), at(6), near_y, send, recv),
        remote(5, at(5), at(7), near_x, send, recv),
    )


def await_slot(i, copies):
    x_top, y_end, x_end, y_top, far_top, far_end = copies

    @pl.when(i == 2)
    def _():
        x_top.wait_recv()
        far_top.start()
        y_end.wait_recv()
        far_end.start()

    for n, c in ((4, x_end), (5, y_top), (6, far_top), (7, far_end)):

        @pl.when(i == n)
        def _(c=c):
            c.wait_recv()


def fetch_next(i, refs, buf, sem):
    def fetch(j):
        pltpu.make_async_copy(refs[j], buf.at[j % 2], sem.at[j % 2]).start()

    for j in range(len(refs)):

        @pl.when(i == max(j - 1, 0) if j else i == 0)
        def _(j=j):
            fetch(j)

    pltpu.make_async_copy(refs[0], buf.at[i % 2], sem.at[i % 2]).wait()


def gather_norm_kernel(nd, x_ref, small_ref, pos_ref, inv_ref, h_ref, full_ref, keep_ref, above_ref, below_ref,
                       all_s, full_s, stage, send, recv, local, small_send, small_recv, out_sem):
    d = lax.axis_index("dp")
    near_x, near_y = neighbours()
    half = x_ref.shape[0] // 2
    width = small_ref.shape[1]
    own = pltpu.make_async_copy(x_ref, all_s.at[pl.ds(0, 2 * half)], local)
    own.start()
    barrier = pltpu.get_barrier_semaphore()
    for near in (near_x, near_y):
        pl.semaphore_signal(barrier, inc=1, device_id={"tensor": near}, device_id_type=MESH)
    for k in range(1, nd):
        pl.semaphore_signal(barrier, inc=1, device_id={"dp": lax.rem(d + k, nd)}, device_id_type=MESH)
    pl.semaphore_wait(barrier, nd + 1)
    own.wait()
    copies = square_copies(all_s, half, send, recv)
    for c in copies[:4]:
        c.start()
    small = []
    for k in range(1, nd):
        c = pltpu.make_async_remote_copy(
            src_ref=small_ref,
            dst_ref=full_s.at[d],
            send_sem=small_send.at[k],
            recv_sem=small_recv.at[k],
            device_id={"dp": lax.rem(d + k, nd)},
            device_id_type=MESH,
        )
        c.start()
        small.append(c)
    full_s[d] = small_ref[...]
    for c in small:
        c.wait_recv()
    for n in range(nd):
        full_ref[:, n * width : (n + 1) * width] = full_s[n]
    step = 32
    lane = lax.broadcasted_iota(jnp.int32, (256, PAIR), 1) % HEAD_DIM

    def turns(at):
        angles = pos_ref[at, :] * inv_ref[...]
        cos_part, sine_part = jnp.cos(angles), jnp.sin(angles)
        keep_ref[at, :] = jnp.where(lane < ROT, cos_part, 1.0)
        above_ref[at, :] = jnp.where(lane < ROT // 2, -sine_part, 0.0)
        below_ref[at, :] = jnp.where((lane >= ROT // 2) & (lane < ROT), sine_part, 0.0)

    def out(buf, row):
        return pltpu.make_async_copy(stage.at[buf], h_ref.at[pl.ds(row, half)], out_sem.at[buf])

    def body_step(i, carry):
        await_slot(i, copies)
        row = pl.multiple_of(arrival_slot(i) * half, half)
        buf = i % 2

        @pl.when(i >= 2)
        def _():
            out(buf, row).wait()

        @pl.loop(0, half // step)
        def _(r):
            at = pl.ds(pl.multiple_of(r * step, step), step)
            x = all_s[pl.ds(pl.multiple_of(row + r * step, step), step), :].astype(jnp.float32)
            c = x - jnp.mean(x, axis=-1, keepdims=True)
            s = lax.rsqrt(jnp.mean(c * c, axis=-1, keepdims=True) + norm_eps)
            stage[buf, at, :] = (c * s * full_ref[0:1, :] + full_ref[2:3, :]).astype(low_type)

        out(buf, row).start()

        @pl.when(i < 4)
        def _():
            turns(pl.ds(pl.multiple_of(i * 512, 256), 256))
            turns(pl.ds(pl.multiple_of(i * 512 + 256, 256), 256))

        return carry

    lax.fori_loop(0, 8, body_step, 0)
    for buf in (0, 1):
        out(buf, 0).wait()
    for c in copies:
        c.wait_send()
    for c in small:
        c.wait_send()


def gather_norm(x, small, pos, inverse):
    nd = lax.axis_size("dp")
    rows, model = x.shape
    total = 4 * rows
    count, width = small.shape
    vmem = pl.BlockSpec(memory_space=pltpu.VMEM)
    table = jax.ShapeDtypeStruct((total, PAIR), jnp.float32)
    return pl.pallas_call(
        functools.partial(gather_norm_kernel, nd),
        in_specs=[ANY, vmem, vmem, vmem],
        out_specs=[ANY, vmem, vmem, vmem, vmem],
        out_shape=[
            jax.ShapeDtypeStruct((total, model), low_type),
            jax.ShapeDtypeStruct((count, width * nd), jnp.float32),
            table,
            table,
            table,
        ],
        scratch_shapes=[
            pltpu.VMEM((total, model), low_type),
            pltpu.VMEM((nd, count, width), jnp.float32),
            pltpu.VMEM((2, rows // 2, model), low_type),
            pltpu.SemaphoreType.DMA((6,)),
            pltpu.SemaphoreType.DMA((6,)),
            pltpu.SemaphoreType.DMA,
            pltpu.SemaphoreType.DMA((nd,)),
            pltpu.SemaphoreType.DMA((nd,)),
            pltpu.SemaphoreType.DMA((2,)),
        ],
        cost_estimate=cost(20 * total * model, 4 * total * model),
        compiler_params=pltpu.CompilerParams(vmem_limit_bytes=40 * MIB, collective_id=3, has_side_effects=True),
        name="gather_norm",
    )(x, small, pos, inverse)


def gather_do_kernel(d_ref, act_ref, h_hbm, dup_hbm, o_a_ref, o_b_ref, wo_ref, wd_hbm, do_ref, grad_ref, mlp_ref, up_ref,
                     all_s, wd_s, dup_s, acc, act_s, h_s, stage, up_s, send, recv, local, act_sem, h_sem, out_sem, up_sem):
    near_x, near_y = neighbours()
    half = d_ref.shape[0] // 2
    model = d_ref.shape[1]
    part = o_a_ref.shape[1]
    tile = 512
    own = pltpu.make_async_copy(d_ref, all_s.at[pl.ds(0, 2 * half)], local.at[0])
    own.start()
    weights = pltpu.make_async_copy(wd_hbm, wd_s, local.at[1])
    weights.start()
    cotangent = pltpu.make_async_copy(dup_hbm, dup_s, local.at[2])
    cotangent.start()
    greet(near_x, near_y)
    own.wait()
    copies = square_copies(all_s, half, send, recv)
    for c in copies[:4]:
        c.start()
    acc[...] = jnp.zeros_like(acc)
    weights.wait()
    cotangent.wait()
    strip = model // 8

    def loads(i):
        at = pl.ds(pl.multiple_of(i * half, half), half)
        cols = pl.ds(pl.multiple_of(i * strip, strip), strip)
        return [
            pltpu.make_async_copy(act_ref.at[at], act_s.at[i % 2], act_sem.at[i % 2]),
            pltpu.make_async_copy(h_hbm.at[:, cols], h_s.at[i % 2], h_sem.at[i % 2]),
        ]

    def outs(i):
        at = pl.ds(pl.multiple_of(i * half, half), half)
        side = pl.ds(pl.multiple_of(i * strip, strip), strip)
        return [
            pltpu.make_async_copy(stage.at[i % 2], mlp_ref.at[at], out_sem.at[i % 2]),
            pltpu.make_async_copy(up_s.at[i % 2], up_ref.at[side], up_sem.at[i % 2]),
        ]

    for c in loads(0):
        c.start()

    def step(i, carry):
        @pl.when(i < 7)
        def _():
            for c in loads(i + 1):
                c.start()

        for c in loads(i):
            c.wait()

        @pl.when(i >= 2)
        def _():
            for c in outs(i - 2):
                c.wait()

        stage[i % 2] = dot32(act_s[i % 2], wd_s[...]).astype(low_type)
        up_s[i % 2] = dot32(h_s[i % 2], dup_s[...], contract_first).astype(low_type)
        for c in outs(i):
            c.start()
        await_slot(i, copies)
        at = pl.ds(pl.multiple_of(arrival_slot(i) * half, half), half)
        dattn = all_s[at, :]
        do_ref[at, :] = dot32(dattn, wo_ref[...], contract_last).astype(low_type)
        acc[:part, :] += dot32(o_a_ref[at, :], dattn, contract_first)
        acc[part:, :] += dot32(o_b_ref[at, :], dattn, contract_first)
        return carry

    lax.fori_loop(0, 8, step, 0)

    @pl.loop(0, model // tile)
    def _(n):
        cols = pl.ds(pl.multiple_of(n * tile, tile), tile)
        grad_ref[cols, :] = acc[:, cols].T.astype(low_type)

    for i in (6, 7):
        for c in outs(i):
            c.wait()
    for c in copies:
        c.wait_send()


def gather_do(dattn, act, h, dup, o_a, o_b, wo, wd):
    rows, model = dattn.shape
    total = 4 * rows
    depth = act.shape[1]
    width = wo.shape[0]
    vmem = pl.BlockSpec(memory_space=pltpu.VMEM)
    return pl.pallas_call(
        gather_do_kernel,
        in_specs=[ANY, ANY, ANY, ANY, vmem, vmem, vmem, ANY],
        out_specs=[vmem, vmem, ANY, ANY],
        out_shape=[
            jax.ShapeDtypeStruct((total, width), low_type),
            jax.ShapeDtypeStruct((model, width), low_type),
            jax.ShapeDtypeStruct((total, model), low_type),
            jax.ShapeDtypeStruct((model, depth), low_type),
        ],
        scratch_shapes=[
            pltpu.VMEM((total, model), low_type),
            pltpu.VMEM(wd.shape, low_type),
            pltpu.VMEM(dup.shape, low_type),
            pltpu.VMEM((width, model), jnp.float32),
            pltpu.VMEM((2, rows // 2, depth), low_type),
            pltpu.VMEM((2, total, model // 8), low_type),
            pltpu.VMEM((2, rows // 2, model), low_type),
            pltpu.VMEM((2, model // 8, depth), low_type),
            pltpu.SemaphoreType.DMA((6,)),
            pltpu.SemaphoreType.DMA((6,)),
            pltpu.SemaphoreType.DMA((3,)),
            pltpu.SemaphoreType.DMA((2,)),
            pltpu.SemaphoreType.DMA((2,)),
            pltpu.SemaphoreType.DMA((2,)),
            pltpu.SemaphoreType.DMA((2,)),
        ],
        cost_estimate=cost(2 * total * model * (depth + 2 * width), 6 * total * model),
        compiler_params=pltpu.CompilerParams(vmem_limit_bytes=56 * MIB, collective_id=4, has_side_effects=True),
        name="gather_do",
    )(dattn, act, h, dup, o_a, o_b, wo, wd)


def exchange(rows, partial, bufs, send, recv, fill_one, fill_two):
    far_s, for_x, for_y, top_s, end_s, from_x, from_y = bufs
    near_x, near_y = neighbours()
    half = rows // 2
    t, e = pl.ds(0, half), pl.ds(half, half)
    copies = [
        remote(0, far_s.at[t], top_s, near_x, send, recv),
        remote(1, far_s.at[e], end_s, near_y, send, recv),
        remote(2, for_x.at[t], from_x.at[t], near_x, send, recv),
        remote(3, for_y.at[e], from_y.at[e], near_y, send, recv),
        remote(4, for_x.at[e], from_x.at[e], near_x, send, recv),
        remote(5, for_y.at[t], from_y.at[t], near_y, send, recv),
    ]

    def into(ref, which):
        def store(cols, value):
            ref[pl.ds(which * half, half), cols] = value.astype(low_type)

        return store

    def added(ref, which, other):
        def store(cols, value):
            ref[pl.ds(which * half, half), cols] = (value + other[:, cols].astype(jnp.float32)).astype(low_type)

        return store

    partial(3, 0, into(far_s, 0))
    copies[0].start()
    partial(3, 1, into(far_s, 1))
    copies[1].start()
    partial(1, 0, into(for_x, 0))
    copies[2].start()
    partial(2, 1, into(for_y, 1))
    copies[3].start()
    fill_one()
    copies[0].wait_recv()
    partial(2, 0, added(for_y, 0, top_s))
    copies[5].start()
    copies[1].wait_recv()
    partial(1, 1, added(for_x, 1, end_s))
    copies[4].start()
    fill_two()
    return copies


def finish_back(copies, rows, gain_row, v_ref, base_ref, own_ref, live_ref, norm_ref, from_x, from_y, dx_ref, low_ref, gain_ref, shift_ref):
    half = rows // 2
    step = 16
    gain_ref[...] = jnp.zeros_like(gain_ref)
    shift_ref[...] = jnp.zeros_like(shift_ref)

    def finish(which):
        @pl.loop(0, half // step)
        def _(r):
            at = pl.ds(pl.multiple_of(which * half + r * step, step), step)
            e = own_ref[at, :].astype(jnp.float32) + from_x[at, :].astype(jnp.float32) + from_y[at, :].astype(jnp.float32)
            v = v_ref[at, :].astype(jnp.float32)
            c = v - jnp.mean(v, axis=-1, keepdims=True)
            s = lax.rsqrt(jnp.mean(c * c, axis=-1, keepdims=True) + norm_eps)
            xh = c * s
            w = e * norm_ref[gain_row : gain_row + 1, :]
            back = s * (w - jnp.mean(w, axis=-1, keepdims=True) - xh * jnp.mean(w * xh, axis=-1, keepdims=True))
            dx = base_ref[at, :].astype(jnp.float32) + back
            dx_ref[at, :] = dx.astype(dx_ref.dtype)
            if low_ref is not None:
                low_ref[at, :] = (dx * live_ref[at, :]).astype(low_type)
            gain_ref[...] += jnp.sum(e * xh, axis=0, keepdims=True)
            shift_ref[...] += jnp.sum(e, axis=0, keepdims=True)

    copies[2].wait_recv()
    copies[5].wait_recv()
    finish(0)
    copies[3].wait_recv()
    copies[4].wait_recv()
    finish(1)
    for c in copies:
        c.wait_send()


def exchange_scratch(rows, model):
    big = pltpu.VMEM((rows, model), low_type)
    small = pltpu.VMEM((rows // 2, model), low_type)
    return [big, big, big, small, small, big, big, pltpu.SemaphoreType.DMA((6,)), pltpu.SemaphoreType.DMA((6,))]


def hidden_scatter_kernel(dgate_hbm, dup_hbm, w_hbm, h_hbm, x1_ref, og_ref, live_ref, norm_ref,
                          grad_ref, dx_ref, low_ref, gain_ref, shift_ref,
                          *scratch):
    bufs, (send, recv, g_s, w_s, h_s, stage, local, h_sem, out_sem) = scratch[:7], scratch[7:]
    rows, model = x1_ref.shape
    half = rows // 2
    near_x, near_y = neighbours()
    loads = [
        pltpu.make_async_copy(dgate_hbm, g_s.at[0], local.at[0]),
        pltpu.make_async_copy(dup_hbm, g_s.at[1], local.at[1]),
        pltpu.make_async_copy(w_hbm, w_s, local.at[2]),
    ]
    for c in loads:
        c.start()
    greet(near_x, near_y)
    for c in loads:
        c.wait()
    tile = 512

    def partial(slot, which, store):
        at = pl.ds(slot * rows + which * half, half)

        @pl.loop(0, model // tile)
        def _(n):
            cols = pl.ds(pl.multiple_of(n * tile, tile), tile)
            value = dot32(g_s[0, at, :], w_s[0, cols, :], contract_last)
            store(cols, value + dot32(g_s[1, at, :], w_s[1, cols, :], contract_last))

    def own(which):
        def store(cols, value):
            dx_ref[pl.ds(which * half, half), cols] = value

        return store

    strip = 256

    def load(i):
        return pltpu.make_async_copy(h_hbm.at[:, pl.ds(pl.multiple_of(i * strip, strip), strip)], h_s.at[i % 2], h_sem.at[i % 2])

    def out(i):
        at = pl.ds(pl.multiple_of(i * strip, strip), strip)
        return pltpu.make_async_copy(stage.at[i % 2], grad_ref.at[at], out_sem.at[i % 2])

    strips = model // strip
    load(0).start()

    def strip_step(i, carry):
        @pl.when(i < strips - 1)
        def _():
            load(i + 1).start()

        load(i).wait()

        @pl.when(i >= 2)
        def _():
            out(i - 2).wait()

        stage[i % 2] = dot32(h_s[i % 2], g_s[0], contract_first).astype(low_type)
        out(i).start()
        return carry

    def fill_one():
        partial(0, 0, own(0))
        partial(0, 1, own(1))
        lax.fori_loop(0, 2, strip_step, 0)

    def fill_two():
        lax.fori_loop(2, strips, strip_step, 0)

    copies = exchange(rows, partial, bufs, send, recv, fill_one, fill_two)
    finish_back(copies, rows, 1, x1_ref, og_ref, dx_ref, live_ref, norm_ref, bufs[5], bufs[6], dx_ref, low_ref, gain_ref, shift_ref)
    out(strips - 2).wait()
    out(strips - 1).wait()


def hidden_scatter(dgate, dup, w, h, x1, out_grad, live, norm):
    rows, model = x1.shape
    total, depth = dgate.shape
    vmem = pl.BlockSpec(memory_space=pltpu.VMEM)
    line = jax.ShapeDtypeStruct((1, model), jnp.float32)
    return pl.pallas_call(
        hidden_scatter_kernel,
        in_specs=[ANY, ANY, ANY, ANY, vmem, vmem, vmem, vmem],
        out_specs=[ANY, vmem, vmem, vmem, vmem],
        out_shape=[
            jax.ShapeDtypeStruct((model, depth), low_type),
            jax.ShapeDtypeStruct((rows, model), jnp.float32),
            jax.ShapeDtypeStruct((rows, model), low_type),
            line,
            line,
        ],
        scratch_shapes=exchange_scratch(rows, model)
        + [
            pltpu.VMEM((2, total, depth), low_type),
            pltpu.VMEM(w.shape, low_type),
            pltpu.VMEM((2, total, 256), low_type),
            pltpu.VMEM((2, 256, depth), low_type),
            pltpu.SemaphoreType.DMA((3,)),
            pltpu.SemaphoreType.DMA((2,)),
            pltpu.SemaphoreType.DMA((2,)),
        ],
        cost_estimate=cost(8 * total * model * depth, 16 * total * model),
        compiler_params=pltpu.CompilerParams(vmem_limit_bytes=62 * MIB, collective_id=5, has_side_effects=True),
        name="hidden_scatter",
    )(dgate, dup, w, h, x1, out_grad, live, norm)


def first_scatter_kernel(count, *refs):
    lefts = refs[:count]
    w_ref, x_ref, base_ref, norm_ref, dx_ref, gain_ref, shift_ref = refs[count : count + 7]
    scratch = refs[count + 7 :]
    bufs, (send, recv, own_s) = scratch[:7], scratch[7:]
    rows, model = x_ref.shape
    half = rows // 2
    tile = 512
    near_x, near_y = neighbours()
    greet(near_x, near_y)

    def partial(slot, which, store):
        at = pl.ds(slot * rows + which * half, half)

        @pl.loop(0, model // tile)
        def _(n):
            cols = pl.ds(pl.multiple_of(n * tile, tile), tile)
            value = None
            for m, left in enumerate(lefts):
                depth = left.shape[1]
                per = w_ref.shape[2] // depth
                side = slice((m % per) * depth, (m % per + 1) * depth)
                term = dot32(left[at, :], w_ref[m // per, cols, side], contract_last)
                value = term if value is None else value + term
            store(cols, value)

    def own(which):
        def store(cols, value):
            own_s[pl.ds(which * half, half), cols] = value

        return store

    def fill_one():
        partial(0, 0, own(0))
        partial(0, 1, own(1))

    copies = exchange(rows, partial, bufs, send, recv, fill_one, lambda: None)
    finish_back(copies, rows, 0, x_ref, base_ref, own_s, None, norm_ref, bufs[5], bufs[6], dx_ref, None, gain_ref, shift_ref)


def first_scatter(lefts, w, x, base, norm):
    rows, model = x.shape
    vmem = pl.BlockSpec(memory_space=pltpu.VMEM)
    line = jax.ShapeDtypeStruct((1, model), jnp.float32)
    return pl.pallas_call(
        functools.partial(first_scatter_kernel, len(lefts)),
        in_specs=[vmem] * (len(lefts) + 4),
        out_specs=[vmem] * 3,
        out_shape=[jax.ShapeDtypeStruct((rows, model), low_type), line, line],
        scratch_shapes=exchange_scratch(rows, model) + [pltpu.VMEM((rows, model), jnp.float32)],
        cost_estimate=cost(24 * rows * model * w.shape[2], 30 * rows * model),
        compiler_params=pltpu.CompilerParams(vmem_limit_bytes=56 * MIB, collective_id=6, has_side_effects=True),
        name="first_scatter",
    )(*lefts, w, x, base, norm)

def gather_gate_up_kernel(count, h_ref, w_hbm, *rest):
    blocks, (all_ref, act_ref, one_ref, two_ref, grad_ref) = rest[:count], rest[count : count + 5]
    w_s, all_s, stage, acc, turned, dm_s, send, recv, local, h_sem, out_sem, dm_sem = rest[count + 5 :]
    near_x, near_y = neighbours()
    half = h_ref.shape[0] // 2
    own = pltpu.make_async_copy(h_ref, all_s.at[pl.ds(0, 2 * half)], local.at[0])
    own.start()
    weights = pltpu.make_async_copy(w_hbm, w_s, local.at[1])
    weights.start()
    greet(near_x, near_y)
    own.wait()
    copies = square_copies(all_s, half, send, recv)
    for c in copies[:4]:
        c.start()
    acc[...] = jnp.zeros_like(acc)
    weights.wait()
    in_order = [blocks[n] for n in arrival]
    tile = 512

    def outs(buf, row):
        return [
            pltpu.make_async_copy(stage.at[buf, n], ref.at[pl.ds(row, half)], out_sem.at[buf, n])
            for n, ref in enumerate((act_ref, one_ref, two_ref))
        ]

    def keep(i, row):
        return pltpu.make_async_copy(all_s.at[pl.ds(row, half)], all_ref.at[pl.ds(row, half)], h_sem.at[i])

    def step(i, carry):
        await_slot(i, copies)
        row = pl.multiple_of(arrival_slot(i) * half, half)
        buf = i % 2
        keep(i, row).start()

        @pl.when(i >= 2)
        def _():
            for c in outs(buf, row):
                c.wait()

        h = all_s[pl.ds(row, half), :]
        gate = dot32(h, w_s[0])
        up = dot32(h, w_s[1])
        sig = 1.0 / (1.0 + jnp.exp(-gate))
        silu = gate * sig
        act = (silu * up).astype(low_type)
        stage[buf, 0] = act
        stage[buf, 1] = (up * sig * (1.0 + gate * (1.0 - sig))).astype(low_type)
        stage[buf, 2] = silu.astype(low_type)
        for c in outs(buf, row):
            c.start()
        turned[...] = act.T
        fetch_next(i, in_order, dm_s, dm_sem)

        @pl.loop(0, acc.shape[1] // tile)
        def _(n):
            cols = pl.ds(pl.multiple_of(n * tile, tile), tile)
            acc[:, cols] += dot32(turned[...], dm_s[buf, :, cols])

        return carry

    lax.fori_loop(0, 8, step, 0)
    for buf in (0, 1):
        for c in outs(buf, 0):
            c.wait()
    for i in range(8):
        keep(i, 0).wait()
    for c in copies:
        c.wait_send()
    depth = acc.shape[0]
    strip = depth // 8

    @pl.loop(0, 8)
    def _(n):
        at = pl.ds(pl.multiple_of(n * strip, strip), strip)
        all_s[at, :] = acc[at, :].astype(low_type)

    last = pltpu.make_async_copy(all_s.at[pl.ds(0, depth)], grad_ref, local.at[0])
    last.start()
    last.wait()


def gather_gate_up(h, w, dm_blocks):
    rows, model = h.shape
    depth = w.shape[2]
    total = 4 * rows
    half = rows // 2
    deep = jax.ShapeDtypeStruct((total, depth), low_type)
    return pl.pallas_call(
        functools.partial(gather_gate_up_kernel, len(dm_blocks)),
        in_specs=[ANY] * (2 + len(dm_blocks)),
        out_specs=[ANY] * 5,
        out_shape=[
            jax.ShapeDtypeStruct((total, model), low_type),
            deep,
            deep,
            deep,
            jax.ShapeDtypeStruct((depth, model), low_type),
        ],
        scratch_shapes=[
            pltpu.VMEM(w.shape, low_type),
            pltpu.VMEM((total, model), low_type),
            pltpu.VMEM((2, 3, half, depth), low_type),
            pltpu.VMEM((depth, model), jnp.float32),
            pltpu.VMEM((depth, half), low_type),
            pltpu.VMEM((2, half, model), low_type),
            pltpu.SemaphoreType.DMA((6,)),
            pltpu.SemaphoreType.DMA((6,)),
            pltpu.SemaphoreType.DMA((2,)),
            pltpu.SemaphoreType.DMA((8,)),
            pltpu.SemaphoreType.DMA((2, 3)),
            pltpu.SemaphoreType.DMA((2,)),
        ],
        cost_estimate=cost(6 * total * model * depth, 4 * model * depth + 4 * total * model + 6 * total * depth),
        compiler_params=pltpu.CompilerParams(vmem_limit_bytes=60 * MIB, collective_id=1, has_side_effects=True),
        name="gather_gate_up",
    )(h, w, *dm_blocks)


def small_kernel(nd, nt, x_ref, o_ref, groups, partial, shares, send, recv, send_t, recv_t):
    d, t = lax.axis_index("dp"), lax.axis_index("tensor")
    width = o_ref.shape[1]
    barrier = pltpu.get_barrier_semaphore()
    for k in range(1, nd):
        pl.semaphore_signal(barrier, inc=1, device_id={"dp": lax.rem(d + k, nd)}, device_id_type=MESH)
    for k in range(1, nt):
        pl.semaphore_signal(barrier, inc=1, device_id={"tensor": lax.rem(t + k, nt)}, device_id_type=MESH)
    pl.semaphore_wait(barrier, nd + nt - 2)
    copies = []
    for k in range(1, nd):
        peer = lax.rem(d + k, nd)
        c = pltpu.make_async_remote_copy(
            src_ref=x_ref.at[:, pl.ds(pl.multiple_of(peer * width, width), width)],
            dst_ref=groups.at[k],
            send_sem=send.at[k],
            recv_sem=recv.at[k],
            device_id={"dp": peer},
            device_id_type=MESH,
        )
        c.start()
        copies.append(c)
    total = x_ref[:, pl.ds(pl.multiple_of(d * width, width), width)]
    for k in range(1, nd):
        copies[k - 1].wait_recv()
        total += groups[k]
    partial[...] = total
    shares[t] = total
    for k in range(1, nt):
        c = pltpu.make_async_remote_copy(
            src_ref=partial,
            dst_ref=shares.at[t],
            send_sem=send_t.at[k],
            recv_sem=recv_t.at[k],
            device_id={"tensor": lax.rem(t + k, nt)},
            device_id_type=MESH,
        )
        c.start()
        copies.append(c)
    for k in range(1, nt):
        copies[nd - 2 + k].wait_recv()
    total = shares[0]
    for k in range(1, nt):
        total += shares[k]
    o_ref[...] = total
    for c in copies:
        c.wait_send()


def sum_small(x):
    nd, nt = lax.axis_size("dp"), lax.axis_size("tensor")
    rows, model = x.shape
    width = model // nd
    vmem = pl.BlockSpec(memory_space=pltpu.VMEM)
    return pl.pallas_call(
        functools.partial(small_kernel, nd, nt),
        in_specs=[vmem],
        out_specs=vmem,
        out_shape=jax.ShapeDtypeStruct((rows, width), jnp.float32),
        scratch_shapes=[
            pltpu.VMEM((nd, rows, width), jnp.float32),
            pltpu.VMEM((rows, width), jnp.float32),
            pltpu.VMEM((nt, rows, width), jnp.float32),
            pltpu.SemaphoreType.DMA((nd,)),
            pltpu.SemaphoreType.DMA((nd,)),
            pltpu.SemaphoreType.DMA((nt,)),
            pltpu.SemaphoreType.DMA((nt,)),
        ],
        cost_estimate=cost(rows * model, 8 * rows * model),
        compiler_params=pltpu.CompilerParams(collective_id=2, has_side_effects=True),
        name="sum_small",
    )(x)


def body(
    tokens,
    out_grad,
    lengths,
    norm_gain,
    norm_bias,
    qkv_weight,
    qkv_bias,
    out_weight,
    gate_up_weight,
    down_weight,
    first_norm_gain,
    first_norm_bias,
    first_qkv_weight,
    first_qkv_bias,
    first_out_weight,
    first_gate_up_weight,
    first_down_weight,
    second_norm_gain,
    second_norm_bias,
    second_qkv_weight,
    second_qkv_bias,
    second_out_weight,
    second_gate_up_weight,
    second_down_weight,
):
    slots = lax.axis_size("tensor")
    rank = lax.axis_index("tensor")
    own_rows = tokens.shape[0]
    group_rows = own_rows * slots
    width = out_weight.shape[0]
    order = rank if square(slots) else jnp.zeros_like(rank)

    chunk = jnp.bitwise_xor(jnp.arange(slots, dtype=jnp.int32), order)
    row_index = (chunk[:, None] * own_rows + jnp.arange(own_rows, dtype=jnp.int32)[None, :]).reshape(-1)
    seq_start, _ = layout(lengths[0], row_index)
    position = row_index - seq_start
    own_index = rank * own_rows + jnp.arange(own_rows, dtype=jnp.int32)
    live = layout(lengths[0], own_index)[1][:, None]
    block_start, _ = layout(lengths[0], jnp.arange(group_rows // BLOCK, dtype=jnp.int32) * BLOCK)
    table = jnp.concatenate([order.reshape(1).astype(jnp.int32), block_start // BLOCK])
    starts = seq_start[None, :]
    small_low = jnp.concatenate([norm_gain, norm_bias, qkv_bias, qkv_bias[:1]], axis=0).astype(low_type)
    own_bias = lambda full: lax.dynamic_slice_in_dim(full[4:7], rank * width, width, 1)[:, None, :]

    if square(slots):
        qkv_full = lax.all_gather(qkv_weight.astype(low_type), "dp", axis=1, tiled=True)
        lane = jnp.arange(PAIR, dtype=jnp.int32) % (ROT // 2)
        inverse = jnp.power(rope_base, -lane.astype(jnp.float32) * (2.0 / ROT))[None, :]
        h1, small_full, *tables = gather_norm(
            tokens, small_low.astype(jnp.float32), position.astype(jnp.float32)[:, None], inverse
        )
        norm = small_full[:4]
        out_low = after(out_weight.astype(low_type), qkv_full, h1)
        out_full = lax.all_gather(out_low, "dp", axis=1, tiled=True)
        dm_own = (after(out_grad, h1).astype(jnp.float32) * live).astype(low_type)
        dm_first, dm_rest = gather_rows(*halves(dm_own))
        q, k, v, kt, vt = qkv_all(h1, qkv_full, own_bias(small_full), tables)

        o_a, lse_a = attn_fwd(0, slots, table, q, k, vt, starts)
        gate_up_low = after(gate_up_weight.astype(low_type), out_full, o_a)
        gate_up_full = lax.all_gather(gate_up_low, "dp", axis=1, tiled=True)
        dm_far = dm_rest(o_a)
        o_b, lse_b = attn_fwd(1, slots, table, after(q, o_a, *dm_first), k, vt, starts)
        o_b = after(o_b, *dm_far)
        dm_blocks = dm_first + dm_far

        x1, h2_own = out_scatter(o_a, o_b, out_full, tokens, live, norm)
        down_low = after(down_weight.astype(low_type), gate_up_full, h2_own)
        down_full = lax.all_gather(down_low, "dp", axis=1, tiled=True)
        h2, act, slope_gate, slope_up, grad_down = gather_gate_up(h2_own, gate_up_full, dm_blocks)
        grad_down_own = lax.psum_scatter(after(grad_down, down_full), "dp", scatter_dimension=1, tiled=True)

        dgate, dup = back_through_down(dm_blocks, slope_gate, slope_up, down_full)
        grad_gate, dx1, dattn_own, gain_two, shift_two = hidden_scatter(
            dgate, dup, gate_up_full, h2, x1, out_grad, live, norm
        )
        grad_gate = after(grad_gate, grad_down_own)
        grad_gate_own = lax.psum_scatter(grad_gate, "dp", scatter_dimension=0, tiled=True)

        do, grad_out, mlp, grad_up = gather_do(dattn_own, act, h2, dup, o_a, o_b, out_full, down_full)
        grad_up = after(grad_up, grad_gate_own)
        grad_up_own = lax.psum_scatter(grad_up, "dp", scatter_dimension=0, tiled=True)
        grad_gate_up_own = jnp.stack([grad_gate_own, grad_up_own])
        mlp = [mlp[j * own_rows : (j + 1) * own_rows] for j in range(slots)]
        mlp_first = scatter_first(mlp)
        back_a = attn_bwd(0, slots, table, q, do, o_a, k, v, kt, starts, lse_a, tables)
        mlp_parts = scatter_last(mlp, [after(part, back_a[0]) for part in mlp_first])
        back_b = attn_bwd(1, slots, table, q, after(do, back_a[0], *mlp_first), o_b, k, v, kt, starts, lse_b, tables)
        dlin = [side for pair in zip(back_a, back_b) for side in pair]
        grad_rest, bias_local = qkv_grad(h1, [after(dlin[0], *mlp_parts)] + dlin[1:], grad_out)
        late = [after(dlin[0], grad_rest)] + dlin[1:]
        input_grad, gain_one, shift_one = first_scatter(late, qkv_full, tokens, dx1, norm)
        grad_rest = after(grad_rest, grad_up_own)
        grad_rest_own = lax.psum_scatter(grad_rest, "dp", scatter_dimension=1, tiled=True)
        grad_qkv_own = grad_rest_own[:3]
        grad_out_own = lax.optimization_barrier(grad_rest_own[3].T)
        layer_out = (x1 + live * sum(part.astype(jnp.float32) for part in mlp_parts)).astype(low_type)
    else:
        everyone = lambda value: lax.all_gather(value, "tensor", axis=0, tiled=True)
        scatter = lambda value, axis, at: lax.psum_scatter(value.astype(low_type), axis, scatter_dimension=at, tiled=True)
        small_full = lax.all_gather(small_low, "dp", axis=1, tiled=True).astype(jnp.float32)
        qkv_full, out_full, gate_up_full, down_full = (
            lax.all_gather(w.astype(low_type), "dp", axis=1, tiled=True)
            for w in (qkv_weight, out_weight, gate_up_weight, down_weight)
        )
        gain_rows, shift_rows = small_full[0:2], small_full[2:4]
        rows_in, cotangent = tokens.astype(jnp.float32), out_grad.astype(jnp.float32)
        tables = rotary_tables(position)
        h1 = everyone(layer_norm(rows_in, gain_rows[0], shift_rows[0]).astype(low_type))
        q, k, v, kt, vt = qkv_all(h1, qkv_full, own_bias(small_full), tables)
        o_a, lse_a = attn_fwd(0, slots, table, q, k, vt, starts)
        o_b, lse_b = attn_fwd(1, slots, table, q, k, vt, starts)
        o = jnp.concatenate([o_a, o_b], axis=1)
        x1 = rows_in + live * scatter(dot32(o, out_full), "tensor", 0).astype(jnp.float32)
        h2 = everyone(layer_norm(x1, gain_rows[1], shift_rows[1]).astype(low_type))
        gate, up = dot32(h2, gate_up_full[0]), dot32(h2, gate_up_full[1])
        sig = 1.0 / (1.0 + jnp.exp(-gate))
        act = (gate * sig * up).astype(low_type)
        mlp_rows = scatter(dot32(act, down_full), "tensor", 0).astype(jnp.float32)
        layer_out = (x1 + live * mlp_rows).astype(low_type)
        dm = everyone((cotangent * live).astype(low_type))
        da = dot32(dm, down_full, contract_last)
        dgate = (da * up * sig * (1.0 + gate * (1.0 - sig))).astype(low_type)
        dup = (da * gate * sig).astype(low_type)
        grad_down_own = scatter(dot32(act, dm, contract_first), "dp", 1)
        grad_gate_up = jnp.stack([dot32(h2, dgate, contract_first), dot32(h2, dup, contract_first)])
        grad_gate_up_own = scatter(grad_gate_up, "dp", 1)
        dh2 = dot32(dgate, gate_up_full[0], contract_last) + dot32(dup, gate_up_full[1], contract_last)
        dh2 = scatter(dh2, "tensor", 0).astype(jnp.float32)
        back, gain_two, shift_two = jax.vjp(layer_norm, x1, gain_rows[1], shift_rows[1])[1](dh2)
        dx1 = cotangent + back
        dattn = everyone((dx1 * live).astype(low_type))
        do = dot32(dattn, out_full, contract_last).astype(low_type)
        grad_out = dot32(dattn, o, contract_first).astype(low_type)
        back_a = attn_bwd(0, slots, table, q, do, o_a, k, v, kt, starts, lse_a, tables)
        back_b = attn_bwd(1, slots, table, q, do, o_b, k, v, kt, starts, lse_b, tables)
        dlin = [side for pair in zip(back_a, back_b) for side in pair]
        grad_rest, bias_local = qkv_grad(h1, dlin, grad_out)
        grad_rest_own = scatter(grad_rest, "dp", 1)
        grad_qkv_own, grad_out_own = grad_rest_own[:3], grad_rest_own[3].T
        dh1 = sum(
            dot32(jnp.concatenate(dlin[2 * n : 2 * n + 2], axis=1), qkv_full[n], contract_last) for n in range(3)
        )
        dh1 = scatter(dh1, "tensor", 0).astype(jnp.float32)
        back, gain_one, shift_one = jax.vjp(layer_norm, rows_in, gain_rows[0], shift_rows[0])[1](dh1)
        input_grad = (dx1 + back).astype(low_type)
        gain_one, gain_two, shift_one, shift_two = (
            value[None, :] for value in (gain_one, gain_two, shift_one, shift_two)
        )

    bias_placed = lax.dynamic_update_slice(
        jnp.zeros((3, small_full.shape[1]), jnp.float32), bias_local, (jnp.int32(0), rank * width)
    )
    small_local = jnp.concatenate([gain_one, gain_two, shift_one, shift_two, bias_placed, bias_placed[:1]], axis=0)
    small_own = sum_small(small_local)

    own_grads = (
        small_own[0:2],
        small_own[2:4],
        grad_qkv_own.astype(jnp.float32),
        small_own[4:7],
        grad_out_own.astype(jnp.float32),
        grad_gate_up_own.astype(jnp.float32),
        grad_down_own.astype(jnp.float32),
    )
    masters = (norm_gain, norm_bias, qkv_weight, qkv_bias, out_weight, gate_up_weight, down_weight)
    firsts = (
        first_norm_gain,
        first_norm_bias,
        first_qkv_weight,
        first_qkv_bias,
        first_out_weight,
        first_gate_up_weight,
        first_down_weight,
    )
    seconds = (
        second_norm_gain,
        second_norm_bias,
        second_qkv_weight,
        second_qkv_bias,
        second_out_weight,
        second_gate_up_weight,
        second_down_weight,
    )
    decays = (0.0, 0.0, weight_decay, 0.0, weight_decay, weight_decay, weight_decay)
    new_change = []
    new_first = []
    new_second = []
    for weight_now, gradient, moment_one, moment_two, decay_rate in zip(
        masters, own_grads, firsts, seconds, decays
    ):
        change, moment_next, square_next = adamw_update(
            weight_now, gradient, moment_one, moment_two, decay_rate
        )
        new_change.append(change)
        new_first.append(moment_next)
        new_second.append(square_next)
    return (
        (layer_out, input_grad)
        + own_grads
        + tuple(new_change)
        + tuple(new_first)
        + tuple(new_second)
    )


def solution(mesh):
    return jax.shard_map(
        body,
        mesh=mesh,
        in_specs=(
            P(("dp", "tensor"), None),
            P(("dp", "tensor"), None),
            P("dp", None),
            P(None, "dp"),
            P(None, "dp"),
            P(None, "dp", "tensor"),
            P(None, "dp"),
            P("tensor", "dp"),
            P(None, "dp", "tensor"),
            P("tensor", "dp"),
            P(None, "dp"),
            P(None, "dp"),
            P(None, "dp", "tensor"),
            P(None, "dp"),
            P("tensor", "dp"),
            P(None, "dp", "tensor"),
            P("tensor", "dp"),
            P(None, "dp"),
            P(None, "dp"),
            P(None, "dp", "tensor"),
            P(None, "dp"),
            P("tensor", "dp"),
            P(None, "dp", "tensor"),
            P("tensor", "dp"),
        ),
        out_specs=(
            P(("dp", "tensor"), None),
            P(("dp", "tensor"), None),
            P(None, "dp"),
            P(None, "dp"),
            P(None, "dp", "tensor"),
            P(None, "dp"),
            P("tensor", "dp"),
            P(None, "dp", "tensor"),
            P("tensor", "dp"),
            P(None, "dp"),
            P(None, "dp"),
            P(None, "dp", "tensor"),
            P(None, "dp"),
            P("tensor", "dp"),
            P(None, "dp", "tensor"),
            P("tensor", "dp"),
            P(None, "dp"),
            P(None, "dp"),
            P(None, "dp", "tensor"),
            P(None, "dp"),
            P("tensor", "dp"),
            P(None, "dp", "tensor"),
            P("tensor", "dp"),
            P(None, "dp"),
            P(None, "dp"),
            P(None, "dp", "tensor"),
            P(None, "dp"),
            P("tensor", "dp"),
            P(None, "dp", "tensor"),
            P("tensor", "dp"),
        ),
        check_vma=False,
    )
```

```python
import functools

import jax
import jax.numpy as jnp
from jax import lax
from jax.experimental import pallas as pl
from jax.experimental.pallas import tpu as pltpu
from jax.sharding import PartitionSpec as P

HEAD_DIM = 64
ROT = 16
PAIR = 2 * HEAD_DIM
BLOCK = 256

norm_eps = 1e-05
rope_base = 10000.0
beta_one = 0.9
beta_two = 0.95
adam_eps = 1e-08
learn_rate = 0.01
weight_decay = 0.1
step_count = 10.0
masked_score = -1e30
contract_last = (((1,), (1,)), ((), ()))
contract_first = (((0,), (0,)), ((), ()))
low_type = jnp.bfloat16
MIB = 2**20


def layout(seq_lengths, row_index):
    slot = jnp.arange(seq_lengths.shape[0])
    seq_ends = jnp.sum(
        jnp.where(slot[:, None] <= slot[None, :], seq_lengths[:, None], 0), axis=0
    )
    passed = row_index[:, None] >= seq_ends[None, :]
    seq_start = jnp.sum(jnp.where(passed, seq_lengths[None, :], 0), axis=1)
    live_rows = (row_index < jnp.sum(seq_lengths)).astype(jnp.float32)
    return (seq_start, live_rows)


def rotary_tables(position):
    half_rot = ROT // 2
    lane = jnp.arange(PAIR, dtype=jnp.int32) % HEAD_DIM
    powers = (lane % half_rot).astype(jnp.float32) * (2.0 / ROT)
    inverse = jnp.power(rope_base, -powers)
    angles = position.astype(jnp.float32)[:, None] * inverse[None, :]
    cos_part, sine_part = jnp.cos(angles), jnp.sin(angles)
    lane = lane[None, :]
    keep = jnp.where(lane < ROT, cos_part, 1.0)
    above = jnp.where(lane < half_rot, -sine_part, 0.0)
    below = jnp.where((lane >= half_rot) & (lane < ROT), sine_part, 0.0)
    return (keep, above, below)


def dot32(a, b, dims=None):
    if dims is None:
        return jnp.dot(a, b, preferred_element_type=jnp.float32)
    return lax.dot_general(a, b, dims, preferred_element_type=jnp.float32)


def turn(values, keep, above, below):
    up = pltpu.roll(values, PAIR - ROT // 2, 1)
    down = pltpu.roll(values, ROT // 2, 1)
    return values * keep + up * above + down * below


def turn_back(values, keep, above, below):
    up = pltpu.roll(values, PAIR - ROT // 2, 1)
    down = pltpu.roll(values, ROT // 2, 1)
    return values * keep - up * above - down * below


def adamw_update(weight_now, gradient, moment_one, moment_two, decay_rate):
    moment_one = beta_one * moment_one + (1.0 - beta_one) * gradient
    moment_two = beta_two * moment_two + (1.0 - beta_two) * gradient * gradient
    scaled_one = moment_one / (1.0 - beta_one**step_count)
    scaled_two = moment_two / (1.0 - beta_two**step_count)
    change = scaled_one / (jnp.sqrt(scaled_two) + adam_eps) + decay_rate * weight_now
    return (-learn_rate * change, moment_one, moment_two)


def cost(flops, moved, exps=0):
    return pl.CostEstimate(flops=int(flops) // 16, bytes_accessed=int(moved) // 16, transcendentals=int(exps) // 16)


def params(limit):
    return pltpu.CompilerParams(vmem_limit_bytes=limit * MIB)


ANY = pl.BlockSpec(memory_space=pl.ANY)


def stream(refs, buf, sem):
    step = pl.program_id(0)

    def fetch(j, slot):
        pltpu.make_async_copy(refs[j], buf.at[slot], sem.at[slot]).start()

    @pl.when(step == 0)
    def _():
        fetch(0, 0)

    for j in range(1, len(refs)):

        @pl.when(step == j - 1)
        def _(j=j):
            fetch(j, j % 2)

    now = step % 2
    pltpu.make_async_copy(refs[0], buf.at[now], sem.at[now]).wait()
    return now


def layer_norm(values, gain_row, shift_row):
    center = values - jnp.mean(values, axis=-1, keepdims=True)
    spread = jnp.mean(center * center, axis=-1, keepdims=True)
    return center * lax.rsqrt(spread + norm_eps) * gain_row + shift_row


def qkv_kernel(scale, h_ref, w_ref, bias_ref, keep_ref, above_ref, below_ref, q_ref, k_ref, v_ref, kt_ref, vt_ref):
    h = h_ref[...]
    keep, above, below = keep_ref[...], above_ref[...], below_ref[...]
    width = q_ref.shape[1]
    lin = dot32(h, w_ref[0]) + bias_ref[0]
    for c in range(0, width, PAIR):
        u = turn(lin[:, c : c + PAIR], keep, above, below)
        q_ref[:, c : c + PAIR] = (u.astype(low_type) * scale).astype(low_type)
    lin = dot32(h, w_ref[1]) + bias_ref[1]
    for c in range(0, width, PAIR):
        u = turn(lin[:, c : c + PAIR], keep, above, below)
        k_ref[:, c : c + PAIR] = u.astype(low_type)
        kt_ref[c : c + PAIR, :] = u.T.astype(low_type)
    lin = dot32(h, w_ref[2]) + bias_ref[2]
    v_ref[...] = lin.astype(low_type)
    vt_ref[...] = lin.T.astype(low_type)


def qkv_all(h, w, bias, tables):
    total, model = h.shape
    rows = 256
    width = w.shape[2]
    row = lambda n: pl.BlockSpec((rows, n), lambda i: (i, 0))
    col = pl.BlockSpec((width, rows), lambda i: (0, i))
    flat = jax.ShapeDtypeStruct((total, width), low_type)
    turned = jax.ShapeDtypeStruct((width, total), low_type)
    return pl.pallas_call(
        functools.partial(qkv_kernel, HEAD_DIM ** (-0.5)),
        grid=(total // rows,),
        in_specs=[
            row(model),
            pl.BlockSpec(w.shape, lambda i: (0, 0, 0), pipeline_mode=pl.Buffered(1)),
            pl.BlockSpec(bias.shape, lambda i: (0, 0, 0)),
            row(PAIR),
            row(PAIR),
            row(PAIR),
        ],
        out_specs=[row(width), row(width), row(width), col, col],
        out_shape=[flat, flat, flat, turned, turned],
        cost_estimate=cost(6 * total * model * width, 6 * model * width + 10 * total * model),
        compiler_params=params(48),
        name="qkv",
    )(h, w, bias, *tables)


def place(block, rank, per):
    return jnp.bitwise_xor(block // per, rank) * per + block % per


def attn_fwd_kernel(per, table_ref, q_ref, k_ref, vt_ref, start_ref, o_ref, lse_ref, m_s, l_s, acc_s):
    i = pl.program_id(0)
    rank = table_ref[0]
    heads = q_ref.shape[1] // HEAD_DIM
    first = lax.broadcasted_iota(jnp.int32, (BLOCK, PAIR), 1) < HEAD_DIM
    queries = []
    for h in range(heads):
        pair = q_ref[:, (h // 2) * PAIR : (h // 2 + 1) * PAIR]
        keep = first if h % 2 == 0 else jnp.logical_not(first)
        queries.append(jnp.where(keep, pair, jnp.zeros_like(pair)))
    m_s[...] = jnp.full_like(m_s, -jnp.inf)
    l_s[...] = jnp.zeros_like(l_s)
    acc_s[...] = jnp.zeros_like(acc_s)
    start = start_ref[...]
    row = i * BLOCK + lax.broadcasted_iota(jnp.int32, (BLOCK, BLOCK), 1)

    def step(kb, carry):
        col = kb * BLOCK + lax.broadcasted_iota(jnp.int32, (BLOCK, BLOCK), 0)
        bias = jnp.where((col >= start) & (col <= row), 0.0, masked_score)
        at = pl.ds(pl.multiple_of(place(kb, rank, per) * BLOCK, BLOCK), BLOCK)
        scores = [
            dot32(k_ref[at, (h // 2) * PAIR : (h // 2 + 1) * PAIR], queries[h], contract_last) for h in range(heads)
        ]
        probs, alphas = [], []
        for h in range(heads):
            s = scores[h] + bias
            m_old = m_s[h : h + 1, :]
            m_new = jnp.maximum(m_old, jnp.max(s, axis=0, keepdims=True))
            alpha = jnp.exp(m_old - m_new)
            p = jnp.exp(s - m_new)
            l_s[h : h + 1, :] = l_s[h : h + 1, :] * alpha + jnp.sum(p, axis=0, keepdims=True)
            m_s[h : h + 1, :] = m_new
            probs.append(p.astype(low_type))
            alphas.append(alpha)
        for h in range(heads):
            own = slice(h * HEAD_DIM, (h + 1) * HEAD_DIM)
            acc_s[own, :] = acc_s[own, :] * alphas[h] + dot32(vt_ref[own, at], probs[h])
        return carry

    lax.fori_loop(table_ref[1 + i], i + 1, step, 0)
    for h in range(heads):
        own = slice(h * HEAD_DIM, (h + 1) * HEAD_DIM)
        acc_s[own, :] = acc_s[own, :] / l_s[h : h + 1, :]
    o_ref[...] = acc_s[...].T.astype(low_type)
    lse_ref[0] = m_s[...] + jnp.log(l_s[...])


def attn_fwd(half, slots, table, q, k, vt, start):
    rows, width = q.shape
    part = width // 2
    heads = part // HEAD_DIM
    count = rows // BLOCK
    per = rows // slots // BLOCK
    at = lambda i, t: place(i, t[0], per)
    return pl.pallas_call(
        functools.partial(attn_fwd_kernel, per),
        grid_spec=pltpu.PrefetchScalarGridSpec(
            num_scalar_prefetch=1,
            grid=(count,),
            in_specs=[
                pl.BlockSpec((BLOCK, part), lambda i, t: (at(i, t), half)),
                pl.BlockSpec((rows, part), lambda i, t: (0, half)),
                pl.BlockSpec((part, rows), lambda i, t: (half, 0)),
                pl.BlockSpec((1, BLOCK), lambda i, t: (0, at(i, t))),
            ],
            out_specs=[
                pl.BlockSpec((BLOCK, part), lambda i, t: (at(i, t), 0)),
                pl.BlockSpec((1, heads, BLOCK), lambda i, t: (at(i, t), 0, 0)),
            ],
            scratch_shapes=[
                pltpu.VMEM((heads, BLOCK), jnp.float32),
                pltpu.VMEM((heads, BLOCK), jnp.float32),
                pltpu.VMEM((part, BLOCK), jnp.float32),
            ],
        ),
        out_shape=[
            jax.ShapeDtypeStruct((rows, part), low_type),
            jax.ShapeDtypeStruct((count, heads, BLOCK), jnp.float32),
        ],
        cost_estimate=cost(half * 10**13, rows * part, 0),
        compiler_params=params(40),
        name="attn_fwd",
    )(table, q, k, vt, start)


def attn_bwd_kernel(per, slots, table_ref, q_ref, do_ref, o_ref, k_ref, v_ref, kt_ref, start_ref, lse_ref,
                    keep_ref, above_ref, below_ref, dq_ref, dk_ref, dv_ref, dq_s, dk_s, dv_s):
    i = pl.program_id(0)
    rank = table_ref[0]
    width = q_ref.shape[1]
    heads = width // HEAD_DIM
    first = lax.broadcasted_iota(jnp.int32, (BLOCK, PAIR), 1) < HEAD_DIM

    @pl.when(i == 0)
    def _():
        dk_s[...] = jnp.zeros_like(dk_s)
        dv_s[...] = jnp.zeros_like(dv_s)

    dq_s[...] = jnp.zeros_like(dq_s)
    queries, cotangents, inner = [], [], []
    product = (do_ref[...].astype(jnp.float32) * o_ref[...].astype(jnp.float32)).T
    for h in range(heads):
        cols = slice((h // 2) * PAIR, (h // 2 + 1) * PAIR)
        keep = first if h % 2 == 0 else jnp.logical_not(first)
        pair = q_ref[:, cols]
        queries.append(jnp.where(keep, pair, jnp.zeros_like(pair)))
        pair = do_ref[:, cols]
        cotangents.append(jnp.where(keep, pair, jnp.zeros_like(pair)))
        inner.append(jnp.sum(product[h * HEAD_DIM : (h + 1) * HEAD_DIM, :], axis=0, keepdims=True))
    start = start_ref[...]
    row = i * BLOCK + lax.broadcasted_iota(jnp.int32, (BLOCK, BLOCK), 1)

    def step(kb, carry):
        col = kb * BLOCK + lax.broadcasted_iota(jnp.int32, (BLOCK, BLOCK), 0)
        bias = jnp.where((col >= start) & (col <= row), 0.0, masked_score)
        at = pl.ds(pl.multiple_of(place(kb, rank, per) * BLOCK, BLOCK), BLOCK)
        raw, grads = [], []
        for h in range(heads):
            cols = slice((h // 2) * PAIR, (h // 2 + 1) * PAIR)
            raw.append(dot32(k_ref[at, cols], queries[h], contract_last))
            grads.append(dot32(v_ref[at, cols], cotangents[h], contract_last))
        probs, scores = [], []
        for h in range(heads):
            p = jnp.exp(raw[h] + bias - lse_ref[0, h : h + 1, :])
            scores.append((p * (grads[h] - inner[h])).astype(low_type))
            probs.append(p.astype(low_type))
        for h in range(heads):
            own = slice(h * HEAD_DIM, (h + 1) * HEAD_DIM)
            dq_s[own, :] += dot32(kt_ref[own, at], scores[h])
        for one in range(0, heads, 2):
            cols = slice(one * HEAD_DIM, one * HEAD_DIM + PAIR)
            dv_s[at, cols] += dot32(probs[one], cotangents[one]) + dot32(probs[one + 1], cotangents[one + 1])
            dk_s[at, cols] += dot32(scores[one], queries[one]) + dot32(scores[one + 1], queries[one + 1])
        return carry

    lax.fori_loop(table_ref[1 + i], i + 1, step, 0)
    dq = dq_s[...].T * (HEAD_DIM ** (-0.5))
    here = pl.ds(pl.multiple_of(place(i, rank, per) * BLOCK, BLOCK), BLOCK)
    for c in range(0, width, PAIR):
        dq_ref[:, c : c + PAIR] = turn_back(
            dq[:, c : c + PAIR], keep_ref[here, :], above_ref[here, :], below_ref[here, :]
        ).astype(low_type)

    @pl.when(i == pl.num_programs(0) - 1)
    def _():
        @pl.loop(0, dk_s.shape[0] // BLOCK)
        def _(b):
            at = pl.ds(pl.multiple_of(b * BLOCK, BLOCK), BLOCK)
            for c in range(0, width, PAIR):
                cols = slice(c, c + PAIR)
                dk_ref[at, cols] = turn_back(
                    dk_s[at, cols], keep_ref[at, :], above_ref[at, :], below_ref[at, :]
                ).astype(low_type)
                dv_ref[at, cols] = dv_s[at, cols].astype(low_type)


def attn_bwd(half, slots, table, q, do, o, k, v, kt, start, lse, tables):
    rows, width = q.shape
    part = width // 2
    heads = part // HEAD_DIM
    count = rows // BLOCK
    per = rows // slots // BLOCK
    at = lambda i, t: place(i, t[0], per)
    whole = pl.BlockSpec((rows, part), lambda i, t: (0, half))
    turns = pl.BlockSpec((rows, PAIR), lambda i, t: (0, 0))
    result = pl.BlockSpec((rows, part), lambda i, t: (0, 0))
    return pl.pallas_call(
        functools.partial(attn_bwd_kernel, per, slots),
        grid_spec=pltpu.PrefetchScalarGridSpec(
            num_scalar_prefetch=1,
            grid=(count,),
            in_specs=[
                pl.BlockSpec((BLOCK, part), lambda i, t: (at(i, t), half)),
                pl.BlockSpec((BLOCK, part), lambda i, t: (at(i, t), half)),
                pl.BlockSpec((BLOCK, part), lambda i, t: (at(i, t), 0)),
                whole,
                whole,
                pl.BlockSpec((part, rows), lambda i, t: (half, 0)),
                pl.BlockSpec((1, BLOCK), lambda i, t: (0, at(i, t))),
                pl.BlockSpec((1, heads, BLOCK), lambda i, t: (at(i, t), 0, 0)),
                turns,
                turns,
                turns,
            ],
            out_specs=[pl.BlockSpec((BLOCK, part), lambda i, t: (at(i, t), 0)), result, result],
            scratch_shapes=[
                pltpu.VMEM((part, BLOCK), jnp.float32),
                pltpu.VMEM((rows, part), jnp.float32),
                pltpu.VMEM((rows, part), jnp.float32),
            ],
        ),
        out_shape=[jax.ShapeDtypeStruct((rows, part), low_type)] * 3,
        cost_estimate=cost(25 * rows * rows * part // 2, 16 * rows * part, 8 * rows * rows // 4),
        compiler_params=params(48),
        name="attn_bwd",
    )(table, q, do, o, k, v, kt, start, lse, *tables)


def qkv_grad_kernel(*refs):
    left_ref, other_ref, rights, (out_ref, sum_ref) = refs[0], refs[1], refs[2:-2], refs[-2:]
    part = rights[0].shape[1]

    @pl.when(pl.program_id(0) == 0)
    def _():
        for n, right in enumerate(rights):
            sum_ref[n // 2 : n // 2 + 1, (n % 2) * part : (n % 2 + 1) * part] = jnp.sum(
                right[...].astype(jnp.float32), axis=0, keepdims=True
            )

    left = left_ref[...]
    for n, right in enumerate(rights):
        out_ref[n // 2, :, (n % 2) * part : (n % 2 + 1) * part] = dot32(left, right[...], contract_first).astype(low_type)
    out_ref[len(rights) // 2] = other_ref[...]


def qkv_grad(left, rights, other):
    rows, model = left.shape
    part = rights[0].shape[1]
    count = len(rights) // 2
    tile = 512
    return pl.pallas_call(
        qkv_grad_kernel,
        grid=(model // tile,),
        in_specs=[pl.BlockSpec((rows, tile), lambda n: (0, n)), pl.BlockSpec((tile, 2 * part), lambda n: (n, 0))]
        + [pl.BlockSpec((rows, part), lambda n: (0, 0), pipeline_mode=pl.Buffered(1))] * len(rights),
        out_specs=[
            pl.BlockSpec((count + 1, tile, 2 * part), lambda n: (0, n, 0)),
            pl.BlockSpec((count, 2 * part), lambda n: (0, 0)),
        ],
        out_shape=[
            jax.ShapeDtypeStruct((count + 1, model, 2 * part), low_type),
            jax.ShapeDtypeStruct((count, 2 * part), jnp.float32),
        ],
        cost_estimate=cost(4 * count * rows * model * part, 4 * rows * model),
        compiler_params=params(48),
        name="qkv_grad",
    )(left, other, *rights)


def stream(refs, buf, sem):
    step = pl.program_id(0)
    fetch_next(step, refs, buf, sem)
    return step % 2


def back_kernel(count, one_ref, two_ref, w_ref, *rest):
    dgate_ref, dup_ref, buf, sem = rest[count:]
    now = stream(rest[:count], buf, sem)
    da = dot32(buf[now], w_ref[...], contract_last)
    dgate_ref[...] = (da * one_ref[...].astype(jnp.float32)).astype(low_type)
    dup_ref[...] = (da * two_ref[...].astype(jnp.float32)).astype(low_type)


def back_through_down(dm_blocks, one, two, w):
    depth, model = w.shape
    count = len(dm_blocks)
    block = dm_blocks[0].shape[0]
    rows = block * count
    row = pl.BlockSpec((block, depth), lambda r: (r, 0))
    deep = jax.ShapeDtypeStruct((rows, depth), low_type)
    return pl.pallas_call(
        functools.partial(back_kernel, count),
        grid=(count,),
        in_specs=[row, row, pl.BlockSpec(w.shape, lambda r: (0, 0), pipeline_mode=pl.Buffered(1))] + [ANY] * count,
        out_specs=[row, row],
        out_shape=[deep, deep],
        scratch_shapes=[pltpu.VMEM((2, block, model), low_type), pltpu.SemaphoreType.DMA((2,))],
        cost_estimate=cost(2 * rows * model * depth, 2 * model * depth + 2 * rows * model + 8 * rows * depth),
        compiler_params=params(56),
        name="back_down",
    )(one, two, w, *dm_blocks)


swap_x = [(0, 1), (1, 0), (2, 3), (3, 2)]
swap_y = [(0, 2), (2, 0), (1, 3), (3, 1)]


def square(count):
    return count == 4


def gather_rows(top, end):
    x_top = lax.ppermute(top, "tensor", swap_x)
    y_end = lax.ppermute(end, "tensor", swap_y)
    x_end = lax.ppermute(end, "tensor", swap_x)
    y_top = lax.ppermute(top, "tensor", swap_y)
    first = [top, end, x_top, x_end, y_top, y_end]

    def rest(*between):
        far_top = lax.ppermute(after(x_top, *between), "tensor", swap_y)
        far_end = lax.ppermute(after(y_end, *between), "tensor", swap_x)
        return [far_top, far_end]

    return first, rest


def after(value, *others):
    return lax.optimization_barrier((value,) + others)[0]


def halves(value):
    half = value.shape[0] // 2
    return value[:half], value[half:]


def add_low(a, b):
    return (a.astype(jnp.float32) + b.astype(jnp.float32)).astype(low_type)


def scatter_first(values):
    far, half = values[3], values[3].shape[0] // 2
    top = lax.ppermute(far[:half], "tensor", swap_x)
    end = lax.ppermute(far[half:], "tensor", swap_y)
    return [top, end]


def scatter_last(values, first):
    top, end = first
    half = top.shape[0]
    for_x, for_y = values[1], values[2]
    for_y = jnp.concatenate([add_low(for_y[:half], top), for_y[half:]], axis=0)
    for_x = jnp.concatenate([for_x[:half], add_low(for_x[half:], end)], axis=0)
    from_x = lax.ppermute(for_x, "tensor", swap_x)
    from_y = lax.ppermute(for_y, "tensor", swap_y)
    return [values[0], from_x, from_y]


MESH = pl.DeviceIdType.MESH


def greet(near_x, near_y):
    barrier = pltpu.get_barrier_semaphore()
    for near in (near_x, near_y):
        pl.semaphore_signal(barrier, inc=1, device_id={"tensor": near}, device_id_type=MESH)
    pl.semaphore_wait(barrier, 2)


def neighbours():
    rank = lax.axis_index("tensor")
    return jnp.bitwise_xor(rank, 1), jnp.bitwise_xor(rank, 2)


def remote(index, source, target, near, send, recv):
    return pltpu.make_async_remote_copy(
        src_ref=source,
        dst_ref=target,
        send_sem=send.at[index],
        recv_sem=recv.at[index],
        device_id={"tensor": near},
        device_id_type=MESH,
    )


arrival = (0, 1, 2, 5, 3, 4, 6, 7)


def arrival_slot(i):
    return jnp.where(i == 3, 5, jnp.where(i == 4, 3, jnp.where(i == 5, 4, i)))


def square_copies(all_s, half, send, recv):
    near_x, near_y = neighbours()
    at = lambda n: all_s.at[pl.ds(n * half, half)]
    return (
        remote(0, at(0), at(2), near_x, send, recv),
        remote(1, at(1), at(5), near_y, send, recv),
        remote(2, at(1), at(3), near_x, send, recv),
        remote(3, at(0), at(4), near_y, send, recv),
        remote(4, at(2), at(6), near_y, send, recv),
        remote(5, at(5), at(7), near_x, send, recv),
    )


def await_slot(i, copies):
    x_top, y_end, x_end, y_top, far_top, far_end = copies

    @pl.when(i == 2)
    def _():
        x_top.wait_recv()
        far_top.start()
        y_end.wait_recv()
        far_end.start()

    for n, c in ((4, x_end), (5, y_top), (6, far_top), (7, far_end)):

        @pl.when(i == n)
        def _(c=c):
            c.wait_recv()


def fetch_next(i, refs, buf, sem):
    def fetch(j):
        pltpu.make_async_copy(refs[j], buf.at[j % 2], sem.at[j % 2]).start()

    for j in range(len(refs)):

        @pl.when(i == max(j - 1, 0) if j else i == 0)
        def _(j=j):
            fetch(j)

    pltpu.make_async_copy(refs[0], buf.at[i % 2], sem.at[i % 2]).wait()


def gather_norm_kernel(nd, x_ref, small_ref, pos_ref, inv_ref, h_ref, full_ref, keep_ref, above_ref, below_ref,
                       all_s, full_s, stage, send, recv, local, small_send, small_recv, out_sem):
    d = lax.axis_index("dp")
    near_x, near_y = neighbours()
    half = x_ref.shape[0] // 2
    width = small_ref.shape[1]
    own = pltpu.make_async_copy(x_ref, all_s.at[pl.ds(0, 2 * half)], local)
    own.start()
    barrier = pltpu.get_barrier_semaphore()
    for near in (near_x, near_y):
        pl.semaphore_signal(barrier, inc=1, device_id={"tensor": near}, device_id_type=MESH)
    for k in range(1, nd):
        pl.semaphore_signal(barrier, inc=1, device_id={"dp": lax.rem(d + k, nd)}, device_id_type=MESH)
    pl.semaphore_wait(barrier, nd + 1)
    own.wait()
    copies = square_copies(all_s, half, send, recv)
    for c in copies[:4]:
        c.start()
    small = []
    for k in range(1, nd):
        c = pltpu.make_async_remote_copy(
            src_ref=small_ref,
            dst_ref=full_s.at[d],
            send_sem=small_send.at[k],
            recv_sem=small_recv.at[k],
            device_id={"dp": lax.rem(d + k, nd)},
            device_id_type=MESH,
        )
        c.start()
        small.append(c)
    full_s[d] = small_ref[...]
    for c in small:
        c.wait_recv()
    for n in range(nd):
        full_ref[:, n * width : (n + 1) * width] = full_s[n]
    step = 32
    lane = lax.broadcasted_iota(jnp.int32, (256, PAIR), 1) % HEAD_DIM

    def turns(at):
        angles = pos_ref[at, :] * inv_ref[...]
        cos_part, sine_part = jnp.cos(angles), jnp.sin(angles)
        keep_ref[at, :] = jnp.where(lane < ROT, cos_part, 1.0)
        above_ref[at, :] = jnp.where(lane < ROT // 2, -sine_part, 0.0)
        below_ref[at, :] = jnp.where((lane >= ROT // 2) & (lane < ROT), sine_part, 0.0)

    def out(buf, row):
        return pltpu.make_async_copy(stage.at[buf], h_ref.at[pl.ds(row, half)], out_sem.at[buf])

    def body_step(i, carry):
        await_slot(i, copies)
        row = pl.multiple_of(arrival_slot(i) * half, half)
        buf = i % 2

        @pl.when(i >= 2)
        def _():
            out(buf, row).wait()

        @pl.loop(0, half // step)
        def _(r):
            at = pl.ds(pl.multiple_of(r * step, step), step)
            x = all_s[pl.ds(pl.multiple_of(row + r * step, step), step), :].astype(jnp.float32)
            c = x - jnp.mean(x, axis=-1, keepdims=True)
            s = lax.rsqrt(jnp.mean(c * c, axis=-1, keepdims=True) + norm_eps)
            stage[buf, at, :] = (c * s * full_ref[0:1, :] + full_ref[2:3, :]).astype(low_type)

        out(buf, row).start()

        @pl.when(i < 4)
        def _():
            turns(pl.ds(pl.multiple_of(i * 512, 256), 256))
            turns(pl.ds(pl.multiple_of(i * 512 + 256, 256), 256))

        return carry

    lax.fori_loop(0, 8, body_step, 0)
    for buf in (0, 1):
        out(buf, 0).wait()
    for c in copies:
        c.wait_send()
    for c in small:
        c.wait_send()


def gather_norm(x, small, pos, inverse):
    nd = lax.axis_size("dp")
    rows, model = x.shape
    total = 4 * rows
    count, width = small.shape
    vmem = pl.BlockSpec(memory_space=pltpu.VMEM)
    table = jax.ShapeDtypeStruct((total, PAIR), jnp.float32)
    return pl.pallas_call(
        functools.partial(gather_norm_kernel, nd),
        in_specs=[ANY, vmem, vmem, vmem],
        out_specs=[ANY, vmem, vmem, vmem, vmem],
        out_shape=[
            jax.ShapeDtypeStruct((total, model), low_type),
            jax.ShapeDtypeStruct((count, width * nd), jnp.float32),
            table,
            table,
            table,
        ],
        scratch_shapes=[
            pltpu.VMEM((total, model), low_type),
            pltpu.VMEM((nd, count, width), jnp.float32),
            pltpu.VMEM((2, rows // 2, model), low_type),
            pltpu.SemaphoreType.DMA((6,)),
            pltpu.SemaphoreType.DMA((6,)),
            pltpu.SemaphoreType.DMA,
            pltpu.SemaphoreType.DMA((nd,)),
            pltpu.SemaphoreType.DMA((nd,)),
            pltpu.SemaphoreType.DMA((2,)),
        ],
        cost_estimate=cost(20 * total * model, 4 * total * model),
        compiler_params=pltpu.CompilerParams(vmem_limit_bytes=40 * MIB, collective_id=3, has_side_effects=True),
        name="gather_norm",
    )(x, small, pos, inverse)


def gather_do_kernel(d_ref, act_ref, h_hbm, dup_hbm, o_a_ref, o_b_ref, wo_ref, wd_hbm, do_ref, grad_ref, mlp_ref, up_ref,
                     all_s, wd_s, dup_s, acc, act_s, h_s, stage, up_s, send, recv, local, act_sem, h_sem, out_sem, up_sem):
    near_x, near_y = neighbours()
    half = d_ref.shape[0] // 2
    model = d_ref.shape[1]
    part = o_a_ref.shape[1]
    tile = 512
    own = pltpu.make_async_copy(d_ref, all_s.at[pl.ds(0, 2 * half)], local.at[0])
    own.start()
    weights = pltpu.make_async_copy(wd_hbm, wd_s, local.at[1])
    weights.start()
    cotangent = pltpu.make_async_copy(dup_hbm, dup_s, local.at[2])
    cotangent.start()
    greet(near_x, near_y)
    own.wait()
    copies = square_copies(all_s, half, send, recv)
    for c in copies[:4]:
        c.start()
    acc[...] = jnp.zeros_like(acc)
    weights.wait()
    cotangent.wait()
    strip = model // 8

    def loads(i):
        at = pl.ds(pl.multiple_of(i * half, half), half)
        cols = pl.ds(pl.multiple_of(i * strip, strip), strip)
        return [
            pltpu.make_async_copy(act_ref.at[at], act_s.at[i % 2], act_sem.at[i % 2]),
            pltpu.make_async_copy(h_hbm.at[:, cols], h_s.at[i % 2], h_sem.at[i % 2]),
        ]

    def outs(i):
        at = pl.ds(pl.multiple_of(i * half, half), half)
        side = pl.ds(pl.multiple_of(i * strip, strip), strip)
        return [
            pltpu.make_async_copy(stage.at[i % 2], mlp_ref.at[at], out_sem.at[i % 2]),
            pltpu.make_async_copy(up_s.at[i % 2], up_ref.at[side], up_sem.at[i % 2]),
        ]

    for c in loads(0):
        c.start()

    def step(i, carry):
        @pl.when(i < 7)
        def _():
            for c in loads(i + 1):
                c.start()

        for c in loads(i):
            c.wait()

        @pl.when(i >= 2)
        def _():
            for c in outs(i - 2):
                c.wait()

        stage[i % 2] = dot32(act_s[i % 2], wd_s[...]).astype(low_type)
        up_s[i % 2] = dot32(h_s[i % 2], dup_s[...], contract_first).astype(low_type)
        for c in outs(i):
            c.start()
        await_slot(i, copies)
        at = pl.ds(pl.multiple_of(arrival_slot(i) * half, half), half)
        dattn = all_s[at, :]
        do_ref[at, :] = dot32(dattn, wo_ref[...], contract_last).astype(low_type)
        acc[:part, :] += dot32(o_a_ref[at, :], dattn, contract_first)
        acc[part:, :] += dot32(o_b_ref[at, :], dattn, contract_first)
        return carry

    lax.fori_loop(0, 8, step, 0)

    @pl.loop(0, model // tile)
    def _(n):
        cols = pl.ds(pl.multiple_of(n * tile, tile), tile)
        grad_ref[cols, :] = acc[:, cols].T.astype(low_type)

    for i in (6, 7):
        for c in outs(i):
            c.wait()
    for c in copies:
        c.wait_send()


def gather_do(dattn, act, h, dup, o_a, o_b, wo, wd):
    rows, model = dattn.shape
    total = 4 * rows
    depth = act.shape[1]
    width = wo.shape[0]
    vmem = pl.BlockSpec(memory_space=pltpu.VMEM)
    return pl.pallas_call(
        gather_do_kernel,
        in_specs=[ANY, ANY, ANY, ANY, vmem, vmem, vmem, ANY],
        out_specs=[vmem, vmem, ANY, ANY],
        out_shape=[
            jax.ShapeDtypeStruct((total, width), low_type),
            jax.ShapeDtypeStruct((model, width), low_type),
            jax.ShapeDtypeStruct((total, model), low_type),
            jax.ShapeDtypeStruct((model, depth), low_type),
        ],
        scratch_shapes=[
            pltpu.VMEM((total, model), low_type),
            pltpu.VMEM(wd.shape, low_type),
            pltpu.VMEM(dup.shape, low_type),
            pltpu.VMEM((width, model), jnp.float32),
            pltpu.VMEM((2, rows // 2, depth), low_type),
            pltpu.VMEM((2, total, model // 8), low_type),
            pltpu.VMEM((2, rows // 2, model), low_type),
            pltpu.VMEM((2, model // 8, depth), low_type),
            pltpu.SemaphoreType.DMA((6,)),
            pltpu.SemaphoreType.DMA((6,)),
            pltpu.SemaphoreType.DMA((3,)),
            pltpu.SemaphoreType.DMA((2,)),
            pltpu.SemaphoreType.DMA((2,)),
            pltpu.SemaphoreType.DMA((2,)),
            pltpu.SemaphoreType.DMA((2,)),
        ],
        cost_estimate=cost(2 * total * model * (depth + 2 * width), 6 * total * model),
        compiler_params=pltpu.CompilerParams(vmem_limit_bytes=56 * MIB, collective_id=4, has_side_effects=True),
        name="gather_do",
    )(dattn, act, h, dup, o_a, o_b, wo, wd)


def exchange(rows, partial, bufs, send, recv, fill_one, fill_two):
    far_s, for_x, for_y, top_s, end_s, from_x, from_y = bufs
    near_x, near_y = neighbours()
    half = rows // 2
    t, e = pl.ds(0, half), pl.ds(half, half)
    copies = [
        remote(0, far_s.at[t], top_s, near_x, send, recv),
        remote(1, far_s.at[e], end_s, near_y, send, recv),
        remote(2, for_x.at[t], from_x.at[t], near_x, send, recv),
        remote(3, for_y.at[e], from_y.at[e], near_y, send, recv),
    ]
    quarter = half // 2
    for n in range(2):
        at = pl.ds(half + n * quarter, quarter)
        copies.append(remote(4 + n, for_x.at[at], from_x.at[at], near_x, send, recv))
    for n in range(2):
        at = pl.ds(n * quarter, quarter)
        copies.append(remote(6 + n, for_y.at[at], from_y.at[at], near_y, send, recv))

    def into(ref, which):
        def store(cols, value):
            ref[pl.ds(which * half, half), cols] = value.astype(low_type)

        return store

    def added(ref, which, other):
        def store(cols, value):
            ref[pl.ds(which * half, half), cols] = (value + other[:, cols].astype(jnp.float32)).astype(low_type)

        return store

    partial(3, 0, into(far_s, 0))
    copies[0].start()
    partial(3, 1, into(far_s, 1))
    copies[1].start()
    partial(1, 0, into(for_x, 0))
    copies[2].start()
    partial(2, 1, into(for_y, 1))
    copies[3].start()
    fill_one()
    copies[0].wait_recv()
    partial(2, 0, added(for_y, 0, top_s))
    copies[6].start()
    copies[7].start()
    copies[1].wait_recv()
    partial(1, 1, added(for_x, 1, end_s))
    copies[4].start()
    copies[5].start()
    fill_two()
    return copies


def finish_quarters(copies, finish):
    copies[2].wait_recv()
    copies[6].wait_recv()
    finish(0)
    copies[3].wait_recv()
    copies[4].wait_recv()
    finish(2)
    copies[7].wait_recv()
    finish(1)
    copies[5].wait_recv()
    finish(3)
    for c in copies:
        c.wait_send()


def finish_back(copies, rows, gain_row, v_ref, base_ref, own_ref, live_ref, norm_ref, from_x, from_y, dx_ref, low_ref, gain_ref, shift_ref, gain_s, shift_s):
    quarter = rows // 4
    step = 16
    gain_s[...] = jnp.zeros_like(gain_s)
    shift_s[...] = jnp.zeros_like(shift_s)

    def finish(which):
        @pl.loop(0, quarter // step)
        def _(r):
            at = pl.ds(pl.multiple_of(which * quarter + r * step, step), step)
            e = own_ref[at, :].astype(jnp.float32) + from_x[at, :].astype(jnp.float32) + from_y[at, :].astype(jnp.float32)
            v = v_ref[at, :].astype(jnp.float32)
            c = v - jnp.mean(v, axis=-1, keepdims=True)
            s = lax.rsqrt(jnp.mean(c * c, axis=-1, keepdims=True) + norm_eps)
            xh = c * s
            w = e * norm_ref[gain_row : gain_row + 1, :]
            back = s * (w - jnp.mean(w, axis=-1, keepdims=True) - xh * jnp.mean(w * xh, axis=-1, keepdims=True))
            dx = base_ref[at, :].astype(jnp.float32) + back
            dx_ref[at, :] = dx.astype(dx_ref.dtype)
            if low_ref is not None:
                low_ref[at, :] = (dx * live_ref[at, :]).astype(low_type)
            ex = e * xh
            gain_s[...] += ex[:8] + ex[8:]
            shift_s[...] += e[:8] + e[8:]

    finish_quarters(copies, finish)
    gain_ref[...] = jnp.sum(gain_s[...], axis=0, keepdims=True)
    shift_ref[...] = jnp.sum(shift_s[...], axis=0, keepdims=True)


def exchange_scratch(rows, model):
    big = pltpu.VMEM((rows, model), low_type)
    small = pltpu.VMEM((rows // 2, model), low_type)
    line = pltpu.VMEM((8, model), jnp.float32)
    sems = pltpu.SemaphoreType.DMA((8,))
    return [big, big, big, small, small, big, big, line, line, sems, sems]


def out_scatter_kernel(a_ref, b_ref, w_ref, x_ref, live_ref, norm_ref, x1_ref, h_ref, *scratch):
    bufs, (send, recv) = scratch[:7], scratch[9:]
    near_x, near_y = neighbours()
    rows, model = x_ref.shape
    half = rows // 2
    part = a_ref.shape[1]
    tile = 512
    greet(near_x, near_y)

    def partial(slot, which, store):
        at = pl.ds(slot * rows + which * half, half)

        @pl.loop(0, model // tile)
        def _(n):
            cols = pl.ds(pl.multiple_of(n * tile, tile), tile)
            store(cols, dot32(a_ref[at, :], w_ref[:part, cols]) + dot32(b_ref[at, :], w_ref[part:, cols]))

    def own(which):
        def store(cols, value):
            x1_ref[pl.ds(which * half, half), cols] = value

        return store

    def fill_one():
        partial(0, 0, own(0))
        partial(0, 1, own(1))

    copies = exchange(rows, partial, bufs, send, recv, fill_one, lambda: None)
    from_x, from_y = bufs[5:]
    quarter = rows // 4
    step = 32

    def finish(which):
        @pl.loop(0, quarter // step)
        def _(r):
            at = pl.ds(pl.multiple_of(which * quarter + r * step, step), step)
            attn = x1_ref[at, :] + from_x[at, :].astype(jnp.float32) + from_y[at, :].astype(jnp.float32)
            x1 = x_ref[at, :].astype(jnp.float32) + live_ref[at, :] * attn
            x1_ref[at, :] = x1
            c = x1 - jnp.mean(x1, axis=-1, keepdims=True)
            s = lax.rsqrt(jnp.mean(c * c, axis=-1, keepdims=True) + norm_eps)
            h_ref[at, :] = (c * s * norm_ref[1:2, :] + norm_ref[3:4, :]).astype(low_type)

    finish_quarters(copies, finish)


def out_scatter(a, b, w, x, live, norm):
    rows, model = x.shape
    vmem = pl.BlockSpec(memory_space=pltpu.VMEM)
    total = a.shape[0]
    return pl.pallas_call(
        out_scatter_kernel,
        in_specs=[vmem] * 6,
        out_specs=[vmem] * 2,
        out_shape=[jax.ShapeDtypeStruct((rows, model), jnp.float32), jax.ShapeDtypeStruct((rows, model), low_type)],
        scratch_shapes=exchange_scratch(rows, model),
        cost_estimate=cost(2 * total * model * w.shape[0], 20 * rows * model),
        compiler_params=pltpu.CompilerParams(vmem_limit_bytes=48 * MIB, collective_id=0, has_side_effects=True),
        name="out_scatter",
    )(a, b, w, x, live, norm)


def hidden_scatter_kernel(dgate_hbm, dup_hbm, w_hbm, h_hbm, x1_ref, og_ref, live_ref, norm_ref,
                          grad_ref, dx_ref, low_ref, gain_ref, shift_ref,
                          *scratch):
    bufs, (gain_s, shift_s, send, recv, g_s, w_s, h_s, stage, local, h_sem, out_sem) = scratch[:7], scratch[7:]
    rows, model = x1_ref.shape
    half = rows // 2
    near_x, near_y = neighbours()
    loads = [
        pltpu.make_async_copy(dgate_hbm, g_s.at[0], local.at[0]),
        pltpu.make_async_copy(dup_hbm, g_s.at[1], local.at[1]),
        pltpu.make_async_copy(w_hbm, w_s, local.at[2]),
    ]
    for c in loads:
        c.start()
    greet(near_x, near_y)
    for c in loads:
        c.wait()
    tile = 512

    def partial(slot, which, store):
        at = pl.ds(slot * rows + which * half, half)

        @pl.loop(0, model // tile)
        def _(n):
            cols = pl.ds(pl.multiple_of(n * tile, tile), tile)
            value = dot32(g_s[0, at, :], w_s[0, cols, :], contract_last)
            store(cols, value + dot32(g_s[1, at, :], w_s[1, cols, :], contract_last))

    def own(which):
        def store(cols, value):
            dx_ref[pl.ds(which * half, half), cols] = value

        return store

    strip = 256

    def load(i):
        return pltpu.make_async_copy(h_hbm.at[:, pl.ds(pl.multiple_of(i * strip, strip), strip)], h_s.at[i % 2], h_sem.at[i % 2])

    def out(i):
        at = pl.ds(pl.multiple_of(i * strip, strip), strip)
        return pltpu.make_async_copy(stage.at[i % 2], grad_ref.at[at], out_sem.at[i % 2])

    strips = model // strip
    load(0).start()

    def strip_step(i, carry):
        @pl.when(i < strips - 1)
        def _():
            load(i + 1).start()

        load(i).wait()

        @pl.when(i >= 2)
        def _():
            out(i - 2).wait()

        stage[i % 2] = dot32(h_s[i % 2], g_s[0], contract_first).astype(low_type)
        out(i).start()
        return carry

    def fill_one():
        partial(0, 0, own(0))
        partial(0, 1, own(1))
        lax.fori_loop(0, 2, strip_step, 0)

    def fill_two():
        lax.fori_loop(2, strips, strip_step, 0)

    copies = exchange(rows, partial, bufs, send, recv, fill_one, fill_two)
    finish_back(copies, rows, 1, x1_ref, og_ref, dx_ref, live_ref, norm_ref, bufs[5], bufs[6], dx_ref, low_ref, gain_ref, shift_ref, gain_s, shift_s)
    out(strips - 2).wait()
    out(strips - 1).wait()


def hidden_scatter(dgate, dup, w, h, x1, out_grad, live, norm):
    rows, model = x1.shape
    total, depth = dgate.shape
    vmem = pl.BlockSpec(memory_space=pltpu.VMEM)
    line = jax.ShapeDtypeStruct((1, model), jnp.float32)
    return pl.pallas_call(
        hidden_scatter_kernel,
        in_specs=[ANY, ANY, ANY, ANY, vmem, vmem, vmem, vmem],
        out_specs=[ANY, vmem, vmem, vmem, vmem],
        out_shape=[
            jax.ShapeDtypeStruct((model, depth), low_type),
            jax.ShapeDtypeStruct((rows, model), jnp.float32),
            jax.ShapeDtypeStruct((rows, model), low_type),
            line,
            line,
        ],
        scratch_shapes=exchange_scratch(rows, model)
        + [
            pltpu.VMEM((2, total, depth), low_type),
            pltpu.VMEM(w.shape, low_type),
            pltpu.VMEM((2, total, 256), low_type),
            pltpu.VMEM((2, 256, depth), low_type),
            pltpu.SemaphoreType.DMA((3,)),
            pltpu.SemaphoreType.DMA((2,)),
            pltpu.SemaphoreType.DMA((2,)),
        ],
        cost_estimate=cost(8 * total * model * depth, 16 * total * model),
        compiler_params=pltpu.CompilerParams(vmem_limit_bytes=62 * MIB, collective_id=5, has_side_effects=True),
        name="hidden_scatter",
    )(dgate, dup, w, h, x1, out_grad, live, norm)


def flow(first, last, loads, work, stores):
    def all_of(copies, act):
        for c in copies:
            act(c)

    all_of(loads(first), lambda c: c.start())

    def step(i, carry):
        @pl.when(i < last - 1)
        def _():
            all_of(loads(i + 1), lambda c: c.start())

        all_of(loads(i), lambda c: c.wait())

        @pl.when(i >= first + 2)
        def _():
            all_of(stores(i - 2), lambda c: c.wait())

        work(i)
        all_of(stores(i), lambda c: c.start())
        return carry

    lax.fori_loop(first, last, step, 0)
    for i in range(max(first, last - 2), last):
        all_of(stores(i), lambda c: c.wait())


def adam_work(low_s, in_s, out_s, decay_rate):
    def work(i):
        b = i % 2
        gradient = low_s[b].astype(jnp.float32)
        out_s[b, 0] = gradient
        out_s[b, 1], out_s[b, 2], out_s[b, 3] = adamw_update(in_s[b, 0], gradient, in_s[b, 1], in_s[b, 2], decay_rate)

    return work


def first_scatter_kernel(count, *refs):
    lefts_hbm = refs[:count]
    w_hbm, x_ref, base_ref, norm_ref, live_ref = refs[count : count + 5]
    refs = refs[count + 5 :]
    gate_low, up_low, down_low = refs[:3]
    hidden_in, down_in = refs[3:6], refs[6:9]
    x1_hbm, mlp_hbm = refs[9], refs[10:13]
    dx_ref, gain_ref, shift_ref, layer_hbm = refs[13:17]
    hidden_out, down_out = refs[17:21], refs[21:25]
    scratch = refs[25:]
    bufs, (gain_s, shift_s, send, recv, own_s, left_s, w_s) = scratch[:7], scratch[7:14]
    hl_s, hi_s, ho_s, dl_s, di_s, do_s, x1_s, mlp_s, layer_s = scratch[14:23]
    left_sem, in_sem, out_sem, layer_sem = scratch[23:]
    rows, model = x_ref.shape
    half = rows // 2
    tile = 512
    near_x, near_y = neighbours()
    far = pl.ds(3 * rows, rows)
    rest = pl.ds(0, 3 * rows)
    early = [pltpu.make_async_copy(left.at[far], left_s.at[n, far], left_sem.at[n]) for n, left in enumerate(lefts_hbm)]
    early.append(pltpu.make_async_copy(w_hbm, w_s, left_sem.at[2 * count]))
    late = [
        pltpu.make_async_copy(left.at[rest], left_s.at[n, rest], left_sem.at[count + n]) for n, left in enumerate(lefts_hbm)
    ]
    for c in early + late:
        c.start()
    greet(near_x, near_y)
    for c in early:
        c.wait()

    def partial(slot, which, store):
        if slot == 1 and which == 0:
            for c in late:
                c.wait()
        at = pl.ds(slot * rows + which * half, half)

        @pl.loop(0, model // tile)
        def _(n):
            cols = pl.ds(pl.multiple_of(n * tile, tile), tile)
            value = None
            for m in range(count):
                depth = left_s.shape[2]
                per = w_s.shape[2] // depth
                side = slice((m % per) * depth, (m % per + 1) * depth)
                term = dot32(left_s[m, at, :], w_s[m // per, cols, side], contract_last)
                value = term if value is None else value + term
            store(cols, value)

    def own(which):
        def store(cols, value):
            own_s[pl.ds(which * half, half), cols] = value

        return store

    strip = hl_s.shape[1]
    per = gate_low.shape[0] // strip

    def hidden_moves(s):
        at = lambda i: pl.ds(pl.multiple_of(i * strip, strip), strip)

        def loads(i):
            low = (gate_low, up_low)[s]
            return [pltpu.make_async_copy(low.at[at(i)], hl_s.at[i % 2], in_sem.at[i % 2, 0])] + [
                pltpu.make_async_copy(ref.at[s, at(i)], hi_s.at[i % 2, n], in_sem.at[i % 2, 1 + n])
                for n, ref in enumerate(hidden_in)
            ]

        def stores(i):
            return [
                pltpu.make_async_copy(ho_s.at[i % 2, n], ref.at[s, at(i)], out_sem.at[i % 2, n])
                for n, ref in enumerate(hidden_out)
            ]

        flow(0, per, loads, adam_work(hl_s, hi_s, ho_s, weight_decay), stores)

    def down_moves():
        tall = dl_s.shape[1]
        at = lambda i: pl.ds(pl.multiple_of(i * tall, tall), tall)

        def loads(i):
            return [pltpu.make_async_copy(down_low.at[at(i)], dl_s.at[i % 2], in_sem.at[i % 2, 0])] + [
                pltpu.make_async_copy(ref.at[at(i)], di_s.at[i % 2, n], in_sem.at[i % 2, 1 + n])
                for n, ref in enumerate(down_in)
            ]

        def stores(i):
            return [
                pltpu.make_async_copy(do_s.at[i % 2, n], ref.at[at(i)], out_sem.at[i % 2, n])
                for n, ref in enumerate(down_out)
            ]

        flow(0, down_low.shape[0] // tall, loads, adam_work(dl_s, di_s, do_s, weight_decay), stores)

    def layer_moves():
        deep = x1_s.shape[1]
        at = lambda i: pl.ds(pl.multiple_of(i * deep, deep), deep)

        def loads(i):
            return [pltpu.make_async_copy(x1_hbm.at[at(i)], x1_s.at[i % 2], in_sem.at[i % 2, 0])] + [
                pltpu.make_async_copy(ref.at[at(i)], mlp_s.at[i % 2, n], in_sem.at[i % 2, 1 + n])
                for n, ref in enumerate(mlp_hbm)
            ]

        def stores(i):
            return [pltpu.make_async_copy(layer_s.at[i % 2], layer_hbm.at[at(i)], layer_sem.at[i % 2])]

        def work(i):
            b = i % 2
            total = mlp_s[b, 0].astype(jnp.float32) + mlp_s[b, 1].astype(jnp.float32) + mlp_s[b, 2].astype(jnp.float32)
            layer_s[b] = (x1_s[b] + live_ref[at(i), :] * total).astype(low_type)

        flow(0, rows // deep, loads, work, stores)

    def fill_one():
        partial(0, 0, own(0))
        partial(0, 1, own(1))
        down_moves()

    def fill_two():
        hidden_moves(0)
        hidden_moves(1)
        layer_moves()

    copies = exchange(rows, partial, bufs, send, recv, fill_one, fill_two)
    finish_back(copies, rows, 0, x_ref, base_ref, own_s, None, norm_ref, bufs[5], bufs[6], dx_ref, None, gain_ref, shift_ref, gain_s, shift_s)


def first_scatter(lefts, w, x, base, norm, live, lows, hidden, down, x1, mlp_parts):
    rows, model = x.shape
    count = len(lefts)
    total, part = lefts[0].shape
    vmem = pl.BlockSpec(memory_space=pltpu.VMEM)
    line = jax.ShapeDtypeStruct((1, model), jnp.float32)
    strip, tall, deep = 64, down[0].shape[0] // 4, 64
    hidden_block, down_block = (strip, hidden[0].shape[2]), (tall, down[0].shape[1])
    like = lambda value: jax.ShapeDtypeStruct(value.shape, jnp.float32)
    both = lambda block, n, t: pltpu.VMEM((2,) + ((n,) if n else ()) + block, t)
    return pl.pallas_call(
        functools.partial(first_scatter_kernel, count),
        in_specs=[ANY] * (count + 1) + [vmem] * 4 + [ANY] * 13,
        out_specs=[vmem] * 3 + [ANY] * 9,
        out_shape=[jax.ShapeDtypeStruct((rows, model), low_type), line, line, jax.ShapeDtypeStruct((rows, model), low_type)]
        + [like(hidden[0])] * 4
        + [like(down[0])] * 4,
        scratch_shapes=exchange_scratch(rows, model)
        + [
            pltpu.VMEM((rows, model), jnp.float32),
            pltpu.VMEM((count, total, part), low_type),
            pltpu.VMEM(w.shape, low_type),
            both(hidden_block, 0, low_type),
            both(hidden_block, 3, jnp.float32),
            both(hidden_block, 4, jnp.float32),
            both(down_block, 0, low_type),
            both(down_block, 3, jnp.float32),
            both(down_block, 4, jnp.float32),
            both((deep, model), 0, jnp.float32),
            both((deep, model), 3, low_type),
            both((deep, model), 0, low_type),
            pltpu.SemaphoreType.DMA((2 * count + 1,)),
            pltpu.SemaphoreType.DMA((2, 4)),
            pltpu.SemaphoreType.DMA((2, 4)),
            pltpu.SemaphoreType.DMA((2,)),
        ],
        cost_estimate=cost(24 * rows * model * w.shape[2], 30 * rows * model),
        compiler_params=pltpu.CompilerParams(vmem_limit_bytes=60 * MIB, collective_id=6, has_side_effects=True),
        name="first_scatter",
    )(*lefts, w, x, base, norm, live, *lows, *hidden, *down, x1, *mlp_parts)


def adam_rest_kernel(low_ref, *refs):
    part = pl.program_id(0)
    last = pl.num_programs(0) - 1
    qkv_in, out_in, qkv_out, out_out = refs[:3], refs[3:6], refs[6:10], refs[10:]

    @pl.when(part < last)
    def _():
        gradient = low_ref[...].astype(jnp.float32)
        qkv_out[0][...] = gradient
        results = adamw_update(qkv_in[0][...], gradient, qkv_in[1][...], qkv_in[2][...], weight_decay)
        for ref, value in zip(qkv_out[1:], results):
            ref[...] = value

    @pl.when(part == last)
    def _():
        gradient = low_ref[0].astype(jnp.float32).T
        out_out[0][...] = gradient
        results = adamw_update(out_in[0][...], gradient, out_in[1][...], out_in[2][...], weight_decay)
        for ref, value in zip(out_out[1:], results):
            ref[...] = value


def adam_rest(low, qkv, out):
    count, depth, width = low.shape
    stack = lambda k: (jnp.minimum(k, count - 2), 0, 0)
    three = pl.BlockSpec((1, depth, width), stack)
    flat = pl.BlockSpec(out[0].shape, lambda k: (0, 0))
    like = lambda value: jax.ShapeDtypeStruct(value.shape, jnp.float32)
    return pl.pallas_call(
        adam_rest_kernel,
        grid=(count,),
        in_specs=[pl.BlockSpec((1, depth, width), lambda k: (k, 0, 0))] + [three] * 3 + [flat] * 3,
        out_specs=[three] * 4 + [flat] * 4,
        out_shape=[like(qkv[0])] * 4 + [like(out[0])] * 4,
        cost_estimate=cost(30 * count * depth * width, 30 * count * depth * width),
        compiler_params=params(32),
        name="adam_rest",
    )(low, *qkv, *out)


def gather_gate_up_kernel(count, h_ref, w_hbm, *rest):
    blocks, (all_ref, act_ref, one_ref, two_ref, grad_ref) = rest[:count], rest[count : count + 5]
    w_s, all_s, stage, acc, turned, dm_s, send, recv, local, h_sem, out_sem, dm_sem = rest[count + 5 :]
    near_x, near_y = neighbours()
    half = h_ref.shape[0] // 2
    own = pltpu.make_async_copy(h_ref, all_s.at[pl.ds(0, 2 * half)], local.at[0])
    own.start()
    weights = pltpu.make_async_copy(w_hbm, w_s, local.at[1])
    weights.start()
    greet(near_x, near_y)
    own.wait()
    copies = square_copies(all_s, half, send, recv)
    for c in copies[:4]:
        c.start()
    acc[...] = jnp.zeros_like(acc)
    weights.wait()
    in_order = [blocks[n] for n in arrival]
    tile = 512

    def outs(buf, row):
        return [
            pltpu.make_async_copy(stage.at[buf, n], ref.at[pl.ds(row, half)], out_sem.at[buf, n])
            for n, ref in enumerate((act_ref, one_ref, two_ref))
        ]

    def keep(i, row):
        return pltpu.make_async_copy(all_s.at[pl.ds(row, half)], all_ref.at[pl.ds(row, half)], h_sem.at[i])

    def step(i, carry):
        await_slot(i, copies)
        row = pl.multiple_of(arrival_slot(i) * half, half)
        buf = i % 2
        keep(i, row).start()

        @pl.when(i >= 2)
        def _():
            for c in outs(buf, row):
                c.wait()

        h = all_s[pl.ds(row, half), :]
        gate = dot32(h, w_s[0])
        up = dot32(h, w_s[1])
        sig = 1.0 / (1.0 + jnp.exp(-gate))
        silu = gate * sig
        act = (silu * up).astype(low_type)
        stage[buf, 0] = act
        stage[buf, 1] = (up * sig * (1.0 + gate * (1.0 - sig))).astype(low_type)
        stage[buf, 2] = silu.astype(low_type)
        for c in outs(buf, row):
            c.start()
        turned[...] = act.T
        fetch_next(i, in_order, dm_s, dm_sem)

        @pl.loop(0, acc.shape[1] // tile)
        def _(n):
            cols = pl.ds(pl.multiple_of(n * tile, tile), tile)
            acc[:, cols] += dot32(turned[...], dm_s[buf, :, cols])

        return carry

    lax.fori_loop(0, 8, step, 0)
    for buf in (0, 1):
        for c in outs(buf, 0):
            c.wait()
    for i in range(8):
        keep(i, 0).wait()
    for c in copies:
        c.wait_send()
    depth = acc.shape[0]
    strip = depth // 8

    @pl.loop(0, 8)
    def _(n):
        at = pl.ds(pl.multiple_of(n * strip, strip), strip)
        all_s[at, :] = acc[at, :].astype(low_type)

    last = pltpu.make_async_copy(all_s.at[pl.ds(0, depth)], grad_ref, local.at[0])
    last.start()
    last.wait()


def gather_gate_up(h, w, dm_blocks):
    rows, model = h.shape
    depth = w.shape[2]
    total = 4 * rows
    half = rows // 2
    deep = jax.ShapeDtypeStruct((total, depth), low_type)
    return pl.pallas_call(
        functools.partial(gather_gate_up_kernel, len(dm_blocks)),
        in_specs=[ANY] * (2 + len(dm_blocks)),
        out_specs=[ANY] * 5,
        out_shape=[
            jax.ShapeDtypeStruct((total, model), low_type),
            deep,
            deep,
            deep,
            jax.ShapeDtypeStruct((depth, model), low_type),
        ],
        scratch_shapes=[
            pltpu.VMEM(w.shape, low_type),
            pltpu.VMEM((total, model), low_type),
            pltpu.VMEM((2, 3, half, depth), low_type),
            pltpu.VMEM((depth, model), jnp.float32),
            pltpu.VMEM((depth, half), low_type),
            pltpu.VMEM((2, half, model), low_type),
            pltpu.SemaphoreType.DMA((6,)),
            pltpu.SemaphoreType.DMA((6,)),
            pltpu.SemaphoreType.DMA((2,)),
            pltpu.SemaphoreType.DMA((8,)),
            pltpu.SemaphoreType.DMA((2, 3)),
            pltpu.SemaphoreType.DMA((2,)),
        ],
        cost_estimate=cost(6 * total * model * depth, 4 * model * depth + 4 * total * model + 6 * total * depth),
        compiler_params=pltpu.CompilerParams(vmem_limit_bytes=60 * MIB, collective_id=1, has_side_effects=True),
        name="gather_gate_up",
    )(h, w, *dm_blocks)


def small_kernel(nd, nt, x_ref, o_ref, groups, partial, shares, send, recv, send_t, recv_t):
    d, t = lax.axis_index("dp"), lax.axis_index("tensor")
    width = o_ref.shape[1]
    barrier = pltpu.get_barrier_semaphore()
    for k in range(1, nd):
        pl.semaphore_signal(barrier, inc=1, device_id={"dp": lax.rem(d + k, nd)}, device_id_type=MESH)
    for k in range(1, nt):
        pl.semaphore_signal(barrier, inc=1, device_id={"tensor": lax.rem(t + k, nt)}, device_id_type=MESH)
    pl.semaphore_wait(barrier, nd + nt - 2)
    copies = []
    for k in range(1, nd):
        peer = lax.rem(d + k, nd)
        c = pltpu.make_async_remote_copy(
            src_ref=x_ref.at[:, pl.ds(pl.multiple_of(peer * width, width), width)],
            dst_ref=groups.at[k],
            send_sem=send.at[k],
            recv_sem=recv.at[k],
            device_id={"dp": peer},
            device_id_type=MESH,
        )
        c.start()
        copies.append(c)
    total = x_ref[:, pl.ds(pl.multiple_of(d * width, width), width)]
    for k in range(1, nd):
        copies[k - 1].wait_recv()
        total += groups[k]
    partial[...] = total
    shares[t] = total
    for k in range(1, nt):
        c = pltpu.make_async_remote_copy(
            src_ref=partial,
            dst_ref=shares.at[t],
            send_sem=send_t.at[k],
            recv_sem=recv_t.at[k],
            device_id={"tensor": lax.rem(t + k, nt)},
            device_id_type=MESH,
        )
        c.start()
        copies.append(c)
    for k in range(1, nt):
        copies[nd - 2 + k].wait_recv()
    total = shares[0]
    for k in range(1, nt):
        total += shares[k]
    o_ref[...] = total
    for c in copies:
        c.wait_send()


def sum_small(x):
    nd, nt = lax.axis_size("dp"), lax.axis_size("tensor")
    rows, model = x.shape
    width = model // nd
    vmem = pl.BlockSpec(memory_space=pltpu.VMEM)
    return pl.pallas_call(
        functools.partial(small_kernel, nd, nt),
        in_specs=[vmem],
        out_specs=vmem,
        out_shape=jax.ShapeDtypeStruct((rows, width), jnp.float32),
        scratch_shapes=[
            pltpu.VMEM((nd, rows, width), jnp.float32),
            pltpu.VMEM((rows, width), jnp.float32),
            pltpu.VMEM((nt, rows, width), jnp.float32),
            pltpu.SemaphoreType.DMA((nd,)),
            pltpu.SemaphoreType.DMA((nd,)),
            pltpu.SemaphoreType.DMA((nt,)),
            pltpu.SemaphoreType.DMA((nt,)),
        ],
        cost_estimate=cost(rows * model, 8 * rows * model),
        compiler_params=pltpu.CompilerParams(collective_id=2, has_side_effects=True),
        name="sum_small",
    )(x)


def body(
    tokens,
    out_grad,
    lengths,
    norm_gain,
    norm_bias,
    qkv_weight,
    qkv_bias,
    out_weight,
    gate_up_weight,
    down_weight,
    first_norm_gain,
    first_norm_bias,
    first_qkv_weight,
    first_qkv_bias,
    first_out_weight,
    first_gate_up_weight,
    first_down_weight,
    second_norm_gain,
    second_norm_bias,
    second_qkv_weight,
    second_qkv_bias,
    second_out_weight,
    second_gate_up_weight,
    second_down_weight,
):
    slots = lax.axis_size("tensor")
    rank = lax.axis_index("tensor")
    own_rows = tokens.shape[0]
    group_rows = own_rows * slots
    width = out_weight.shape[0]
    order = rank if square(slots) else jnp.zeros_like(rank)

    chunk = jnp.bitwise_xor(jnp.arange(slots, dtype=jnp.int32), order)
    row_index = (chunk[:, None] * own_rows + jnp.arange(own_rows, dtype=jnp.int32)[None, :]).reshape(-1)
    seq_start, _ = layout(lengths[0], row_index)
    position = row_index - seq_start
    own_index = rank * own_rows + jnp.arange(own_rows, dtype=jnp.int32)
    live = layout(lengths[0], own_index)[1][:, None]
    block_start, _ = layout(lengths[0], jnp.arange(group_rows // BLOCK, dtype=jnp.int32) * BLOCK)
    table = jnp.concatenate([order.reshape(1).astype(jnp.int32), block_start // BLOCK])
    starts = seq_start[None, :]
    small_low = jnp.concatenate([norm_gain, norm_bias, qkv_bias, qkv_bias[:1]], axis=0).astype(low_type)
    own_bias = lambda full: lax.dynamic_slice_in_dim(full[4:7], rank * width, width, 1)[:, None, :]

    if square(slots):
        qkv_full = lax.all_gather(qkv_weight.astype(low_type), "dp", axis=1, tiled=True)
        lane = jnp.arange(PAIR, dtype=jnp.int32) % (ROT // 2)
        inverse = jnp.power(rope_base, -lane.astype(jnp.float32) * (2.0 / ROT))[None, :]
        h1, small_full, *tables = gather_norm(
            tokens, small_low.astype(jnp.float32), position.astype(jnp.float32)[:, None], inverse
        )
        norm = small_full[:4]
        out_low = after(out_weight.astype(low_type), qkv_full, h1)
        out_full = lax.all_gather(out_low, "dp", axis=1, tiled=True)
        dm_own = (after(out_grad, h1).astype(jnp.float32) * live).astype(low_type)
        dm_first, dm_rest = gather_rows(*halves(dm_own))
        q, k, v, kt, vt = qkv_all(h1, qkv_full, own_bias(small_full), tables)

        o_a, lse_a = attn_fwd(0, slots, table, q, k, vt, starts)
        gate_up_low = after(gate_up_weight.astype(low_type), out_full, o_a)
        gate_up_full = lax.all_gather(gate_up_low, "dp", axis=1, tiled=True)
        dm_far = dm_rest(o_a)
        o_b, lse_b = attn_fwd(1, slots, table, after(q, o_a, *dm_first), k, vt, starts)
        o_b = after(o_b, *dm_far)
        dm_blocks = dm_first + dm_far

        x1, h2_own = out_scatter(o_a, o_b, out_full, tokens, live, norm)
        down_low = after(down_weight.astype(low_type), gate_up_full, h2_own)
        down_full = lax.all_gather(down_low, "dp", axis=1, tiled=True)
        h2, act, slope_gate, slope_up, grad_down = gather_gate_up(h2_own, gate_up_full, dm_blocks)
        grad_down_own = lax.psum_scatter(after(grad_down, down_full), "dp", scatter_dimension=1, tiled=True)

        dgate, dup = back_through_down(dm_blocks, slope_gate, slope_up, down_full)
        grad_gate, dx1, dattn_own, gain_two, shift_two = hidden_scatter(
            dgate, dup, gate_up_full, h2, x1, out_grad, live, norm
        )
        grad_gate = after(grad_gate, grad_down_own)
        grad_gate_own = lax.psum_scatter(grad_gate, "dp", scatter_dimension=0, tiled=True)

        do, grad_out, mlp, grad_up = gather_do(dattn_own, act, h2, dup, o_a, o_b, out_full, down_full)
        grad_up = after(grad_up, grad_gate_own)
        grad_up_own = lax.psum_scatter(grad_up, "dp", scatter_dimension=0, tiled=True)
        mlp = [mlp[j * own_rows : (j + 1) * own_rows] for j in range(slots)]
        mlp_first = scatter_first(mlp)
        back_a = attn_bwd(0, slots, table, q, do, o_a, k, v, kt, starts, lse_a, tables)
        mlp_parts = scatter_last(mlp, [after(part, back_a[0]) for part in mlp_first])
        back_b = attn_bwd(1, slots, table, q, after(do, back_a[0], *mlp_first), o_b, k, v, kt, starts, lse_b, tables)
        dlin = [side for pair in zip(back_a, back_b) for side in pair]
        grad_rest, bias_local = qkv_grad(h1, [after(dlin[0], *mlp_parts)] + dlin[1:], grad_out)
        late = [after(dlin[0], grad_rest)] + dlin[1:]
        input_grad, gain_one, shift_one, layer_out, *steps = first_scatter(
            late,
            qkv_full,
            tokens,
            dx1,
            norm,
            live,
            (grad_gate_own, grad_up_own, grad_down_own),
            (gate_up_weight, first_gate_up_weight, second_gate_up_weight),
            (down_weight, first_down_weight, second_down_weight),
            x1,
            mlp_parts,
        )
        hidden_step, down_step = steps[:4], steps[4:]
        grad_rest = after(grad_rest, grad_up_own)
        grad_rest_own = lax.psum_scatter(grad_rest, "dp", scatter_dimension=1, tiled=True)
        rest_step = adam_rest(
            grad_rest_own,
            (qkv_weight, first_qkv_weight, second_qkv_weight),
            (out_weight, first_out_weight, second_out_weight),
        )
        qkv_step, out_step = rest_step[:4], rest_step[4:]
    else:
        everyone = lambda value: lax.all_gather(value, "tensor", axis=0, tiled=True)
        scatter = lambda value, axis, at: lax.psum_scatter(value.astype(low_type), axis, scatter_dimension=at, tiled=True)
        small_full = lax.all_gather(small_low, "dp", axis=1, tiled=True).astype(jnp.float32)
        qkv_full, out_full, gate_up_full, down_full = (
            lax.all_gather(w.astype(low_type), "dp", axis=1, tiled=True)
            for w in (qkv_weight, out_weight, gate_up_weight, down_weight)
        )
        gain_rows, shift_rows = small_full[0:2], small_full[2:4]
        rows_in, cotangent = tokens.astype(jnp.float32), out_grad.astype(jnp.float32)
        tables = rotary_tables(position)
        h1 = everyone(layer_norm(rows_in, gain_rows[0], shift_rows[0]).astype(low_type))
        q, k, v, kt, vt = qkv_all(h1, qkv_full, own_bias(small_full), tables)
        o_a, lse_a = attn_fwd(0, slots, table, q, k, vt, starts)
        o_b, lse_b = attn_fwd(1, slots, table, q, k, vt, starts)
        o = jnp.concatenate([o_a, o_b], axis=1)
        x1 = rows_in + live * scatter(dot32(o, out_full), "tensor", 0).astype(jnp.float32)
        h2 = everyone(layer_norm(x1, gain_rows[1], shift_rows[1]).astype(low_type))
        gate, up = dot32(h2, gate_up_full[0]), dot32(h2, gate_up_full[1])
        sig = 1.0 / (1.0 + jnp.exp(-gate))
        act = (gate * sig * up).astype(low_type)
        mlp_rows = scatter(dot32(act, down_full), "tensor", 0).astype(jnp.float32)
        layer_out = (x1 + live * mlp_rows).astype(low_type)
        dm = everyone((cotangent * live).astype(low_type))
        da = dot32(dm, down_full, contract_last)
        dgate = (da * up * sig * (1.0 + gate * (1.0 - sig))).astype(low_type)
        dup = (da * gate * sig).astype(low_type)
        grad_down_own = scatter(dot32(act, dm, contract_first), "dp", 1)
        grad_gate_up = jnp.stack([dot32(h2, dgate, contract_first), dot32(h2, dup, contract_first)])
        grad_gate_up_own = scatter(grad_gate_up, "dp", 1)
        dh2 = dot32(dgate, gate_up_full[0], contract_last) + dot32(dup, gate_up_full[1], contract_last)
        dh2 = scatter(dh2, "tensor", 0).astype(jnp.float32)
        back, gain_two, shift_two = jax.vjp(layer_norm, x1, gain_rows[1], shift_rows[1])[1](dh2)
        dx1 = cotangent + back
        dattn = everyone((dx1 * live).astype(low_type))
        do = dot32(dattn, out_full, contract_last).astype(low_type)
        grad_out = dot32(dattn, o, contract_first).astype(low_type)
        back_a = attn_bwd(0, slots, table, q, do, o_a, k, v, kt, starts, lse_a, tables)
        back_b = attn_bwd(1, slots, table, q, do, o_b, k, v, kt, starts, lse_b, tables)
        dlin = [side for pair in zip(back_a, back_b) for side in pair]
        grad_rest, bias_local = qkv_grad(h1, dlin, grad_out)
        grad_rest_own = scatter(grad_rest, "dp", 1)
        grad_qkv_own, grad_out_own = grad_rest_own[:3], grad_rest_own[3].T
        dh1 = sum(
            dot32(jnp.concatenate(dlin[2 * n : 2 * n + 2], axis=1), qkv_full[n], contract_last) for n in range(3)
        )
        dh1 = scatter(dh1, "tensor", 0).astype(jnp.float32)
        back, gain_one, shift_one = jax.vjp(layer_norm, rows_in, gain_rows[0], shift_rows[0])[1](dh1)
        input_grad = (dx1 + back).astype(low_type)
        gain_one, gain_two, shift_one, shift_two = (
            value[None, :] for value in (gain_one, gain_two, shift_one, shift_two)
        )

        def whole_step(gradient, *held):
            gradient = gradient.astype(jnp.float32)
            return (gradient,) + adamw_update(held[0], gradient, held[1], held[2], weight_decay)

        qkv_step = whole_step(grad_qkv_own, qkv_weight, first_qkv_weight, second_qkv_weight)
        out_step = whole_step(grad_out_own, out_weight, first_out_weight, second_out_weight)
        hidden_step = whole_step(grad_gate_up_own, gate_up_weight, first_gate_up_weight, second_gate_up_weight)
        down_step = whole_step(grad_down_own, down_weight, first_down_weight, second_down_weight)

    bias_placed = lax.dynamic_update_slice(
        jnp.zeros((3, small_full.shape[1]), jnp.float32), bias_local, (jnp.int32(0), rank * width)
    )
    small_local = jnp.concatenate([gain_one, gain_two, shift_one, shift_two, bias_placed, bias_placed[:1]], axis=0)
    small_own = sum_small(small_local)

    def small_step(gradient, *held):
        return (gradient,) + adamw_update(held[0], gradient, held[1], held[2], 0.0)

    gain_step = small_step(small_own[0:2], norm_gain, first_norm_gain, second_norm_gain)
    shift_step = small_step(small_own[2:4], norm_bias, first_norm_bias, second_norm_bias)
    bias_step = small_step(small_own[4:7], qkv_bias, first_qkv_bias, second_qkv_bias)
    steps = (gain_step, shift_step, qkv_step, bias_step, out_step, hidden_step, down_step)
    return (layer_out, input_grad) + tuple(step[n] for n in range(4) for step in steps)


def solution(mesh):
    return jax.shard_map(
        body,
        mesh=mesh,
        in_specs=(
            P(("dp", "tensor"), None),
            P(("dp", "tensor"), None),
            P("dp", None),
            P(None, "dp"),
            P(None, "dp"),
            P(None, "dp", "tensor"),
            P(None, "dp"),
            P("tensor", "dp"),
            P(None, "dp", "tensor"),
            P("tensor", "dp"),
            P(None, "dp"),
            P(None, "dp"),
            P(None, "dp", "tensor"),
            P(None, "dp"),
            P("tensor", "dp"),
            P(None, "dp", "tensor"),
            P("tensor", "dp"),
            P(None, "dp"),
            P(None, "dp"),
            P(None, "dp", "tensor"),
            P(None, "dp"),
            P("tensor", "dp"),
            P(None, "dp", "tensor"),
            P("tensor", "dp"),
        ),
        out_specs=(
            P(("dp", "tensor"), None),
            P(("dp", "tensor"), None),
            P(None, "dp"),
            P(None, "dp"),
            P(None, "dp", "tensor"),
            P(None, "dp"),
            P("tensor", "dp"),
            P(None, "dp", "tensor"),
            P("tensor", "dp"),
            P(None, "dp"),
            P(None, "dp"),
            P(None, "dp", "tensor"),
            P(None, "dp"),
            P("tensor", "dp"),
            P(None, "dp", "tensor"),
            P("tensor", "dp"),
            P(None, "dp"),
            P(None, "dp"),
            P(None, "dp", "tensor"),
            P(None, "dp"),
            P("tensor", "dp"),
            P(None, "dp", "tensor"),
            P("tensor", "dp"),
            P(None, "dp"),
            P(None, "dp"),
            P(None, "dp", "tensor"),
            P(None, "dp"),
            P("tensor", "dp"),
            P(None, "dp", "tensor"),
            P("tensor", "dp"),
        ),
        check_vma=False,
    )
```

```python
import functools

import jax
import jax.numpy as jnp
from jax import lax
from jax.experimental import pallas as pl
from jax.experimental.pallas import tpu as pltpu
from jax.sharding import PartitionSpec as P

HEAD_DIM = 64
ROT = 16
PAIR = 2 * HEAD_DIM
BLOCK = 256

norm_eps = 1e-05
rope_base = 10000.0
beta_one = 0.9
beta_two = 0.95
adam_eps = 1e-08
learn_rate = 0.01
weight_decay = 0.1
step_count = 10.0
masked_score = -1e30
contract_last = (((1,), (1,)), ((), ()))
contract_first = (((0,), (0,)), ((), ()))
low_type = jnp.bfloat16
MIB = 2**20


def layout(seq_lengths, row_index):
    slot = jnp.arange(seq_lengths.shape[0])
    seq_ends = jnp.sum(
        jnp.where(slot[:, None] <= slot[None, :], seq_lengths[:, None], 0), axis=0
    )
    passed = row_index[:, None] >= seq_ends[None, :]
    seq_start = jnp.sum(jnp.where(passed, seq_lengths[None, :], 0), axis=1)
    live_rows = (row_index < jnp.sum(seq_lengths)).astype(jnp.float32)
    return (seq_start, live_rows)


def rotary_tables(position):
    half_rot = ROT // 2
    lane = jnp.arange(PAIR, dtype=jnp.int32) % HEAD_DIM
    powers = (lane % half_rot).astype(jnp.float32) * (2.0 / ROT)
    inverse = jnp.power(rope_base, -powers)
    angles = position.astype(jnp.float32)[:, None] * inverse[None, :]
    cos_part, sine_part = jnp.cos(angles), jnp.sin(angles)
    lane = lane[None, :]
    keep = jnp.where(lane < ROT, cos_part, 1.0)
    above = jnp.where(lane < half_rot, -sine_part, 0.0)
    below = jnp.where((lane >= half_rot) & (lane < ROT), sine_part, 0.0)
    return (keep, above, below)


def dot32(a, b, dims=None):
    if dims is None:
        return jnp.dot(a, b, preferred_element_type=jnp.float32)
    return lax.dot_general(a, b, dims, preferred_element_type=jnp.float32)


def turn(values, keep, above, below):
    up = pltpu.roll(values, PAIR - ROT // 2, 1)
    down = pltpu.roll(values, ROT // 2, 1)
    return values * keep + up * above + down * below


def turn_back(values, keep, above, below):
    up = pltpu.roll(values, PAIR - ROT // 2, 1)
    down = pltpu.roll(values, ROT // 2, 1)
    return values * keep - up * above - down * below


def adamw_update(weight_now, gradient, moment_one, moment_two, decay_rate):
    moment_one = beta_one * moment_one + (1.0 - beta_one) * gradient
    moment_two = beta_two * moment_two + (1.0 - beta_two) * gradient * gradient
    scaled_one = moment_one / (1.0 - beta_one**step_count)
    scaled_two = moment_two / (1.0 - beta_two**step_count)
    change = scaled_one / (jnp.sqrt(scaled_two) + adam_eps) + decay_rate * weight_now
    return (-learn_rate * change, moment_one, moment_two)


def cost(flops, moved, exps=0):
    return pl.CostEstimate(flops=int(flops) // 16, bytes_accessed=int(moved) // 16, transcendentals=int(exps) // 16)


def params(limit):
    return pltpu.CompilerParams(vmem_limit_bytes=limit * MIB)


ANY = pl.BlockSpec(memory_space=pl.ANY)


def layer_norm(values, gain_row, shift_row):
    center = values - jnp.mean(values, axis=-1, keepdims=True)
    spread = jnp.mean(center * center, axis=-1, keepdims=True)
    return center * lax.rsqrt(spread + norm_eps) * gain_row + shift_row


def qkv_kernel(scale, h_ref, w_ref, bias_ref, keep_ref, above_ref, below_ref, q_ref, k_ref, v_ref, kt_ref, vt_ref):
    h = h_ref[...]
    keep, above, below = keep_ref[...], above_ref[...], below_ref[...]
    width = q_ref.shape[1]
    lin = dot32(h, w_ref[0]) + bias_ref[0]
    for c in range(0, width, PAIR):
        u = turn(lin[:, c : c + PAIR], keep, above, below)
        q_ref[:, c : c + PAIR] = (u.astype(low_type) * scale).astype(low_type)
    lin = dot32(h, w_ref[1]) + bias_ref[1]
    for c in range(0, width, PAIR):
        u = turn(lin[:, c : c + PAIR], keep, above, below)
        k_ref[:, c : c + PAIR] = u.astype(low_type)
        kt_ref[c : c + PAIR, :] = u.T.astype(low_type)
    lin = dot32(h, w_ref[2]) + bias_ref[2]
    v_ref[...] = lin.astype(low_type)
    vt_ref[...] = lin.T.astype(low_type)


def qkv_all(h, w, bias, tables):
    total, model = h.shape
    rows = 256
    width = w.shape[2]
    row = lambda n: pl.BlockSpec((rows, n), lambda i: (i, 0))
    col = pl.BlockSpec((width, rows), lambda i: (0, i))
    flat = jax.ShapeDtypeStruct((total, width), low_type)
    turned = jax.ShapeDtypeStruct((width, total), low_type)
    return pl.pallas_call(
        functools.partial(qkv_kernel, HEAD_DIM ** (-0.5)),
        grid=(total // rows,),
        in_specs=[
            row(model),
            pl.BlockSpec(w.shape, lambda i: (0, 0, 0), pipeline_mode=pl.Buffered(1)),
            pl.BlockSpec(bias.shape, lambda i: (0, 0, 0)),
            row(PAIR),
            row(PAIR),
            row(PAIR),
        ],
        out_specs=[row(width), row(width), row(width), col, col],
        out_shape=[flat, flat, flat, turned, turned],
        cost_estimate=cost(6 * total * model * width, 6 * model * width + 10 * total * model),
        compiler_params=params(48),
        name="qkv",
    )(h, w, bias, *tables)


def place(block, rank, per):
    return jnp.bitwise_xor(block // per, rank) * per + block % per


def attn_fwd_kernel(per, table_ref, q_ref, k_ref, vt_ref, start_ref, o_ref, lse_ref, m_s, l_s, acc_s):
    i = pl.program_id(0)
    rank = table_ref[0]
    heads = q_ref.shape[1] // HEAD_DIM
    first = lax.broadcasted_iota(jnp.int32, (BLOCK, PAIR), 1) < HEAD_DIM
    queries = []
    for h in range(heads):
        pair = q_ref[:, (h // 2) * PAIR : (h // 2 + 1) * PAIR]
        keep = first if h % 2 == 0 else jnp.logical_not(first)
        queries.append(jnp.where(keep, pair, jnp.zeros_like(pair)))
    m_s[...] = jnp.full_like(m_s, -jnp.inf)
    l_s[...] = jnp.zeros_like(l_s)
    acc_s[...] = jnp.zeros_like(acc_s)
    start = start_ref[...]
    row = i * BLOCK + lax.broadcasted_iota(jnp.int32, (BLOCK, BLOCK), 1)

    def step(kb, carry):
        col = kb * BLOCK + lax.broadcasted_iota(jnp.int32, (BLOCK, BLOCK), 0)
        bias = jnp.where((col >= start) & (col <= row), 0.0, masked_score)
        at = pl.ds(pl.multiple_of(place(kb, rank, per) * BLOCK, BLOCK), BLOCK)
        scores = [
            dot32(k_ref[at, (h // 2) * PAIR : (h // 2 + 1) * PAIR], queries[h], contract_last) for h in range(heads)
        ]
        probs, alphas = [], []
        for h in range(heads):
            s = scores[h] + bias
            m_old = m_s[h : h + 1, :]
            m_new = jnp.maximum(m_old, jnp.max(s, axis=0, keepdims=True))
            alpha = jnp.exp(m_old - m_new)
            p = jnp.exp(s - m_new)
            l_s[h : h + 1, :] = l_s[h : h + 1, :] * alpha + jnp.sum(p, axis=0, keepdims=True)
            m_s[h : h + 1, :] = m_new
            probs.append(p.astype(low_type))
            alphas.append(alpha)
        for h in range(heads):
            own = slice(h * HEAD_DIM, (h + 1) * HEAD_DIM)
            acc_s[own, :] = acc_s[own, :] * alphas[h] + dot32(vt_ref[own, at], probs[h])
        return carry

    lax.fori_loop(table_ref[1 + i], i + 1, step, 0)
    for h in range(heads):
        own = slice(h * HEAD_DIM, (h + 1) * HEAD_DIM)
        acc_s[own, :] = acc_s[own, :] / l_s[h : h + 1, :]
    o_ref[...] = acc_s[...].T.astype(low_type)
    lse_ref[0] = m_s[...] + jnp.log(l_s[...])


def attn_fwd(half, slots, table, q, k, vt, start):
    rows, width = q.shape
    part = width // 2
    heads = part // HEAD_DIM
    count = rows // BLOCK
    per = rows // slots // BLOCK
    at = lambda i, t: place(i, t[0], per)
    return pl.pallas_call(
        functools.partial(attn_fwd_kernel, per),
        grid_spec=pltpu.PrefetchScalarGridSpec(
            num_scalar_prefetch=1,
            grid=(count,),
            in_specs=[
                pl.BlockSpec((BLOCK, part), lambda i, t: (at(i, t), half)),
                pl.BlockSpec((rows, part), lambda i, t: (0, half)),
                pl.BlockSpec((part, rows), lambda i, t: (half, 0)),
                pl.BlockSpec((1, BLOCK), lambda i, t: (0, at(i, t))),
            ],
            out_specs=[
                pl.BlockSpec((BLOCK, part), lambda i, t: (at(i, t), 0)),
                pl.BlockSpec((1, heads, BLOCK), lambda i, t: (at(i, t), 0, 0)),
            ],
            scratch_shapes=[
                pltpu.VMEM((heads, BLOCK), jnp.float32),
                pltpu.VMEM((heads, BLOCK), jnp.float32),
                pltpu.VMEM((part, BLOCK), jnp.float32),
            ],
        ),
        out_shape=[
            jax.ShapeDtypeStruct((rows, part), low_type),
            jax.ShapeDtypeStruct((count, heads, BLOCK), jnp.float32),
        ],
        cost_estimate=cost(half * 10**13, rows * part, 0),
        compiler_params=params(40),
        name="attn_fwd",
    )(table, q, k, vt, start)


def adam_blocks(low_ref, in_refs, out_refs):
    gradient = low_ref[...].astype(jnp.float32).reshape(out_refs[0].shape)
    results = adamw_update(in_refs[0][...], gradient, in_refs[1][...], in_refs[2][...], weight_decay)
    out_refs[0][...] = gradient
    for ref, value in zip(out_refs[1:], results):
        ref[...] = value


def attn_bwd_kernel(per, adam, table_ref, q_ref, do_ref, o_ref, k_ref, v_ref, kt_ref, start_ref, lse_ref,
                    keep_ref, above_ref, below_ref, *rest):
    (dq_ref, dk_ref, dv_ref), (dq_s, dk_s, dv_s) = rest[4 * adam : 4 * adam + 3], rest[-3:]
    if adam:
        adam_blocks(rest[0], rest[1:4], rest[7:11])
    i = pl.program_id(0)
    rank = table_ref[0]
    width = q_ref.shape[1]
    heads = width // HEAD_DIM
    first = lax.broadcasted_iota(jnp.int32, (BLOCK, PAIR), 1) < HEAD_DIM

    @pl.when(i == 0)
    def _():
        dk_s[...] = jnp.zeros_like(dk_s)
        dv_s[...] = jnp.zeros_like(dv_s)

    dq_s[...] = jnp.zeros_like(dq_s)
    queries, cotangents, inner = [], [], []
    product = (do_ref[...].astype(jnp.float32) * o_ref[...].astype(jnp.float32)).T
    for h in range(heads):
        cols = slice((h // 2) * PAIR, (h // 2 + 1) * PAIR)
        keep = first if h % 2 == 0 else jnp.logical_not(first)
        pair = q_ref[:, cols]
        queries.append(jnp.where(keep, pair, jnp.zeros_like(pair)))
        pair = do_ref[:, cols]
        cotangents.append(jnp.where(keep, pair, jnp.zeros_like(pair)))
        inner.append(jnp.sum(product[h * HEAD_DIM : (h + 1) * HEAD_DIM, :], axis=0, keepdims=True))
    start = start_ref[...]
    row = i * BLOCK + lax.broadcasted_iota(jnp.int32, (BLOCK, BLOCK), 1)

    def step(kb, carry):
        col = kb * BLOCK + lax.broadcasted_iota(jnp.int32, (BLOCK, BLOCK), 0)
        bias = jnp.where((col >= start) & (col <= row), 0.0, masked_score)
        at = pl.ds(pl.multiple_of(place(kb, rank, per) * BLOCK, BLOCK), BLOCK)
        raw, grads = [], []
        for h in range(heads):
            cols = slice((h // 2) * PAIR, (h // 2 + 1) * PAIR)
            raw.append(dot32(k_ref[at, cols], queries[h], contract_last))
            grads.append(dot32(v_ref[at, cols], cotangents[h], contract_last))
        probs, scores = [], []
        for h in range(heads):
            p = jnp.exp(raw[h] + bias - lse_ref[0, h : h + 1, :])
            scores.append((p * (grads[h] - inner[h])).astype(low_type))
            probs.append(p.astype(low_type))
        for h in range(heads):
            own = slice(h * HEAD_DIM, (h + 1) * HEAD_DIM)
            dq_s[own, :] += dot32(kt_ref[own, at], scores[h])
        for one in range(0, heads, 2):
            cols = slice(one * HEAD_DIM, one * HEAD_DIM + PAIR)
            dv_s[at, cols] += dot32(probs[one], cotangents[one]) + dot32(probs[one + 1], cotangents[one + 1])
            dk_s[at, cols] += dot32(scores[one], queries[one]) + dot32(scores[one + 1], queries[one + 1])
        return carry

    lax.fori_loop(table_ref[1 + i], i + 1, step, 0)
    dq = dq_s[...].T * (HEAD_DIM ** (-0.5))
    here = pl.ds(pl.multiple_of(place(i, rank, per) * BLOCK, BLOCK), BLOCK)
    for c in range(0, width, PAIR):
        dq_ref[:, c : c + PAIR] = turn_back(
            dq[:, c : c + PAIR], keep_ref[here, :], above_ref[here, :], below_ref[here, :]
        ).astype(low_type)

    @pl.when(i == pl.num_programs(0) - 1)
    def _():
        @pl.loop(0, dk_s.shape[0] // BLOCK)
        def _(b):
            at = pl.ds(pl.multiple_of(b * BLOCK, BLOCK), BLOCK)
            for c in range(0, width, PAIR):
                cols = slice(c, c + PAIR)
                dk_ref[at, cols] = turn_back(
                    dk_s[at, cols], keep_ref[at, :], above_ref[at, :], below_ref[at, :]
                ).astype(low_type)
                dv_ref[at, cols] = dv_s[at, cols].astype(low_type)


def attn_bwd(half, slots, table, q, do, o, k, v, kt, start, lse, tables, low=None, held=()):
    rows, width = q.shape
    part = width // 2
    heads = part // HEAD_DIM
    count = rows // BLOCK
    per = rows // slots // BLOCK
    at = lambda i, t: place(i, t[0], per)
    whole = pl.BlockSpec((rows, part), lambda i, t: (0, half))
    turns = pl.BlockSpec((rows, PAIR), lambda i, t: (0, 0))
    result = pl.BlockSpec((rows, part), lambda i, t: (0, 0))
    adam = low is not None
    adam_in, adam_out, adam_like = [], [], []
    if adam:
        strip, depth = low.shape[0] // count, low.shape[1]
        flat = pl.BlockSpec((strip, depth), lambda i, t: (i, 0))
        one = flat if held[0].ndim == 2 else pl.BlockSpec((1, strip, depth), lambda i, t: (0, i, 0))
        adam_in, adam_out = [flat, one, one, one], [one] * 4
        adam_like = [jax.ShapeDtypeStruct(held[0].shape, jnp.float32)] * 4
    return pl.pallas_call(
        functools.partial(attn_bwd_kernel, per, int(adam)),
        grid_spec=pltpu.PrefetchScalarGridSpec(
            num_scalar_prefetch=1,
            grid=(count,),
            in_specs=[
                pl.BlockSpec((BLOCK, part), lambda i, t: (at(i, t), half)),
                pl.BlockSpec((BLOCK, part), lambda i, t: (at(i, t), half)),
                pl.BlockSpec((BLOCK, part), lambda i, t: (at(i, t), 0)),
                whole,
                whole,
                pl.BlockSpec((part, rows), lambda i, t: (half, 0)),
                pl.BlockSpec((1, BLOCK), lambda i, t: (0, at(i, t))),
                pl.BlockSpec((1, heads, BLOCK), lambda i, t: (at(i, t), 0, 0)),
                turns,
                turns,
                turns,
            ]
            + adam_in,
            out_specs=[pl.BlockSpec((BLOCK, part), lambda i, t: (at(i, t), 0)), result, result] + adam_out,
            scratch_shapes=[
                pltpu.VMEM((part, BLOCK), jnp.float32),
                pltpu.VMEM((rows, part), jnp.float32),
                pltpu.VMEM((rows, part), jnp.float32),
            ],
        ),
        out_shape=[jax.ShapeDtypeStruct((rows, part), low_type)] * 3 + adam_like,
        cost_estimate=cost(25 * rows * rows * part // 2, 16 * rows * part, 8 * rows * rows // 4),
        compiler_params=params(48),
        name="attn_bwd",
    )(table, q, do, o, k, v, kt, start, lse, *tables, *((low,) + tuple(held) if adam else ()))


def qkv_grad_kernel(count, adam, *refs):
    left_ref, other_ref, rights = refs[0], refs[1], refs[2 : 2 + count]
    out_ref, sum_ref = refs[2 + count + 8 * adam : 4 + count + 8 * adam]
    if adam:
        adam_blocks(refs[2 + count], refs[3 + count : 6 + count], refs[-4:])
    part = rights[0].shape[1]

    @pl.when(pl.program_id(0) == 0)
    def _():
        for n, right in enumerate(rights):
            sum_ref[n // 2 : n // 2 + 1, (n % 2) * part : (n % 2 + 1) * part] = jnp.sum(
                right[...].astype(jnp.float32), axis=0, keepdims=True
            )

    left = left_ref[...]
    for n, right in enumerate(rights):
        out_ref[n // 2, :, (n % 2) * part : (n % 2 + 1) * part] = dot32(left, right[...], contract_first).astype(low_type)
    out_ref[len(rights) // 2] = other_ref[...]


def qkv_grad(left, rights, other, low=None, held=(), begun=()):
    rows, model = left.shape
    part = rights[0].shape[1]
    count = len(rights) // 2
    tile = 512
    adam = low is not None
    adam_in, adam_out, adam_like, extra = [], [], [], ()
    if adam:
        strip, depth = low.shape[0] // (model // tile), low.shape[1]
        one = pl.BlockSpec((1, strip, depth), lambda n: (1, n, 0))
        adam_in = [pl.BlockSpec((strip, depth), lambda n: (n, 0)), one, one, one] + [ANY] * 4
        adam_out = [one] * 4
        adam_like = [jax.ShapeDtypeStruct(held[0].shape, jnp.float32)] * 4
        extra = (low,) + tuple(held) + tuple(begun)
    first = 2 + len(rights) + 4
    return pl.pallas_call(
        functools.partial(qkv_grad_kernel, len(rights), int(adam)),
        grid=(model // tile,),
        in_specs=[pl.BlockSpec((rows, tile), lambda n: (0, n)), pl.BlockSpec((tile, 2 * part), lambda n: (n, 0))]
        + [pl.BlockSpec((rows, part), lambda n: (0, 0), pipeline_mode=pl.Buffered(1))] * len(rights)
        + adam_in,
        input_output_aliases={first + n: 2 + n for n in range(4)} if adam else {},
        out_specs=[
            pl.BlockSpec((count + 1, tile, 2 * part), lambda n: (0, n, 0)),
            pl.BlockSpec((count, 2 * part), lambda n: (0, 0)),
        ]
        + adam_out,
        out_shape=[
            jax.ShapeDtypeStruct((count + 1, model, 2 * part), low_type),
            jax.ShapeDtypeStruct((count, 2 * part), jnp.float32),
        ]
        + adam_like,
        cost_estimate=cost(4 * count * rows * model * part, 4 * rows * model),
        compiler_params=params(48),
        name="qkv_grad",
    )(left, other, *rights, *extra)


swap_x = [(0, 1), (1, 0), (2, 3), (3, 2)]
swap_y = [(0, 2), (2, 0), (1, 3), (3, 1)]


def square(count):
    return count == 4


def gather_rows(top, end):
    x_top = lax.ppermute(top, "tensor", swap_x)
    y_end = lax.ppermute(end, "tensor", swap_y)
    x_end = lax.ppermute(end, "tensor", swap_x)
    y_top = lax.ppermute(top, "tensor", swap_y)
    first = [top, end, x_top, x_end, y_top, y_end]

    def rest(*between):
        far_top = lax.ppermute(after(x_top, *between), "tensor", swap_y)
        far_end = lax.ppermute(after(y_end, *between), "tensor", swap_x)
        return [far_top, far_end]

    return first, rest


def after(value, *others):
    return lax.optimization_barrier((value,) + others)[0]


def add_low(a, b):
    return (a.astype(jnp.float32) + b.astype(jnp.float32)).astype(low_type)


def scatter_first(values):
    far, half = values[3], values[3].shape[0] // 2
    top = lax.ppermute(far[:half], "tensor", swap_x)
    end = lax.ppermute(far[half:], "tensor", swap_y)
    return [top, end]


def scatter_last(values, first):
    top, end = first
    half = top.shape[0]
    for_x, for_y = values[1], values[2]
    for_y = jnp.concatenate([add_low(for_y[:half], top), for_y[half:]], axis=0)
    for_x = jnp.concatenate([for_x[:half], add_low(for_x[half:], end)], axis=0)
    from_x = lax.ppermute(for_x, "tensor", swap_x)
    from_y = lax.ppermute(for_y, "tensor", swap_y)
    return [values[0], from_x, from_y]


MESH = pl.DeviceIdType.MESH


def greet(near_x, near_y):
    barrier = pltpu.get_barrier_semaphore()
    for near in (near_x, near_y):
        pl.semaphore_signal(barrier, inc=1, device_id={"tensor": near}, device_id_type=MESH)
    pl.semaphore_wait(barrier, 2)


def neighbours():
    rank = lax.axis_index("tensor")
    return jnp.bitwise_xor(rank, 1), jnp.bitwise_xor(rank, 2)


def remote(index, source, target, near, send, recv):
    return pltpu.make_async_remote_copy(
        src_ref=source,
        dst_ref=target,
        send_sem=send.at[index],
        recv_sem=recv.at[index],
        device_id={"tensor": near},
        device_id_type=MESH,
    )


arrival = (0, 1, 2, 5, 3, 4, 6, 7)


def arrival_slot(i):
    return jnp.where(i == 3, 5, jnp.where(i == 4, 3, jnp.where(i == 5, 4, i)))


def square_copies(all_s, half, send, recv):
    near_x, near_y = neighbours()
    at = lambda n: all_s.at[pl.ds(n * half, half)]
    return (
        remote(0, at(0), at(2), near_x, send, recv),
        remote(1, at(1), at(5), near_y, send, recv),
        remote(2, at(1), at(3), near_x, send, recv),
        remote(3, at(0), at(4), near_y, send, recv),
        remote(4, at(2), at(6), near_y, send, recv),
        remote(5, at(5), at(7), near_x, send, recv),
    )


def await_slot(i, copies):
    x_top, y_end, x_end, y_top, far_top, far_end = copies

    @pl.when(i == 2)
    def _():
        x_top.wait_recv()
        far_top.start()
        y_end.wait_recv()
        far_end.start()

    for n, c in ((4, x_end), (5, y_top), (6, far_top), (7, far_end)):

        @pl.when(i == n)
        def _(c=c):
            c.wait_recv()


def fetch_next(i, refs, buf, sem):
    def fetch(j):
        pltpu.make_async_copy(refs[j], buf.at[j % 2], sem.at[j % 2]).start()

    for j in range(len(refs)):

        @pl.when(i == max(j - 1, 0) if j else i == 0)
        def _(j=j):
            fetch(j)

    pltpu.make_async_copy(refs[0], buf.at[i % 2], sem.at[i % 2]).wait()


def flow(first, last, loads, work, stores):
    def all_of(copies, act):
        for c in copies:
            act(c)

    all_of(loads(first), lambda c: c.start())

    def step(i, carry):
        @pl.when(i < last - 1)
        def _():
            all_of(loads(i + 1), lambda c: c.start())

        all_of(loads(i), lambda c: c.wait())

        @pl.when(i >= first + 2)
        def _():
            all_of(stores(i - 2), lambda c: c.wait())

        work(i)
        all_of(stores(i), lambda c: c.start())
        return carry

    lax.fori_loop(first, last, step, 0)
    for i in range(max(first, last - 2), last):
        all_of(stores(i), lambda c: c.wait())


def gather_norm_kernel(nd, x_ref, small_ref, pos_ref, inv_ref, og_ref, live_ref, w_hbm,
                       h_ref, full_ref, keep_ref, above_ref, below_ref, top_ref, end_ref, low_hbm,
                       all_s, full_s, stage, w_s, low_s, send, recv, local, small_send, small_recv, out_sem, w_sem, low_sem):
    d = lax.axis_index("dp")
    near_x, near_y = neighbours()
    half = x_ref.shape[0] // 2
    width = small_ref.shape[1]
    own = pltpu.make_async_copy(x_ref, all_s.at[pl.ds(0, 2 * half)], local)
    own.start()
    barrier = pltpu.get_barrier_semaphore()
    for near in (near_x, near_y):
        pl.semaphore_signal(barrier, inc=1, device_id={"tensor": near}, device_id_type=MESH)
    for k in range(1, nd):
        pl.semaphore_signal(barrier, inc=1, device_id={"dp": lax.rem(d + k, nd)}, device_id_type=MESH)
    pl.semaphore_wait(barrier, nd + 1)
    own.wait()
    copies = square_copies(all_s, half, send, recv)
    for c in copies[:4]:
        c.start()
    small = []
    for k in range(1, nd):
        c = pltpu.make_async_remote_copy(
            src_ref=small_ref,
            dst_ref=full_s.at[d],
            send_sem=small_send.at[k],
            recv_sem=small_recv.at[k],
            device_id={"dp": lax.rem(d + k, nd)},
            device_id_type=MESH,
        )
        c.start()
        small.append(c)
    full_s[d] = small_ref[...]
    for n, ref in enumerate((top_ref, end_ref)):

        @pl.loop(0, half // 32)
        def _(r, n=n, ref=ref):
            to = pl.ds(pl.multiple_of(r * 32, 32), 32)
            at = pl.ds(pl.multiple_of(n * half + r * 32, 32), 32)
            ref[to, :] = (og_ref[at, :].astype(jnp.float32) * live_ref[at, :]).astype(low_type)

    strip = w_s.shape[1]
    per = w_hbm.shape[1] // strip

    def side(i):
        return i // per, pl.ds(pl.multiple_of((i % per) * strip, strip), strip)

    def cast(i):
        low_s[i % 2] = w_s[i % 2].astype(low_type)

    flow(
        0,
        w_hbm.shape[0] * per,
        lambda i: [pltpu.make_async_copy(w_hbm.at[side(i)], w_s.at[i % 2], w_sem.at[i % 2])],
        cast,
        lambda i: [pltpu.make_async_copy(low_s.at[i % 2], low_hbm.at[side(i)], low_sem.at[i % 2])],
    )
    for c in small:
        c.wait_recv()
    for n in range(nd):
        full_ref[:, n * width : (n + 1) * width] = full_s[n]
    step = 32
    lane = lax.broadcasted_iota(jnp.int32, (256, PAIR), 1) % HEAD_DIM

    def turns(at):
        angles = pos_ref[at, :] * inv_ref[...]
        cos_part, sine_part = jnp.cos(angles), jnp.sin(angles)
        keep_ref[at, :] = jnp.where(lane < ROT, cos_part, 1.0)
        above_ref[at, :] = jnp.where(lane < ROT // 2, -sine_part, 0.0)
        below_ref[at, :] = jnp.where((lane >= ROT // 2) & (lane < ROT), sine_part, 0.0)

    def out(buf, row):
        return pltpu.make_async_copy(stage.at[buf], h_ref.at[pl.ds(row, half)], out_sem.at[buf])

    def body_step(i, carry):
        await_slot(i, copies)
        row = pl.multiple_of(arrival_slot(i) * half, half)
        buf = i % 2

        @pl.when(i >= 2)
        def _():
            out(buf, row).wait()

        @pl.loop(0, half // step)
        def _(r):
            at = pl.ds(pl.multiple_of(r * step, step), step)
            x = all_s[pl.ds(pl.multiple_of(row + r * step, step), step), :].astype(jnp.float32)
            c = x - jnp.mean(x, axis=-1, keepdims=True)
            s = lax.rsqrt(jnp.mean(c * c, axis=-1, keepdims=True) + norm_eps)
            stage[buf, at, :] = (c * s * full_ref[0:1, :] + full_ref[2:3, :]).astype(low_type)

        out(buf, row).start()

        @pl.when(i < 4)
        def _():
            turns(pl.ds(pl.multiple_of(i * 512, 256), 256))
            turns(pl.ds(pl.multiple_of(i * 512 + 256, 256), 256))

        return carry

    lax.fori_loop(0, 8, body_step, 0)
    for buf in (0, 1):
        out(buf, 0).wait()
    for c in copies:
        c.wait_send()
    for c in small:
        c.wait_send()


def gather_norm(x, small, pos, inverse, out_grad, live, w):
    nd = lax.axis_size("dp")
    rows, model = x.shape
    total = 4 * rows
    count, width = small.shape
    vmem = pl.BlockSpec(memory_space=pltpu.VMEM)
    table = jax.ShapeDtypeStruct((total, PAIR), jnp.float32)
    return pl.pallas_call(
        functools.partial(gather_norm_kernel, nd),
        in_specs=[ANY, vmem, vmem, vmem, vmem, vmem, ANY],
        out_specs=[ANY, vmem, vmem, vmem, vmem, vmem, vmem, ANY],
        out_shape=[
            jax.ShapeDtypeStruct((total, model), low_type),
            jax.ShapeDtypeStruct((count, width * nd), jnp.float32),
            table,
            table,
            table,
            jax.ShapeDtypeStruct((rows // 2, model), low_type),
            jax.ShapeDtypeStruct((rows // 2, model), low_type),
            jax.ShapeDtypeStruct(w.shape, low_type),
        ],
        scratch_shapes=[
            pltpu.VMEM((total, model), low_type),
            pltpu.VMEM((nd, count, width), jnp.float32),
            pltpu.VMEM((2, rows // 2, model), low_type),
            pltpu.VMEM((2, 64, w.shape[2]), jnp.float32),
            pltpu.VMEM((2, 64, w.shape[2]), low_type),
            pltpu.SemaphoreType.DMA((6,)),
            pltpu.SemaphoreType.DMA((6,)),
            pltpu.SemaphoreType.DMA,
            pltpu.SemaphoreType.DMA((nd,)),
            pltpu.SemaphoreType.DMA((nd,)),
            pltpu.SemaphoreType.DMA((2,)),
            pltpu.SemaphoreType.DMA((2,)),
            pltpu.SemaphoreType.DMA((2,)),
        ],
        cost_estimate=cost(20 * total * model, 4 * total * model),
        compiler_params=pltpu.CompilerParams(vmem_limit_bytes=40 * MIB, collective_id=3, has_side_effects=True),
        name="gather_norm",
    )(x, small, pos, inverse, out_grad, live, w)


def gather_do_kernel(d_ref, act_ref, h_hbm, dup_hbm, o_a_ref, o_b_ref, wo_ref, wd_hbm, do_ref, grad_ref, mlp_ref, up_ref,
                     all_s, wd_s, dup_s, acc, act_s, h_s, stage, up_s, send, recv, local, act_sem, h_sem, out_sem, up_sem):
    near_x, near_y = neighbours()
    half = d_ref.shape[0] // 2
    model = d_ref.shape[1]
    part = o_a_ref.shape[1]
    tile = 512
    own = pltpu.make_async_copy(d_ref, all_s.at[pl.ds(0, 2 * half)], local.at[0])
    own.start()
    weights = pltpu.make_async_copy(wd_hbm, wd_s, local.at[1])
    weights.start()
    cotangent = pltpu.make_async_copy(dup_hbm, dup_s, local.at[2])
    cotangent.start()
    greet(near_x, near_y)
    own.wait()
    copies = square_copies(all_s, half, send, recv)
    for c in copies[:4]:
        c.start()
    acc[...] = jnp.zeros_like(acc)
    weights.wait()
    cotangent.wait()
    strip = model // 8

    def loads(i):
        at = pl.ds(pl.multiple_of(i * half, half), half)
        cols = pl.ds(pl.multiple_of(i * strip, strip), strip)
        return [
            pltpu.make_async_copy(act_ref.at[at], act_s.at[i % 2], act_sem.at[i % 2]),
            pltpu.make_async_copy(h_hbm.at[:, cols], h_s.at[i % 2], h_sem.at[i % 2]),
        ]

    def outs(i):
        at = pl.ds(pl.multiple_of(i * half, half), half)
        side = pl.ds(pl.multiple_of(i * strip, strip), strip)
        return [
            pltpu.make_async_copy(stage.at[i % 2], mlp_ref.at[at], out_sem.at[i % 2]),
            pltpu.make_async_copy(up_s.at[i % 2], up_ref.at[side], up_sem.at[i % 2]),
        ]

    for c in loads(0):
        c.start()

    def beside(p):
        @pl.when(p < 7)
        def _():
            for c in loads(p + 1):
                c.start()

        for c in loads(p):
            c.wait()

        @pl.when(p >= 2)
        def _():
            for c in outs(p - 2):
                c.wait()

        stage[p % 2] = dot32(act_s[p % 2], wd_s[...]).astype(low_type)
        up_s[p % 2] = dot32(h_s[p % 2], dup_s[...], contract_first).astype(low_type)
        for c in outs(p):
            c.start()

    def step(i, carry):
        @pl.when(i < 6)
        def _():
            beside(jnp.where(i == 5, 6, i))

        @pl.when((i == 4) | (i == 5))
        def _():
            beside(2 * i - 3)

        await_slot(i, copies)
        at = pl.ds(pl.multiple_of(arrival_slot(i) * half, half), half)
        dattn = all_s[at, :]
        do_ref[at, :] = dot32(dattn, wo_ref[...], contract_last).astype(low_type)
        acc[:part, :] += dot32(o_a_ref[at, :], dattn, contract_first)
        acc[part:, :] += dot32(o_b_ref[at, :], dattn, contract_first)
        return carry

    lax.fori_loop(0, 8, step, 0)

    @pl.loop(0, model // tile)
    def _(n):
        cols = pl.ds(pl.multiple_of(n * tile, tile), tile)
        grad_ref[cols, :] = acc[:, cols].T.astype(low_type)

    for i in (6, 7):
        for c in outs(i):
            c.wait()
    for c in copies:
        c.wait_send()


def gather_do(dattn, act, h, dup, o_a, o_b, wo, wd):
    rows, model = dattn.shape
    total = 4 * rows
    depth = act.shape[1]
    width = wo.shape[0]
    vmem = pl.BlockSpec(memory_space=pltpu.VMEM)
    return pl.pallas_call(
        gather_do_kernel,
        in_specs=[ANY, ANY, ANY, ANY, vmem, vmem, vmem, ANY],
        out_specs=[vmem, vmem, ANY, ANY],
        out_shape=[
            jax.ShapeDtypeStruct((total, width), low_type),
            jax.ShapeDtypeStruct((model, width), low_type),
            jax.ShapeDtypeStruct((total, model), low_type),
            jax.ShapeDtypeStruct((model, depth), low_type),
        ],
        scratch_shapes=[
            pltpu.VMEM((total, model), low_type),
            pltpu.VMEM(wd.shape, low_type),
            pltpu.VMEM(dup.shape, low_type),
            pltpu.VMEM((width, model), jnp.float32),
            pltpu.VMEM((2, rows // 2, depth), low_type),
            pltpu.VMEM((2, total, model // 8), low_type),
            pltpu.VMEM((2, rows // 2, model), low_type),
            pltpu.VMEM((2, model // 8, depth), low_type),
            pltpu.SemaphoreType.DMA((6,)),
            pltpu.SemaphoreType.DMA((6,)),
            pltpu.SemaphoreType.DMA((3,)),
            pltpu.SemaphoreType.DMA((2,)),
            pltpu.SemaphoreType.DMA((2,)),
            pltpu.SemaphoreType.DMA((2,)),
            pltpu.SemaphoreType.DMA((2,)),
        ],
        cost_estimate=cost(2 * total * model * (depth + 2 * width), 6 * total * model),
        compiler_params=pltpu.CompilerParams(vmem_limit_bytes=56 * MIB, collective_id=4, has_side_effects=True),
        name="gather_do",
    )(dattn, act, h, dup, o_a, o_b, wo, wd)


def exchange(rows, partial, bufs, send, recv, fill_one, fill_two):
    far_s, for_x, for_y, top_s, end_s, from_x, from_y = bufs
    near_x, near_y = neighbours()
    half = rows // 2
    t, e = pl.ds(0, half), pl.ds(half, half)
    copies = [
        remote(0, far_s.at[t], top_s, near_x, send, recv),
        remote(1, far_s.at[e], end_s, near_y, send, recv),
        remote(2, for_x.at[t], from_x.at[t], near_x, send, recv),
        remote(3, for_y.at[e], from_y.at[e], near_y, send, recv),
    ]
    quarter = half // 2
    for n in range(2):
        at = pl.ds(half + n * quarter, quarter)
        copies.append(remote(4 + n, for_x.at[at], from_x.at[at], near_x, send, recv))
    for n in range(2):
        at = pl.ds(n * quarter, quarter)
        copies.append(remote(6 + n, for_y.at[at], from_y.at[at], near_y, send, recv))

    def into(ref, which):
        def store(cols, value):
            ref[pl.ds(which * half, half), cols] = value.astype(low_type)

        return store

    def added(ref, which, other):
        def store(cols, value):
            ref[pl.ds(which * half, half), cols] = (value + other[:, cols].astype(jnp.float32)).astype(low_type)

        return store

    partial(3, 0, into(far_s, 0))
    copies[0].start()
    partial(3, 1, into(far_s, 1))
    copies[1].start()
    partial(1, 0, into(for_x, 0))
    copies[2].start()
    partial(2, 1, into(for_y, 1))
    copies[3].start()
    fill_one()
    copies[0].wait_recv()
    partial(2, 0, added(for_y, 0, top_s))
    copies[6].start()
    copies[7].start()
    copies[1].wait_recv()
    partial(1, 1, added(for_x, 1, end_s))
    copies[4].start()
    copies[5].start()
    fill_two()
    return copies


def finish_quarters(copies, finish, sent=0):
    copies[2].wait_recv()
    copies[6].wait_recv()
    finish(0)
    copies[3].wait_recv()
    copies[4].wait_recv()
    finish(2)
    copies[7].wait_recv()
    finish(1)
    copies[5].wait_recv()
    finish(3)
    for c in copies[sent:]:
        c.wait_send()


def finish_back(copies, rows, gain_row, v_ref, base_ref, own_ref, live_ref, norm_ref, from_x, from_y, dx_ref, low_ref, gain_ref, shift_ref, gain_s, shift_s, sent=0):
    quarter = rows // 4
    step = 16
    gain_s[...] = jnp.zeros_like(gain_s)
    shift_s[...] = jnp.zeros_like(shift_s)

    def finish(which):
        @pl.loop(0, quarter // step)
        def _(r):
            at = pl.ds(pl.multiple_of(which * quarter + r * step, step), step)
            e = own_ref[at, :].astype(jnp.float32) + from_x[at, :].astype(jnp.float32) + from_y[at, :].astype(jnp.float32)
            v = v_ref[at, :].astype(jnp.float32)
            c = v - jnp.mean(v, axis=-1, keepdims=True)
            s = lax.rsqrt(jnp.mean(c * c, axis=-1, keepdims=True) + norm_eps)
            xh = c * s
            w = e * norm_ref[gain_row : gain_row + 1, :]
            back = s * (w - jnp.mean(w, axis=-1, keepdims=True) - xh * jnp.mean(w * xh, axis=-1, keepdims=True))
            dx = base_ref[at, :].astype(jnp.float32) + back
            dx_ref[at, :] = dx.astype(dx_ref.dtype)
            if low_ref is not None:
                low_ref[at, :] = (dx * live_ref[at, :]).astype(low_type)
            ex = e * xh
            gain_s[...] += ex[:8] + ex[8:]
            shift_s[...] += e[:8] + e[8:]

    finish_quarters(copies, finish, sent)
    gain_ref[...] = jnp.sum(gain_s[...], axis=0, keepdims=True)
    shift_ref[...] = jnp.sum(shift_s[...], axis=0, keepdims=True)


def exchange_scratch(rows, model):
    big = pltpu.VMEM((rows, model), low_type)
    small = pltpu.VMEM((rows // 2, model), low_type)
    line = pltpu.VMEM((8, model), jnp.float32)
    sems = pltpu.SemaphoreType.DMA((8,))
    return [big, big, big, small, small, big, big, line, line, sems, sems]


def out_scatter_kernel(a_ref, b_ref, w_ref, x_ref, live_ref, norm_ref, x1_ref, h_ref, *scratch):
    bufs, (send, recv) = scratch[:7], scratch[9:]
    near_x, near_y = neighbours()
    rows, model = x_ref.shape
    half = rows // 2
    part = a_ref.shape[1]
    tile = 512
    greet(near_x, near_y)

    def partial(slot, which, store):
        at = pl.ds(slot * rows + which * half, half)

        @pl.loop(0, model // tile)
        def _(n):
            cols = pl.ds(pl.multiple_of(n * tile, tile), tile)
            store(cols, dot32(a_ref[at, :], w_ref[:part, cols]) + dot32(b_ref[at, :], w_ref[part:, cols]))

    def own(which):
        def store(cols, value):
            x1_ref[pl.ds(which * half, half), cols] = value

        return store

    def fill_one():
        partial(0, 0, own(0))
        partial(0, 1, own(1))

    copies = exchange(rows, partial, bufs, send, recv, fill_one, lambda: None)
    from_x, from_y = bufs[5:]
    quarter = rows // 4
    step = 32

    def finish(which):
        @pl.loop(0, quarter // step)
        def _(r):
            at = pl.ds(pl.multiple_of(which * quarter + r * step, step), step)
            attn = x1_ref[at, :] + from_x[at, :].astype(jnp.float32) + from_y[at, :].astype(jnp.float32)
            x1 = x_ref[at, :].astype(jnp.float32) + live_ref[at, :] * attn
            x1_ref[at, :] = x1
            c = x1 - jnp.mean(x1, axis=-1, keepdims=True)
            s = lax.rsqrt(jnp.mean(c * c, axis=-1, keepdims=True) + norm_eps)
            h_ref[at, :] = (c * s * norm_ref[1:2, :] + norm_ref[3:4, :]).astype(low_type)

    finish_quarters(copies, finish)


def out_scatter(a, b, w, x, live, norm):
    rows, model = x.shape
    vmem = pl.BlockSpec(memory_space=pltpu.VMEM)
    total = a.shape[0]
    return pl.pallas_call(
        out_scatter_kernel,
        in_specs=[vmem] * 6,
        out_specs=[vmem] * 2,
        out_shape=[jax.ShapeDtypeStruct((rows, model), jnp.float32), jax.ShapeDtypeStruct((rows, model), low_type)],
        scratch_shapes=exchange_scratch(rows, model),
        cost_estimate=cost(2 * total * model * w.shape[0], 20 * rows * model),
        compiler_params=pltpu.CompilerParams(vmem_limit_bytes=48 * MIB, collective_id=0, has_side_effects=True),
        name="out_scatter",
    )(a, b, w, x, live, norm)


sending = (6, 7, 2, 5, 0, 1, 4, 3)


def sending_slot(j):
    slot = jnp.int32(sending[-1])
    for n in range(7):
        slot = jnp.where(j == n, sending[n], slot)
    return slot


def hidden_scatter_kernel(count, *refs):
    dm_refs, refs = refs[:count], refs[count:]
    one_hbm, two_hbm, wd_hbm, w_hbm, h_hbm, x1_hbm, og_hbm, live_ref, norm_ref = refs[:9]
    grad_ref, dup_ref, dx_ref, low_ref, gain_ref, shift_ref = refs[9:15]
    scratch = refs[15:]
    bufs, (gain_s, shift_s, send, recv) = scratch[:7], scratch[7:11]
    g_s, w_s, wd_s, dm_s, slope_s, h_s, stage, local, dm_sem, slope_sem, h_sem, out_sem = scratch[11:]
    rows, model = dx_ref.shape
    half = rows // 2
    near_x, near_y = neighbours()
    down_load = pltpu.make_async_copy(wd_hbm, wd_s, local.at[0])
    weight_load = pltpu.make_async_copy(w_hbm, w_s, local.at[1])
    x1_load = pltpu.make_async_copy(x1_hbm, dx_ref, local.at[2])
    og_load = pltpu.make_async_copy(og_hbm, bufs[0], local.at[3])
    dup_store = pltpu.make_async_copy(g_s.at[1], dup_ref, local.at[4])

    def slope_loads(j):
        at = pl.ds(pl.multiple_of(sending_slot(j) * half, half), half)
        return [
            pltpu.make_async_copy(ref.at[at], slope_s.at[j % 2, n], slope_sem.at[j % 2, n])
            for n, ref in enumerate((one_hbm, two_hbm))
        ]

    def dm_load(n):
        return pltpu.make_async_copy(dm_refs[sending[n]], dm_s.at[n % 2], dm_sem.at[n % 2])

    down_load.start()
    dm_load(0).start()
    for c in slope_loads(0):
        c.start()
    weight_load.start()
    x1_load.start()
    greet(near_x, near_y)
    down_load.wait()

    def back_step(j, carry):
        @pl.when(j < 7)
        def _():
            for c in slope_loads(j + 1):
                c.start()

        for n in range(1, 8):

            @pl.when(j == n - 1)
            def _(n=n):
                dm_load(n).start()

        b = j % 2
        pltpu.make_async_copy(dm_refs[0], dm_s.at[b], dm_sem.at[b]).wait()
        for c in slope_loads(j):
            c.wait()
        at = pl.ds(pl.multiple_of(sending_slot(j) * half, half), half)
        da = dot32(dm_s[b], wd_s[...], contract_last)
        g_s[0, at, :] = (da * slope_s[b, 0].astype(jnp.float32)).astype(low_type)
        g_s[1, at, :] = (da * slope_s[b, 1].astype(jnp.float32)).astype(low_type)
        return carry

    def back(first, last):
        lax.fori_loop(first, last, back_step, 0)

    tile = 512

    def partial(slot, which, store):
        if slot == 3 and which == 0:
            back(0, 2)
            weight_load.wait()
        if slot == 1 and which == 0:
            back(2, 4)
        at = pl.ds(slot * rows + which * half, half)

        @pl.loop(0, model // tile)
        def _(n):
            cols = pl.ds(pl.multiple_of(n * tile, tile), tile)
            value = dot32(g_s[0, at, :], w_s[0, cols, :], contract_last)
            store(cols, value + dot32(g_s[1, at, :], w_s[1, cols, :], contract_last))

    def own(which):
        def store(cols, value):
            low_ref[pl.ds(which * half, half), cols] = value.astype(low_type)

        return store

    strip = 256

    def load(i):
        return pltpu.make_async_copy(h_hbm.at[:, pl.ds(pl.multiple_of(i * strip, strip), strip)], h_s.at[i % 2], h_sem.at[i % 2])

    def out(i):
        at = pl.ds(pl.multiple_of(i * strip, strip), strip)
        return pltpu.make_async_copy(stage.at[i % 2], grad_ref.at[at], out_sem.at[i % 2])

    strips = model // strip

    def strip_step(i, carry):
        @pl.when(i < strips - 1)
        def _():
            load(i + 1).start()

        load(i).wait()

        @pl.when(i >= 2)
        def _():
            out(i - 2).wait()

        stage[i % 2] = dot32(h_s[i % 2], g_s[0], contract_first).astype(low_type)
        out(i).start()
        return carry

    def fill_one():
        back(4, 8)
        dup_store.start()
        load(0).start()
        partial(0, 0, own(0))

    def fill_two():
        partial(0, 1, own(1))
        lax.fori_loop(0, strips, strip_step, 0)

    copies = exchange(rows, partial, bufs, send, recv, fill_one, fill_two)
    copies[0].wait_send()
    copies[1].wait_send()
    og_load.start()
    x1_load.wait()
    og_load.wait()
    finish_back(copies, rows, 1, dx_ref, bufs[0], low_ref, live_ref, norm_ref, bufs[5], bufs[6], dx_ref, low_ref, gain_ref, shift_ref, gain_s, shift_s, 2)
    out(strips - 2).wait()
    out(strips - 1).wait()
    dup_store.wait()


def hidden_scatter(dm_blocks, one, two, wd, w, h, x1, out_grad, live, norm):
    rows, model = x1.shape
    total, depth = one.shape
    half = rows // 2
    vmem = pl.BlockSpec(memory_space=pltpu.VMEM)
    line = jax.ShapeDtypeStruct((1, model), jnp.float32)
    return pl.pallas_call(
        functools.partial(hidden_scatter_kernel, len(dm_blocks)),
        in_specs=[ANY] * (len(dm_blocks) + 7) + [vmem, vmem],
        out_specs=[ANY, ANY, vmem, vmem, vmem, vmem],
        out_shape=[
            jax.ShapeDtypeStruct((model, depth), low_type),
            jax.ShapeDtypeStruct((total, depth), low_type),
            jax.ShapeDtypeStruct((rows, model), jnp.float32),
            jax.ShapeDtypeStruct((rows, model), low_type),
            line,
            line,
        ],
        scratch_shapes=exchange_scratch(rows, model)
        + [
            pltpu.VMEM((2, total, depth), low_type),
            pltpu.VMEM(w.shape, low_type),
            pltpu.VMEM(wd.shape, low_type),
            pltpu.VMEM((2, half, model), low_type),
            pltpu.VMEM((2, 2, half, depth), low_type),
            pltpu.VMEM((2, total, 256), low_type),
            pltpu.VMEM((2, 256, depth), low_type),
            pltpu.SemaphoreType.DMA((5,)),
            pltpu.SemaphoreType.DMA((2,)),
            pltpu.SemaphoreType.DMA((2, 2)),
            pltpu.SemaphoreType.DMA((2,)),
            pltpu.SemaphoreType.DMA((2,)),
        ],
        cost_estimate=cost(8 * total * model * depth, 16 * total * model),
        compiler_params=pltpu.CompilerParams(vmem_limit_bytes=62 * MIB, collective_id=5, has_side_effects=True),
        name="hidden_scatter",
    )(*dm_blocks, one, two, wd, w, h, x1, out_grad, live, norm)


def first_scatter_kernel(count, *refs):
    lefts_hbm = refs[:count]
    w_hbm, x_ref, base_ref, norm_ref, live_ref = refs[count : count + 5]
    refs = refs[count + 5 :]
    x1_hbm, mlp_hbm = refs[0], refs[1:4]
    dx_ref, gain_ref, shift_ref, layer_hbm = refs[4:8]
    scratch = refs[8:]
    bufs, (gain_s, shift_s, send, recv, own_s, left_s, w_s) = scratch[:7], scratch[7:14]
    x1_s, mlp_s, layer_s, left_sem, in_sem, layer_sem = scratch[14:]
    rows, model = x_ref.shape
    half = rows // 2
    tile = 512
    near_x, near_y = neighbours()
    far = pl.ds(3 * rows, rows)
    rest = pl.ds(0, 3 * rows)
    early = [pltpu.make_async_copy(left.at[far], left_s.at[n, far], left_sem.at[n]) for n, left in enumerate(lefts_hbm)]
    early.append(pltpu.make_async_copy(w_hbm, w_s, left_sem.at[2 * count]))
    late = [
        pltpu.make_async_copy(left.at[rest], left_s.at[n, rest], left_sem.at[count + n]) for n, left in enumerate(lefts_hbm)
    ]
    for c in early + late:
        c.start()
    greet(near_x, near_y)
    for c in early:
        c.wait()

    def partial(slot, which, store):
        if slot == 1 and which == 0:
            for c in late:
                c.wait()
        at = pl.ds(slot * rows + which * half, half)

        @pl.loop(0, model // tile)
        def _(n):
            cols = pl.ds(pl.multiple_of(n * tile, tile), tile)
            value = None
            for m in range(count):
                depth = left_s.shape[2]
                per = w_s.shape[2] // depth
                side = slice((m % per) * depth, (m % per + 1) * depth)
                term = dot32(left_s[m, at, :], w_s[m // per, cols, side], contract_last)
                value = term if value is None else value + term
            store(cols, value)

    def own(which):
        def store(cols, value):
            own_s[pl.ds(which * half, half), cols] = value

        return store

    def layer_moves():
        deep = x1_s.shape[1]
        at = lambda i: pl.ds(pl.multiple_of(i * deep, deep), deep)

        def loads(i):
            return [pltpu.make_async_copy(x1_hbm.at[at(i)], x1_s.at[i % 2], in_sem.at[i % 2, 0])] + [
                pltpu.make_async_copy(ref.at[at(i)], mlp_s.at[i % 2, n], in_sem.at[i % 2, 1 + n])
                for n, ref in enumerate(mlp_hbm)
            ]

        def stores(i):
            return [pltpu.make_async_copy(layer_s.at[i % 2], layer_hbm.at[at(i)], layer_sem.at[i % 2])]

        def work(i):
            b = i % 2
            total = mlp_s[b, 0].astype(jnp.float32) + mlp_s[b, 1].astype(jnp.float32) + mlp_s[b, 2].astype(jnp.float32)
            layer_s[b] = (x1_s[b] + live_ref[at(i), :] * total).astype(low_type)

        flow(0, rows // deep, loads, work, stores)

    def fill_one():
        partial(0, 0, own(0))
        partial(0, 1, own(1))

    def fill_two():
        layer_moves()

    copies = exchange(rows, partial, bufs, send, recv, fill_one, fill_two)
    finish_back(copies, rows, 0, x_ref, base_ref, own_s, None, norm_ref, bufs[5], bufs[6], dx_ref, None, gain_ref, shift_ref, gain_s, shift_s)


def first_scatter(lefts, w, x, base, norm, live, x1, mlp_parts):
    rows, model = x.shape
    count = len(lefts)
    total, part = lefts[0].shape
    vmem = pl.BlockSpec(memory_space=pltpu.VMEM)
    line = jax.ShapeDtypeStruct((1, model), jnp.float32)
    deep = 64
    both = lambda block, n, t: pltpu.VMEM((2,) + ((n,) if n else ()) + block, t)
    return pl.pallas_call(
        functools.partial(first_scatter_kernel, count),
        in_specs=[ANY] * (count + 1) + [vmem] * 4 + [ANY] * 4,
        out_specs=[vmem] * 3 + [ANY],
        out_shape=[jax.ShapeDtypeStruct((rows, model), low_type), line, line, jax.ShapeDtypeStruct((rows, model), low_type)],
        scratch_shapes=exchange_scratch(rows, model)
        + [
            pltpu.VMEM((rows, model), jnp.float32),
            pltpu.VMEM((count, total, part), low_type),
            pltpu.VMEM(w.shape, low_type),
            both((deep, model), 0, jnp.float32),
            both((deep, model), 3, low_type),
            both((deep, model), 0, low_type),
            pltpu.SemaphoreType.DMA((2 * count + 1,)),
            pltpu.SemaphoreType.DMA((2, 4)),
            pltpu.SemaphoreType.DMA((2,)),
        ],
        cost_estimate=cost(10**13, 30 * rows * model),
        compiler_params=pltpu.CompilerParams(vmem_limit_bytes=60 * MIB, collective_id=6, has_side_effects=True),
        name="first_scatter",
    )(*lefts, w, x, base, norm, live, x1, *mlp_parts)


def adam_rest_kernel(low_ref, *refs):
    part = pl.program_id(0)
    last = pl.num_programs(0) - 1
    qkv_in, out_in, qkv_out, out_out = refs[:3], refs[3:6], refs[6:10], refs[10:]

    @pl.when(part < last)
    def _():
        gradient = low_ref[...].astype(jnp.float32)
        qkv_out[0][...] = gradient
        results = adamw_update(qkv_in[0][...], gradient, qkv_in[1][...], qkv_in[2][...], weight_decay)
        for ref, value in zip(qkv_out[1:], results):
            ref[...] = value

    @pl.when(part == last)
    def _():
        gradient = low_ref[0].astype(jnp.float32).T
        out_out[0][...] = gradient
        results = adamw_update(out_in[0][...], gradient, out_in[1][...], out_in[2][...], weight_decay)
        for ref, value in zip(out_out[1:], results):
            ref[...] = value


def adam_rest(low, qkv, out):
    count, depth, width = low.shape
    stack = lambda k: (jnp.minimum(k, count - 2), 0, 0)
    three = pl.BlockSpec((1, depth, width), stack)
    flat = pl.BlockSpec(out[0].shape, lambda k: (0, 0))
    like = lambda value: jax.ShapeDtypeStruct(value.shape, jnp.float32)
    return pl.pallas_call(
        adam_rest_kernel,
        grid=(count,),
        in_specs=[pl.BlockSpec((1, depth, width), lambda k: (k, 0, 0))] + [three] * 3 + [flat] * 3,
        out_specs=[three] * 4 + [flat] * 4,
        out_shape=[like(qkv[0])] * 4 + [like(out[0])] * 4,
        cost_estimate=cost(30 * count * depth * width, 30 * count * depth * width),
        compiler_params=params(32),
        name="adam_rest",
    )(low, *qkv, *out)


def gather_gate_up_kernel(count, h_ref, w_hbm, *rest):
    blocks, (all_ref, act_ref, one_ref, two_ref, grad_ref) = rest[:count], rest[count : count + 5]
    w_s, all_s, stage, acc, turned, dm_s, send, recv, local, h_sem, out_sem, dm_sem = rest[count + 5 :]
    near_x, near_y = neighbours()
    half = h_ref.shape[0] // 2
    own = pltpu.make_async_copy(h_ref, all_s.at[pl.ds(0, 2 * half)], local.at[0])
    own.start()
    weights = pltpu.make_async_copy(w_hbm, w_s, local.at[1])
    weights.start()
    greet(near_x, near_y)
    own.wait()
    copies = square_copies(all_s, half, send, recv)
    for c in copies[:4]:
        c.start()
    acc[...] = jnp.zeros_like(acc)
    weights.wait()
    in_order = [blocks[n] for n in arrival]
    tile = 512

    def outs(buf, row):
        return [
            pltpu.make_async_copy(stage.at[buf, n], ref.at[pl.ds(row, half)], out_sem.at[buf, n])
            for n, ref in enumerate((act_ref, one_ref, two_ref))
        ]

    def keep(i, row):
        return pltpu.make_async_copy(all_s.at[pl.ds(row, half)], all_ref.at[pl.ds(row, half)], h_sem.at[i])

    def step(i, carry):
        await_slot(i, copies)
        row = pl.multiple_of(arrival_slot(i) * half, half)
        buf = i % 2
        keep(i, row).start()

        @pl.when(i >= 2)
        def _():
            for c in outs(buf, row):
                c.wait()

        h = all_s[pl.ds(row, half), :]
        gate = dot32(h, w_s[0])
        up = dot32(h, w_s[1])
        sig = 1.0 / (1.0 + jnp.exp(-gate))
        silu = gate * sig
        act = (silu * up).astype(low_type)
        stage[buf, 0] = act
        stage[buf, 1] = (up * sig * (1.0 + gate * (1.0 - sig))).astype(low_type)
        stage[buf, 2] = silu.astype(low_type)
        for c in outs(buf, row):
            c.start()
        turned[...] = act.T
        fetch_next(i, in_order, dm_s, dm_sem)

        @pl.loop(0, acc.shape[1] // tile)
        def _(n):
            cols = pl.ds(pl.multiple_of(n * tile, tile), tile)
            acc[:, cols] += dot32(turned[...], dm_s[buf, :, cols])

        return carry

    lax.fori_loop(0, 8, step, 0)
    for buf in (0, 1):
        for c in outs(buf, 0):
            c.wait()
    for i in range(8):
        keep(i, 0).wait()
    for c in copies:
        c.wait_send()
    depth = acc.shape[0]
    strip = depth // 8

    @pl.loop(0, 8)
    def _(n):
        at = pl.ds(pl.multiple_of(n * strip, strip), strip)
        all_s[at, :] = acc[at, :].astype(low_type)

    last = pltpu.make_async_copy(all_s.at[pl.ds(0, depth)], grad_ref, local.at[0])
    last.start()
    last.wait()


def gather_gate_up(h, w, dm_blocks):
    rows, model = h.shape
    depth = w.shape[2]
    total = 4 * rows
    half = rows // 2
    deep = jax.ShapeDtypeStruct((total, depth), low_type)
    return pl.pallas_call(
        functools.partial(gather_gate_up_kernel, len(dm_blocks)),
        in_specs=[ANY] * (2 + len(dm_blocks)),
        out_specs=[ANY] * 5,
        out_shape=[
            jax.ShapeDtypeStruct((total, model), low_type),
            deep,
            deep,
            deep,
            jax.ShapeDtypeStruct((depth, model), low_type),
        ],
        scratch_shapes=[
            pltpu.VMEM(w.shape, low_type),
            pltpu.VMEM((total, model), low_type),
            pltpu.VMEM((2, 3, half, depth), low_type),
            pltpu.VMEM((depth, model), jnp.float32),
            pltpu.VMEM((depth, half), low_type),
            pltpu.VMEM((2, half, model), low_type),
            pltpu.SemaphoreType.DMA((6,)),
            pltpu.SemaphoreType.DMA((6,)),
            pltpu.SemaphoreType.DMA((2,)),
            pltpu.SemaphoreType.DMA((8,)),
            pltpu.SemaphoreType.DMA((2, 3)),
            pltpu.SemaphoreType.DMA((2,)),
        ],
        cost_estimate=cost(6 * total * model * depth, 4 * model * depth + 4 * total * model + 6 * total * depth),
        compiler_params=pltpu.CompilerParams(vmem_limit_bytes=60 * MIB, collective_id=1, has_side_effects=True),
        name="gather_gate_up",
    )(h, w, *dm_blocks)


def small_kernel(nd, nt, x_ref, o_ref, groups, partial, shares, send, recv, send_t, recv_t):
    d, t = lax.axis_index("dp"), lax.axis_index("tensor")
    width = o_ref.shape[1]
    barrier = pltpu.get_barrier_semaphore()
    for k in range(1, nd):
        pl.semaphore_signal(barrier, inc=1, device_id={"dp": lax.rem(d + k, nd)}, device_id_type=MESH)
    for k in range(1, nt):
        pl.semaphore_signal(barrier, inc=1, device_id={"tensor": lax.rem(t + k, nt)}, device_id_type=MESH)
    pl.semaphore_wait(barrier, nd + nt - 2)
    copies = []
    for k in range(1, nd):
        peer = lax.rem(d + k, nd)
        c = pltpu.make_async_remote_copy(
            src_ref=x_ref.at[:, pl.ds(pl.multiple_of(peer * width, width), width)],
            dst_ref=groups.at[k],
            send_sem=send.at[k],
            recv_sem=recv.at[k],
            device_id={"dp": peer},
            device_id_type=MESH,
        )
        c.start()
        copies.append(c)
    total = x_ref[:, pl.ds(pl.multiple_of(d * width, width), width)]
    for k in range(1, nd):
        copies[k - 1].wait_recv()
        total += groups[k]
    partial[...] = total
    shares[t] = total
    for k in range(1, nt):
        c = pltpu.make_async_remote_copy(
            src_ref=partial,
            dst_ref=shares.at[t],
            send_sem=send_t.at[k],
            recv_sem=recv_t.at[k],
            device_id={"tensor": lax.rem(t + k, nt)},
            device_id_type=MESH,
        )
        c.start()
        copies.append(c)
    for k in range(1, nt):
        copies[nd - 2 + k].wait_recv()
    total = shares[0]
    for k in range(1, nt):
        total += shares[k]
    o_ref[...] = total
    for c in copies:
        c.wait_send()


def sum_small(x):
    nd, nt = lax.axis_size("dp"), lax.axis_size("tensor")
    rows, model = x.shape
    width = model // nd
    vmem = pl.BlockSpec(memory_space=pltpu.VMEM)
    return pl.pallas_call(
        functools.partial(small_kernel, nd, nt),
        in_specs=[vmem],
        out_specs=vmem,
        out_shape=jax.ShapeDtypeStruct((rows, width), jnp.float32),
        scratch_shapes=[
            pltpu.VMEM((nd, rows, width), jnp.float32),
            pltpu.VMEM((rows, width), jnp.float32),
            pltpu.VMEM((nt, rows, width), jnp.float32),
            pltpu.SemaphoreType.DMA((nd,)),
            pltpu.SemaphoreType.DMA((nd,)),
            pltpu.SemaphoreType.DMA((nt,)),
            pltpu.SemaphoreType.DMA((nt,)),
        ],
        cost_estimate=cost(rows * model, 8 * rows * model),
        compiler_params=pltpu.CompilerParams(collective_id=2, has_side_effects=True),
        name="sum_small",
    )(x)


def body(
    tokens,
    out_grad,
    lengths,
    norm_gain,
    norm_bias,
    qkv_weight,
    qkv_bias,
    out_weight,
    gate_up_weight,
    down_weight,
    first_norm_gain,
    first_norm_bias,
    first_qkv_weight,
    first_qkv_bias,
    first_out_weight,
    first_gate_up_weight,
    first_down_weight,
    second_norm_gain,
    second_norm_bias,
    second_qkv_weight,
    second_qkv_bias,
    second_out_weight,
    second_gate_up_weight,
    second_down_weight,
):
    slots = lax.axis_size("tensor")
    rank = lax.axis_index("tensor")
    own_rows = tokens.shape[0]
    group_rows = own_rows * slots
    width = out_weight.shape[0]
    order = rank if square(slots) else jnp.zeros_like(rank)

    chunk = jnp.bitwise_xor(jnp.arange(slots, dtype=jnp.int32), order)
    row_index = (chunk[:, None] * own_rows + jnp.arange(own_rows, dtype=jnp.int32)[None, :]).reshape(-1)
    seq_start, _ = layout(lengths[0], row_index)
    position = row_index - seq_start
    own_index = rank * own_rows + jnp.arange(own_rows, dtype=jnp.int32)
    live = layout(lengths[0], own_index)[1][:, None]
    block_start, _ = layout(lengths[0], jnp.arange(group_rows // BLOCK, dtype=jnp.int32) * BLOCK)
    table = jnp.concatenate([order.reshape(1).astype(jnp.int32), block_start // BLOCK])
    starts = seq_start[None, :]
    small_low = jnp.concatenate([norm_gain, norm_bias, qkv_bias, qkv_bias[:1]], axis=0).astype(low_type)
    own_bias = lambda full: lax.dynamic_slice_in_dim(full[4:7], rank * width, width, 1)[:, None, :]

    if square(slots):
        qkv_full = lax.all_gather(qkv_weight.astype(low_type), "dp", axis=1, tiled=True)
        lane = jnp.arange(PAIR, dtype=jnp.int32) % (ROT // 2)
        inverse = jnp.power(rope_base, -lane.astype(jnp.float32) * (2.0 / ROT))[None, :]
        position = position.astype(jnp.float32)[:, None]
        h1, small_full, *tables, dm_top, dm_end, gate_up_low = gather_norm(
            tokens, small_low.astype(jnp.float32), position, inverse, out_grad, live, gate_up_weight
        )
        norm = small_full[:4]
        out_low = after(out_weight.astype(low_type), qkv_full, h1)
        out_full = lax.all_gather(out_low, "dp", axis=1, tiled=True)
        dm_first, dm_rest = gather_rows(dm_top, dm_end)
        q, k, v, kt, vt = qkv_all(h1, qkv_full, own_bias(small_full), tables)

        o_a, lse_a = attn_fwd(0, slots, table, q, k, vt, starts)
        gate_up_low = after(gate_up_low, out_full, o_a)
        gate_up_full = lax.all_gather(gate_up_low, "dp", axis=1, tiled=True)
        dm_far = dm_rest(o_a)
        o_b, lse_b = attn_fwd(1, slots, table, after(q, o_a, *dm_first), k, vt, starts)
        o_b = after(o_b, *dm_far)
        dm_blocks = dm_first + dm_far

        x1, h2_own = out_scatter(o_a, o_b, out_full, tokens, live, norm)
        down_low = after(down_weight.astype(low_type), gate_up_full, h2_own)
        down_full = lax.all_gather(down_low, "dp", axis=1, tiled=True)
        h2, act, slope_gate, slope_up, grad_down = gather_gate_up(h2_own, gate_up_full, dm_blocks)
        grad_down_own = lax.psum_scatter(after(grad_down, down_full), "dp", scatter_dimension=1, tiled=True)

        grad_gate, dup, dx1, dattn_own, gain_two, shift_two = hidden_scatter(
            dm_blocks, slope_gate, slope_up, down_full, gate_up_full, h2, x1, out_grad, live, norm
        )
        grad_gate = after(grad_gate, grad_down_own)
        grad_gate_own = lax.psum_scatter(grad_gate, "dp", scatter_dimension=0, tiled=True)

        do, grad_out, mlp, grad_up = gather_do(dattn_own, act, h2, dup, o_a, o_b, out_full, down_full)
        grad_up = after(grad_up, grad_gate_own)
        grad_up_own = lax.psum_scatter(grad_up, "dp", scatter_dimension=0, tiled=True)
        mlp = [mlp[j * own_rows : (j + 1) * own_rows] for j in range(slots)]
        mlp_first = scatter_first(mlp)
        *back_a, grad_down_full, down_one, down_two, down_three = attn_bwd(
            0, slots, table, q, do, o_a, k, v, kt, starts, lse_a, tables,
            grad_down_own, (down_weight, first_down_weight, second_down_weight),
        )
        down_step = (grad_down_full, down_one, down_two, down_three)
        hidden = (gate_up_weight, first_gate_up_weight, second_gate_up_weight)
        mlp_parts = scatter_last(mlp, [after(part, back_a[0]) for part in mlp_first])
        results = attn_bwd(
            1, slots, table, q, after(do, back_a[0], *mlp_first), o_b, k, v, kt, starts, lse_b, tables, grad_gate_own, hidden
        )
        back_b, begun = results[:3], results[3:]
        dlin = [side for pair in zip(back_a, back_b) for side in pair]
        grad_rest, bias_local, *hidden_step = qkv_grad(h1, dlin, grad_out, grad_up_own, hidden, begun)
        late = [after(dlin[0], grad_rest, *mlp_parts)] + dlin[1:]
        input_grad, gain_one, shift_one, layer_out = first_scatter(
            late, qkv_full, tokens, dx1, norm, live, x1, mlp_parts
        )
        grad_rest = after(grad_rest, grad_up_own)
        grad_rest_own = lax.psum_scatter(grad_rest, "dp", scatter_dimension=1, tiled=True)
        rest_step = adam_rest(
            grad_rest_own,
            (qkv_weight, first_qkv_weight, second_qkv_weight),
            (out_weight, first_out_weight, second_out_weight),
        )
        qkv_step, out_step = rest_step[:4], rest_step[4:]
    else:
        everyone = lambda value: lax.all_gather(value, "tensor", axis=0, tiled=True)
        scatter = lambda value, axis, at: lax.psum_scatter(value.astype(low_type), axis, scatter_dimension=at, tiled=True)
        small_full = lax.all_gather(small_low, "dp", axis=1, tiled=True).astype(jnp.float32)
        qkv_full, out_full, gate_up_full, down_full = (
            lax.all_gather(w.astype(low_type), "dp", axis=1, tiled=True)
            for w in (qkv_weight, out_weight, gate_up_weight, down_weight)
        )
        gain_rows, shift_rows = small_full[0:2], small_full[2:4]
        rows_in, cotangent = tokens.astype(jnp.float32), out_grad.astype(jnp.float32)
        tables = rotary_tables(position)
        h1 = everyone(layer_norm(rows_in, gain_rows[0], shift_rows[0]).astype(low_type))
        q, k, v, kt, vt = qkv_all(h1, qkv_full, own_bias(small_full), tables)
        o_a, lse_a = attn_fwd(0, slots, table, q, k, vt, starts)
        o_b, lse_b = attn_fwd(1, slots, table, q, k, vt, starts)
        o = jnp.concatenate([o_a, o_b], axis=1)
        x1 = rows_in + live * scatter(dot32(o, out_full), "tensor", 0).astype(jnp.float32)
        h2 = everyone(layer_norm(x1, gain_rows[1], shift_rows[1]).astype(low_type))
        gate, up = dot32(h2, gate_up_full[0]), dot32(h2, gate_up_full[1])
        sig = 1.0 / (1.0 + jnp.exp(-gate))
        act = (gate * sig * up).astype(low_type)
        mlp_rows = scatter(dot32(act, down_full), "tensor", 0).astype(jnp.float32)
        layer_out = (x1 + live * mlp_rows).astype(low_type)
        dm = everyone((cotangent * live).astype(low_type))
        da = dot32(dm, down_full, contract_last)
        dgate = (da * up * sig * (1.0 + gate * (1.0 - sig))).astype(low_type)
        dup = (da * gate * sig).astype(low_type)
        grad_down_own = scatter(dot32(act, dm, contract_first), "dp", 1)
        grad_gate_up = jnp.stack([dot32(h2, dgate, contract_first), dot32(h2, dup, contract_first)])
        grad_gate_up_own = scatter(grad_gate_up, "dp", 1)
        dh2 = dot32(dgate, gate_up_full[0], contract_last) + dot32(dup, gate_up_full[1], contract_last)
        dh2 = scatter(dh2, "tensor", 0).astype(jnp.float32)
        back, gain_two, shift_two = jax.vjp(layer_norm, x1, gain_rows[1], shift_rows[1])[1](dh2)
        dx1 = cotangent + back
        dattn = everyone((dx1 * live).astype(low_type))
        do = dot32(dattn, out_full, contract_last).astype(low_type)
        grad_out = dot32(dattn, o, contract_first).astype(low_type)
        back_a = attn_bwd(0, slots, table, q, do, o_a, k, v, kt, starts, lse_a, tables)
        back_b = attn_bwd(1, slots, table, q, do, o_b, k, v, kt, starts, lse_b, tables)
        dlin = [side for pair in zip(back_a, back_b) for side in pair]
        grad_rest, bias_local = qkv_grad(h1, dlin, grad_out)
        grad_rest_own = scatter(grad_rest, "dp", 1)
        grad_qkv_own, grad_out_own = grad_rest_own[:3], grad_rest_own[3].T
        dh1 = sum(
            dot32(jnp.concatenate(dlin[2 * n : 2 * n + 2], axis=1), qkv_full[n], contract_last) for n in range(3)
        )
        dh1 = scatter(dh1, "tensor", 0).astype(jnp.float32)
        back, gain_one, shift_one = jax.vjp(layer_norm, rows_in, gain_rows[0], shift_rows[0])[1](dh1)
        input_grad = (dx1 + back).astype(low_type)
        gain_one, gain_two, shift_one, shift_two = (
            value[None, :] for value in (gain_one, gain_two, shift_one, shift_two)
        )

        def whole_step(gradient, *held):
            gradient = gradient.astype(jnp.float32)
            return (gradient,) + adamw_update(held[0], gradient, held[1], held[2], weight_decay)

        qkv_step = whole_step(grad_qkv_own, qkv_weight, first_qkv_weight, second_qkv_weight)
        out_step = whole_step(grad_out_own, out_weight, first_out_weight, second_out_weight)
        hidden_step = whole_step(grad_gate_up_own, gate_up_weight, first_gate_up_weight, second_gate_up_weight)
        down_step = whole_step(grad_down_own, down_weight, first_down_weight, second_down_weight)

    bias_placed = lax.dynamic_update_slice(
        jnp.zeros((3, small_full.shape[1]), jnp.float32), bias_local, (jnp.int32(0), rank * width)
    )
    small_local = jnp.concatenate([gain_one, gain_two, shift_one, shift_two, bias_placed, bias_placed[:1]], axis=0)
    small_own = sum_small(small_local)

    def small_step(gradient, *held):
        return (gradient,) + adamw_update(held[0], gradient, held[1], held[2], 0.0)

    gain_step = small_step(small_own[0:2], norm_gain, first_norm_gain, second_norm_gain)
    shift_step = small_step(small_own[2:4], norm_bias, first_norm_bias, second_norm_bias)
    bias_step = small_step(small_own[4:7], qkv_bias, first_qkv_bias, second_qkv_bias)
    steps = (gain_step, shift_step, qkv_step, bias_step, out_step, hidden_step, down_step)
    return (layer_out, input_grad) + tuple(step[n] for n in range(4) for step in steps)


def solution(mesh):
    return jax.shard_map(
        body,
        mesh=mesh,
        in_specs=(
            P(("dp", "tensor"), None),
            P(("dp", "tensor"), None),
            P("dp", None),
            P(None, "dp"),
            P(None, "dp"),
            P(None, "dp", "tensor"),
            P(None, "dp"),
            P("tensor", "dp"),
            P(None, "dp", "tensor"),
            P("tensor", "dp"),
            P(None, "dp"),
            P(None, "dp"),
            P(None, "dp", "tensor"),
            P(None, "dp"),
            P("tensor", "dp"),
            P(None, "dp", "tensor"),
            P("tensor", "dp"),
            P(None, "dp"),
            P(None, "dp"),
            P(None, "dp", "tensor"),
            P(None, "dp"),
            P("tensor", "dp"),
            P(None, "dp", "tensor"),
            P("tensor", "dp"),
        ),
        out_specs=(
            P(("dp", "tensor"), None),
            P(("dp", "tensor"), None),
            P(None, "dp"),
            P(None, "dp"),
            P(None, "dp", "tensor"),
            P(None, "dp"),
            P("tensor", "dp"),
            P(None, "dp", "tensor"),
            P("tensor", "dp"),
            P(None, "dp"),
            P(None, "dp"),
            P(None, "dp", "tensor"),
            P(None, "dp"),
            P("tensor", "dp"),
            P(None, "dp", "tensor"),
            P("tensor", "dp"),
            P(None, "dp"),
            P(None, "dp"),
            P(None, "dp", "tensor"),
            P(None, "dp"),
            P("tensor", "dp"),
            P(None, "dp", "tensor"),
            P("tensor", "dp"),
            P(None, "dp"),
            P(None, "dp"),
            P(None, "dp", "tensor"),
            P(None, "dp"),
            P("tensor", "dp"),
            P(None, "dp", "tensor"),
            P("tensor", "dp"),
        ),
        check_vma=False,
    )
```

```python
import functools

import jax
import jax.numpy as jnp
from jax import lax
from jax.experimental import pallas as pl
from jax.experimental.pallas import tpu as pltpu
from jax.sharding import PartitionSpec as P

HEAD_DIM = 64
ROT = 16
PAIR = 2 * HEAD_DIM
BLOCK = 256

norm_eps = 1e-05
rope_base = 10000.0
beta_one = 0.9
beta_two = 0.95
adam_eps = 1e-08
learn_rate = 0.01
weight_decay = 0.1
step_count = 10.0
masked_score = -1e30
contract_last = (((1,), (1,)), ((), ()))
contract_first = (((0,), (0,)), ((), ()))
low_type = jnp.bfloat16
MIB = 2**20


def layout(seq_lengths, row_index):
    slot = jnp.arange(seq_lengths.shape[0])
    seq_ends = jnp.sum(
        jnp.where(slot[:, None] <= slot[None, :], seq_lengths[:, None], 0), axis=0
    )
    passed = row_index[:, None] >= seq_ends[None, :]
    seq_start = jnp.sum(jnp.where(passed, seq_lengths[None, :], 0), axis=1)
    live_rows = (row_index < jnp.sum(seq_lengths)).astype(jnp.float32)
    return (seq_start, live_rows)


def rotary_tables(position):
    half_rot = ROT // 2
    lane = jnp.arange(PAIR, dtype=jnp.int32) % HEAD_DIM
    powers = (lane % half_rot).astype(jnp.float32) * (2.0 / ROT)
    inverse = jnp.power(rope_base, -powers)
    angles = position.astype(jnp.float32)[:, None] * inverse[None, :]
    cos_part, sine_part = jnp.cos(angles), jnp.sin(angles)
    lane = lane[None, :]
    keep = jnp.where(lane < ROT, cos_part, 1.0)
    above = jnp.where(lane < half_rot, -sine_part, 0.0)
    below = jnp.where((lane >= half_rot) & (lane < ROT), sine_part, 0.0)
    return (keep, above, below)


def dot32(a, b, dims=None):
    if dims is None:
        return jnp.dot(a, b, preferred_element_type=jnp.float32)
    return lax.dot_general(a, b, dims, preferred_element_type=jnp.float32)


def turn(values, keep, above, below):
    up = pltpu.roll(values, PAIR - ROT // 2, 1)
    down = pltpu.roll(values, ROT // 2, 1)
    return values * keep + up * above + down * below


def turn_back(values, keep, above, below):
    up = pltpu.roll(values, PAIR - ROT // 2, 1)
    down = pltpu.roll(values, ROT // 2, 1)
    return values * keep - up * above - down * below


def adamw_update(weight_now, gradient, moment_one, moment_two, decay_rate):
    moment_one = beta_one * moment_one + (1.0 - beta_one) * gradient
    moment_two = beta_two * moment_two + (1.0 - beta_two) * gradient * gradient
    scaled_one = moment_one / (1.0 - beta_one**step_count)
    scaled_two = moment_two / (1.0 - beta_two**step_count)
    change = scaled_one / (jnp.sqrt(scaled_two) + adam_eps) + decay_rate * weight_now
    return (-learn_rate * change, moment_one, moment_two)


def cost(flops, moved, exps=0):
    return pl.CostEstimate(flops=int(flops) // 16, bytes_accessed=int(moved) // 16, transcendentals=int(exps) // 16)


def params(limit):
    return pltpu.CompilerParams(vmem_limit_bytes=limit * MIB)


ANY = pl.BlockSpec(memory_space=pl.ANY)


def layer_norm(values, gain_row, shift_row):
    center = values - jnp.mean(values, axis=-1, keepdims=True)
    spread = jnp.mean(center * center, axis=-1, keepdims=True)
    return center * lax.rsqrt(spread + norm_eps) * gain_row + shift_row


def qkv_kernel(scale, h_ref, w_ref, bias_ref, keep_ref, above_ref, below_ref, q_ref, k_ref, v_ref, kt_ref, vt_ref):
    h = h_ref[...]
    keep, above, below = keep_ref[...], above_ref[...], below_ref[...]
    width = q_ref.shape[1]
    lin = dot32(h, w_ref[0]) + bias_ref[0]
    for c in range(0, width, PAIR):
        u = turn(lin[:, c : c + PAIR], keep, above, below)
        q_ref[:, c : c + PAIR] = (u.astype(low_type) * scale).astype(low_type)
    lin = dot32(h, w_ref[1]) + bias_ref[1]
    for c in range(0, width, PAIR):
        u = turn(lin[:, c : c + PAIR], keep, above, below)
        k_ref[:, c : c + PAIR] = u.astype(low_type)
        kt_ref[c : c + PAIR, :] = u.T.astype(low_type)
    lin = dot32(h, w_ref[2]) + bias_ref[2]
    v_ref[...] = lin.astype(low_type)
    vt_ref[...] = lin.T.astype(low_type)


def qkv_all(h, w, bias, tables):
    total, model = h.shape
    rows = 256
    width = w.shape[2]
    row = lambda n: pl.BlockSpec((rows, n), lambda i: (i, 0))
    col = pl.BlockSpec((width, rows), lambda i: (0, i))
    flat = jax.ShapeDtypeStruct((total, width), low_type)
    turned = jax.ShapeDtypeStruct((width, total), low_type)
    return pl.pallas_call(
        functools.partial(qkv_kernel, HEAD_DIM ** (-0.5)),
        grid=(total // rows,),
        in_specs=[
            row(model),
            pl.BlockSpec((3,) + w.shape[1:], lambda i: (0, 0, 0), pipeline_mode=pl.Buffered(1)),
            pl.BlockSpec(bias.shape, lambda i: (0, 0, 0)),
            row(PAIR),
            row(PAIR),
            row(PAIR),
        ],
        out_specs=[row(width), row(width), row(width), col, col],
        out_shape=[flat, flat, flat, turned, turned],
        cost_estimate=cost(6 * total * model * width, 6 * model * width + 10 * total * model),
        compiler_params=params(60),
        name="qkv",
    )(h, w, bias, *tables)


def place(block, rank, per):
    return jnp.bitwise_xor(block // per, rank) * per + block % per


def attn_fwd_kernel(per, table_ref, q_ref, k_ref, vt_ref, start_ref, o_ref, lse_ref, m_s, l_s, acc_s):
    i = pl.program_id(0)
    rank = table_ref[0]
    heads = q_ref.shape[1] // HEAD_DIM
    first = lax.broadcasted_iota(jnp.int32, (BLOCK, PAIR), 1) < HEAD_DIM
    queries = []
    for h in range(heads):
        pair = q_ref[:, (h // 2) * PAIR : (h // 2 + 1) * PAIR]
        keep = first if h % 2 == 0 else jnp.logical_not(first)
        queries.append(jnp.where(keep, pair, jnp.zeros_like(pair)))
    m_s[...] = jnp.full_like(m_s, -jnp.inf)
    l_s[...] = jnp.zeros_like(l_s)
    acc_s[...] = jnp.zeros_like(acc_s)
    start = start_ref[...]
    row = i * BLOCK + lax.broadcasted_iota(jnp.int32, (BLOCK, BLOCK), 1)

    def step(kb, carry):
        col = kb * BLOCK + lax.broadcasted_iota(jnp.int32, (BLOCK, BLOCK), 0)
        bias = jnp.where((col >= start) & (col <= row), 0.0, masked_score)
        at = pl.ds(pl.multiple_of(place(kb, rank, per) * BLOCK, BLOCK), BLOCK)
        scores = [
            dot32(k_ref[at, (h // 2) * PAIR : (h // 2 + 1) * PAIR], queries[h], contract_last) for h in range(heads)
        ]
        probs, alphas = [], []
        for h in range(heads):
            s = scores[h] + bias
            m_old = m_s[h : h + 1, :]
            m_new = jnp.maximum(m_old, jnp.max(s, axis=0, keepdims=True))
            alpha = jnp.exp(m_old - m_new)
            p = jnp.exp(s - m_new)
            l_s[h : h + 1, :] = l_s[h : h + 1, :] * alpha + jnp.sum(p, axis=0, keepdims=True)
            m_s[h : h + 1, :] = m_new
            probs.append(p.astype(low_type))
            alphas.append(alpha)
        for h in range(heads):
            own = slice(h * HEAD_DIM, (h + 1) * HEAD_DIM)
            acc_s[own, :] = acc_s[own, :] * alphas[h] + dot32(vt_ref[own, at], probs[h])
        return carry

    lax.fori_loop(table_ref[1 + i], i + 1, step, 0)
    for h in range(heads):
        own = slice(h * HEAD_DIM, (h + 1) * HEAD_DIM)
        acc_s[own, :] = acc_s[own, :] / l_s[h : h + 1, :]
    o_ref[...] = acc_s[...].T.astype(low_type)
    lse_ref[0] = m_s[...] + jnp.log(l_s[...])


def attn_fwd(half, slots, table, q, k, vt, start):
    rows, width = q.shape
    part = width // 2
    heads = part // HEAD_DIM
    count = rows // BLOCK
    per = rows // slots // BLOCK
    at = lambda i, t: place(i, t[0], per)
    return pl.pallas_call(
        functools.partial(attn_fwd_kernel, per),
        grid_spec=pltpu.PrefetchScalarGridSpec(
            num_scalar_prefetch=1,
            grid=(count,),
            in_specs=[
                pl.BlockSpec((BLOCK, part), lambda i, t: (at(i, t), half)),
                pl.BlockSpec((rows, part), lambda i, t: (0, half)),
                pl.BlockSpec((part, rows), lambda i, t: (half, 0)),
                pl.BlockSpec((1, BLOCK), lambda i, t: (0, at(i, t))),
            ],
            out_specs=[
                pl.BlockSpec((BLOCK, part), lambda i, t: (at(i, t), 0)),
                pl.BlockSpec((1, heads, BLOCK), lambda i, t: (at(i, t), 0, 0)),
            ],
            scratch_shapes=[
                pltpu.VMEM((heads, BLOCK), jnp.float32),
                pltpu.VMEM((heads, BLOCK), jnp.float32),
                pltpu.VMEM((part, BLOCK), jnp.float32),
            ],
        ),
        out_shape=[
            jax.ShapeDtypeStruct((rows, part), low_type),
            jax.ShapeDtypeStruct((count, heads, BLOCK), jnp.float32),
        ],
        cost_estimate=cost(rows * rows, rows * part),
        compiler_params=params(60),
        name="attn_fwd",
    )(table, q, k, vt, start)


def adam_blocks(low_ref, in_refs, out_refs):
    gradient = low_ref[...].astype(jnp.float32).reshape(out_refs[0].shape)
    results = adamw_update(in_refs[0][...], gradient, in_refs[1][...], in_refs[2][...], weight_decay)
    out_refs[0][...] = gradient
    for ref, value in zip(out_refs[1:], results):
        ref[...] = value


def attn_bwd_kernel(per, adam, table_ref, q_ref, do_ref, o_ref, k_ref, v_ref, kt_ref, start_ref, lse_ref,
                    keep_ref, above_ref, below_ref, *rest):
    (dq_ref, dk_ref, dv_ref), (dq_s, dk_s, dv_s) = rest[4 * adam : 4 * adam + 3], rest[-3:]
    if adam:
        adam_blocks(rest[0], rest[1:4], rest[7:11])
    i = pl.program_id(0)
    rank = table_ref[0]
    width = q_ref.shape[1]
    heads = width // HEAD_DIM
    first = lax.broadcasted_iota(jnp.int32, (BLOCK, PAIR), 1) < HEAD_DIM

    @pl.when(i == 0)
    def _():
        dk_s[...] = jnp.zeros_like(dk_s)
        dv_s[...] = jnp.zeros_like(dv_s)

    dq_s[...] = jnp.zeros_like(dq_s)
    queries, cotangents, inner = [], [], []
    product = (do_ref[...].astype(jnp.float32) * o_ref[...].astype(jnp.float32)).T
    for h in range(heads):
        cols = slice((h // 2) * PAIR, (h // 2 + 1) * PAIR)
        keep = first if h % 2 == 0 else jnp.logical_not(first)
        pair = q_ref[:, cols]
        queries.append(jnp.where(keep, pair, jnp.zeros_like(pair)))
        pair = do_ref[:, cols]
        cotangents.append(jnp.where(keep, pair, jnp.zeros_like(pair)))
        inner.append(jnp.sum(product[h * HEAD_DIM : (h + 1) * HEAD_DIM, :], axis=0, keepdims=True))
    start = start_ref[...]
    row = i * BLOCK + lax.broadcasted_iota(jnp.int32, (BLOCK, BLOCK), 1)

    def step(kb, carry):
        col = kb * BLOCK + lax.broadcasted_iota(jnp.int32, (BLOCK, BLOCK), 0)
        bias = jnp.where((col >= start) & (col <= row), 0.0, masked_score)
        at = pl.ds(pl.multiple_of(place(kb, rank, per) * BLOCK, BLOCK), BLOCK)
        raw, grads = [], []
        for h in range(heads):
            cols = slice((h // 2) * PAIR, (h // 2 + 1) * PAIR)
            raw.append(dot32(k_ref[at, cols], queries[h], contract_last))
            grads.append(dot32(v_ref[at, cols], cotangents[h], contract_last))
        probs, scores = [], []
        for h in range(heads):
            p = jnp.exp(raw[h] + bias - lse_ref[0, h : h + 1, :])
            scores.append((p * (grads[h] - inner[h])).astype(low_type))
            probs.append(p.astype(low_type))
        for h in range(heads):
            own = slice(h * HEAD_DIM, (h + 1) * HEAD_DIM)
            dq_s[own, :] += dot32(kt_ref[own, at], scores[h])
        for one in range(0, heads, 2):
            cols = slice(one * HEAD_DIM, one * HEAD_DIM + PAIR)
            dv_s[at, cols] += dot32(probs[one], cotangents[one]) + dot32(probs[one + 1], cotangents[one + 1])
            dk_s[at, cols] += dot32(scores[one], queries[one]) + dot32(scores[one + 1], queries[one + 1])
        return carry

    lax.fori_loop(table_ref[1 + i], i + 1, step, 0)
    dq = dq_s[...].T * (HEAD_DIM ** (-0.5))
    here = pl.ds(pl.multiple_of(place(i, rank, per) * BLOCK, BLOCK), BLOCK)
    for c in range(0, width, PAIR):
        dq_ref[:, c : c + PAIR] = turn_back(
            dq[:, c : c + PAIR], keep_ref[here, :], above_ref[here, :], below_ref[here, :]
        ).astype(low_type)

    @pl.when(i == pl.num_programs(0) - 1)
    def _():
        @pl.loop(0, dk_s.shape[0] // BLOCK)
        def _(b):
            at = pl.ds(pl.multiple_of(b * BLOCK, BLOCK), BLOCK)
            for c in range(0, width, PAIR):
                cols = slice(c, c + PAIR)
                dk_ref[at, cols] = turn_back(
                    dk_s[at, cols], keep_ref[at, :], above_ref[at, :], below_ref[at, :]
                ).astype(low_type)
                dv_ref[at, cols] = dv_s[at, cols].astype(low_type)


def attn_bwd(half, slots, table, q, do, o, k, v, kt, start, lse, tables, low=None, held=()):
    rows, width = q.shape
    part = width // 2
    heads = part // HEAD_DIM
    count = rows // BLOCK
    per = rows // slots // BLOCK
    at = lambda i, t: place(i, t[0], per)
    whole = pl.BlockSpec((rows, part), lambda i, t: (0, half))
    turns = pl.BlockSpec((rows, PAIR), lambda i, t: (0, 0))
    result = pl.BlockSpec((rows, part), lambda i, t: (0, 0))
    adam = low is not None
    adam_in, adam_out, adam_like = [], [], []
    if adam:
        strip, depth = low.shape[0] // count, low.shape[1]
        flat = pl.BlockSpec((strip, depth), lambda i, t: (i, 0))
        one = flat if held[0].ndim == 2 else pl.BlockSpec((1, strip, depth), lambda i, t: (0, i, 0))
        adam_in, adam_out = [flat, one, one, one], [one] * 4
        adam_like = [jax.ShapeDtypeStruct(held[0].shape, jnp.float32)] * 4
    return pl.pallas_call(
        functools.partial(attn_bwd_kernel, per, int(adam)),
        grid_spec=pltpu.PrefetchScalarGridSpec(
            num_scalar_prefetch=1,
            grid=(count,),
            in_specs=[
                pl.BlockSpec((BLOCK, part), lambda i, t: (at(i, t), half)),
                pl.BlockSpec((BLOCK, part), lambda i, t: (at(i, t), half)),
                pl.BlockSpec((BLOCK, part), lambda i, t: (at(i, t), 0)),
                whole,
                whole,
                pl.BlockSpec((part, rows), lambda i, t: (half, 0)),
                pl.BlockSpec((1, BLOCK), lambda i, t: (0, at(i, t))),
                pl.BlockSpec((1, heads, BLOCK), lambda i, t: (at(i, t), 0, 0)),
                turns,
                turns,
                turns,
            ]
            + adam_in,
            out_specs=[pl.BlockSpec((BLOCK, part), lambda i, t: (at(i, t), 0)), result, result] + adam_out,
            scratch_shapes=[
                pltpu.VMEM((part, BLOCK), jnp.float32),
                pltpu.VMEM((rows, part), jnp.float32),
                pltpu.VMEM((rows, part), jnp.float32),
            ],
        ),
        out_shape=[jax.ShapeDtypeStruct((rows, part), low_type)] * 3 + adam_like,
        cost_estimate=cost(25 * rows * rows * part // 2, 16 * rows * part, 8 * rows * rows // 4),
        compiler_params=params(60),
        name="attn_bwd",
    )(table, q, do, o, k, v, kt, start, lse, *tables, *((low,) + tuple(held) if adam else ()))


def qkv_grad_kernel(count, adam, *refs):
    left_ref, other_ref, rights = refs[0], refs[1], refs[2 : 2 + count]
    out_ref, sum_ref = refs[2 + count + 8 * adam : 4 + count + 8 * adam]
    if adam:
        adam_blocks(refs[2 + count], refs[3 + count : 6 + count], refs[-4:])
    part = rights[0].shape[1]

    @pl.when(pl.program_id(0) == 0)
    def _():
        for n, right in enumerate(rights):
            sum_ref[n // 2 : n // 2 + 1, (n % 2) * part : (n % 2 + 1) * part] = jnp.sum(
                right[...].astype(jnp.float32), axis=0, keepdims=True
            )

    left = left_ref[...]
    for n, right in enumerate(rights):
        out_ref[n // 2, :, (n % 2) * part : (n % 2 + 1) * part] = dot32(left, right[...], contract_first).astype(low_type)
    out_ref[len(rights) // 2] = other_ref[...]


def qkv_grad(left, rights, other, low=None, held=(), begun=()):
    rows, model = left.shape
    part = rights[0].shape[1]
    count = len(rights) // 2
    tile = 512
    adam = low is not None
    adam_in, adam_out, adam_like, extra = [], [], [], ()
    if adam:
        strip, depth = low.shape[0] // (model // tile), low.shape[1]
        one = pl.BlockSpec((1, strip, depth), lambda n: (1, n, 0))
        adam_in = [pl.BlockSpec((strip, depth), lambda n: (n, 0)), one, one, one] + [ANY] * 4
        adam_out = [one] * 4
        adam_like = [jax.ShapeDtypeStruct(held[0].shape, jnp.float32)] * 4
        extra = (low,) + tuple(held) + tuple(begun)
    first = 2 + len(rights) + 4
    return pl.pallas_call(
        functools.partial(qkv_grad_kernel, len(rights), int(adam)),
        grid=(model // tile,),
        in_specs=[pl.BlockSpec((rows, tile), lambda n: (0, n)), pl.BlockSpec((tile, 2 * part), lambda n: (n, 0))]
        + [pl.BlockSpec((rows, part), lambda n: (0, 0), pipeline_mode=pl.Buffered(1))] * len(rights)
        + adam_in,
        input_output_aliases={first + n: 2 + n for n in range(4)} if adam else {},
        out_specs=[
            pl.BlockSpec((count + 1, tile, 2 * part), lambda n: (0, n, 0)),
            pl.BlockSpec((count, 2 * part), lambda n: (0, 0)),
        ]
        + adam_out,
        out_shape=[
            jax.ShapeDtypeStruct((count + 1, model, 2 * part), low_type),
            jax.ShapeDtypeStruct((count, 2 * part), jnp.float32),
        ]
        + adam_like,
        cost_estimate=cost(4 * count * rows * model * part, 4 * rows * model),
        compiler_params=params(60),
        name="qkv_grad",
    )(left, other, *rights, *extra)


swap_x = [(0, 1), (1, 0), (2, 3), (3, 2)]
swap_y = [(0, 2), (2, 0), (1, 3), (3, 1)]


def square(count):
    return count == 4


def gather_rows(top, end):
    x_top = lax.ppermute(top, "tensor", swap_x)
    y_end = lax.ppermute(end, "tensor", swap_y)
    x_end = lax.ppermute(end, "tensor", swap_x)
    y_top = lax.ppermute(top, "tensor", swap_y)
    first = [top, end, x_top, x_end, y_top, y_end]

    def rest(*between):
        far_top = lax.ppermute(after(x_top, *between), "tensor", swap_y)
        far_end = lax.ppermute(after(y_end, *between), "tensor", swap_x)
        return [far_top, far_end]

    return first, rest


def after(value, *others):
    return lax.optimization_barrier((value,) + others)[0]


def add_low(a, b):
    return (a.astype(jnp.float32) + b.astype(jnp.float32)).astype(low_type)


def scatter_first(values):
    far, half = values[3], values[3].shape[0] // 2
    top = lax.ppermute(far[:half], "tensor", swap_x)
    end = lax.ppermute(far[half:], "tensor", swap_y)
    return [top, end]


def scatter_last(values, first):
    top, end = first
    half = top.shape[0]
    for_x, for_y = values[1], values[2]
    for_y = jnp.concatenate([add_low(for_y[:half], top), for_y[half:]], axis=0)
    for_x = jnp.concatenate([for_x[:half], add_low(for_x[half:], end)], axis=0)
    from_x = lax.ppermute(for_x, "tensor", swap_x)
    from_y = lax.ppermute(for_y, "tensor", swap_y)
    return [values[0], from_x, from_y]


MESH = pl.DeviceIdType.MESH


def greet(near_x, near_y):
    barrier = pltpu.get_barrier_semaphore()
    for near in (near_x, near_y):
        pl.semaphore_signal(barrier, inc=1, device_id={"tensor": near}, device_id_type=MESH)
    pl.semaphore_wait(barrier, 2)


def neighbours():
    rank = lax.axis_index("tensor")
    return jnp.bitwise_xor(rank, 1), jnp.bitwise_xor(rank, 2)


def remote(index, source, target, near, send, recv):
    return pltpu.make_async_remote_copy(
        src_ref=source,
        dst_ref=target,
        send_sem=send.at[index],
        recv_sem=recv.at[index],
        device_id={"tensor": near},
        device_id_type=MESH,
    )


arrival = (0, 1, 2, 5, 3, 4, 6, 7)


def arrival_slot(i):
    return jnp.where(i == 3, 5, jnp.where(i == 4, 3, jnp.where(i == 5, 4, i)))


def square_copies(all_s, half, send, recv):
    near_x, near_y = neighbours()
    at = lambda n: all_s.at[pl.ds(n * half, half)]
    return (
        remote(0, at(0), at(2), near_x, send, recv),
        remote(1, at(1), at(5), near_y, send, recv),
        remote(2, at(1), at(3), near_x, send, recv),
        remote(3, at(0), at(4), near_y, send, recv),
        remote(4, at(2), at(6), near_y, send, recv),
        remote(5, at(5), at(7), near_x, send, recv),
    )


def await_slot(i, copies):
    x_top, y_end, x_end, y_top, far_top, far_end = copies

    @pl.when(i == 2)
    def _():
        x_top.wait_recv()
        far_top.start()
        y_end.wait_recv()
        far_end.start()

    for n, c in ((4, x_end), (5, y_top), (6, far_top), (7, far_end)):

        @pl.when(i == n)
        def _(c=c):
            c.wait_recv()


def fetch_next(i, refs, buf, sem):
    def fetch(j):
        pltpu.make_async_copy(refs[j], buf.at[j % 2], sem.at[j % 2]).start()

    for j in range(len(refs)):

        @pl.when(i == max(j - 1, 0) if j else i == 0)
        def _(j=j):
            fetch(j)

    pltpu.make_async_copy(refs[0], buf.at[i % 2], sem.at[i % 2]).wait()


def flow(first, last, loads, work, stores):
    def all_of(copies, act):
        for c in copies:
            act(c)

    all_of(loads(first), lambda c: c.start())

    def step(i, carry):
        @pl.when(i < last - 1)
        def _():
            all_of(loads(i + 1), lambda c: c.start())

        all_of(loads(i), lambda c: c.wait())

        @pl.when(i >= first + 2)
        def _():
            all_of(stores(i - 2), lambda c: c.wait())

        work(i)
        all_of(stores(i), lambda c: c.start())
        return carry

    lax.fori_loop(first, last, step, 0)
    for i in range(max(first, last - 2), last):
        all_of(stores(i), lambda c: c.wait())


def gather_norm_kernel(nd, x_ref, small_ref, pos_ref, inv_ref, og_ref, live_ref, w_hbm,
                       h_ref, full_ref, keep_ref, above_ref, below_ref, top_ref, end_ref, low_hbm,
                       all_s, full_s, stage, w_s, low_s, send, recv, local, small_send, small_recv, out_sem, w_sem, low_sem):
    d = lax.axis_index("dp")
    near_x, near_y = neighbours()
    half = x_ref.shape[0] // 2
    width = small_ref.shape[1]
    own = pltpu.make_async_copy(x_ref, all_s.at[pl.ds(0, 2 * half)], local)
    own.start()
    barrier = pltpu.get_barrier_semaphore()
    for near in (near_x, near_y):
        pl.semaphore_signal(barrier, inc=1, device_id={"tensor": near}, device_id_type=MESH)
    for k in range(1, nd):
        pl.semaphore_signal(barrier, inc=1, device_id={"dp": lax.rem(d + k, nd)}, device_id_type=MESH)
    pl.semaphore_wait(barrier, nd + 1)
    own.wait()
    copies = square_copies(all_s, half, send, recv)
    for c in copies[:4]:
        c.start()
    small = []
    for k in range(1, nd):
        c = pltpu.make_async_remote_copy(
            src_ref=small_ref,
            dst_ref=full_s.at[d],
            send_sem=small_send.at[k],
            recv_sem=small_recv.at[k],
            device_id={"dp": lax.rem(d + k, nd)},
            device_id_type=MESH,
        )
        c.start()
        small.append(c)
    full_s[d] = small_ref[...]
    for n, ref in enumerate((top_ref, end_ref)):

        @pl.loop(0, half // 32)
        def _(r, n=n, ref=ref):
            to = pl.ds(pl.multiple_of(r * 32, 32), 32)
            at = pl.ds(pl.multiple_of(n * half + r * 32, 32), 32)
            ref[to, :] = (og_ref[at, :].astype(jnp.float32) * live_ref[at, :]).astype(low_type)

    strip = w_s.shape[1]
    per = w_hbm.shape[1] // strip

    def side(i):
        return i // per, pl.ds(pl.multiple_of((i % per) * strip, strip), strip)

    def cast(i):
        low_s[i % 2] = w_s[i % 2].astype(low_type)

    flow(
        0,
        w_hbm.shape[0] * per,
        lambda i: [pltpu.make_async_copy(w_hbm.at[side(i)], w_s.at[i % 2], w_sem.at[i % 2])],
        cast,
        lambda i: [pltpu.make_async_copy(low_s.at[i % 2], low_hbm.at[side(i)], low_sem.at[i % 2])],
    )
    for c in small:
        c.wait_recv()
    for n in range(nd):
        full_ref[:, n * width : (n + 1) * width] = full_s[n]
    step = 32
    lane = lax.broadcasted_iota(jnp.int32, (256, PAIR), 1) % HEAD_DIM

    def turns(n):
        at = pl.ds(pl.multiple_of(n * 256, 256), 256)
        angles = jnp.broadcast_to(pos_ref[pl.ds(n, 1), :], (PAIR, 256)).T * inv_ref[...]
        cos_part, sine_part = jnp.cos(angles), jnp.sin(angles)
        keep_ref[at, :] = jnp.where(lane < ROT, cos_part, 1.0)
        above_ref[at, :] = jnp.where(lane < ROT // 2, -sine_part, 0.0)
        below_ref[at, :] = jnp.where((lane >= ROT // 2) & (lane < ROT), sine_part, 0.0)

    def out(buf, row):
        return pltpu.make_async_copy(stage.at[buf], h_ref.at[pl.ds(row, half)], out_sem.at[buf])

    def body_step(i, carry):
        await_slot(i, copies)
        row = pl.multiple_of(arrival_slot(i) * half, half)
        buf = i % 2

        @pl.when(i >= 2)
        def _():
            out(buf, row).wait()

        @pl.loop(0, half // step)
        def _(r):
            at = pl.ds(pl.multiple_of(r * step, step), step)
            x = all_s[pl.ds(pl.multiple_of(row + r * step, step), step), :].astype(jnp.float32)
            c = x - jnp.mean(x, axis=-1, keepdims=True)
            s = lax.rsqrt(jnp.mean(c * c, axis=-1, keepdims=True) + norm_eps)
            stage[buf, at, :] = (c * s * full_ref[0:1, :] + full_ref[2:3, :]).astype(low_type)

        out(buf, row).start()

        @pl.when(i < 4)
        def _():
            turns(2 * i)
            turns(2 * i + 1)

        return carry

    lax.fori_loop(0, 8, body_step, 0)
    for buf in (0, 1):
        out(buf, 0).wait()
    for c in copies:
        c.wait_send()
    for c in small:
        c.wait_send()


def gather_norm(x, small, pos, inverse, out_grad, live, w):
    nd = lax.axis_size("dp")
    rows, model = x.shape
    total = 4 * rows
    count, width = small.shape
    vmem = pl.BlockSpec(memory_space=pltpu.VMEM)
    table = jax.ShapeDtypeStruct((total, PAIR), jnp.float32)
    return pl.pallas_call(
        functools.partial(gather_norm_kernel, nd),
        in_specs=[ANY, vmem, vmem, vmem, vmem, vmem, ANY],
        out_specs=[ANY, vmem, vmem, vmem, vmem, vmem, vmem, ANY],
        out_shape=[
            jax.ShapeDtypeStruct((total, model), low_type),
            jax.ShapeDtypeStruct((count, width * nd), jnp.float32),
            table,
            table,
            table,
            jax.ShapeDtypeStruct((rows // 2, model), low_type),
            jax.ShapeDtypeStruct((rows // 2, model), low_type),
            jax.ShapeDtypeStruct(w.shape, low_type),
        ],
        scratch_shapes=[
            pltpu.VMEM((total, model), low_type),
            pltpu.VMEM((nd, count, width), jnp.float32),
            pltpu.VMEM((2, rows // 2, model), low_type),
            pltpu.VMEM((2, 64, w.shape[2]), jnp.float32),
            pltpu.VMEM((2, 64, w.shape[2]), low_type),
            pltpu.SemaphoreType.DMA((6,)),
            pltpu.SemaphoreType.DMA((6,)),
            pltpu.SemaphoreType.DMA,
            pltpu.SemaphoreType.DMA((nd,)),
            pltpu.SemaphoreType.DMA((nd,)),
            pltpu.SemaphoreType.DMA((2,)),
            pltpu.SemaphoreType.DMA((2,)),
            pltpu.SemaphoreType.DMA((2,)),
        ],
        cost_estimate=cost(20 * total * model, 4 * total * model),
        compiler_params=pltpu.CompilerParams(vmem_limit_bytes=62 * MIB, collective_id=3, has_side_effects=True),
        name="gather_norm",
    )(x, small, pos, inverse, out_grad, live, w)


def gather_do_kernel(d_ref, act_ref, h_hbm, dup_hbm, o_a_ref, o_b_ref, wo_hbm, wd_hbm, do_ref, grad_ref, mlp_ref, up_ref,
                     all_s, wo_s, wd_s, dup_s, acc, act_s, h_s, stage, up_s, send, recv, local, act_sem, h_sem, out_sem, up_sem):
    near_x, near_y = neighbours()
    half = d_ref.shape[0] // 2
    model = d_ref.shape[1]
    part = o_a_ref.shape[1]
    tile = 512
    own = pltpu.make_async_copy(d_ref, all_s.at[pl.ds(0, 2 * half)], local.at[0])
    own.start()
    weights = pltpu.make_async_copy(wd_hbm, wd_s, local.at[1])
    weights.start()
    cotangent = pltpu.make_async_copy(dup_hbm, dup_s, local.at[2])
    cotangent.start()
    turned = pltpu.make_async_copy(wo_hbm.at[3], wo_s, local.at[3])
    turned.start()
    greet(near_x, near_y)
    own.wait()
    copies = square_copies(all_s, half, send, recv)
    for c in copies[:4]:
        c.start()
    acc[...] = jnp.zeros_like(acc)
    weights.wait()
    cotangent.wait()
    turned.wait()
    strip = model // 8

    def loads(i):
        at = pl.ds(pl.multiple_of(i * half, half), half)
        cols = pl.ds(pl.multiple_of(i * strip, strip), strip)
        return [
            pltpu.make_async_copy(act_ref.at[at], act_s.at[i % 2], act_sem.at[i % 2]),
            pltpu.make_async_copy(h_hbm.at[:, cols], h_s.at[i % 2], h_sem.at[i % 2]),
        ]

    def outs(i):
        at = pl.ds(pl.multiple_of(i * half, half), half)
        side = pl.ds(pl.multiple_of(i * strip, strip), strip)
        return [
            pltpu.make_async_copy(stage.at[i % 2], mlp_ref.at[at], out_sem.at[i % 2]),
            pltpu.make_async_copy(up_s.at[i % 2], up_ref.at[side], up_sem.at[i % 2]),
        ]

    for c in loads(0):
        c.start()

    def beside(p):
        @pl.when(p < 7)
        def _():
            for c in loads(p + 1):
                c.start()

        for c in loads(p):
            c.wait()

        @pl.when(p >= 2)
        def _():
            for c in outs(p - 2):
                c.wait()

        stage[p % 2] = dot32(act_s[p % 2], wd_s[...]).astype(low_type)
        up_s[p % 2] = dot32(h_s[p % 2], dup_s[...], contract_first).astype(low_type)
        for c in outs(p):
            c.start()

    def step(i, carry):
        @pl.when(i < 6)
        def _():
            beside(jnp.where(i == 5, 6, i))

        @pl.when((i == 4) | (i == 5))
        def _():
            beside(2 * i - 3)

        await_slot(i, copies)
        at = pl.ds(pl.multiple_of(arrival_slot(i) * half, half), half)
        dattn = all_s[at, :]
        do_ref[at, :] = dot32(dattn, wo_s[...]).astype(low_type)
        acc[:part, :] += dot32(o_a_ref[at, :], dattn, contract_first)
        acc[part:, :] += dot32(o_b_ref[at, :], dattn, contract_first)
        return carry

    lax.fori_loop(0, 8, step, 0)

    @pl.loop(0, model // tile)
    def _(n):
        cols = pl.ds(pl.multiple_of(n * tile, tile), tile)
        grad_ref[cols, :] = acc[:, cols].T.astype(low_type)

    for i in (6, 7):
        for c in outs(i):
            c.wait()
    for c in copies:
        c.wait_send()


def gather_do(dattn, act, h, dup, o_a, o_b, wo, wd):
    rows, model = dattn.shape
    total = 4 * rows
    depth = act.shape[1]
    width = wo.shape[2]
    vmem = pl.BlockSpec(memory_space=pltpu.VMEM)
    return pl.pallas_call(
        gather_do_kernel,
        in_specs=[ANY, ANY, ANY, ANY, vmem, vmem, ANY, ANY],
        out_specs=[vmem, vmem, ANY, ANY],
        out_shape=[
            jax.ShapeDtypeStruct((total, width), low_type),
            jax.ShapeDtypeStruct((model, width), low_type),
            jax.ShapeDtypeStruct((total, model), low_type),
            jax.ShapeDtypeStruct((model, depth), low_type),
        ],
        scratch_shapes=[
            pltpu.VMEM((total, model), low_type),
            pltpu.VMEM(wo.shape[1:], low_type),
            pltpu.VMEM(wd.shape, low_type),
            pltpu.VMEM(dup.shape, low_type),
            pltpu.VMEM((width, model), jnp.float32),
            pltpu.VMEM((2, rows // 2, depth), low_type),
            pltpu.VMEM((2, total, model // 8), low_type),
            pltpu.VMEM((2, rows // 2, model), low_type),
            pltpu.VMEM((2, model // 8, depth), low_type),
            pltpu.SemaphoreType.DMA((6,)),
            pltpu.SemaphoreType.DMA((6,)),
            pltpu.SemaphoreType.DMA((4,)),
            pltpu.SemaphoreType.DMA((2,)),
            pltpu.SemaphoreType.DMA((2,)),
            pltpu.SemaphoreType.DMA((2,)),
            pltpu.SemaphoreType.DMA((2,)),
        ],
        cost_estimate=cost(2 * total * model * (depth + 2 * width), 6 * total * model),
        compiler_params=pltpu.CompilerParams(vmem_limit_bytes=62 * MIB, collective_id=4, has_side_effects=True),
        name="gather_do",
    )(dattn, act, h, dup, o_a, o_b, wo, wd)


def exchange(rows, partial, bufs, send, recv, fill_one, fill_two):
    far_s, for_x, for_y, top_s, end_s, from_x, from_y = bufs
    near_x, near_y = neighbours()
    half = rows // 2
    t, e = pl.ds(0, half), pl.ds(half, half)
    copies = [
        remote(0, far_s.at[t], top_s, near_x, send, recv),
        remote(1, far_s.at[e], end_s, near_y, send, recv),
        remote(2, for_x.at[t], from_x.at[t], near_x, send, recv),
        remote(3, for_y.at[e], from_y.at[e], near_y, send, recv),
    ]
    quarter = half // 2
    for n in range(2):
        at = pl.ds(half + n * quarter, quarter)
        copies.append(remote(4 + n, for_x.at[at], from_x.at[at], near_x, send, recv))
    for n in range(2):
        at = pl.ds(n * quarter, quarter)
        copies.append(remote(6 + n, for_y.at[at], from_y.at[at], near_y, send, recv))

    def into(ref, which):
        def store(cols, value):
            ref[pl.ds(which * half, half), cols] = value.astype(low_type)

        return store

    def added(ref, which, other):
        def store(cols, value):
            ref[pl.ds(which * half, half), cols] = (value + other[:, cols].astype(jnp.float32)).astype(low_type)

        return store

    partial(3, 0, into(far_s, 0))
    copies[0].start()
    partial(3, 1, into(far_s, 1))
    copies[1].start()
    partial(1, 0, into(for_x, 0))
    copies[2].start()
    partial(2, 1, into(for_y, 1))
    copies[3].start()
    fill_one()
    copies[0].wait_recv()
    partial(2, 0, added(for_y, 0, top_s))
    copies[6].start()
    copies[7].start()
    copies[1].wait_recv()
    partial(1, 1, added(for_x, 1, end_s))
    copies[4].start()
    copies[5].start()
    fill_two()
    return copies


def finish_quarters(copies, finish, sent=0):
    copies[2].wait_recv()
    copies[6].wait_recv()
    finish(0)
    copies[3].wait_recv()
    copies[4].wait_recv()
    finish(2)
    copies[7].wait_recv()
    finish(1)
    copies[5].wait_recv()
    finish(3)
    for c in copies[sent:]:
        c.wait_send()


def finish_back(copies, rows, gain_row, v_ref, base_ref, own_ref, live_ref, norm_ref, from_x, from_y, dx_ref, low_ref, gain_ref, shift_ref, gain_s, shift_s, sent=0):
    quarter = rows // 4
    step = 16
    gain_s[...] = jnp.zeros_like(gain_s)
    shift_s[...] = jnp.zeros_like(shift_s)

    def finish(which):
        @pl.loop(0, quarter // step)
        def _(r):
            at = pl.ds(pl.multiple_of(which * quarter + r * step, step), step)
            e = own_ref[at, :].astype(jnp.float32) + from_x[at, :].astype(jnp.float32) + from_y[at, :].astype(jnp.float32)
            v = v_ref[at, :].astype(jnp.float32)
            c = v - jnp.mean(v, axis=-1, keepdims=True)
            s = lax.rsqrt(jnp.mean(c * c, axis=-1, keepdims=True) + norm_eps)
            xh = c * s
            w = e * norm_ref[gain_row : gain_row + 1, :]
            back = s * (w - jnp.mean(w, axis=-1, keepdims=True) - xh * jnp.mean(w * xh, axis=-1, keepdims=True))
            dx = base_ref[at, :].astype(jnp.float32) + back
            dx_ref[at, :] = dx.astype(dx_ref.dtype)
            if low_ref is not None:
                low_ref[at, :] = (dx * live_ref[at, :]).astype(low_type)
            ex = e * xh
            gain_s[...] += ex[:8] + ex[8:]
            shift_s[...] += e[:8] + e[8:]

    finish_quarters(copies, finish, sent)
    gain_ref[...] = jnp.sum(gain_s[...], axis=0, keepdims=True)
    shift_ref[...] = jnp.sum(shift_s[...], axis=0, keepdims=True)


def exchange_scratch(rows, model):
    big = pltpu.VMEM((rows, model), low_type)
    small = pltpu.VMEM((rows // 2, model), low_type)
    line = pltpu.VMEM((8, model), jnp.float32)
    sems = pltpu.SemaphoreType.DMA((8,))
    return [big, big, big, small, small, big, big, line, line, sems, sems]


def out_scatter_kernel(a_ref, b_ref, w_hbm, x_ref, live_ref, norm_ref, x1_ref, h_ref, *scratch):
    bufs, (send, recv, w_s, local) = scratch[:7], scratch[9:]
    weights = pltpu.make_async_copy(w_hbm.at[3], w_s, local)
    weights.start()
    near_x, near_y = neighbours()
    rows, model = x_ref.shape
    half = rows // 2
    part = a_ref.shape[1]
    tile = 512
    greet(near_x, near_y)
    weights.wait()

    def partial(slot, which, store):
        at = pl.ds(slot * rows + which * half, half)

        @pl.loop(0, model // tile)
        def _(n):
            cols = pl.ds(pl.multiple_of(n * tile, tile), tile)
            value = dot32(a_ref[at, :], w_s[cols, :part], contract_last)
            store(cols, value + dot32(b_ref[at, :], w_s[cols, part:], contract_last))

    def own(which):
        def store(cols, value):
            x1_ref[pl.ds(which * half, half), cols] = value

        return store

    def fill_one():
        partial(0, 0, own(0))
        partial(0, 1, own(1))

    copies = exchange(rows, partial, bufs, send, recv, fill_one, lambda: None)
    from_x, from_y = bufs[5:]
    quarter = rows // 4
    step = 32

    def finish(which):
        @pl.loop(0, quarter // step)
        def _(r):
            at = pl.ds(pl.multiple_of(which * quarter + r * step, step), step)
            attn = x1_ref[at, :] + from_x[at, :].astype(jnp.float32) + from_y[at, :].astype(jnp.float32)
            x1 = x_ref[at, :].astype(jnp.float32) + live_ref[at, :] * attn
            x1_ref[at, :] = x1
            c = x1 - jnp.mean(x1, axis=-1, keepdims=True)
            s = lax.rsqrt(jnp.mean(c * c, axis=-1, keepdims=True) + norm_eps)
            h_ref[at, :] = (c * s * norm_ref[1:2, :] + norm_ref[3:4, :]).astype(low_type)

    finish_quarters(copies, finish)


def out_scatter(a, b, w, x, live, norm):
    rows, model = x.shape
    vmem = pl.BlockSpec(memory_space=pltpu.VMEM)
    total = a.shape[0]
    return pl.pallas_call(
        out_scatter_kernel,
        in_specs=[vmem, vmem, ANY, vmem, vmem, vmem],
        out_specs=[vmem] * 2,
        out_shape=[jax.ShapeDtypeStruct((rows, model), jnp.float32), jax.ShapeDtypeStruct((rows, model), low_type)],
        scratch_shapes=exchange_scratch(rows, model) + [pltpu.VMEM(w.shape[1:], low_type), pltpu.SemaphoreType.DMA],
        cost_estimate=cost(2 * total * model * w.shape[2], 20 * rows * model),
        compiler_params=pltpu.CompilerParams(vmem_limit_bytes=62 * MIB, collective_id=0, has_side_effects=True),
        name="out_scatter",
    )(a, b, w, x, live, norm)


sending = (6, 7, 2, 5, 0, 1, 4, 3)


def sending_slot(j):
    slot = jnp.int32(sending[-1])
    for n in range(7):
        slot = jnp.where(j == n, sending[n], slot)
    return slot


def hidden_scatter_kernel(count, *refs):
    dm_refs, refs = refs[:count], refs[count:]
    one_hbm, two_hbm, wd_hbm, w_hbm, h_hbm, x1_hbm, og_hbm, live_ref, norm_ref = refs[:9]
    grad_ref, dup_ref, dx_ref, low_ref, gain_ref, shift_ref = refs[9:15]
    scratch = refs[15:]
    bufs, (gain_s, shift_s, send, recv) = scratch[:7], scratch[7:11]
    g_s, w_s, wd_s, dm_s, slope_s, h_s, stage, local, dm_sem, slope_sem, h_sem, out_sem = scratch[11:]
    rows, model = dx_ref.shape
    half = rows // 2
    near_x, near_y = neighbours()
    down_load = pltpu.make_async_copy(wd_hbm, wd_s, local.at[0])
    weight_load = pltpu.make_async_copy(w_hbm, w_s, local.at[1])
    x1_load = pltpu.make_async_copy(x1_hbm, dx_ref, local.at[2])
    og_load = pltpu.make_async_copy(og_hbm, bufs[0], local.at[3])
    dup_store = pltpu.make_async_copy(g_s.at[1], dup_ref, local.at[4])

    def slope_loads(j):
        at = pl.ds(pl.multiple_of(sending_slot(j) * half, half), half)
        return [
            pltpu.make_async_copy(ref.at[at], slope_s.at[j % 2, n], slope_sem.at[j % 2, n])
            for n, ref in enumerate((one_hbm, two_hbm))
        ]

    def dm_load(n):
        return pltpu.make_async_copy(dm_refs[sending[n]], dm_s.at[n % 2], dm_sem.at[n % 2])

    down_load.start()
    dm_load(0).start()
    for c in slope_loads(0):
        c.start()
    weight_load.start()
    x1_load.start()
    greet(near_x, near_y)
    down_load.wait()

    def back_step(j, carry):
        @pl.when(j < 7)
        def _():
            for c in slope_loads(j + 1):
                c.start()

        for n in range(1, 8):

            @pl.when(j == n - 1)
            def _(n=n):
                dm_load(n).start()

        b = j % 2
        pltpu.make_async_copy(dm_refs[0], dm_s.at[b], dm_sem.at[b]).wait()
        for c in slope_loads(j):
            c.wait()
        at = pl.ds(pl.multiple_of(sending_slot(j) * half, half), half)
        da = dot32(dm_s[b], wd_s[...], contract_last)
        g_s[0, at, :] = (da * slope_s[b, 0].astype(jnp.float32)).astype(low_type)
        g_s[1, at, :] = (da * slope_s[b, 1].astype(jnp.float32)).astype(low_type)
        return carry

    def back(first, last):
        lax.fori_loop(first, last, back_step, 0)

    tile = 512

    def partial(slot, which, store):
        if slot == 3:
            back(which, which + 1)
        if slot == 3 and which == 0:
            weight_load.wait()
        if slot == 1 and which == 0:
            back(2, 4)
        at = pl.ds(slot * rows + which * half, half)

        @pl.loop(0, model // tile)
        def _(n):
            cols = pl.ds(pl.multiple_of(n * tile, tile), tile)
            value = dot32(g_s[0, at, :], w_s[0, cols, :], contract_last)
            store(cols, value + dot32(g_s[1, at, :], w_s[1, cols, :], contract_last))

    def own(which):
        def store(cols, value):
            low_ref[pl.ds(which * half, half), cols] = value.astype(low_type)

        return store

    strip = 256

    def load(i):
        return pltpu.make_async_copy(h_hbm.at[:, pl.ds(pl.multiple_of(i * strip, strip), strip)], h_s.at[i % 2], h_sem.at[i % 2])

    def out(i):
        at = pl.ds(pl.multiple_of(i * strip, strip), strip)
        return pltpu.make_async_copy(stage.at[i % 2], grad_ref.at[at], out_sem.at[i % 2])

    strips = model // strip

    def strip_step(i, carry):
        @pl.when(i < strips - 1)
        def _():
            load(i + 1).start()

        load(i).wait()

        @pl.when(i >= 2)
        def _():
            out(i - 2).wait()

        stage[i % 2] = dot32(h_s[i % 2], g_s[0], contract_first).astype(low_type)
        out(i).start()
        return carry

    def fill_one():
        back(4, 8)
        dup_store.start()
        load(0).start()
        partial(0, 0, own(0))

    def fill_two():
        partial(0, 1, own(1))
        lax.fori_loop(0, strips, strip_step, 0)

    copies = exchange(rows, partial, bufs, send, recv, fill_one, fill_two)
    copies[0].wait_send()
    copies[1].wait_send()
    og_load.start()
    x1_load.wait()
    og_load.wait()
    finish_back(copies, rows, 1, dx_ref, bufs[0], low_ref, live_ref, norm_ref, bufs[5], bufs[6], dx_ref, low_ref, gain_ref, shift_ref, gain_s, shift_s, 2)
    out(strips - 2).wait()
    out(strips - 1).wait()
    dup_store.wait()


def hidden_scatter(dm_blocks, one, two, wd, w, h, x1, out_grad, live, norm):
    rows, model = x1.shape
    total, depth = one.shape
    half = rows // 2
    vmem = pl.BlockSpec(memory_space=pltpu.VMEM)
    line = jax.ShapeDtypeStruct((1, model), jnp.float32)
    return pl.pallas_call(
        functools.partial(hidden_scatter_kernel, len(dm_blocks)),
        in_specs=[ANY] * (len(dm_blocks) + 7) + [vmem, vmem],
        out_specs=[ANY, ANY, vmem, vmem, vmem, vmem],
        out_shape=[
            jax.ShapeDtypeStruct((model, depth), low_type),
            jax.ShapeDtypeStruct((total, depth), low_type),
            jax.ShapeDtypeStruct((rows, model), jnp.float32),
            jax.ShapeDtypeStruct((rows, model), low_type),
            line,
            line,
        ],
        scratch_shapes=exchange_scratch(rows, model)
        + [
            pltpu.VMEM((2, total, depth), low_type),
            pltpu.VMEM(w.shape, low_type),
            pltpu.VMEM(wd.shape, low_type),
            pltpu.VMEM((2, half, model), low_type),
            pltpu.VMEM((2, 2, half, depth), low_type),
            pltpu.VMEM((2, total, 256), low_type),
            pltpu.VMEM((2, 256, depth), low_type),
            pltpu.SemaphoreType.DMA((5,)),
            pltpu.SemaphoreType.DMA((2,)),
            pltpu.SemaphoreType.DMA((2, 2)),
            pltpu.SemaphoreType.DMA((2,)),
            pltpu.SemaphoreType.DMA((2,)),
        ],
        cost_estimate=cost(8 * total * model * depth, 16 * total * model),
        compiler_params=pltpu.CompilerParams(vmem_limit_bytes=62 * MIB, collective_id=5, has_side_effects=True),
        name="hidden_scatter",
    )(*dm_blocks, one, two, wd, w, h, x1, out_grad, live, norm)


def first_scatter_kernel(count, *refs):
    lefts_hbm = refs[:count]
    w_hbm, x_ref, base_ref, norm_ref, live_ref = refs[count : count + 5]
    refs = refs[count + 5 :]
    x1_hbm, mlp_hbm = refs[0], refs[1:4]
    dx_ref, gain_ref, shift_ref, layer_hbm = refs[4:8]
    scratch = refs[8:]
    bufs, (gain_s, shift_s, send, recv, own_s, left_s, w_s) = scratch[:7], scratch[7:14]
    x1_s, mlp_s, layer_s, left_sem, in_sem, layer_sem = scratch[14:]
    rows, model = x_ref.shape
    half = rows // 2
    tile = 512
    near_x, near_y = neighbours()
    far = pl.ds(3 * rows, rows)
    rest = pl.ds(0, 3 * rows)
    early = [pltpu.make_async_copy(left.at[far], left_s.at[n, far], left_sem.at[n]) for n, left in enumerate(lefts_hbm)]
    early.append(pltpu.make_async_copy(w_hbm.at[pl.ds(0, 3)], w_s, left_sem.at[2 * count]))
    late = [
        pltpu.make_async_copy(left.at[rest], left_s.at[n, rest], left_sem.at[count + n]) for n, left in enumerate(lefts_hbm)
    ]
    for c in early + late:
        c.start()
    greet(near_x, near_y)
    for c in early:
        c.wait()

    def partial(slot, which, store):
        if slot == 1 and which == 0:
            for c in late:
                c.wait()
        at = pl.ds(slot * rows + which * half, half)

        @pl.loop(0, model // tile)
        def _(n):
            cols = pl.ds(pl.multiple_of(n * tile, tile), tile)
            value = None
            for m in range(count):
                depth = left_s.shape[2]
                per = w_s.shape[2] // depth
                side = slice((m % per) * depth, (m % per + 1) * depth)
                term = dot32(left_s[m, at, :], w_s[m // per, cols, side], contract_last)
                value = term if value is None else value + term
            store(cols, value)

    def own(which):
        def store(cols, value):
            own_s[pl.ds(which * half, half), cols] = value

        return store

    def layer_moves():
        deep = x1_s.shape[1]
        at = lambda i: pl.ds(pl.multiple_of(i * deep, deep), deep)

        def loads(i):
            return [pltpu.make_async_copy(x1_hbm.at[at(i)], x1_s.at[i % 2], in_sem.at[i % 2, 0])] + [
                pltpu.make_async_copy(ref.at[at(i)], mlp_s.at[i % 2, n], in_sem.at[i % 2, 1 + n])
                for n, ref in enumerate(mlp_hbm)
            ]

        def stores(i):
            return [pltpu.make_async_copy(layer_s.at[i % 2], layer_hbm.at[at(i)], layer_sem.at[i % 2])]

        def work(i):
            b = i % 2
            total = mlp_s[b, 0].astype(jnp.float32) + mlp_s[b, 1].astype(jnp.float32) + mlp_s[b, 2].astype(jnp.float32)
            layer_s[b] = (x1_s[b] + live_ref[at(i), :] * total).astype(low_type)

        flow(0, rows // deep, loads, work, stores)

    def fill_one():
        partial(0, 0, own(0))
        partial(0, 1, own(1))

    def fill_two():
        layer_moves()

    copies = exchange(rows, partial, bufs, send, recv, fill_one, fill_two)
    finish_back(copies, rows, 0, x_ref, base_ref, own_s, None, norm_ref, bufs[5], bufs[6], dx_ref, None, gain_ref, shift_ref, gain_s, shift_s)


def first_scatter(lefts, w, x, base, norm, live, x1, mlp_parts):
    rows, model = x.shape
    count = len(lefts)
    total, part = lefts[0].shape
    vmem = pl.BlockSpec(memory_space=pltpu.VMEM)
    line = jax.ShapeDtypeStruct((1, model), jnp.float32)
    deep = 64
    both = lambda block, n, t: pltpu.VMEM((2,) + ((n,) if n else ()) + block, t)
    return pl.pallas_call(
        functools.partial(first_scatter_kernel, count),
        in_specs=[ANY] * (count + 1) + [vmem] * 4 + [ANY] * 4,
        out_specs=[vmem] * 3 + [ANY],
        out_shape=[jax.ShapeDtypeStruct((rows, model), low_type), line, line, jax.ShapeDtypeStruct((rows, model), low_type)],
        scratch_shapes=exchange_scratch(rows, model)
        + [
            pltpu.VMEM((rows, model), jnp.float32),
            pltpu.VMEM((count, total, part), low_type),
            pltpu.VMEM((3,) + w.shape[1:], low_type),
            both((deep, model), 0, jnp.float32),
            both((deep, model), 3, low_type),
            both((deep, model), 0, low_type),
            pltpu.SemaphoreType.DMA((2 * count + 1,)),
            pltpu.SemaphoreType.DMA((2, 4)),
            pltpu.SemaphoreType.DMA((2,)),
        ],
        cost_estimate=cost(10**13, 30 * rows * model),
        compiler_params=pltpu.CompilerParams(vmem_limit_bytes=62 * MIB, collective_id=6, has_side_effects=True),
        name="first_scatter",
    )(*lefts, w, x, base, norm, live, x1, *mlp_parts)


def adam_rest_kernel(low_ref, *refs):
    part = pl.program_id(0)
    last = pl.num_programs(0) - 1
    qkv_in, out_in, qkv_out, out_out = refs[:3], refs[3:6], refs[6:10], refs[10:]

    @pl.when(part < last)
    def _():
        gradient = low_ref[...].astype(jnp.float32)
        qkv_out[0][...] = gradient
        results = adamw_update(qkv_in[0][...], gradient, qkv_in[1][...], qkv_in[2][...], weight_decay)
        for ref, value in zip(qkv_out[1:], results):
            ref[...] = value

    @pl.when(part == last)
    def _():
        gradient = low_ref[0].astype(jnp.float32).T
        out_out[0][...] = gradient
        results = adamw_update(out_in[0][...], gradient, out_in[1][...], out_in[2][...], weight_decay)
        for ref, value in zip(out_out[1:], results):
            ref[...] = value


def adam_rest(low, qkv, out):
    count, depth, width = low.shape
    stack = lambda k: (jnp.minimum(k, count - 2), 0, 0)
    three = pl.BlockSpec((1, depth, width), stack)
    flat = pl.BlockSpec(out[0].shape, lambda k: (0, 0))
    like = lambda value: jax.ShapeDtypeStruct(value.shape, jnp.float32)
    return pl.pallas_call(
        adam_rest_kernel,
        grid=(count,),
        in_specs=[pl.BlockSpec((1, depth, width), lambda k: (k, 0, 0))] + [three] * 3 + [flat] * 3,
        out_specs=[three] * 4 + [flat] * 4,
        out_shape=[like(qkv[0])] * 4 + [like(out[0])] * 4,
        cost_estimate=cost(30 * count * depth * width, 30 * count * depth * width),
        compiler_params=params(60),
        name="adam_rest",
    )(low, *qkv, *out)


def gather_gate_up_kernel(count, h_ref, w_hbm, *rest):
    blocks, (all_ref, act_ref, one_ref, two_ref, grad_ref) = rest[:count], rest[count : count + 5]
    w_s, all_s, stage, acc, turned, dm_s, send, recv, local, h_sem, out_sem, dm_sem = rest[count + 5 :]
    near_x, near_y = neighbours()
    half = h_ref.shape[0] // 2
    own = pltpu.make_async_copy(h_ref, all_s.at[pl.ds(0, 2 * half)], local.at[0])
    own.start()
    weights = pltpu.make_async_copy(w_hbm, w_s, local.at[1])
    weights.start()
    greet(near_x, near_y)
    own.wait()
    copies = square_copies(all_s, half, send, recv)
    for c in copies[:4]:
        c.start()
    acc[...] = jnp.zeros_like(acc)
    weights.wait()
    in_order = [blocks[n] for n in arrival]
    tile = 512

    def outs(buf, row):
        return [
            pltpu.make_async_copy(stage.at[buf, n], ref.at[pl.ds(row, half)], out_sem.at[buf, n])
            for n, ref in enumerate((act_ref, one_ref, two_ref))
        ]

    def keep(i, row):
        return pltpu.make_async_copy(all_s.at[pl.ds(row, half)], all_ref.at[pl.ds(row, half)], h_sem.at[i])

    def step(i, carry):
        await_slot(i, copies)
        row = pl.multiple_of(arrival_slot(i) * half, half)
        buf = i % 2
        keep(i, row).start()

        @pl.when(i >= 2)
        def _():
            for c in outs(buf, row):
                c.wait()

        h = all_s[pl.ds(row, half), :]
        gate = dot32(h, w_s[0])
        up = dot32(h, w_s[1])
        sig = 1.0 / (1.0 + jnp.exp(-gate))
        silu = gate * sig
        act = (silu * up).astype(low_type)
        stage[buf, 0] = act
        stage[buf, 1] = (up * sig * (1.0 + gate * (1.0 - sig))).astype(low_type)
        stage[buf, 2] = silu.astype(low_type)
        for c in outs(buf, row):
            c.start()
        turned[...] = act.T
        fetch_next(i, in_order, dm_s, dm_sem)

        @pl.loop(0, acc.shape[1] // tile)
        def _(n):
            cols = pl.ds(pl.multiple_of(n * tile, tile), tile)
            acc[:, cols] += dot32(turned[...], dm_s[buf, :, cols])

        return carry

    lax.fori_loop(0, 8, step, 0)
    for buf in (0, 1):
        for c in outs(buf, 0):
            c.wait()
    for i in range(8):
        keep(i, 0).wait()
    for c in copies:
        c.wait_send()
    depth = acc.shape[0]
    strip = depth // 8

    @pl.loop(0, 8)
    def _(n):
        at = pl.ds(pl.multiple_of(n * strip, strip), strip)
        all_s[at, :] = acc[at, :].astype(low_type)

    last = pltpu.make_async_copy(all_s.at[pl.ds(0, depth)], grad_ref, local.at[0])
    last.start()
    last.wait()


def gather_gate_up(h, w, dm_blocks):
    rows, model = h.shape
    depth = w.shape[2]
    total = 4 * rows
    half = rows // 2
    deep = jax.ShapeDtypeStruct((total, depth), low_type)
    return pl.pallas_call(
        functools.partial(gather_gate_up_kernel, len(dm_blocks)),
        in_specs=[ANY] * (2 + len(dm_blocks)),
        out_specs=[ANY] * 5,
        out_shape=[
            jax.ShapeDtypeStruct((total, model), low_type),
            deep,
            deep,
            deep,
            jax.ShapeDtypeStruct((depth, model), low_type),
        ],
        scratch_shapes=[
            pltpu.VMEM(w.shape, low_type),
            pltpu.VMEM((total, model), low_type),
            pltpu.VMEM((2, 3, half, depth), low_type),
            pltpu.VMEM((depth, model), jnp.float32),
            pltpu.VMEM((depth, half), low_type),
            pltpu.VMEM((2, half, model), low_type),
            pltpu.SemaphoreType.DMA((6,)),
            pltpu.SemaphoreType.DMA((6,)),
            pltpu.SemaphoreType.DMA((2,)),
            pltpu.SemaphoreType.DMA((8,)),
            pltpu.SemaphoreType.DMA((2, 3)),
            pltpu.SemaphoreType.DMA((2,)),
        ],
        cost_estimate=cost(6 * total * model * depth, 4 * model * depth + 4 * total * model + 6 * total * depth),
        compiler_params=pltpu.CompilerParams(vmem_limit_bytes=62 * MIB, collective_id=1, has_side_effects=True),
        name="gather_gate_up",
    )(h, w, *dm_blocks)


def small_kernel(nd, nt, x_ref, o_ref, groups, partial, shares, send, recv, send_t, recv_t):
    d, t = lax.axis_index("dp"), lax.axis_index("tensor")
    width = o_ref.shape[1]
    barrier = pltpu.get_barrier_semaphore()
    for k in range(1, nd):
        pl.semaphore_signal(barrier, inc=1, device_id={"dp": lax.rem(d + k, nd)}, device_id_type=MESH)
    for k in range(1, nt):
        pl.semaphore_signal(barrier, inc=1, device_id={"tensor": lax.rem(t + k, nt)}, device_id_type=MESH)
    pl.semaphore_wait(barrier, nd + nt - 2)
    copies = []
    for k in range(1, nd):
        peer = lax.rem(d + k, nd)
        c = pltpu.make_async_remote_copy(
            src_ref=x_ref.at[:, pl.ds(pl.multiple_of(peer * width, width), width)],
            dst_ref=groups.at[k],
            send_sem=send.at[k],
            recv_sem=recv.at[k],
            device_id={"dp": peer},
            device_id_type=MESH,
        )
        c.start()
        copies.append(c)
    total = x_ref[:, pl.ds(pl.multiple_of(d * width, width), width)]
    for k in range(1, nd):
        copies[k - 1].wait_recv()
        total += groups[k]
    partial[...] = total
    shares[t] = total
    for k in range(1, nt):
        c = pltpu.make_async_remote_copy(
            src_ref=partial,
            dst_ref=shares.at[t],
            send_sem=send_t.at[k],
            recv_sem=recv_t.at[k],
            device_id={"tensor": lax.rem(t + k, nt)},
            device_id_type=MESH,
        )
        c.start()
        copies.append(c)
    for k in range(1, nt):
        copies[nd - 2 + k].wait_recv()
    total = shares[0]
    for k in range(1, nt):
        total += shares[k]
    o_ref[...] = total
    for c in copies:
        c.wait_send()


def sum_small(x):
    nd, nt = lax.axis_size("dp"), lax.axis_size("tensor")
    rows, model = x.shape
    width = model // nd
    vmem = pl.BlockSpec(memory_space=pltpu.VMEM)
    return pl.pallas_call(
        functools.partial(small_kernel, nd, nt),
        in_specs=[vmem],
        out_specs=vmem,
        out_shape=jax.ShapeDtypeStruct((rows, width), jnp.float32),
        scratch_shapes=[
            pltpu.VMEM((nd, rows, width), jnp.float32),
            pltpu.VMEM((rows, width), jnp.float32),
            pltpu.VMEM((nt, rows, width), jnp.float32),
            pltpu.SemaphoreType.DMA((nd,)),
            pltpu.SemaphoreType.DMA((nd,)),
            pltpu.SemaphoreType.DMA((nt,)),
            pltpu.SemaphoreType.DMA((nt,)),
        ],
        cost_estimate=cost(rows * model, 8 * rows * model),
        compiler_params=pltpu.CompilerParams(collective_id=2, has_side_effects=True),
        name="sum_small",
    )(x)


def body(
    tokens,
    out_grad,
    lengths,
    norm_gain,
    norm_bias,
    qkv_weight,
    qkv_bias,
    out_weight,
    gate_up_weight,
    down_weight,
    first_norm_gain,
    first_norm_bias,
    first_qkv_weight,
    first_qkv_bias,
    first_out_weight,
    first_gate_up_weight,
    first_down_weight,
    second_norm_gain,
    second_norm_bias,
    second_qkv_weight,
    second_qkv_bias,
    second_out_weight,
    second_gate_up_weight,
    second_down_weight,
):
    slots = lax.axis_size("tensor")
    rank = lax.axis_index("tensor")
    own_rows = tokens.shape[0]
    group_rows = own_rows * slots
    width = out_weight.shape[0]
    order = rank if square(slots) else jnp.zeros_like(rank)

    chunk = jnp.bitwise_xor(jnp.arange(slots, dtype=jnp.int32), order)
    row_index = (chunk[:, None] * own_rows + jnp.arange(own_rows, dtype=jnp.int32)[None, :]).reshape(-1)
    seq_start, _ = layout(lengths[0], row_index)
    position = row_index - seq_start
    own_index = rank * own_rows + jnp.arange(own_rows, dtype=jnp.int32)
    live = layout(lengths[0], own_index)[1][:, None]
    block_start, _ = layout(lengths[0], jnp.arange(group_rows // BLOCK, dtype=jnp.int32) * BLOCK)
    table = jnp.concatenate([order.reshape(1).astype(jnp.int32), block_start // BLOCK])
    starts = seq_start[None, :]
    small_low = jnp.concatenate([norm_gain, norm_bias, qkv_bias, qkv_bias[:1]], axis=0).astype(low_type)
    own_bias = lambda full: lax.dynamic_slice_in_dim(full[4:7], rank * width, width, 1)[:, None, :]

    if square(slots):
        attn_low = jnp.concatenate([qkv_weight, out_weight.T[None]], axis=0).astype(low_type)
        attn_full = lax.all_gather(attn_low, "dp", axis=1, tiled=True)
        lane = jnp.arange(PAIR, dtype=jnp.int32) % (ROT // 2)
        inverse = jnp.power(rope_base, -lane.astype(jnp.float32) * (2.0 / ROT))[None, :]
        position = position.astype(jnp.float32).reshape(-1, 256)
        h1, small_full, *tables, dm_top, dm_end, gate_up_low = gather_norm(
            tokens, small_low.astype(jnp.float32), position, inverse, out_grad, live, gate_up_weight
        )
        norm = small_full[:4]
        gate_up_full = lax.all_gather(after(gate_up_low, attn_full), "dp", axis=1, tiled=True)
        dm_first, dm_rest = gather_rows(dm_top, dm_end)
        q, k, v, kt, vt = qkv_all(h1, attn_full, own_bias(small_full), tables)

        o_a, lse_a = attn_fwd(0, slots, table, q, k, vt, starts)
        dm_far = dm_rest(o_a)
        o_b, lse_b = attn_fwd(1, slots, table, after(q, o_a, *dm_first), k, vt, starts)
        o_b = after(o_b, *dm_far)
        dm_blocks = dm_first + dm_far

        x1, h2_own = out_scatter(o_a, o_b, attn_full, tokens, live, norm)
        down_low = after(down_weight.astype(low_type), gate_up_full, h2_own)
        down_full = lax.all_gather(down_low, "dp", axis=1, tiled=True)
        h2, act, slope_gate, slope_up, grad_down = gather_gate_up(h2_own, gate_up_full, dm_blocks)
        grad_down_own = lax.psum_scatter(after(grad_down, down_full), "dp", scatter_dimension=1, tiled=True)

        grad_gate, dup, dx1, dattn_own, gain_two, shift_two = hidden_scatter(
            dm_blocks, slope_gate, slope_up, down_full, gate_up_full, h2, x1, out_grad, live, norm
        )
        grad_gate = after(grad_gate, grad_down_own)
        grad_gate_own = lax.psum_scatter(grad_gate, "dp", scatter_dimension=0, tiled=True)

        do, grad_out, mlp, grad_up = gather_do(dattn_own, act, h2, dup, o_a, o_b, attn_full, down_full)
        grad_up = after(grad_up, grad_gate_own)
        grad_up_own = lax.psum_scatter(grad_up, "dp", scatter_dimension=0, tiled=True)
        mlp_rows, mlp = mlp, [mlp[j * own_rows : (j + 1) * own_rows] for j in range(slots)]
        mlp_first = scatter_first(mlp)
        *back_a, grad_down_full, down_one, down_two, down_three = attn_bwd(
            0, slots, table, q, do, o_a, k, v, kt, starts, lse_a, tables,
            grad_down_own, (down_weight, first_down_weight, second_down_weight),
        )
        down_step = (grad_down_full, down_one, down_two, down_three)
        hidden = (gate_up_weight, first_gate_up_weight, second_gate_up_weight)
        mlp_parts = scatter_last(mlp, [after(part, back_a[0]) for part in mlp_first])
        results = attn_bwd(
            1, slots, table, q, after(do, back_a[0], *mlp_first), o_b, k, v, kt, starts, lse_b, tables, grad_gate_own, hidden
        )
        back_b, begun = results[:3], results[3:]
        dlin = [side for pair in zip(back_a, back_b) for side in pair]
        grad_rest, bias_local, *hidden_step = qkv_grad(h1, dlin, grad_out, grad_up_own, hidden, begun)
        late = [after(dlin[0], grad_rest, *mlp_parts[1:])] + dlin[1:]
        input_grad, gain_one, shift_one, layer_out = first_scatter(
            late, attn_full, tokens, dx1, norm, live, x1, [mlp_rows] + mlp_parts[1:]
        )
        grad_rest = after(grad_rest, grad_up_own)
        grad_rest_own = lax.psum_scatter(grad_rest, "dp", scatter_dimension=1, tiled=True)
        rest_step = adam_rest(
            grad_rest_own,
            (qkv_weight, first_qkv_weight, second_qkv_weight),
            (out_weight, first_out_weight, second_out_weight),
        )
        qkv_step, out_step = rest_step[:4], rest_step[4:]
    else:
        everyone = lambda value: lax.all_gather(value, "tensor", axis=0, tiled=True)
        scatter = lambda value, axis, at: lax.psum_scatter(value.astype(low_type), axis, scatter_dimension=at, tiled=True)
        small_full = lax.all_gather(small_low, "dp", axis=1, tiled=True).astype(jnp.float32)
        qkv_full, out_full, gate_up_full, down_full = (
            lax.all_gather(w.astype(low_type), "dp", axis=1, tiled=True)
            for w in (qkv_weight, out_weight, gate_up_weight, down_weight)
        )
        gain_rows, shift_rows = small_full[0:2], small_full[2:4]
        rows_in, cotangent = tokens.astype(jnp.float32), out_grad.astype(jnp.float32)
        tables = rotary_tables(position)
        h1 = everyone(layer_norm(rows_in, gain_rows[0], shift_rows[0]).astype(low_type))
        q, k, v, kt, vt = qkv_all(h1, qkv_full, own_bias(small_full), tables)
        o_a, lse_a = attn_fwd(0, slots, table, q, k, vt, starts)
        o_b, lse_b = attn_fwd(1, slots, table, q, k, vt, starts)
        o = jnp.concatenate([o_a, o_b], axis=1)
        x1 = rows_in + live * scatter(dot32(o, out_full), "tensor", 0).astype(jnp.float32)
        h2 = everyone(layer_norm(x1, gain_rows[1], shift_rows[1]).astype(low_type))
        gate, up = dot32(h2, gate_up_full[0]), dot32(h2, gate_up_full[1])
        sig = 1.0 / (1.0 + jnp.exp(-gate))
        act = (gate * sig * up).astype(low_type)
        mlp_rows = scatter(dot32(act, down_full), "tensor", 0).astype(jnp.float32)
        layer_out = (x1 + live * mlp_rows).astype(low_type)
        dm = everyone((cotangent * live).astype(low_type))
        da = dot32(dm, down_full, contract_last)
        dgate = (da * up * sig * (1.0 + gate * (1.0 - sig))).astype(low_type)
        dup = (da * gate * sig).astype(low_type)
        grad_down_own = scatter(dot32(act, dm, contract_first), "dp", 1)
        grad_gate_up = jnp.stack([dot32(h2, dgate, contract_first), dot32(h2, dup, contract_first)])
        grad_gate_up_own = scatter(grad_gate_up, "dp", 1)
        dh2 = dot32(dgate, gate_up_full[0], contract_last) + dot32(dup, gate_up_full[1], contract_last)
        dh2 = scatter(dh2, "tensor", 0).astype(jnp.float32)
        back, gain_two, shift_two = jax.vjp(layer_norm, x1, gain_rows[1], shift_rows[1])[1](dh2)
        dx1 = cotangent + back
        dattn = everyone((dx1 * live).astype(low_type))
        do = dot32(dattn, out_full, contract_last).astype(low_type)
        grad_out = dot32(dattn, o, contract_first).astype(low_type)
        back_a = attn_bwd(0, slots, table, q, do, o_a, k, v, kt, starts, lse_a, tables)
        back_b = attn_bwd(1, slots, table, q, do, o_b, k, v, kt, starts, lse_b, tables)
        dlin = [side for pair in zip(back_a, back_b) for side in pair]
        grad_rest, bias_local = qkv_grad(h1, dlin, grad_out)
        grad_rest_own = scatter(grad_rest, "dp", 1)
        grad_qkv_own, grad_out_own = grad_rest_own[:3], grad_rest_own[3].T
        dh1 = sum(
            dot32(jnp.concatenate(dlin[2 * n : 2 * n + 2], axis=1), qkv_full[n], contract_last) for n in range(3)
        )
        dh1 = scatter(dh1, "tensor", 0).astype(jnp.float32)
        back, gain_one, shift_one = jax.vjp(layer_norm, rows_in, gain_rows[0], shift_rows[0])[1](dh1)
        input_grad = (dx1 + back).astype(low_type)
        gain_one, gain_two, shift_one, shift_two = (
            value[None, :] for value in (gain_one, gain_two, shift_one, shift_two)
        )

        def whole_step(gradient, *held):
            gradient = gradient.astype(jnp.float32)
            return (gradient,) + adamw_update(held[0], gradient, held[1], held[2], weight_decay)

        qkv_step = whole_step(grad_qkv_own, qkv_weight, first_qkv_weight, second_qkv_weight)
        out_step = whole_step(grad_out_own, out_weight, first_out_weight, second_out_weight)
        hidden_step = whole_step(grad_gate_up_own, gate_up_weight, first_gate_up_weight, second_gate_up_weight)
        down_step = whole_step(grad_down_own, down_weight, first_down_weight, second_down_weight)

    bias_placed = lax.dynamic_update_slice(
        jnp.zeros((3, small_full.shape[1]), jnp.float32), bias_local, (jnp.int32(0), rank * width)
    )
    small_local = jnp.concatenate([gain_one, gain_two, shift_one, shift_two, bias_placed, bias_placed[:1]], axis=0)
    small_own = sum_small(small_local)

    def small_step(gradient, *held):
        return (gradient,) + adamw_update(held[0], gradient, held[1], held[2], 0.0)

    gain_step = small_step(small_own[0:2], norm_gain, first_norm_gain, second_norm_gain)
    shift_step = small_step(small_own[2:4], norm_bias, first_norm_bias, second_norm_bias)
    bias_step = small_step(small_own[4:7], qkv_bias, first_qkv_bias, second_qkv_bias)
    steps = (gain_step, shift_step, qkv_step, bias_step, out_step, hidden_step, down_step)
    return (layer_out, input_grad) + tuple(step[n] for n in range(4) for step in steps)


def solution(mesh):
    return jax.shard_map(
        body,
        mesh=mesh,
        in_specs=(
            P(("dp", "tensor"), None),
            P(("dp", "tensor"), None),
            P("dp", None),
            P(None, "dp"),
            P(None, "dp"),
            P(None, "dp", "tensor"),
            P(None, "dp"),
            P("tensor", "dp"),
            P(None, "dp", "tensor"),
            P("tensor", "dp"),
            P(None, "dp"),
            P(None, "dp"),
            P(None, "dp", "tensor"),
            P(None, "dp"),
            P("tensor", "dp"),
            P(None, "dp", "tensor"),
            P("tensor", "dp"),
            P(None, "dp"),
            P(None, "dp"),
            P(None, "dp", "tensor"),
            P(None, "dp"),
            P("tensor", "dp"),
            P(None, "dp", "tensor"),
            P("tensor", "dp"),
        ),
        out_specs=(
            P(("dp", "tensor"), None),
            P(("dp", "tensor"), None),
            P(None, "dp"),
            P(None, "dp"),
            P(None, "dp", "tensor"),
            P(None, "dp"),
            P("tensor", "dp"),
            P(None, "dp", "tensor"),
            P("tensor", "dp"),
            P(None, "dp"),
            P(None, "dp"),
            P(None, "dp", "tensor"),
            P(None, "dp"),
            P("tensor", "dp"),
            P(None, "dp", "tensor"),
            P("tensor", "dp"),
            P(None, "dp"),
            P(None, "dp"),
            P(None, "dp", "tensor"),
            P(None, "dp"),
            P("tensor", "dp"),
            P(None, "dp", "tensor"),
            P("tensor", "dp"),
            P(None, "dp"),
            P(None, "dp"),
            P(None, "dp", "tensor"),
            P(None, "dp"),
            P("tensor", "dp"),
            P(None, "dp", "tensor"),
            P("tensor", "dp"),
        ),
        check_vma=False,
    )
```

```python
import functools

import jax
import jax.numpy as jnp
from jax import lax
from jax.experimental import pallas as pl
from jax.experimental.pallas import tpu as pltpu
from jax.sharding import PartitionSpec as P

HEAD_DIM = 64
ROT = 16
PAIR = 2 * HEAD_DIM
BLOCK = 256

norm_eps = 1e-05
rope_base = 10000.0
beta_one = 0.9
beta_two = 0.95
adam_eps = 1e-08
learn_rate = 0.01
weight_decay = 0.1
step_count = 10.0
masked_score = -1e30
contract_last = (((1,), (1,)), ((), ()))
contract_first = (((0,), (0,)), ((), ()))
low_type = jnp.bfloat16
MIB = 2**20


def layout(seq_lengths, row_index):
    slot = jnp.arange(seq_lengths.shape[0])
    seq_ends = jnp.sum(
        jnp.where(slot[:, None] <= slot[None, :], seq_lengths[:, None], 0), axis=0
    )
    passed = row_index[:, None] >= seq_ends[None, :]
    seq_start = jnp.sum(jnp.where(passed, seq_lengths[None, :], 0), axis=1)
    live_rows = (row_index < jnp.sum(seq_lengths)).astype(jnp.float32)
    return (seq_start, live_rows)


def rotary_tables(position):
    half_rot = ROT // 2
    lane = jnp.arange(PAIR, dtype=jnp.int32) % HEAD_DIM
    powers = (lane % half_rot).astype(jnp.float32) * (2.0 / ROT)
    inverse = jnp.power(rope_base, -powers)
    angles = position.astype(jnp.float32)[:, None] * inverse[None, :]
    cos_part, sine_part = jnp.cos(angles), jnp.sin(angles)
    lane = lane[None, :]
    keep = jnp.where(lane < ROT, cos_part, 1.0)
    above = jnp.where(lane < half_rot, -sine_part, 0.0)
    below = jnp.where((lane >= half_rot) & (lane < ROT), sine_part, 0.0)
    return (keep, above, below)


def dot32(a, b, dims=None):
    if dims is None:
        return jnp.dot(a, b, preferred_element_type=jnp.float32)
    return lax.dot_general(a, b, dims, preferred_element_type=jnp.float32)


def turn(values, keep, above, below):
    up = pltpu.roll(values, PAIR - ROT // 2, 1)
    down = pltpu.roll(values, ROT // 2, 1)
    return values * keep + up * above + down * below


def turn_back(values, keep, above, below):
    up = pltpu.roll(values, PAIR - ROT // 2, 1)
    down = pltpu.roll(values, ROT // 2, 1)
    return values * keep - up * above - down * below


def adamw_update(weight_now, gradient, moment_one, moment_two, decay_rate):
    moment_one = beta_one * moment_one + (1.0 - beta_one) * gradient
    moment_two = beta_two * moment_two + (1.0 - beta_two) * gradient * gradient
    scaled_one = moment_one / (1.0 - beta_one**step_count)
    scaled_two = moment_two / (1.0 - beta_two**step_count)
    change = scaled_one / (jnp.sqrt(scaled_two) + adam_eps) + decay_rate * weight_now
    return (-learn_rate * change, moment_one, moment_two)


def cost(flops, moved, exps=0):
    return pl.CostEstimate(flops=int(flops) // 16, bytes_accessed=int(moved) // 16, transcendentals=int(exps) // 16)


def params(limit):
    return pltpu.CompilerParams(vmem_limit_bytes=limit * MIB)


ANY = pl.BlockSpec(memory_space=pl.ANY)


def layer_norm(values, gain_row, shift_row):
    center = values - jnp.mean(values, axis=-1, keepdims=True)
    spread = jnp.mean(center * center, axis=-1, keepdims=True)
    return center * lax.rsqrt(spread + norm_eps) * gain_row + shift_row


def qkv_kernel(scale, h_ref, w_ref, bias_ref, keep_ref, above_ref, below_ref, q_ref, k_ref, v_ref, kt_ref, vt_ref):
    h = h_ref[...]
    keep, above, below = keep_ref[...], above_ref[...], below_ref[...]
    width = q_ref.shape[1]
    lin = dot32(h, w_ref[0]) + bias_ref[0]
    for c in range(0, width, PAIR):
        u = turn(lin[:, c : c + PAIR], keep, above, below)
        q_ref[:, c : c + PAIR] = (u.astype(low_type) * scale).astype(low_type)
    lin = dot32(h, w_ref[1]) + bias_ref[1]
    for c in range(0, width, PAIR):
        u = turn(lin[:, c : c + PAIR], keep, above, below)
        k_ref[:, c : c + PAIR] = u.astype(low_type)
        kt_ref[c : c + PAIR, :] = u.T.astype(low_type)
    lin = dot32(h, w_ref[2]) + bias_ref[2]
    v_ref[...] = lin.astype(low_type)
    vt_ref[...] = lin.T.astype(low_type)


def qkv_all(h, w, bias, tables):
    total, model = h.shape
    rows = 256
    width = w.shape[2]
    row = lambda n: pl.BlockSpec((rows, n), lambda i: (i, 0))
    col = pl.BlockSpec((width, rows), lambda i: (0, i))
    flat = jax.ShapeDtypeStruct((total, width), low_type)
    turned = jax.ShapeDtypeStruct((width, total), low_type)
    return pl.pallas_call(
        functools.partial(qkv_kernel, HEAD_DIM ** (-0.5)),
        grid=(total // rows,),
        in_specs=[
            row(model),
            pl.BlockSpec((3,) + w.shape[1:], lambda i: (0, 0, 0), pipeline_mode=pl.Buffered(1)),
            pl.BlockSpec(bias.shape, lambda i: (0, 0, 0)),
            row(PAIR),
            row(PAIR),
            row(PAIR),
        ],
        out_specs=[row(width), row(width), row(width), col, col],
        out_shape=[flat, flat, flat, turned, turned],
        cost_estimate=cost(6 * total * model * width, 6 * model * width + 10 * total * model),
        compiler_params=params(60),
        name="qkv",
    )(h, w, bias, *tables)


def place(block, rank, per):
    return jnp.bitwise_xor(block // per, rank) * per + block % per


def attn_fwd_kernel(per, table_ref, q_ref, k_ref, vt_ref, start_ref, o_ref, lse_ref, m_s, l_s, acc_s):
    i = pl.program_id(0)
    rank = table_ref[0]
    heads = q_ref.shape[1] // HEAD_DIM
    first = lax.broadcasted_iota(jnp.int32, (BLOCK, PAIR), 1) < HEAD_DIM
    queries = []
    for h in range(heads):
        pair = q_ref[:, (h // 2) * PAIR : (h // 2 + 1) * PAIR]
        keep = first if h % 2 == 0 else jnp.logical_not(first)
        queries.append(jnp.where(keep, pair, jnp.zeros_like(pair)))
    m_s[...] = jnp.full_like(m_s, -jnp.inf)
    l_s[...] = jnp.zeros_like(l_s)
    acc_s[...] = jnp.zeros_like(acc_s)
    start = start_ref[...]
    row = i * BLOCK + lax.broadcasted_iota(jnp.int32, (BLOCK, BLOCK), 1)

    def step(kb, carry):
        col = kb * BLOCK + lax.broadcasted_iota(jnp.int32, (BLOCK, BLOCK), 0)
        bias = jnp.where((col >= start) & (col <= row), 0.0, masked_score)
        at = pl.ds(pl.multiple_of(place(kb, rank, per) * BLOCK, BLOCK), BLOCK)
        scores = [
            dot32(k_ref[at, (h // 2) * PAIR : (h // 2 + 1) * PAIR], queries[h], contract_last) for h in range(heads)
        ]
        probs, alphas = [], []
        for h in range(heads):
            s = scores[h] + bias
            m_old = m_s[h : h + 1, :]
            m_new = jnp.maximum(m_old, jnp.max(s, axis=0, keepdims=True))
            alpha = jnp.exp(m_old - m_new)
            p = jnp.exp(s - m_new)
            l_s[h : h + 1, :] = l_s[h : h + 1, :] * alpha + jnp.sum(p, axis=0, keepdims=True)
            m_s[h : h + 1, :] = m_new
            probs.append(p.astype(low_type))
            alphas.append(alpha)
        for h in range(heads):
            own = slice(h * HEAD_DIM, (h + 1) * HEAD_DIM)
            acc_s[own, :] = acc_s[own, :] * alphas[h] + dot32(vt_ref[own, at], probs[h])
        return carry

    lax.fori_loop(table_ref[1 + i], i + 1, step, 0)
    for h in range(heads):
        own = slice(h * HEAD_DIM, (h + 1) * HEAD_DIM)
        acc_s[own, :] = acc_s[own, :] / l_s[h : h + 1, :]
    o_ref[...] = acc_s[...].T.astype(low_type)
    lse_ref[0] = m_s[...] + jnp.log(l_s[...])


def attn_fwd(half, slots, table, q, k, vt, start):
    rows, width = q.shape
    part = width // 2
    heads = part // HEAD_DIM
    count = rows // BLOCK
    per = rows // slots // BLOCK
    at = lambda i, t: place(i, t[0], per)
    return pl.pallas_call(
        functools.partial(attn_fwd_kernel, per),
        grid_spec=pltpu.PrefetchScalarGridSpec(
            num_scalar_prefetch=1,
            grid=(count,),
            in_specs=[
                pl.BlockSpec((BLOCK, part), lambda i, t: (at(i, t), half)),
                pl.BlockSpec((rows, part), lambda i, t: (0, half)),
                pl.BlockSpec((part, rows), lambda i, t: (half, 0)),
                pl.BlockSpec((1, BLOCK), lambda i, t: (0, at(i, t))),
            ],
            out_specs=[
                pl.BlockSpec((BLOCK, part), lambda i, t: (at(i, t), 0)),
                pl.BlockSpec((1, heads, BLOCK), lambda i, t: (at(i, t), 0, 0)),
            ],
            scratch_shapes=[
                pltpu.VMEM((heads, BLOCK), jnp.float32),
                pltpu.VMEM((heads, BLOCK), jnp.float32),
                pltpu.VMEM((part, BLOCK), jnp.float32),
            ],
        ),
        out_shape=[
            jax.ShapeDtypeStruct((rows, part), low_type),
            jax.ShapeDtypeStruct((count, heads, BLOCK), jnp.float32),
        ],
        cost_estimate=cost(rows * rows, rows * part),
        compiler_params=params(60),
        name="attn_fwd",
    )(table, q, k, vt, start)


def adam_blocks(low_ref, in_refs, out_refs):
    gradient = low_ref[...].astype(jnp.float32).reshape(out_refs[0].shape)
    results = adamw_update(in_refs[0][...], gradient, in_refs[1][...], in_refs[2][...], weight_decay)
    out_refs[0][...] = gradient
    for ref, value in zip(out_refs[1:], results):
        ref[...] = value


def attn_bwd_kernel(per, adam, table_ref, q_ref, do_ref, o_ref, k_ref, v_ref, kt_ref, start_ref, lse_ref,
                    keep_ref, above_ref, below_ref, *rest):
    (dq_ref, dk_ref, dv_ref), (dq_s, dk_s, dv_s) = rest[4 * adam : 4 * adam + 3], rest[-3:]
    if adam:
        adam_blocks(rest[0], rest[1:4], rest[7:11])
    i = pl.program_id(0)
    rank = table_ref[0]
    width = q_ref.shape[1]
    heads = width // HEAD_DIM
    first = lax.broadcasted_iota(jnp.int32, (BLOCK, PAIR), 1) < HEAD_DIM

    @pl.when(i == 0)
    def _():
        dk_s[...] = jnp.zeros_like(dk_s)
        dv_s[...] = jnp.zeros_like(dv_s)

    dq_s[...] = jnp.zeros_like(dq_s)
    queries, cotangents, inner = [], [], []
    product = (do_ref[...].astype(jnp.float32) * o_ref[...].astype(jnp.float32)).T
    for h in range(heads):
        cols = slice((h // 2) * PAIR, (h // 2 + 1) * PAIR)
        keep = first if h % 2 == 0 else jnp.logical_not(first)
        pair = q_ref[:, cols]
        queries.append(jnp.where(keep, pair, jnp.zeros_like(pair)))
        pair = do_ref[:, cols]
        cotangents.append(jnp.where(keep, pair, jnp.zeros_like(pair)))
        inner.append(jnp.sum(product[h * HEAD_DIM : (h + 1) * HEAD_DIM, :], axis=0, keepdims=True))
    start = start_ref[...]
    row = i * BLOCK + lax.broadcasted_iota(jnp.int32, (BLOCK, BLOCK), 1)

    def step(kb, carry):
        col = kb * BLOCK + lax.broadcasted_iota(jnp.int32, (BLOCK, BLOCK), 0)
        bias = jnp.where((col >= start) & (col <= row), 0.0, masked_score)
        at = pl.ds(pl.multiple_of(place(kb, rank, per) * BLOCK, BLOCK), BLOCK)
        raw, grads = [], []
        for h in range(heads):
            cols = slice((h // 2) * PAIR, (h // 2 + 1) * PAIR)
            raw.append(dot32(k_ref[at, cols], queries[h], contract_last))
            grads.append(dot32(v_ref[at, cols], cotangents[h], contract_last))
        probs, scores = [], []
        for h in range(heads):
            p = jnp.exp(raw[h] + bias - lse_ref[0, h : h + 1, :])
            scores.append((p * (grads[h] - inner[h])).astype(low_type))
            probs.append(p.astype(low_type))
        for h in range(heads):
            own = slice(h * HEAD_DIM, (h + 1) * HEAD_DIM)
            dq_s[own, :] += dot32(kt_ref[own, at], scores[h])
        for one in range(0, heads, 2):
            cols = slice(one * HEAD_DIM, one * HEAD_DIM + PAIR)
            dv_s[at, cols] += dot32(probs[one], cotangents[one]) + dot32(probs[one + 1], cotangents[one + 1])
            dk_s[at, cols] += dot32(scores[one], queries[one]) + dot32(scores[one + 1], queries[one + 1])
        return carry

    lax.fori_loop(table_ref[1 + i], i + 1, step, 0)
    dq = dq_s[...].T * (HEAD_DIM ** (-0.5))
    here = pl.ds(pl.multiple_of(place(i, rank, per) * BLOCK, BLOCK), BLOCK)
    for c in range(0, width, PAIR):
        dq_ref[:, c : c + PAIR] = turn_back(
            dq[:, c : c + PAIR], keep_ref[here, :], above_ref[here, :], below_ref[here, :]
        ).astype(low_type)

    @pl.when(i == pl.num_programs(0) - 1)
    def _():
        @pl.loop(0, dk_s.shape[0] // BLOCK)
        def _(b):
            at = pl.ds(pl.multiple_of(b * BLOCK, BLOCK), BLOCK)
            for c in range(0, width, PAIR):
                cols = slice(c, c + PAIR)
                dk_ref[at, cols] = turn_back(
                    dk_s[at, cols], keep_ref[at, :], above_ref[at, :], below_ref[at, :]
                ).astype(low_type)
                dv_ref[at, cols] = dv_s[at, cols].astype(low_type)


def attn_bwd(half, slots, table, q, do, o, k, v, kt, start, lse, tables, low=None, held=()):
    rows, width = q.shape
    part = width // 2
    heads = part // HEAD_DIM
    count = rows // BLOCK
    per = rows // slots // BLOCK
    at = lambda i, t: place(i, t[0], per)
    whole = pl.BlockSpec((rows, part), lambda i, t: (0, half))
    turns = pl.BlockSpec((rows, PAIR), lambda i, t: (0, 0))
    result = pl.BlockSpec((rows, part), lambda i, t: (0, 0))
    adam = low is not None
    adam_in, adam_out, adam_like = [], [], []
    if adam:
        strip, depth = low.shape[0] // count, low.shape[1]
        flat = pl.BlockSpec((strip, depth), lambda i, t: (i, 0))
        one = flat if held[0].ndim == 2 else pl.BlockSpec((1, strip, depth), lambda i, t: (0, i, 0))
        adam_in, adam_out = [flat, one, one, one], [one] * 4
        adam_like = [jax.ShapeDtypeStruct(held[0].shape, jnp.float32)] * 4
    return pl.pallas_call(
        functools.partial(attn_bwd_kernel, per, int(adam)),
        grid_spec=pltpu.PrefetchScalarGridSpec(
            num_scalar_prefetch=1,
            grid=(count,),
            in_specs=[
                pl.BlockSpec((BLOCK, part), lambda i, t: (at(i, t), half)),
                pl.BlockSpec((BLOCK, part), lambda i, t: (at(i, t), half)),
                pl.BlockSpec((BLOCK, part), lambda i, t: (at(i, t), 0)),
                whole,
                whole,
                pl.BlockSpec((part, rows), lambda i, t: (half, 0)),
                pl.BlockSpec((1, BLOCK), lambda i, t: (0, at(i, t))),
                pl.BlockSpec((1, heads, BLOCK), lambda i, t: (at(i, t), 0, 0)),
                turns,
                turns,
                turns,
            ]
            + adam_in,
            out_specs=[pl.BlockSpec((BLOCK, part), lambda i, t: (at(i, t), 0)), result, result] + adam_out,
            scratch_shapes=[
                pltpu.VMEM((part, BLOCK), jnp.float32),
                pltpu.VMEM((rows, part), jnp.float32),
                pltpu.VMEM((rows, part), jnp.float32),
            ],
        ),
        out_shape=[jax.ShapeDtypeStruct((rows, part), low_type)] * 3 + adam_like,
        cost_estimate=cost(25 * rows * rows * part // 2, 16 * rows * part, 8 * rows * rows // 4),
        compiler_params=params(60),
        name="attn_bwd",
    )(table, q, do, o, k, v, kt, start, lse, *tables, *((low,) + tuple(held) if adam else ()))


def qkv_grad_kernel(count, adam, *refs):
    left_ref, other_ref, rights = refs[0], refs[1], refs[2 : 2 + count]
    out_ref, sum_ref = refs[2 + count + 8 * adam : 4 + count + 8 * adam]
    if adam:
        adam_blocks(refs[2 + count], refs[3 + count : 6 + count], refs[-4:])
    part = rights[0].shape[1]

    @pl.when(pl.program_id(0) == 0)
    def _():
        for n, right in enumerate(rights):
            sum_ref[n // 2 : n // 2 + 1, (n % 2) * part : (n % 2 + 1) * part] = jnp.sum(
                right[...].astype(jnp.float32), axis=0, keepdims=True
            )

    left = left_ref[...]
    for n, right in enumerate(rights):
        out_ref[n // 2, :, (n % 2) * part : (n % 2 + 1) * part] = dot32(left, right[...], contract_first).astype(low_type)
    out_ref[len(rights) // 2] = other_ref[...]


def qkv_grad(left, rights, other, low=None, held=(), begun=()):
    rows, model = left.shape
    part = rights[0].shape[1]
    count = len(rights) // 2
    tile = 512
    adam = low is not None
    adam_in, adam_out, adam_like, extra = [], [], [], ()
    if adam:
        strip, depth = low.shape[0] // (model // tile), low.shape[1]
        one = pl.BlockSpec((1, strip, depth), lambda n: (1, n, 0))
        adam_in = [pl.BlockSpec((strip, depth), lambda n: (n, 0)), one, one, one] + [ANY] * 4
        adam_out = [one] * 4
        adam_like = [jax.ShapeDtypeStruct(held[0].shape, jnp.float32)] * 4
        extra = (low,) + tuple(held) + tuple(begun)
    first = 2 + len(rights) + 4
    return pl.pallas_call(
        functools.partial(qkv_grad_kernel, len(rights), int(adam)),
        grid=(model // tile,),
        in_specs=[pl.BlockSpec((rows, tile), lambda n: (0, n)), pl.BlockSpec((tile, 2 * part), lambda n: (n, 0))]
        + [pl.BlockSpec((rows, part), lambda n: (0, 0), pipeline_mode=pl.Buffered(1))] * len(rights)
        + adam_in,
        input_output_aliases={first + n: 2 + n for n in range(4)} if adam else {},
        out_specs=[
            pl.BlockSpec((count + 1, tile, 2 * part), lambda n: (0, n, 0)),
            pl.BlockSpec((count, 2 * part), lambda n: (0, 0)),
        ]
        + adam_out,
        out_shape=[
            jax.ShapeDtypeStruct((count + 1, model, 2 * part), low_type),
            jax.ShapeDtypeStruct((count, 2 * part), jnp.float32),
        ]
        + adam_like,
        cost_estimate=cost(4 * count * rows * model * part, 4 * rows * model),
        compiler_params=params(60),
        name="qkv_grad",
    )(left, other, *rights, *extra)


swap_x = [(0, 1), (1, 0), (2, 3), (3, 2)]
swap_y = [(0, 2), (2, 0), (1, 3), (3, 1)]


def square(count):
    return count == 4


def gather_rows(top, end):
    x_top = lax.ppermute(top, "tensor", swap_x)
    y_end = lax.ppermute(end, "tensor", swap_y)
    x_end = lax.ppermute(end, "tensor", swap_x)
    y_top = lax.ppermute(top, "tensor", swap_y)
    first = [top, end, x_top, x_end, y_top, y_end]

    def rest(*between):
        far_top = lax.ppermute(after(x_top, *between), "tensor", swap_y)
        far_end = lax.ppermute(after(y_end, *between), "tensor", swap_x)
        return [far_top, far_end]

    return first, rest


def after(value, *others):
    return lax.optimization_barrier((value,) + others)[0]


def pass_on_kernel(one_ref, two_ref, top_ref, end_ref, for_x_ref, for_y_ref):
    i, half = pl.program_id(0), pl.num_programs(0) // 2
    add = lambda a, b: (a[...].astype(jnp.float32) + b[...].astype(jnp.float32)).astype(low_type)

    @pl.when(i < half)
    def _():
        for_x_ref[...] = one_ref[...]
        for_y_ref[...] = add(two_ref, top_ref)

    @pl.when(i >= half)
    def _():
        for_x_ref[...] = add(one_ref, end_ref)
        for_y_ref[...] = two_ref[...]


def pass_on(rows_in, top, end):
    half, model = top.shape
    block = 64
    per = 2 * half // block
    spec = lambda index: pl.BlockSpec((block, model), lambda i: (index(i), 0))
    return pl.pallas_call(
        pass_on_kernel,
        grid=(per,),
        in_specs=[
            spec(lambda i: per + i),
            spec(lambda i: 2 * per + i),
            spec(lambda i: jnp.minimum(i, per // 2 - 1)),
            spec(lambda i: jnp.maximum(i, per // 2) - per // 2),
        ],
        out_specs=[spec(lambda i: i)] * 2,
        out_shape=[jax.ShapeDtypeStruct((2 * half, model), low_type)] * 2,
        cost_estimate=cost(4 * half * model, 20 * half * model),
        compiler_params=params(60),
        name="pass_on",
    )(rows_in, rows_in, top, end)


MESH = pl.DeviceIdType.MESH


def greet(near_x, near_y):
    barrier = pltpu.get_barrier_semaphore()
    for near in (near_x, near_y):
        pl.semaphore_signal(barrier, inc=1, device_id={"tensor": near}, device_id_type=MESH)
    pl.semaphore_wait(barrier, 2)


def neighbours():
    rank = lax.axis_index("tensor")
    return jnp.bitwise_xor(rank, 1), jnp.bitwise_xor(rank, 2)


def remote(index, source, target, near, send, recv):
    return pltpu.make_async_remote_copy(
        src_ref=source,
        dst_ref=target,
        send_sem=send.at[index],
        recv_sem=recv.at[index],
        device_id={"tensor": near},
        device_id_type=MESH,
    )


arrival = (0, 1, 2, 5, 3, 4, 6, 7)


def arrival_slot(i):
    return jnp.where(i == 3, 5, jnp.where(i == 4, 3, jnp.where(i == 5, 4, i)))


def square_copies(all_s, half, send, recv):
    near_x, near_y = neighbours()
    at = lambda n: all_s.at[pl.ds(n * half, half)]
    return (
        remote(0, at(0), at(2), near_x, send, recv),
        remote(1, at(1), at(5), near_y, send, recv),
        remote(2, at(1), at(3), near_x, send, recv),
        remote(3, at(0), at(4), near_y, send, recv),
        remote(4, at(2), at(6), near_y, send, recv),
        remote(5, at(5), at(7), near_x, send, recv),
    )


def await_slot(i, copies):
    x_top, y_end, x_end, y_top, far_top, far_end = copies

    @pl.when(i == 2)
    def _():
        x_top.wait_recv()
        far_top.start()
        y_end.wait_recv()
        far_end.start()

    for n, c in ((4, x_end), (5, y_top), (6, far_top), (7, far_end)):

        @pl.when(i == n)
        def _(c=c):
            c.wait_recv()


def fetch_next(i, refs, buf, sem):
    def fetch(j):
        pltpu.make_async_copy(refs[j], buf.at[j % 2], sem.at[j % 2]).start()

    for j in range(len(refs)):

        @pl.when(i == max(j - 1, 0) if j else i == 0)
        def _(j=j):
            fetch(j)

    pltpu.make_async_copy(refs[0], buf.at[i % 2], sem.at[i % 2]).wait()


def flow(first, last, loads, work, stores):
    def all_of(copies, act):
        for c in copies:
            act(c)

    all_of(loads(first), lambda c: c.start())

    def step(i, carry):
        @pl.when(i < last - 1)
        def _():
            all_of(loads(i + 1), lambda c: c.start())

        all_of(loads(i), lambda c: c.wait())

        @pl.when(i >= first + 2)
        def _():
            all_of(stores(i - 2), lambda c: c.wait())

        work(i)
        all_of(stores(i), lambda c: c.start())
        return carry

    lax.fori_loop(first, last, step, 0)
    for i in range(max(first, last - 2), last):
        all_of(stores(i), lambda c: c.wait())


def gather_norm_kernel(nd, x_ref, small_ref, pos_ref, inv_ref, og_ref, live_ref, w_hbm,
                       h_ref, full_ref, keep_ref, above_ref, below_ref, top_ref, end_ref, low_hbm,
                       all_s, full_s, stage, w_s, low_s, send, recv, local, small_send, small_recv, out_sem, w_sem, low_sem):
    d = lax.axis_index("dp")
    near_x, near_y = neighbours()
    half = x_ref.shape[0] // 2
    width = small_ref.shape[1]
    own = pltpu.make_async_copy(x_ref, all_s.at[pl.ds(0, 2 * half)], local)
    own.start()
    barrier = pltpu.get_barrier_semaphore()
    for near in (near_x, near_y):
        pl.semaphore_signal(barrier, inc=1, device_id={"tensor": near}, device_id_type=MESH)
    for k in range(1, nd):
        pl.semaphore_signal(barrier, inc=1, device_id={"dp": lax.rem(d + k, nd)}, device_id_type=MESH)
    pl.semaphore_wait(barrier, nd + 1)
    own.wait()
    copies = square_copies(all_s, half, send, recv)
    for c in copies[:4]:
        c.start()
    small = []
    for k in range(1, nd):
        c = pltpu.make_async_remote_copy(
            src_ref=small_ref,
            dst_ref=full_s.at[d],
            send_sem=small_send.at[k],
            recv_sem=small_recv.at[k],
            device_id={"dp": lax.rem(d + k, nd)},
            device_id_type=MESH,
        )
        c.start()
        small.append(c)
    full_s[d] = small_ref[...]
    for n, ref in enumerate((top_ref, end_ref)):

        @pl.loop(0, half // 32)
        def _(r, n=n, ref=ref):
            to = pl.ds(pl.multiple_of(r * 32, 32), 32)
            at = pl.ds(pl.multiple_of(n * half + r * 32, 32), 32)
            ref[to, :] = (og_ref[at, :].astype(jnp.float32) * live_ref[at, :]).astype(low_type)

    strip = w_s.shape[1]
    per = w_hbm.shape[1] // strip

    def side(i):
        return i // per, pl.ds(pl.multiple_of((i % per) * strip, strip), strip)

    def cast(i):
        low_s[i % 2] = w_s[i % 2].astype(low_type)

    flow(
        0,
        w_hbm.shape[0] * per,
        lambda i: [pltpu.make_async_copy(w_hbm.at[side(i)], w_s.at[i % 2], w_sem.at[i % 2])],
        cast,
        lambda i: [pltpu.make_async_copy(low_s.at[i % 2], low_hbm.at[side(i)], low_sem.at[i % 2])],
    )
    for c in small:
        c.wait_recv()
    for n in range(nd):
        full_ref[:, n * width : (n + 1) * width] = full_s[n]
    step = 32
    lane = lax.broadcasted_iota(jnp.int32, (256, PAIR), 1) % HEAD_DIM

    def turns(n):
        at = pl.ds(pl.multiple_of(n * 256, 256), 256)
        angles = jnp.broadcast_to(pos_ref[pl.ds(n, 1), :], (PAIR, 256)).T * inv_ref[...]
        cos_part, sine_part = jnp.cos(angles), jnp.sin(angles)
        keep_ref[at, :] = jnp.where(lane < ROT, cos_part, 1.0)
        above_ref[at, :] = jnp.where(lane < ROT // 2, -sine_part, 0.0)
        below_ref[at, :] = jnp.where((lane >= ROT // 2) & (lane < ROT), sine_part, 0.0)

    def out(buf, row):
        return pltpu.make_async_copy(stage.at[buf], h_ref.at[pl.ds(row, half)], out_sem.at[buf])

    def body_step(i, carry):
        await_slot(i, copies)
        row = pl.multiple_of(arrival_slot(i) * half, half)
        buf = i % 2

        @pl.when(i >= 2)
        def _():
            out(buf, row).wait()

        @pl.loop(0, half // step)
        def _(r):
            at = pl.ds(pl.multiple_of(r * step, step), step)
            x = all_s[pl.ds(pl.multiple_of(row + r * step, step), step), :].astype(jnp.float32)
            c = x - jnp.mean(x, axis=-1, keepdims=True)
            s = lax.rsqrt(jnp.mean(c * c, axis=-1, keepdims=True) + norm_eps)
            stage[buf, at, :] = (c * s * full_ref[0:1, :] + full_ref[2:3, :]).astype(low_type)

        out(buf, row).start()

        @pl.when((i >= 2) & (i < 6))
        def _():
            turns(2 * i - 4)
            turns(2 * i - 3)

        return carry

    lax.fori_loop(0, 8, body_step, 0)
    for buf in (0, 1):
        out(buf, 0).wait()
    for c in copies:
        c.wait_send()
    for c in small:
        c.wait_send()


def gather_norm(x, small, pos, inverse, out_grad, live, w):
    nd = lax.axis_size("dp")
    rows, model = x.shape
    total = 4 * rows
    count, width = small.shape
    vmem = pl.BlockSpec(memory_space=pltpu.VMEM)
    table = jax.ShapeDtypeStruct((total, PAIR), jnp.float32)
    return pl.pallas_call(
        functools.partial(gather_norm_kernel, nd),
        in_specs=[ANY, vmem, vmem, vmem, vmem, vmem, ANY],
        out_specs=[ANY, vmem, vmem, vmem, vmem, vmem, vmem, ANY],
        out_shape=[
            jax.ShapeDtypeStruct((total, model), low_type),
            jax.ShapeDtypeStruct((count, width * nd), jnp.float32),
            table,
            table,
            table,
            jax.ShapeDtypeStruct((rows // 2, model), low_type),
            jax.ShapeDtypeStruct((rows // 2, model), low_type),
            jax.ShapeDtypeStruct(w.shape, low_type),
        ],
        scratch_shapes=[
            pltpu.VMEM((total, model), low_type),
            pltpu.VMEM((nd, count, width), jnp.float32),
            pltpu.VMEM((2, rows // 2, model), low_type),
            pltpu.VMEM((2, 64, w.shape[2]), jnp.float32),
            pltpu.VMEM((2, 64, w.shape[2]), low_type),
            pltpu.SemaphoreType.DMA((6,)),
            pltpu.SemaphoreType.DMA((6,)),
            pltpu.SemaphoreType.DMA,
            pltpu.SemaphoreType.DMA((nd,)),
            pltpu.SemaphoreType.DMA((nd,)),
            pltpu.SemaphoreType.DMA((2,)),
            pltpu.SemaphoreType.DMA((2,)),
            pltpu.SemaphoreType.DMA((2,)),
        ],
        cost_estimate=cost(20 * total * model, 4 * total * model),
        compiler_params=pltpu.CompilerParams(vmem_limit_bytes=62 * MIB, collective_id=3, has_side_effects=True),
        name="gather_norm",
    )(x, small, pos, inverse, out_grad, live, w)


def gather_do_kernel(d_ref, act_ref, h_hbm, dup_hbm, o_a_ref, o_b_ref, wo_hbm, wd_hbm, do_ref, grad_ref, mlp_ref, top_ref, end_ref, up_ref,
                     all_s, wo_s, wd_s, dup_s, acc, act_s, h_s, stage, up_s, send, recv, local, act_sem, h_sem, out_sem, up_sem):
    near_x, near_y = neighbours()
    half = d_ref.shape[0] // 2
    model = d_ref.shape[1]
    part = o_a_ref.shape[1]
    tile = 512
    own = pltpu.make_async_copy(d_ref, all_s.at[pl.ds(0, 2 * half)], local.at[0])
    own.start()
    weights = pltpu.make_async_copy(wd_hbm, wd_s, local.at[1])
    weights.start()
    cotangent = pltpu.make_async_copy(dup_hbm, dup_s, local.at[2])
    cotangent.start()
    turned = pltpu.make_async_copy(wo_hbm.at[3], wo_s, local.at[3])
    turned.start()
    greet(near_x, near_y)
    own.wait()
    copies = square_copies(all_s, half, send, recv)
    for c in copies[:4]:
        c.start()
    acc[...] = jnp.zeros_like(acc)
    weights.wait()
    cotangent.wait()
    turned.wait()
    strip = model // 8

    def loads(i):
        at = pl.ds(pl.multiple_of(i * half, half), half)
        cols = pl.ds(pl.multiple_of(i * strip, strip), strip)
        return [
            pltpu.make_async_copy(act_ref.at[at], act_s.at[i % 2], act_sem.at[i % 2]),
            pltpu.make_async_copy(h_hbm.at[:, cols], h_s.at[i % 2], h_sem.at[i % 2]),
        ]

    def outs(i, target=top_ref):
        side = pl.ds(pl.multiple_of(i * strip, strip), strip)
        return [
            pltpu.make_async_copy(stage.at[i % 2], target, out_sem.at[i % 2]),
            pltpu.make_async_copy(up_s.at[i % 2], up_ref.at[side], up_sem.at[i % 2]),
        ]

    for c in loads(0):
        c.start()

    def beside(p):
        @pl.when(p < 7)
        def _():
            for c in loads(p + 1):
                c.start()

        for c in loads(p):
            c.wait()

        @pl.when(p >= 2)
        def _():
            for c in outs(p - 2):
                c.wait()

        stage[p % 2] = dot32(act_s[p % 2], wd_s[...]).astype(low_type)
        up_s[p % 2] = dot32(h_s[p % 2], dup_s[...], contract_first).astype(low_type)

        @pl.when(p < 6)
        def _():
            for c in outs(p, mlp_ref.at[pl.ds(pl.multiple_of(p * half, half), half)]):
                c.start()

        for n, ref in ((6, top_ref), (7, end_ref)):

            @pl.when(p == n)
            def _(ref=ref):
                for c in outs(p, ref):
                    c.start()

    def step(i, carry):
        @pl.when(i < 6)
        def _():
            beside(jnp.where(i == 5, 6, i))

        @pl.when((i == 4) | (i == 5))
        def _():
            beside(2 * i - 3)

        await_slot(i, copies)
        at = pl.ds(pl.multiple_of(arrival_slot(i) * half, half), half)
        dattn = all_s[at, :]
        do_ref[at, :] = dot32(dattn, wo_s[...]).astype(low_type)
        acc[:part, :] += dot32(o_a_ref[at, :], dattn, contract_first)
        acc[part:, :] += dot32(o_b_ref[at, :], dattn, contract_first)
        return carry

    lax.fori_loop(0, 8, step, 0)

    @pl.loop(0, model // tile)
    def _(n):
        cols = pl.ds(pl.multiple_of(n * tile, tile), tile)
        grad_ref[cols, :] = acc[:, cols].T.astype(low_type)

    for i in (6, 7):
        for c in outs(i):
            c.wait()
    for c in copies:
        c.wait_send()


def gather_do(dattn, act, h, dup, o_a, o_b, wo, wd):
    rows, model = dattn.shape
    total = 4 * rows
    depth = act.shape[1]
    width = wo.shape[2]
    vmem = pl.BlockSpec(memory_space=pltpu.VMEM)
    return pl.pallas_call(
        gather_do_kernel,
        in_specs=[ANY, ANY, ANY, ANY, vmem, vmem, ANY, ANY],
        out_specs=[vmem, vmem, ANY, ANY, ANY, ANY],
        out_shape=[
            jax.ShapeDtypeStruct((total, width), low_type),
            jax.ShapeDtypeStruct((model, width), low_type),
            jax.ShapeDtypeStruct((3 * rows, model), low_type),
            jax.ShapeDtypeStruct((rows // 2, model), low_type),
            jax.ShapeDtypeStruct((rows // 2, model), low_type),
            jax.ShapeDtypeStruct((model, depth), low_type),
        ],
        scratch_shapes=[
            pltpu.VMEM((total, model), low_type),
            pltpu.VMEM(wo.shape[1:], low_type),
            pltpu.VMEM(wd.shape, low_type),
            pltpu.VMEM(dup.shape, low_type),
            pltpu.VMEM((width, model), jnp.float32),
            pltpu.VMEM((2, rows // 2, depth), low_type),
            pltpu.VMEM((2, total, model // 8), low_type),
            pltpu.VMEM((2, rows // 2, model), low_type),
            pltpu.VMEM((2, model // 8, depth), low_type),
            pltpu.SemaphoreType.DMA((6,)),
            pltpu.SemaphoreType.DMA((6,)),
            pltpu.SemaphoreType.DMA((4,)),
            pltpu.SemaphoreType.DMA((2,)),
            pltpu.SemaphoreType.DMA((2,)),
            pltpu.SemaphoreType.DMA((2,)),
            pltpu.SemaphoreType.DMA((2,)),
        ],
        cost_estimate=cost(2 * total * model * (depth + 2 * width), 6 * total * model),
        compiler_params=pltpu.CompilerParams(vmem_limit_bytes=62 * MIB, collective_id=4, has_side_effects=True),
        name="gather_do",
    )(dattn, act, h, dup, o_a, o_b, wo, wd)


def exchange(rows, partial, bufs, send, recv, fill_one, fill_two):
    far_s, for_x, for_y, top_s, end_s, from_x, from_y = bufs
    near_x, near_y = neighbours()
    half = rows // 2
    t, e = pl.ds(0, half), pl.ds(half, half)
    copies = [
        remote(0, far_s.at[t], top_s, near_x, send, recv),
        remote(1, far_s.at[e], end_s, near_y, send, recv),
        remote(2, for_x.at[t], from_x.at[t], near_x, send, recv),
        remote(3, for_y.at[e], from_y.at[e], near_y, send, recv),
    ]
    quarter = half // 2
    for n in range(2):
        at = pl.ds(half + n * quarter, quarter)
        copies.append(remote(4 + n, for_x.at[at], from_x.at[at], near_x, send, recv))
    for n in range(2):
        at = pl.ds(n * quarter, quarter)
        copies.append(remote(6 + n, for_y.at[at], from_y.at[at], near_y, send, recv))

    def into(ref, which):
        def store(cols, value):
            ref[pl.ds(which * half, half), cols] = value.astype(low_type)

        return store

    def added(ref, which, other):
        def store(cols, value):
            ref[pl.ds(which * half, half), cols] = (value + other[:, cols].astype(jnp.float32)).astype(low_type)

        return store

    partial(3, 0, into(far_s, 0))
    copies[0].start()
    partial(3, 1, into(far_s, 1))
    copies[1].start()
    partial(1, 0, into(for_x, 0))
    copies[2].start()
    partial(2, 1, into(for_y, 1))
    copies[3].start()
    fill_one()
    copies[0].wait_recv()
    partial(2, 0, added(for_y, 0, top_s))
    copies[6].start()
    copies[7].start()
    copies[1].wait_recv()
    partial(1, 1, added(for_x, 1, end_s))
    copies[4].start()
    copies[5].start()
    fill_two()
    return copies


def finish_quarters(copies, finish, sent=0):
    copies[2].wait_recv()
    copies[6].wait_recv()
    finish(0)
    copies[3].wait_recv()
    copies[4].wait_recv()
    finish(2)
    copies[7].wait_recv()
    finish(1)
    copies[5].wait_recv()
    finish(3)
    for c in copies[sent:]:
        c.wait_send()


def finish_back(copies, rows, gain_row, v_ref, base_ref, own_ref, live_ref, norm_ref, from_x, from_y, dx_ref, low_ref, gain_ref, shift_ref, gain_s, shift_s, sent=0):
    quarter = rows // 4
    step = 16
    gain_s[...] = jnp.zeros_like(gain_s)
    shift_s[...] = jnp.zeros_like(shift_s)

    def finish(which):
        @pl.loop(0, quarter // step)
        def _(r):
            at = pl.ds(pl.multiple_of(which * quarter + r * step, step), step)
            e = own_ref[at, :].astype(jnp.float32) + from_x[at, :].astype(jnp.float32) + from_y[at, :].astype(jnp.float32)
            v = v_ref[at, :].astype(jnp.float32)
            c = v - jnp.mean(v, axis=-1, keepdims=True)
            s = lax.rsqrt(jnp.mean(c * c, axis=-1, keepdims=True) + norm_eps)
            xh = c * s
            w = e * norm_ref[gain_row : gain_row + 1, :]
            back = s * (w - jnp.mean(w, axis=-1, keepdims=True) - xh * jnp.mean(w * xh, axis=-1, keepdims=True))
            dx = base_ref[at, :].astype(jnp.float32) + back
            dx_ref[at, :] = dx.astype(dx_ref.dtype)
            if low_ref is not None:
                low_ref[at, :] = (dx * live_ref[at, :]).astype(low_type)
            ex = e * xh
            gain_s[...] += ex[:8] + ex[8:]
            shift_s[...] += e[:8] + e[8:]

    finish_quarters(copies, finish, sent)
    gain_ref[...] = jnp.sum(gain_s[...], axis=0, keepdims=True)
    shift_ref[...] = jnp.sum(shift_s[...], axis=0, keepdims=True)


def exchange_scratch(rows, model):
    big = pltpu.VMEM((rows, model), low_type)
    small = pltpu.VMEM((rows // 2, model), low_type)
    line = pltpu.VMEM((8, model), jnp.float32)
    sems = pltpu.SemaphoreType.DMA((8,))
    return [big, big, big, small, small, big, big, line, line, sems, sems]


def out_scatter_kernel(a_ref, b_ref, w_hbm, x_ref, live_ref, norm_ref, x1_ref, h_ref, *scratch):
    bufs, (send, recv, w_s, local) = scratch[:7], scratch[9:]
    weights = pltpu.make_async_copy(w_hbm.at[3], w_s, local)
    weights.start()
    near_x, near_y = neighbours()
    rows, model = x_ref.shape
    half = rows // 2
    part = a_ref.shape[1]
    tile = 512
    greet(near_x, near_y)
    weights.wait()

    def partial(slot, which, store):
        at = pl.ds(slot * rows + which * half, half)

        @pl.loop(0, model // tile)
        def _(n):
            cols = pl.ds(pl.multiple_of(n * tile, tile), tile)
            value = dot32(a_ref[at, :], w_s[cols, :part], contract_last)
            store(cols, value + dot32(b_ref[at, :], w_s[cols, part:], contract_last))

    def own(which):
        def store(cols, value):
            x1_ref[pl.ds(which * half, half), cols] = value

        return store

    def fill_one():
        partial(0, 0, own(0))
        partial(0, 1, own(1))

    copies = exchange(rows, partial, bufs, send, recv, fill_one, lambda: None)
    from_x, from_y = bufs[5:]
    quarter = rows // 4
    step = 32

    def finish(which):
        @pl.loop(0, quarter // step)
        def _(r):
            at = pl.ds(pl.multiple_of(which * quarter + r * step, step), step)
            attn = x1_ref[at, :] + from_x[at, :].astype(jnp.float32) + from_y[at, :].astype(jnp.float32)
            x1 = x_ref[at, :].astype(jnp.float32) + live_ref[at, :] * attn
            x1_ref[at, :] = x1
            c = x1 - jnp.mean(x1, axis=-1, keepdims=True)
            s = lax.rsqrt(jnp.mean(c * c, axis=-1, keepdims=True) + norm_eps)
            h_ref[at, :] = (c * s * norm_ref[1:2, :] + norm_ref[3:4, :]).astype(low_type)

    finish_quarters(copies, finish)


def out_scatter(a, b, w, x, live, norm):
    rows, model = x.shape
    vmem = pl.BlockSpec(memory_space=pltpu.VMEM)
    total = a.shape[0]
    return pl.pallas_call(
        out_scatter_kernel,
        in_specs=[vmem, vmem, ANY, vmem, vmem, vmem],
        out_specs=[vmem] * 2,
        out_shape=[jax.ShapeDtypeStruct((rows, model), jnp.float32), jax.ShapeDtypeStruct((rows, model), low_type)],
        scratch_shapes=exchange_scratch(rows, model) + [pltpu.VMEM(w.shape[1:], low_type), pltpu.SemaphoreType.DMA],
        cost_estimate=cost(2 * total * model * w.shape[2], 20 * rows * model),
        compiler_params=pltpu.CompilerParams(vmem_limit_bytes=62 * MIB, collective_id=0, has_side_effects=True),
        name="out_scatter",
    )(a, b, w, x, live, norm)


sending = (6, 7, 2, 5, 0, 1, 4, 3)


def sending_slot(j):
    slot = jnp.int32(sending[-1])
    for n in range(7):
        slot = jnp.where(j == n, sending[n], slot)
    return slot


def hidden_scatter_kernel(count, *refs):
    dm_refs, refs = refs[:count], refs[count:]
    one_hbm, two_hbm, wd_hbm, w_hbm, h_hbm, x1_hbm, og_hbm, live_ref, norm_ref = refs[:9]
    grad_ref, dup_ref, dx_ref, low_ref, gain_ref, shift_ref = refs[9:15]
    scratch = refs[15:]
    bufs, (gain_s, shift_s, send, recv) = scratch[:7], scratch[7:11]
    g_s, w_s, wd_s, dm_s, slope_s, h_s, stage, local, dm_sem, slope_sem, h_sem, out_sem = scratch[11:]
    rows, model = dx_ref.shape
    half = rows // 2
    near_x, near_y = neighbours()
    down_load = pltpu.make_async_copy(wd_hbm, wd_s, local.at[0])
    weight_load = pltpu.make_async_copy(w_hbm, w_s, local.at[1])
    x1_load = pltpu.make_async_copy(x1_hbm, dx_ref, local.at[2])
    og_load = pltpu.make_async_copy(og_hbm, bufs[0], local.at[3])
    dup_store = pltpu.make_async_copy(g_s.at[1], dup_ref, local.at[4])

    def slope_loads(j):
        at = pl.ds(pl.multiple_of(sending_slot(j) * half, half), half)
        return [
            pltpu.make_async_copy(ref.at[at], slope_s.at[j % 2, n], slope_sem.at[j % 2, n])
            for n, ref in enumerate((one_hbm, two_hbm))
        ]

    def dm_load(n):
        return pltpu.make_async_copy(dm_refs[sending[n]], dm_s.at[n % 2], dm_sem.at[n % 2])

    down_load.start()
    dm_load(0).start()
    for c in slope_loads(0):
        c.start()
    weight_load.start()
    x1_load.start()
    greet(near_x, near_y)
    down_load.wait()

    def back_step(j, carry):
        @pl.when(j < 7)
        def _():
            for c in slope_loads(j + 1):
                c.start()

        for n in range(1, 8):

            @pl.when(j == n - 1)
            def _(n=n):
                dm_load(n).start()

        b = j % 2
        pltpu.make_async_copy(dm_refs[0], dm_s.at[b], dm_sem.at[b]).wait()
        for c in slope_loads(j):
            c.wait()
        at = pl.ds(pl.multiple_of(sending_slot(j) * half, half), half)
        da = dot32(dm_s[b], wd_s[...], contract_last)
        g_s[0, at, :] = (da * slope_s[b, 0].astype(jnp.float32)).astype(low_type)
        g_s[1, at, :] = (da * slope_s[b, 1].astype(jnp.float32)).astype(low_type)
        return carry

    def back(first, last):
        lax.fori_loop(first, last, back_step, 0)

    tile = 512

    def partial(slot, which, store):
        if slot == 3:
            back(which, which + 1)
        if slot == 3 and which == 0:
            weight_load.wait()
        if slot == 1 and which == 0:
            back(2, 4)
        at = pl.ds(slot * rows + which * half, half)

        @pl.loop(0, model // tile)
        def _(n):
            cols = pl.ds(pl.multiple_of(n * tile, tile), tile)
            value = dot32(g_s[0, at, :], w_s[0, cols, :], contract_last)
            store(cols, value + dot32(g_s[1, at, :], w_s[1, cols, :], contract_last))

    def own(which):
        def store(cols, value):
            low_ref[pl.ds(which * half, half), cols] = value.astype(low_type)

        return store

    strip = 256

    def load(i):
        return pltpu.make_async_copy(h_hbm.at[:, pl.ds(pl.multiple_of(i * strip, strip), strip)], h_s.at[i % 2], h_sem.at[i % 2])

    def out(i):
        at = pl.ds(pl.multiple_of(i * strip, strip), strip)
        return pltpu.make_async_copy(stage.at[i % 2], grad_ref.at[at], out_sem.at[i % 2])

    strips = model // strip

    def strip_step(i, carry):
        @pl.when(i < strips - 1)
        def _():
            load(i + 1).start()

        load(i).wait()

        @pl.when(i >= 2)
        def _():
            out(i - 2).wait()

        stage[i % 2] = dot32(h_s[i % 2], g_s[0], contract_first).astype(low_type)
        out(i).start()
        return carry

    def fill_one():
        back(4, 8)
        dup_store.start()
        load(0).start()
        partial(0, 0, own(0))

    def fill_two():
        partial(0, 1, own(1))
        lax.fori_loop(0, strips, strip_step, 0)

    copies = exchange(rows, partial, bufs, send, recv, fill_one, fill_two)
    copies[0].wait_send()
    copies[1].wait_send()
    og_load.start()
    x1_load.wait()
    og_load.wait()
    finish_back(copies, rows, 1, dx_ref, bufs[0], low_ref, live_ref, norm_ref, bufs[5], bufs[6], dx_ref, low_ref, gain_ref, shift_ref, gain_s, shift_s, 2)
    out(strips - 2).wait()
    out(strips - 1).wait()
    dup_store.wait()


def hidden_scatter(dm_blocks, one, two, wd, w, h, x1, out_grad, live, norm):
    rows, model = x1.shape
    total, depth = one.shape
    half = rows // 2
    vmem = pl.BlockSpec(memory_space=pltpu.VMEM)
    line = jax.ShapeDtypeStruct((1, model), jnp.float32)
    return pl.pallas_call(
        functools.partial(hidden_scatter_kernel, len(dm_blocks)),
        in_specs=[ANY] * (len(dm_blocks) + 7) + [vmem, vmem],
        out_specs=[ANY, ANY, vmem, vmem, vmem, vmem],
        out_shape=[
            jax.ShapeDtypeStruct((model, depth), low_type),
            jax.ShapeDtypeStruct((total, depth), low_type),
            jax.ShapeDtypeStruct((rows, model), jnp.float32),
            jax.ShapeDtypeStruct((rows, model), low_type),
            line,
            line,
        ],
        scratch_shapes=exchange_scratch(rows, model)
        + [
            pltpu.VMEM((2, total, depth), low_type),
            pltpu.VMEM(w.shape, low_type),
            pltpu.VMEM(wd.shape, low_type),
            pltpu.VMEM((2, half, model), low_type),
            pltpu.VMEM((2, 2, half, depth), low_type),
            pltpu.VMEM((2, total, 256), low_type),
            pltpu.VMEM((2, 256, depth), low_type),
            pltpu.SemaphoreType.DMA((5,)),
            pltpu.SemaphoreType.DMA((2,)),
            pltpu.SemaphoreType.DMA((2, 2)),
            pltpu.SemaphoreType.DMA((2,)),
            pltpu.SemaphoreType.DMA((2,)),
        ],
        cost_estimate=cost(8 * total * model * depth, 16 * total * model),
        compiler_params=pltpu.CompilerParams(vmem_limit_bytes=62 * MIB, collective_id=5, has_side_effects=True),
        name="hidden_scatter",
    )(*dm_blocks, one, two, wd, w, h, x1, out_grad, live, norm)


def first_scatter_kernel(count, *refs):
    lefts_hbm = refs[:count]
    w_hbm, x_ref, base_ref, norm_ref, live_ref = refs[count : count + 5]
    refs = refs[count + 5 :]
    x1_hbm, mlp_hbm = refs[0], refs[1:4]
    dx_ref, gain_ref, shift_ref, layer_hbm = refs[4:8]
    scratch = refs[8:]
    bufs, (gain_s, shift_s, send, recv, own_s, left_s, w_s) = scratch[:7], scratch[7:14]
    x1_s, mlp_s, layer_s, left_sem, in_sem, layer_sem = scratch[14:]
    rows, model = x_ref.shape
    half = rows // 2
    tile = 512
    near_x, near_y = neighbours()
    far = pl.ds(3 * rows, rows)
    rest = pl.ds(0, 3 * rows)
    early = [pltpu.make_async_copy(left.at[far], left_s.at[n, far], left_sem.at[n]) for n, left in enumerate(lefts_hbm)]
    early.append(pltpu.make_async_copy(w_hbm.at[pl.ds(0, 3)], w_s, left_sem.at[2 * count]))
    late = [
        pltpu.make_async_copy(left.at[rest], left_s.at[n, rest], left_sem.at[count + n]) for n, left in enumerate(lefts_hbm)
    ]
    for c in early + late:
        c.start()
    greet(near_x, near_y)
    for c in early:
        c.wait()

    def partial(slot, which, store):
        if slot == 1 and which == 0:
            for c in late:
                c.wait()
        at = pl.ds(slot * rows + which * half, half)

        @pl.loop(0, model // tile)
        def _(n):
            cols = pl.ds(pl.multiple_of(n * tile, tile), tile)
            value = None
            for m in range(count):
                depth = left_s.shape[2]
                per = w_s.shape[2] // depth
                side = slice((m % per) * depth, (m % per + 1) * depth)
                term = dot32(left_s[m, at, :], w_s[m // per, cols, side], contract_last)
                value = term if value is None else value + term
            store(cols, value)

    def own(which):
        def store(cols, value):
            own_s[pl.ds(which * half, half), cols] = value

        return store

    def layer_moves():
        deep = x1_s.shape[1]
        at = lambda i: pl.ds(pl.multiple_of(i * deep, deep), deep)

        def loads(i):
            return [pltpu.make_async_copy(x1_hbm.at[at(i)], x1_s.at[i % 2], in_sem.at[i % 2, 0])] + [
                pltpu.make_async_copy(ref.at[at(i)], mlp_s.at[i % 2, n], in_sem.at[i % 2, 1 + n])
                for n, ref in enumerate(mlp_hbm)
            ]

        def stores(i):
            return [pltpu.make_async_copy(layer_s.at[i % 2], layer_hbm.at[at(i)], layer_sem.at[i % 2])]

        def work(i):
            b = i % 2
            total = mlp_s[b, 0].astype(jnp.float32) + mlp_s[b, 1].astype(jnp.float32) + mlp_s[b, 2].astype(jnp.float32)
            layer_s[b] = (x1_s[b] + live_ref[at(i), :] * total).astype(low_type)

        flow(0, rows // deep, loads, work, stores)

    def fill_one():
        partial(0, 0, own(0))
        partial(0, 1, own(1))

    def fill_two():
        layer_moves()

    copies = exchange(rows, partial, bufs, send, recv, fill_one, fill_two)
    finish_back(copies, rows, 0, x_ref, base_ref, own_s, None, norm_ref, bufs[5], bufs[6], dx_ref, None, gain_ref, shift_ref, gain_s, shift_s)


def first_scatter(lefts, w, x, base, norm, live, x1, mlp_parts):
    rows, model = x.shape
    count = len(lefts)
    total, part = lefts[0].shape
    vmem = pl.BlockSpec(memory_space=pltpu.VMEM)
    line = jax.ShapeDtypeStruct((1, model), jnp.float32)
    deep = 64
    both = lambda block, n, t: pltpu.VMEM((2,) + ((n,) if n else ()) + block, t)
    return pl.pallas_call(
        functools.partial(first_scatter_kernel, count),
        in_specs=[ANY] * (count + 1) + [vmem] * 4 + [ANY] * 4,
        out_specs=[vmem] * 3 + [ANY],
        out_shape=[jax.ShapeDtypeStruct((rows, model), low_type), line, line, jax.ShapeDtypeStruct((rows, model), low_type)],
        scratch_shapes=exchange_scratch(rows, model)
        + [
            pltpu.VMEM((rows, model), jnp.float32),
            pltpu.VMEM((count, total, part), low_type),
            pltpu.VMEM((3,) + w.shape[1:], low_type),
            both((deep, model), 0, jnp.float32),
            both((deep, model), 3, low_type),
            both((deep, model), 0, low_type),
            pltpu.SemaphoreType.DMA((2 * count + 1,)),
            pltpu.SemaphoreType.DMA((2, 4)),
            pltpu.SemaphoreType.DMA((2,)),
        ],
        cost_estimate=cost(10**13, 30 * rows * model),
        compiler_params=pltpu.CompilerParams(vmem_limit_bytes=62 * MIB, collective_id=6, has_side_effects=True),
        name="first_scatter",
    )(*lefts, w, x, base, norm, live, x1, *mlp_parts)


def adam_rest_kernel(low_ref, turned_ref, *refs):
    qkv_in, out_in, qkv_out, out_out = refs[:3], refs[3:6], refs[6:10], refs[10:]
    step = pl.program_id(0)
    last = pl.num_programs(0) - 2

    @pl.when(step < last)
    def _():
        adam_blocks(low_ref, qkv_in, qkv_out)

    @pl.when(step >= last)
    def _():
        gradient = turned_ref[0].astype(jnp.float32).T
        out_out[0][...] = gradient
        results = adamw_update(out_in[0][...], gradient, out_in[1][...], out_in[2][...], weight_decay)
        for ref, value in zip(out_out[1:], results):
            ref[...] = value


def adam_rest(low, qkv, out):
    count, depth, width = low.shape
    half = depth // 2
    last = 2 * count - 2
    stack = lambda k: (jnp.minimum(k, last - 1) // 2, jnp.minimum(k, last - 1) % 2, 0)
    late = lambda k: jnp.maximum(k, last) - last
    three = pl.BlockSpec((1, half, width), stack)
    flat = pl.BlockSpec((width, half), lambda k: (0, late(k)))
    like = lambda value: jax.ShapeDtypeStruct(value.shape, jnp.float32)
    return pl.pallas_call(
        adam_rest_kernel,
        grid=(last + 2,),
        in_specs=[three, pl.BlockSpec((1, half, width), lambda k: (count - 1, late(k), 0))] + [three] * 3 + [flat] * 3,
        out_specs=[three] * 4 + [flat] * 4,
        out_shape=[like(qkv[0])] * 4 + [like(out[0])] * 4,
        cost_estimate=cost(30 * count * depth * width, 30 * count * depth * width),
        compiler_params=params(60),
        name="adam_rest",
    )(low, low, *qkv, *out)


def gather_gate_up_kernel(count, h_ref, w_hbm, *rest):
    blocks, (all_ref, act_ref, one_ref, two_ref, grad_ref) = rest[:count], rest[count : count + 5]
    w_s, all_s, stage, acc, turned, dm_s, send, recv, local, h_sem, out_sem, dm_sem = rest[count + 5 :]
    near_x, near_y = neighbours()
    half = h_ref.shape[0] // 2
    own = pltpu.make_async_copy(h_ref, all_s.at[pl.ds(0, 2 * half)], local.at[0])
    own.start()
    weights = pltpu.make_async_copy(w_hbm, w_s, local.at[1])
    weights.start()
    greet(near_x, near_y)
    own.wait()
    copies = square_copies(all_s, half, send, recv)
    for c in copies[:4]:
        c.start()
    acc[...] = jnp.zeros_like(acc)
    weights.wait()
    in_order = [blocks[n] for n in arrival]
    tile = 512

    def outs(buf, row):
        return [
            pltpu.make_async_copy(stage.at[buf, n], ref.at[pl.ds(row, half)], out_sem.at[buf, n])
            for n, ref in enumerate((act_ref, one_ref, two_ref))
        ]

    def keep(i, row):
        return pltpu.make_async_copy(all_s.at[pl.ds(row, half)], all_ref.at[pl.ds(row, half)], h_sem.at[i])

    def step(i, carry):
        await_slot(i, copies)
        row = pl.multiple_of(arrival_slot(i) * half, half)
        buf = i % 2
        keep(i, row).start()

        @pl.when(i >= 2)
        def _():
            for c in outs(buf, row):
                c.wait()

        h = all_s[pl.ds(row, half), :]
        gate = dot32(h, w_s[0])
        up = dot32(h, w_s[1])
        sig = 1.0 / (1.0 + jnp.exp(-gate))
        silu = gate * sig
        act = (silu * up).astype(low_type)
        stage[buf, 0] = act
        stage[buf, 1] = (up * sig * (1.0 + gate * (1.0 - sig))).astype(low_type)
        stage[buf, 2] = silu.astype(low_type)
        for c in outs(buf, row):
            c.start()
        turned[...] = act.T
        fetch_next(i, in_order, dm_s, dm_sem)

        @pl.loop(0, acc.shape[1] // tile)
        def _(n):
            cols = pl.ds(pl.multiple_of(n * tile, tile), tile)
            acc[:, cols] += dot32(turned[...], dm_s[buf, :, cols])

        return carry

    lax.fori_loop(0, 8, step, 0)
    for buf in (0, 1):
        for c in outs(buf, 0):
            c.wait()
    for i in range(8):
        keep(i, 0).wait()
    for c in copies:
        c.wait_send()
    depth = acc.shape[0]
    strip = depth // 8

    @pl.loop(0, 8)
    def _(n):
        at = pl.ds(pl.multiple_of(n * strip, strip), strip)
        all_s[at, :] = acc[at, :].astype(low_type)

    last = pltpu.make_async_copy(all_s.at[pl.ds(0, depth)], grad_ref, local.at[0])
    last.start()
    last.wait()


def gather_gate_up(h, w, dm_blocks):
    rows, model = h.shape
    depth = w.shape[2]
    total = 4 * rows
    half = rows // 2
    deep = jax.ShapeDtypeStruct((total, depth), low_type)
    return pl.pallas_call(
        functools.partial(gather_gate_up_kernel, len(dm_blocks)),
        in_specs=[ANY] * (2 + len(dm_blocks)),
        out_specs=[ANY] * 5,
        out_shape=[
            jax.ShapeDtypeStruct((total, model), low_type),
            deep,
            deep,
            deep,
            jax.ShapeDtypeStruct((depth, model), low_type),
        ],
        scratch_shapes=[
            pltpu.VMEM(w.shape, low_type),
            pltpu.VMEM((total, model), low_type),
            pltpu.VMEM((2, 3, half, depth), low_type),
            pltpu.VMEM((depth, model), jnp.float32),
            pltpu.VMEM((depth, half), low_type),
            pltpu.VMEM((2, half, model), low_type),
            pltpu.SemaphoreType.DMA((6,)),
            pltpu.SemaphoreType.DMA((6,)),
            pltpu.SemaphoreType.DMA((2,)),
            pltpu.SemaphoreType.DMA((8,)),
            pltpu.SemaphoreType.DMA((2, 3)),
            pltpu.SemaphoreType.DMA((2,)),
        ],
        cost_estimate=cost(6 * total * model * depth, 4 * model * depth + 4 * total * model + 6 * total * depth),
        compiler_params=pltpu.CompilerParams(vmem_limit_bytes=62 * MIB, collective_id=1, has_side_effects=True),
        name="gather_gate_up",
    )(h, w, *dm_blocks)


def small_kernel(nd, nt, x_ref, o_ref, groups, partial, shares, send, recv, send_t, recv_t):
    d, t = lax.axis_index("dp"), lax.axis_index("tensor")
    width = o_ref.shape[1]
    barrier = pltpu.get_barrier_semaphore()
    for k in range(1, nd):
        pl.semaphore_signal(barrier, inc=1, device_id={"dp": lax.rem(d + k, nd)}, device_id_type=MESH)
    for k in range(1, nt):
        pl.semaphore_signal(barrier, inc=1, device_id={"tensor": lax.rem(t + k, nt)}, device_id_type=MESH)
    pl.semaphore_wait(barrier, nd + nt - 2)
    copies = []
    for k in range(1, nd):
        peer = lax.rem(d + k, nd)
        c = pltpu.make_async_remote_copy(
            src_ref=x_ref.at[:, pl.ds(pl.multiple_of(peer * width, width), width)],
            dst_ref=groups.at[k],
            send_sem=send.at[k],
            recv_sem=recv.at[k],
            device_id={"dp": peer},
            device_id_type=MESH,
        )
        c.start()
        copies.append(c)
    total = x_ref[:, pl.ds(pl.multiple_of(d * width, width), width)]
    for k in range(1, nd):
        copies[k - 1].wait_recv()
        total += groups[k]
    partial[...] = total
    shares[t] = total
    for k in range(1, nt):
        c = pltpu.make_async_remote_copy(
            src_ref=partial,
            dst_ref=shares.at[t],
            send_sem=send_t.at[k],
            recv_sem=recv_t.at[k],
            device_id={"tensor": lax.rem(t + k, nt)},
            device_id_type=MESH,
        )
        c.start()
        copies.append(c)
    for k in range(1, nt):
        copies[nd - 2 + k].wait_recv()
    total = shares[0]
    for k in range(1, nt):
        total += shares[k]
    o_ref[...] = total
    for c in copies:
        c.wait_send()


def sum_small(x):
    nd, nt = lax.axis_size("dp"), lax.axis_size("tensor")
    rows, model = x.shape
    width = model // nd
    vmem = pl.BlockSpec(memory_space=pltpu.VMEM)
    return pl.pallas_call(
        functools.partial(small_kernel, nd, nt),
        in_specs=[vmem],
        out_specs=vmem,
        out_shape=jax.ShapeDtypeStruct((rows, width), jnp.float32),
        scratch_shapes=[
            pltpu.VMEM((nd, rows, width), jnp.float32),
            pltpu.VMEM((rows, width), jnp.float32),
            pltpu.VMEM((nt, rows, width), jnp.float32),
            pltpu.SemaphoreType.DMA((nd,)),
            pltpu.SemaphoreType.DMA((nd,)),
            pltpu.SemaphoreType.DMA((nt,)),
            pltpu.SemaphoreType.DMA((nt,)),
        ],
        cost_estimate=cost(rows * model, 8 * rows * model),
        compiler_params=pltpu.CompilerParams(collective_id=2, has_side_effects=True),
        name="sum_small",
    )(x)


def body(
    tokens,
    out_grad,
    lengths,
    norm_gain,
    norm_bias,
    qkv_weight,
    qkv_bias,
    out_weight,
    gate_up_weight,
    down_weight,
    first_norm_gain,
    first_norm_bias,
    first_qkv_weight,
    first_qkv_bias,
    first_out_weight,
    first_gate_up_weight,
    first_down_weight,
    second_norm_gain,
    second_norm_bias,
    second_qkv_weight,
    second_qkv_bias,
    second_out_weight,
    second_gate_up_weight,
    second_down_weight,
):
    slots = lax.axis_size("tensor")
    rank = lax.axis_index("tensor")
    own_rows = tokens.shape[0]
    group_rows = own_rows * slots
    width = out_weight.shape[0]
    order = rank if square(slots) else jnp.zeros_like(rank)

    chunk = jnp.bitwise_xor(jnp.arange(slots, dtype=jnp.int32), order)
    row_index = (chunk[:, None] * own_rows + jnp.arange(own_rows, dtype=jnp.int32)[None, :]).reshape(-1)
    seq_start, _ = layout(lengths[0], row_index)
    position = row_index - seq_start
    own_index = rank * own_rows + jnp.arange(own_rows, dtype=jnp.int32)
    live = layout(lengths[0], own_index)[1][:, None]
    block_start, _ = layout(lengths[0], jnp.arange(group_rows // BLOCK, dtype=jnp.int32) * BLOCK)
    table = jnp.concatenate([order.reshape(1).astype(jnp.int32), block_start // BLOCK])
    starts = seq_start[None, :]
    small_low = jnp.concatenate([norm_gain, norm_bias, qkv_bias, qkv_bias[:1]], axis=0).astype(low_type)
    own_bias = lambda full: lax.dynamic_slice_in_dim(full[4:7], rank * width, width, 1)[:, None, :]

    if square(slots):
        attn_low = jnp.concatenate([qkv_weight, out_weight.T[None]], axis=0).astype(low_type)
        attn_full = lax.all_gather(attn_low, "dp", axis=1, tiled=True)
        lane = jnp.arange(PAIR, dtype=jnp.int32) % (ROT // 2)
        inverse = jnp.power(rope_base, -lane.astype(jnp.float32) * (2.0 / ROT))[None, :]
        position = position.astype(jnp.float32).reshape(-1, 256)
        h1, small_full, *tables, dm_top, dm_end, gate_up_low = gather_norm(
            tokens, small_low.astype(jnp.float32), position, inverse, out_grad, live, gate_up_weight
        )
        norm = small_full[:4]
        gate_up_full = lax.all_gather(after(gate_up_low, attn_full), "dp", axis=1, tiled=True)
        dm_first, dm_rest = gather_rows(dm_top, dm_end)
        q, k, v, kt, vt = qkv_all(h1, attn_full, own_bias(small_full), tables)

        o_a, lse_a = attn_fwd(0, slots, table, q, k, vt, starts)
        dm_far = dm_rest(o_a)
        o_b, lse_b = attn_fwd(1, slots, table, after(q, o_a, *dm_first), k, vt, starts)
        o_b = after(o_b, *dm_far)
        dm_blocks = dm_first + dm_far

        x1, h2_own = out_scatter(o_a, o_b, attn_full, tokens, live, norm)
        down_low = after(down_weight.astype(low_type), gate_up_full, h2_own)
        down_full = lax.all_gather(down_low, "dp", axis=1, tiled=True)
        h2, act, slope_gate, slope_up, grad_down = gather_gate_up(h2_own, gate_up_full, dm_blocks)
        grad_down_own = lax.psum_scatter(after(grad_down, down_full), "dp", scatter_dimension=1, tiled=True)

        grad_gate, dup, dx1, dattn_own, gain_two, shift_two = hidden_scatter(
            dm_blocks, slope_gate, slope_up, down_full, gate_up_full, h2, x1, out_grad, live, norm
        )
        grad_gate = after(grad_gate, grad_down_own)
        grad_gate_own = lax.psum_scatter(grad_gate, "dp", scatter_dimension=0, tiled=True)

        do, grad_out, mlp, far_top, far_end, grad_up = gather_do(dattn_own, act, h2, dup, o_a, o_b, attn_full, down_full)
        grad_up = after(grad_up, grad_gate_own)
        grad_up_own = lax.psum_scatter(grad_up, "dp", scatter_dimension=0, tiled=True)
        mlp_first = [lax.ppermute(far_top, "tensor", swap_x), lax.ppermute(far_end, "tensor", swap_y)]
        *back_a, grad_down_full, down_one, down_two, down_three = attn_bwd(
            0, slots, table, q, do, o_a, k, v, kt, starts, lse_a, tables,
            grad_down_own, (down_weight, first_down_weight, second_down_weight),
        )
        down_step = (grad_down_full, down_one, down_two, down_three)
        hidden = (gate_up_weight, first_gate_up_weight, second_gate_up_weight)
        for_x, for_y = pass_on(mlp, *[after(part, back_a[0]) for part in mlp_first])
        mlp_parts = [mlp, lax.ppermute(for_x, "tensor", swap_x), lax.ppermute(for_y, "tensor", swap_y)]
        results = attn_bwd(
            1, slots, table, q, after(do, back_a[0], for_x), o_b, k, v, kt, starts, lse_b, tables, grad_gate_own, hidden
        )
        back_b, begun = results[:3], results[3:]
        dlin = [side for pair in zip(back_a, back_b) for side in pair]
        grad_rest, bias_local, *hidden_step = qkv_grad(h1, dlin, grad_out, grad_up_own, hidden, begun)
        late = [after(dlin[0], grad_rest, *mlp_parts[1:])] + dlin[1:]
        input_grad, gain_one, shift_one, layer_out = first_scatter(
            late, attn_full, tokens, dx1, norm, live, x1, mlp_parts
        )
        grad_rest = after(grad_rest, grad_up_own)
        grad_rest_own = lax.psum_scatter(grad_rest, "dp", scatter_dimension=1, tiled=True)
        rest_step = adam_rest(
            grad_rest_own,
            (qkv_weight, first_qkv_weight, second_qkv_weight),
            (out_weight, first_out_weight, second_out_weight),
        )
        qkv_step, out_step = rest_step[:4], rest_step[4:]
    else:
        everyone = lambda value: lax.all_gather(value, "tensor", axis=0, tiled=True)
        scatter = lambda value, axis, at: lax.psum_scatter(value.astype(low_type), axis, scatter_dimension=at, tiled=True)
        small_full = lax.all_gather(small_low, "dp", axis=1, tiled=True).astype(jnp.float32)
        qkv_full, out_full, gate_up_full, down_full = (
            lax.all_gather(w.astype(low_type), "dp", axis=1, tiled=True)
            for w in (qkv_weight, out_weight, gate_up_weight, down_weight)
        )
        gain_rows, shift_rows = small_full[0:2], small_full[2:4]
        rows_in, cotangent = tokens.astype(jnp.float32), out_grad.astype(jnp.float32)
        tables = rotary_tables(position)
        h1 = everyone(layer_norm(rows_in, gain_rows[0], shift_rows[0]).astype(low_type))
        q, k, v, kt, vt = qkv_all(h1, qkv_full, own_bias(small_full), tables)
        o_a, lse_a = attn_fwd(0, slots, table, q, k, vt, starts)
        o_b, lse_b = attn_fwd(1, slots, table, q, k, vt, starts)
        o = jnp.concatenate([o_a, o_b], axis=1)
        x1 = rows_in + live * scatter(dot32(o, out_full), "tensor", 0).astype(jnp.float32)
        h2 = everyone(layer_norm(x1, gain_rows[1], shift_rows[1]).astype(low_type))
        gate, up = dot32(h2, gate_up_full[0]), dot32(h2, gate_up_full[1])
        sig = 1.0 / (1.0 + jnp.exp(-gate))
        act = (gate * sig * up).astype(low_type)
        mlp_rows = scatter(dot32(act, down_full), "tensor", 0).astype(jnp.float32)
        layer_out = (x1 + live * mlp_rows).astype(low_type)
        dm = everyone((cotangent * live).astype(low_type))
        da = dot32(dm, down_full, contract_last)
        dgate = (da * up * sig * (1.0 + gate * (1.0 - sig))).astype(low_type)
        dup = (da * gate * sig).astype(low_type)
        grad_down_own = scatter(dot32(act, dm, contract_first), "dp", 1)
        grad_gate_up = jnp.stack([dot32(h2, dgate, contract_first), dot32(h2, dup, contract_first)])
        grad_gate_up_own = scatter(grad_gate_up, "dp", 1)
        dh2 = dot32(dgate, gate_up_full[0], contract_last) + dot32(dup, gate_up_full[1], contract_last)
        dh2 = scatter(dh2, "tensor", 0).astype(jnp.float32)
        back, gain_two, shift_two = jax.vjp(layer_norm, x1, gain_rows[1], shift_rows[1])[1](dh2)
        dx1 = cotangent + back
        dattn = everyone((dx1 * live).astype(low_type))
        do = dot32(dattn, out_full, contract_last).astype(low_type)
        grad_out = dot32(dattn, o, contract_first).astype(low_type)
        back_a = attn_bwd(0, slots, table, q, do, o_a, k, v, kt, starts, lse_a, tables)
        back_b = attn_bwd(1, slots, table, q, do, o_b, k, v, kt, starts, lse_b, tables)
        dlin = [side for pair in zip(back_a, back_b) for side in pair]
        grad_rest, bias_local = qkv_grad(h1, dlin, grad_out)
        grad_rest_own = scatter(grad_rest, "dp", 1)
        grad_qkv_own, grad_out_own = grad_rest_own[:3], grad_rest_own[3].T
        dh1 = sum(
            dot32(jnp.concatenate(dlin[2 * n : 2 * n + 2], axis=1), qkv_full[n], contract_last) for n in range(3)
        )
        dh1 = scatter(dh1, "tensor", 0).astype(jnp.float32)
        back, gain_one, shift_one = jax.vjp(layer_norm, rows_in, gain_rows[0], shift_rows[0])[1](dh1)
        input_grad = (dx1 + back).astype(low_type)
        gain_one, gain_two, shift_one, shift_two = (
            value[None, :] for value in (gain_one, gain_two, shift_one, shift_two)
        )

        def whole_step(gradient, *held):
            gradient = gradient.astype(jnp.float32)
            return (gradient,) + adamw_update(held[0], gradient, held[1], held[2], weight_decay)

        qkv_step = whole_step(grad_qkv_own, qkv_weight, first_qkv_weight, second_qkv_weight)
        out_step = whole_step(grad_out_own, out_weight, first_out_weight, second_out_weight)
        hidden_step = whole_step(grad_gate_up_own, gate_up_weight, first_gate_up_weight, second_gate_up_weight)
        down_step = whole_step(grad_down_own, down_weight, first_down_weight, second_down_weight)

    bias_placed = lax.dynamic_update_slice(
        jnp.zeros((3, small_full.shape[1]), jnp.float32), bias_local, (jnp.int32(0), rank * width)
    )
    small_local = jnp.concatenate([gain_one, gain_two, shift_one, shift_two, bias_placed, bias_placed[:1]], axis=0)
    small_own = sum_small(small_local)

    def small_step(gradient, *held):
        return (gradient,) + adamw_update(held[0], gradient, held[1], held[2], 0.0)

    gain_step = small_step(small_own[0:2], norm_gain, first_norm_gain, second_norm_gain)
    shift_step = small_step(small_own[2:4], norm_bias, first_norm_bias, second_norm_bias)
    bias_step = small_step(small_own[4:7], qkv_bias, first_qkv_bias, second_qkv_bias)
    steps = (gain_step, shift_step, qkv_step, bias_step, out_step, hidden_step, down_step)
    return (layer_out, input_grad) + tuple(step[n] for n in range(4) for step in steps)


def solution(mesh):
    return jax.shard_map(
        body,
        mesh=mesh,
        in_specs=(
            P(("dp", "tensor"), None),
            P(("dp", "tensor"), None),
            P("dp", None),
            P(None, "dp"),
            P(None, "dp"),
            P(None, "dp", "tensor"),
            P(None, "dp"),
            P("tensor", "dp"),
            P(None, "dp", "tensor"),
            P("tensor", "dp"),
            P(None, "dp"),
            P(None, "dp"),
            P(None, "dp", "tensor"),
            P(None, "dp"),
            P("tensor", "dp"),
            P(None, "dp", "tensor"),
            P("tensor", "dp"),
            P(None, "dp"),
            P(None, "dp"),
            P(None, "dp", "tensor"),
            P(None, "dp"),
            P("tensor", "dp"),
            P(None, "dp", "tensor"),
            P("tensor", "dp"),
        ),
        out_specs=(
            P(("dp", "tensor"), None),
            P(("dp", "tensor"), None),
            P(None, "dp"),
            P(None, "dp"),
            P(None, "dp", "tensor"),
            P(None, "dp"),
            P("tensor", "dp"),
            P(None, "dp", "tensor"),
            P("tensor", "dp"),
            P(None, "dp"),
            P(None, "dp"),
            P(None, "dp", "tensor"),
            P(None, "dp"),
            P("tensor", "dp"),
            P(None, "dp", "tensor"),
            P("tensor", "dp"),
            P(None, "dp"),
            P(None, "dp"),
            P(None, "dp", "tensor"),
            P(None, "dp"),
            P("tensor", "dp"),
            P(None, "dp", "tensor"),
            P("tensor", "dp"),
            P(None, "dp"),
            P(None, "dp"),
            P(None, "dp", "tensor"),
            P(None, "dp"),
            P("tensor", "dp"),
            P(None, "dp", "tensor"),
            P("tensor", "dp"),
        ),
        check_vma=False,
    )
```

```python
import functools

import jax
import jax.numpy as jnp
from jax import lax
from jax.experimental import pallas as pl
from jax.experimental.pallas import tpu as pltpu
from jax.sharding import PartitionSpec as P

HEAD_DIM = 64
ROT = 16
PAIR = 2 * HEAD_DIM
BLOCK = 256

norm_eps = 1e-05
rope_base = 10000.0
beta_one = 0.9
beta_two = 0.95
adam_eps = 1e-08
learn_rate = 0.01
weight_decay = 0.1
step_count = 10.0
masked_score = -1e30
contract_last = (((1,), (1,)), ((), ()))
contract_first = (((0,), (0,)), ((), ()))
low_type = jnp.bfloat16
MIB = 2**20


def layout(seq_lengths, row_index):
    slot = jnp.arange(seq_lengths.shape[0])
    seq_ends = jnp.sum(
        jnp.where(slot[:, None] <= slot[None, :], seq_lengths[:, None], 0), axis=0
    )
    passed = row_index[:, None] >= seq_ends[None, :]
    seq_start = jnp.sum(jnp.where(passed, seq_lengths[None, :], 0), axis=1)
    live_rows = (row_index < jnp.sum(seq_lengths)).astype(jnp.float32)
    return (seq_start, live_rows)


def rotary_tables(position):
    half_rot = ROT // 2
    lane = jnp.arange(PAIR, dtype=jnp.int32) % HEAD_DIM
    powers = (lane % half_rot).astype(jnp.float32) * (2.0 / ROT)
    inverse = jnp.power(rope_base, -powers)
    angles = position.astype(jnp.float32)[:, None] * inverse[None, :]
    cos_part, sine_part = jnp.cos(angles), jnp.sin(angles)
    lane = lane[None, :]
    keep = jnp.where(lane < ROT, cos_part, 1.0)
    above = jnp.where(lane < half_rot, -sine_part, 0.0)
    below = jnp.where((lane >= half_rot) & (lane < ROT), sine_part, 0.0)
    return (keep, above, below)


def dot32(a, b, dims=None):
    if dims is None:
        return jnp.dot(a, b, preferred_element_type=jnp.float32)
    return lax.dot_general(a, b, dims, preferred_element_type=jnp.float32)


def turn(values, keep, above, below):
    up = pltpu.roll(values, PAIR - ROT // 2, 1)
    down = pltpu.roll(values, ROT // 2, 1)
    return values * keep + up * above + down * below


def turn_back(values, keep, above, below):
    up = pltpu.roll(values, PAIR - ROT // 2, 1)
    down = pltpu.roll(values, ROT // 2, 1)
    return values * keep - up * above - down * below


def adamw_update(weight_now, gradient, moment_one, moment_two, decay_rate):
    moment_one = beta_one * moment_one + (1.0 - beta_one) * gradient
    moment_two = beta_two * moment_two + (1.0 - beta_two) * gradient * gradient
    scaled_one = moment_one / (1.0 - beta_one**step_count)
    scaled_two = moment_two / (1.0 - beta_two**step_count)
    change = scaled_one / (jnp.sqrt(scaled_two) + adam_eps) + decay_rate * weight_now
    return (-learn_rate * change, moment_one, moment_two)


def cost(flops, moved, exps=0):
    return pl.CostEstimate(flops=int(flops) // 16, bytes_accessed=int(moved) // 16, transcendentals=int(exps) // 16)


def params(limit):
    return pltpu.CompilerParams(vmem_limit_bytes=limit * MIB)


ANY = pl.BlockSpec(memory_space=pl.ANY)


def layer_norm(values, gain_row, shift_row):
    center = values - jnp.mean(values, axis=-1, keepdims=True)
    spread = jnp.mean(center * center, axis=-1, keepdims=True)
    return center * lax.rsqrt(spread + norm_eps) * gain_row + shift_row


def qkv_kernel(scale, h_ref, w_ref, bias_ref, keep_ref, above_ref, below_ref, q_ref, k_ref, v_ref, kt_ref, vt_ref):
    h = h_ref[...]
    keep, above, below = keep_ref[...], above_ref[...], below_ref[...]
    width = q_ref.shape[1]
    lin = dot32(h, w_ref[0]) + bias_ref[0]
    for c in range(0, width, PAIR):
        u = turn(lin[:, c : c + PAIR], keep, above, below)
        q_ref[:, c : c + PAIR] = (u.astype(low_type) * scale).astype(low_type)
    lin = dot32(h, w_ref[1]) + bias_ref[1]
    for c in range(0, width, PAIR):
        u = turn(lin[:, c : c + PAIR], keep, above, below)
        k_ref[:, c : c + PAIR] = u.astype(low_type)
        kt_ref[c : c + PAIR, :] = u.T.astype(low_type)
    lin = dot32(h, w_ref[2]) + bias_ref[2]
    v_ref[...] = lin.astype(low_type)
    vt_ref[...] = lin.T.astype(low_type)


def qkv_all(h, w, bias, tables):
    total, model = h.shape
    rows = 256
    width = w.shape[2]
    row = lambda n: pl.BlockSpec((rows, n), lambda i: (i, 0))
    col = pl.BlockSpec((width, rows), lambda i: (0, i))
    flat = jax.ShapeDtypeStruct((total, width), low_type)
    turned = jax.ShapeDtypeStruct((width, total), low_type)
    return pl.pallas_call(
        functools.partial(qkv_kernel, HEAD_DIM ** (-0.5)),
        grid=(total // rows,),
        in_specs=[
            row(model),
            pl.BlockSpec((3,) + w.shape[1:], lambda i: (0, 0, 0), pipeline_mode=pl.Buffered(1)),
            pl.BlockSpec(bias.shape, lambda i: (0, 0, 0)),
            row(PAIR),
            row(PAIR),
            row(PAIR),
        ],
        out_specs=[row(width), row(width), row(width), col, col],
        out_shape=[flat, flat, flat, turned, turned],
        cost_estimate=cost(6 * total * model * width, 6 * model * width + 10 * total * model),
        compiler_params=params(60),
        name="qkv",
    )(h, w, bias, *tables)


def place(block, rank, per):
    return jnp.bitwise_xor(block // per, rank) * per + block % per


def attn_fwd_kernel(per, table_ref, q_ref, k_ref, vt_ref, start_ref, o_ref, lse_ref, m_s, l_s, acc_s):
    i = pl.program_id(0)
    rank = table_ref[0]
    heads = q_ref.shape[1] // HEAD_DIM
    first = lax.broadcasted_iota(jnp.int32, (BLOCK, PAIR), 1) < HEAD_DIM
    queries = []
    for h in range(heads):
        pair = q_ref[:, (h // 2) * PAIR : (h // 2 + 1) * PAIR]
        keep = first if h % 2 == 0 else jnp.logical_not(first)
        queries.append(jnp.where(keep, pair, jnp.zeros_like(pair)))
    m_s[...] = jnp.full_like(m_s, -jnp.inf)
    l_s[...] = jnp.zeros_like(l_s)
    acc_s[...] = jnp.zeros_like(acc_s)
    start = start_ref[...]
    row = i * BLOCK + lax.broadcasted_iota(jnp.int32, (BLOCK, BLOCK), 1)

    def step(kb, carry):
        col = kb * BLOCK + lax.broadcasted_iota(jnp.int32, (BLOCK, BLOCK), 0)
        bias = jnp.where((col >= start) & (col <= row), 0.0, masked_score)
        at = pl.ds(pl.multiple_of(place(kb, rank, per) * BLOCK, BLOCK), BLOCK)
        scores = [
            dot32(k_ref[at, (h // 2) * PAIR : (h // 2 + 1) * PAIR], queries[h], contract_last) for h in range(heads)
        ]
        probs, alphas = [], []
        for h in range(heads):
            s = scores[h] + bias
            m_old = m_s[h : h + 1, :]
            m_new = jnp.maximum(m_old, jnp.max(s, axis=0, keepdims=True))
            alpha = jnp.exp(m_old - m_new)
            p = jnp.exp(s - m_new)
            l_s[h : h + 1, :] = l_s[h : h + 1, :] * alpha + jnp.sum(p, axis=0, keepdims=True)
            m_s[h : h + 1, :] = m_new
            probs.append(p.astype(low_type))
            alphas.append(alpha)
        for h in range(heads):
            own = slice(h * HEAD_DIM, (h + 1) * HEAD_DIM)
            acc_s[own, :] = acc_s[own, :] * alphas[h] + dot32(vt_ref[own, at], probs[h])
        return carry

    lax.fori_loop(table_ref[1 + i], i + 1, step, 0)
    for h in range(heads):
        own = slice(h * HEAD_DIM, (h + 1) * HEAD_DIM)
        acc_s[own, :] = acc_s[own, :] / l_s[h : h + 1, :]
    o_ref[...] = acc_s[...].T.astype(low_type)
    lse_ref[0] = m_s[...] + jnp.log(l_s[...])


def attn_fwd(half, slots, table, q, k, vt, start):
    rows, width = q.shape
    part = width // 2
    heads = part // HEAD_DIM
    count = rows // BLOCK
    per = rows // slots // BLOCK
    at = lambda i, t: place(i, t[0], per)
    return pl.pallas_call(
        functools.partial(attn_fwd_kernel, per),
        grid_spec=pltpu.PrefetchScalarGridSpec(
            num_scalar_prefetch=1,
            grid=(count,),
            in_specs=[
                pl.BlockSpec((BLOCK, part), lambda i, t: (at(i, t), half)),
                pl.BlockSpec((rows, part), lambda i, t: (0, half)),
                pl.BlockSpec((part, rows), lambda i, t: (half, 0)),
                pl.BlockSpec((1, BLOCK), lambda i, t: (0, at(i, t))),
            ],
            out_specs=[
                pl.BlockSpec((BLOCK, part), lambda i, t: (at(i, t), 0)),
                pl.BlockSpec((1, heads, BLOCK), lambda i, t: (at(i, t), 0, 0)),
            ],
            scratch_shapes=[
                pltpu.VMEM((heads, BLOCK), jnp.float32),
                pltpu.VMEM((heads, BLOCK), jnp.float32),
                pltpu.VMEM((part, BLOCK), jnp.float32),
            ],
        ),
        out_shape=[
            jax.ShapeDtypeStruct((rows, part), low_type),
            jax.ShapeDtypeStruct((count, heads, BLOCK), jnp.float32),
        ],
        cost_estimate=cost(rows * rows, rows * part),
        compiler_params=params(60),
        name="attn_fwd",
    )(table, q, k, vt, start)


def adam_blocks(low_ref, in_refs, out_refs):
    gradient = low_ref[...].astype(jnp.float32).reshape(out_refs[0].shape)
    results = adamw_update(in_refs[0][...], gradient, in_refs[1][...], in_refs[2][...], weight_decay)
    out_refs[0][...] = gradient
    for ref, value in zip(out_refs[1:], results):
        ref[...] = value


def attn_bwd_kernel(per, adam, table_ref, q_ref, do_ref, o_ref, k_ref, v_ref, kt_ref, start_ref, lse_ref,
                    keep_ref, above_ref, below_ref, *rest):
    (dq_ref, dk_ref, dv_ref), (dq_s, dk_s, dv_s) = rest[4 * adam : 4 * adam + 3], rest[-3:]
    if adam:
        adam_blocks(rest[0], rest[1:4], rest[7:11])
    i = pl.program_id(0)
    rank = table_ref[0]
    width = q_ref.shape[1]
    heads = width // HEAD_DIM
    first = lax.broadcasted_iota(jnp.int32, (BLOCK, PAIR), 1) < HEAD_DIM

    @pl.when(i == 0)
    def _():
        dk_s[...] = jnp.zeros_like(dk_s)
        dv_s[...] = jnp.zeros_like(dv_s)

    dq_s[...] = jnp.zeros_like(dq_s)
    queries, cotangents, inner = [], [], []
    product = (do_ref[...].astype(jnp.float32) * o_ref[...].astype(jnp.float32)).T
    for h in range(heads):
        cols = slice((h // 2) * PAIR, (h // 2 + 1) * PAIR)
        keep = first if h % 2 == 0 else jnp.logical_not(first)
        pair = q_ref[:, cols]
        queries.append(jnp.where(keep, pair, jnp.zeros_like(pair)))
        pair = do_ref[:, cols]
        cotangents.append(jnp.where(keep, pair, jnp.zeros_like(pair)))
        inner.append(jnp.sum(product[h * HEAD_DIM : (h + 1) * HEAD_DIM, :], axis=0, keepdims=True))
    start = start_ref[...]
    row = i * BLOCK + lax.broadcasted_iota(jnp.int32, (BLOCK, BLOCK), 1)

    def step(kb, carry):
        col = kb * BLOCK + lax.broadcasted_iota(jnp.int32, (BLOCK, BLOCK), 0)
        bias = jnp.where((col >= start) & (col <= row), 0.0, masked_score)
        at = pl.ds(pl.multiple_of(place(kb, rank, per) * BLOCK, BLOCK), BLOCK)
        raw, grads = [], []
        for h in range(heads):
            cols = slice((h // 2) * PAIR, (h // 2 + 1) * PAIR)
            raw.append(dot32(k_ref[at, cols], queries[h], contract_last))
            grads.append(dot32(v_ref[at, cols], cotangents[h], contract_last))
        probs, scores = [], []
        for h in range(heads):
            p = jnp.exp(raw[h] + bias - lse_ref[0, h : h + 1, :])
            scores.append((p * (grads[h] - inner[h])).astype(low_type))
            probs.append(p.astype(low_type))
        for h in range(heads):
            own = slice(h * HEAD_DIM, (h + 1) * HEAD_DIM)
            dq_s[own, :] += dot32(kt_ref[own, at], scores[h])
        for one in range(0, heads, 2):
            cols = slice(one * HEAD_DIM, one * HEAD_DIM + PAIR)
            dv_s[at, cols] += dot32(probs[one], cotangents[one]) + dot32(probs[one + 1], cotangents[one + 1])
            dk_s[at, cols] += dot32(scores[one], queries[one]) + dot32(scores[one + 1], queries[one + 1])
        return carry

    lax.fori_loop(table_ref[1 + i], i + 1, step, 0)
    dq = dq_s[...].T * (HEAD_DIM ** (-0.5))
    here = pl.ds(pl.multiple_of(place(i, rank, per) * BLOCK, BLOCK), BLOCK)
    for c in range(0, width, PAIR):
        dq_ref[:, c : c + PAIR] = turn_back(
            dq[:, c : c + PAIR], keep_ref[here, :], above_ref[here, :], below_ref[here, :]
        ).astype(low_type)

    @pl.when(i == pl.num_programs(0) - 1)
    def _():
        @pl.loop(0, dk_s.shape[0] // BLOCK)
        def _(b):
            at = pl.ds(pl.multiple_of(b * BLOCK, BLOCK), BLOCK)
            for c in range(0, width, PAIR):
                cols = slice(c, c + PAIR)
                dk_ref[at, cols] = turn_back(
                    dk_s[at, cols], keep_ref[at, :], above_ref[at, :], below_ref[at, :]
                ).astype(low_type)
                dv_ref[at, cols] = dv_s[at, cols].astype(low_type)


def attn_bwd(half, slots, table, q, do, o, k, v, kt, start, lse, tables, low=None, held=()):
    rows, width = q.shape
    part = width // 2
    heads = part // HEAD_DIM
    count = rows // BLOCK
    per = rows // slots // BLOCK
    at = lambda i, t: place(i, t[0], per)
    whole = pl.BlockSpec((rows, part), lambda i, t: (0, half))
    turns = pl.BlockSpec((rows, PAIR), lambda i, t: (0, 0))
    result = pl.BlockSpec((rows, part), lambda i, t: (0, 0))
    adam = low is not None
    adam_in, adam_out, adam_like = [], [], []
    if adam:
        strip, depth = low.shape[0] // count, low.shape[1]
        flat = pl.BlockSpec((strip, depth), lambda i, t: (i, 0))
        one = flat if held[0].ndim == 2 else pl.BlockSpec((1, strip, depth), lambda i, t: (0, i, 0))
        adam_in, adam_out = [flat, one, one, one], [one] * 4
        adam_like = [jax.ShapeDtypeStruct(held[0].shape, jnp.float32)] * 4
    return pl.pallas_call(
        functools.partial(attn_bwd_kernel, per, int(adam)),
        grid_spec=pltpu.PrefetchScalarGridSpec(
            num_scalar_prefetch=1,
            grid=(count,),
            in_specs=[
                pl.BlockSpec((BLOCK, part), lambda i, t: (at(i, t), half)),
                pl.BlockSpec((BLOCK, part), lambda i, t: (at(i, t), half)),
                pl.BlockSpec((BLOCK, part), lambda i, t: (at(i, t), 0)),
                whole,
                whole,
                pl.BlockSpec((part, rows), lambda i, t: (half, 0)),
                pl.BlockSpec((1, BLOCK), lambda i, t: (0, at(i, t))),
                pl.BlockSpec((1, heads, BLOCK), lambda i, t: (at(i, t), 0, 0)),
                turns,
                turns,
                turns,
            ]
            + adam_in,
            out_specs=[pl.BlockSpec((BLOCK, part), lambda i, t: (at(i, t), 0)), result, result] + adam_out,
            scratch_shapes=[
                pltpu.VMEM((part, BLOCK), jnp.float32),
                pltpu.VMEM((rows, part), jnp.float32),
                pltpu.VMEM((rows, part), jnp.float32),
            ],
        ),
        out_shape=[jax.ShapeDtypeStruct((rows, part), low_type)] * 3 + adam_like,
        cost_estimate=cost(25 * rows * rows * part // 2, 16 * rows * part, 8 * rows * rows // 4),
        compiler_params=params(60),
        name="attn_bwd",
    )(table, q, do, o, k, v, kt, start, lse, *tables, *((low,) + tuple(held) if adam else ()))


def qkv_grad_kernel(count, adam, *refs):
    left_ref, other_ref, rights = refs[0], refs[1], refs[2 : 2 + count]
    out_ref, sum_ref = refs[2 + count + 8 * adam : 4 + count + 8 * adam]
    if adam:
        adam_blocks(refs[2 + count], refs[3 + count : 6 + count], refs[-4:])
    part = rights[0].shape[1]

    @pl.when(pl.program_id(0) == 0)
    def _():
        for n, right in enumerate(rights):
            sum_ref[n // 2 : n // 2 + 1, (n % 2) * part : (n % 2 + 1) * part] = jnp.sum(
                right[...].astype(jnp.float32), axis=0, keepdims=True
            )

    left = left_ref[...]
    for n, right in enumerate(rights):
        out_ref[n // 2, :, (n % 2) * part : (n % 2 + 1) * part] = dot32(left, right[...], contract_first).astype(low_type)
    out_ref[len(rights) // 2] = other_ref[...]


def qkv_grad(left, rights, other, low=None, held=(), begun=()):
    rows, model = left.shape
    part = rights[0].shape[1]
    count = len(rights) // 2
    tile = 512
    adam = low is not None
    adam_in, adam_out, adam_like, extra = [], [], [], ()
    if adam:
        strip, depth = low.shape[0] // (model // tile), low.shape[1]
        one = pl.BlockSpec((1, strip, depth), lambda n: (1, n, 0))
        adam_in = [pl.BlockSpec((strip, depth), lambda n: (n, 0)), one, one, one] + [ANY] * 4
        adam_out = [one] * 4
        adam_like = [jax.ShapeDtypeStruct(held[0].shape, jnp.float32)] * 4
        extra = (low,) + tuple(held) + tuple(begun)
    first = 2 + len(rights) + 4
    return pl.pallas_call(
        functools.partial(qkv_grad_kernel, len(rights), int(adam)),
        grid=(model // tile,),
        in_specs=[pl.BlockSpec((rows, tile), lambda n: (0, n)), pl.BlockSpec((tile, 2 * part), lambda n: (n, 0))]
        + [pl.BlockSpec((rows, part), lambda n: (0, 0), pipeline_mode=pl.Buffered(1))] * len(rights)
        + adam_in,
        input_output_aliases={first + n: 2 + n for n in range(4)} if adam else {},
        out_specs=[
            pl.BlockSpec((count + 1, tile, 2 * part), lambda n: (0, n, 0)),
            pl.BlockSpec((count, 2 * part), lambda n: (0, 0)),
        ]
        + adam_out,
        out_shape=[
            jax.ShapeDtypeStruct((count + 1, model, 2 * part), low_type),
            jax.ShapeDtypeStruct((count, 2 * part), jnp.float32),
        ]
        + adam_like,
        cost_estimate=cost(4 * count * rows * model * part, 4 * rows * model),
        compiler_params=params(60),
        name="qkv_grad",
    )(left, other, *rights, *extra)


swap_x = [(0, 1), (1, 0), (2, 3), (3, 2)]
swap_y = [(0, 2), (2, 0), (1, 3), (3, 1)]


def square(count):
    return count == 4


def gather_rows(top, end):
    x_top = lax.ppermute(top, "tensor", swap_x)
    y_end = lax.ppermute(end, "tensor", swap_y)
    x_end = lax.ppermute(end, "tensor", swap_x)
    y_top = lax.ppermute(top, "tensor", swap_y)
    first = [top, end, x_top, x_end, y_top, y_end]

    def rest(*between):
        far_top = lax.ppermute(after(x_top, *between), "tensor", swap_y)
        far_end = lax.ppermute(after(y_end, *between), "tensor", swap_x)
        return [far_top, far_end]

    return first, rest


def after(value, *others):
    return lax.optimization_barrier((value,) + others)[0]


def pass_on_kernel(one_ref, two_ref, top_ref, end_ref, for_x_ref, for_y_ref):
    i, half = pl.program_id(0), pl.num_programs(0) // 2
    add = lambda a, b: (a[...].astype(jnp.float32) + b[...].astype(jnp.float32)).astype(low_type)

    @pl.when(i < half)
    def _():
        for_x_ref[...] = one_ref[...]
        for_y_ref[...] = add(two_ref, top_ref)

    @pl.when(i >= half)
    def _():
        for_x_ref[...] = add(one_ref, end_ref)
        for_y_ref[...] = two_ref[...]


def pass_on(rows_in, top, end):
    half, model = top.shape
    block = 64
    per = 2 * half // block
    spec = lambda index: pl.BlockSpec((block, model), lambda i: (index(i), 0))
    return pl.pallas_call(
        pass_on_kernel,
        grid=(per,),
        in_specs=[
            spec(lambda i: per + i),
            spec(lambda i: 2 * per + i),
            spec(lambda i: jnp.minimum(i, per // 2 - 1)),
            spec(lambda i: jnp.maximum(i, per // 2) - per // 2),
        ],
        out_specs=[spec(lambda i: i)] * 2,
        out_shape=[jax.ShapeDtypeStruct((2 * half, model), low_type)] * 2,
        cost_estimate=cost(4 * half * model, 20 * half * model),
        compiler_params=params(60),
        name="pass_on",
    )(rows_in, rows_in, top, end)


MESH = pl.DeviceIdType.MESH


def greet(near_x, near_y):
    barrier = pltpu.get_barrier_semaphore()
    for near in (near_x, near_y):
        pl.semaphore_signal(barrier, inc=1, device_id={"tensor": near}, device_id_type=MESH)
    pl.semaphore_wait(barrier, 2)


def neighbours():
    rank = lax.axis_index("tensor")
    return jnp.bitwise_xor(rank, 1), jnp.bitwise_xor(rank, 2)


def remote(index, source, target, near, send, recv):
    return pltpu.make_async_remote_copy(
        src_ref=source,
        dst_ref=target,
        send_sem=send.at[index],
        recv_sem=recv.at[index],
        device_id={"tensor": near},
        device_id_type=MESH,
    )


arrival = (0, 1, 2, 5, 3, 4, 6, 7)


def arrival_slot(i):
    return jnp.where(i == 3, 5, jnp.where(i == 4, 3, jnp.where(i == 5, 4, i)))


def square_copies(all_s, half, send, recv):
    near_x, near_y = neighbours()
    at = lambda n: all_s.at[pl.ds(n * half, half)]
    return (
        remote(0, at(0), at(2), near_x, send, recv),
        remote(1, at(1), at(5), near_y, send, recv),
        remote(2, at(1), at(3), near_x, send, recv),
        remote(3, at(0), at(4), near_y, send, recv),
        remote(4, at(2), at(6), near_y, send, recv),
        remote(5, at(5), at(7), near_x, send, recv),
    )


def await_slot(i, copies):
    x_top, y_end, x_end, y_top, far_top, far_end = copies

    @pl.when(i == 2)
    def _():
        x_top.wait_recv()
        far_top.start()
        y_end.wait_recv()
        far_end.start()

    for n, c in ((4, x_end), (5, y_top), (6, far_top), (7, far_end)):

        @pl.when(i == n)
        def _(c=c):
            c.wait_recv()


def fetch_next(i, refs, buf, sem):
    def fetch(j):
        pltpu.make_async_copy(refs[j], buf.at[j % 2], sem.at[j % 2]).start()

    for j in range(len(refs)):

        @pl.when(i == max(j - 1, 0) if j else i == 0)
        def _(j=j):
            fetch(j)

    pltpu.make_async_copy(refs[0], buf.at[i % 2], sem.at[i % 2]).wait()


def flow(first, last, loads, work, stores):
    def all_of(copies, act):
        for c in copies:
            act(c)

    all_of(loads(first), lambda c: c.start())

    def step(i, carry):
        @pl.when(i < last - 1)
        def _():
            all_of(loads(i + 1), lambda c: c.start())

        all_of(loads(i), lambda c: c.wait())

        @pl.when(i >= first + 2)
        def _():
            all_of(stores(i - 2), lambda c: c.wait())

        work(i)
        all_of(stores(i), lambda c: c.start())
        return carry

    lax.fori_loop(first, last, step, 0)
    for i in range(max(first, last - 2), last):
        all_of(stores(i), lambda c: c.wait())


def gather_norm_kernel(nd, x_ref, small_ref, pos_ref, inv_ref, og_ref, live_ref, w_hbm,
                       h_ref, full_ref, keep_ref, above_ref, below_ref, top_ref, end_ref, low_hbm,
                       all_s, full_s, stage, w_s, low_s, send, recv, local, small_send, small_recv, out_sem, w_sem, low_sem):
    d = lax.axis_index("dp")
    near_x, near_y = neighbours()
    half = x_ref.shape[0] // 2
    width = small_ref.shape[1]
    own = pltpu.make_async_copy(x_ref, all_s.at[pl.ds(0, 2 * half)], local)
    own.start()
    barrier = pltpu.get_barrier_semaphore()
    for near in (near_x, near_y):
        pl.semaphore_signal(barrier, inc=1, device_id={"tensor": near}, device_id_type=MESH)
    for k in range(1, nd):
        pl.semaphore_signal(barrier, inc=1, device_id={"dp": lax.rem(d + k, nd)}, device_id_type=MESH)
    pl.semaphore_wait(barrier, nd + 1)
    own.wait()
    copies = square_copies(all_s, half, send, recv)
    for c in copies[:4]:
        c.start()
    small = []
    for k in range(1, nd):
        c = pltpu.make_async_remote_copy(
            src_ref=small_ref,
            dst_ref=full_s.at[d],
            send_sem=small_send.at[k],
            recv_sem=small_recv.at[k],
            device_id={"dp": lax.rem(d + k, nd)},
            device_id_type=MESH,
        )
        c.start()
        small.append(c)
    full_s[d] = small_ref[...]
    for n, ref in enumerate((top_ref, end_ref)):

        @pl.loop(0, half // 32)
        def _(r, n=n, ref=ref):
            to = pl.ds(pl.multiple_of(r * 32, 32), 32)
            at = pl.ds(pl.multiple_of(n * half + r * 32, 32), 32)
            ref[to, :] = (og_ref[at, :].astype(jnp.float32) * live_ref[at, :]).astype(low_type)

    strip = w_s.shape[1]
    per = w_hbm.shape[1] // strip

    def side(i):
        return i // per, pl.ds(pl.multiple_of((i % per) * strip, strip), strip)

    def cast(i):
        low_s[i % 2] = w_s[i % 2].astype(low_type)

    flow(
        0,
        w_hbm.shape[0] * per,
        lambda i: [pltpu.make_async_copy(w_hbm.at[side(i)], w_s.at[i % 2], w_sem.at[i % 2])],
        cast,
        lambda i: [pltpu.make_async_copy(low_s.at[i % 2], low_hbm.at[side(i)], low_sem.at[i % 2])],
    )
    for c in small:
        c.wait_recv()
    for n in range(nd):
        full_ref[:, n * width : (n + 1) * width] = full_s[n]
    step = 32
    lane = lax.broadcasted_iota(jnp.int32, (256, PAIR), 1) % HEAD_DIM

    def turns(n):
        at = pl.ds(pl.multiple_of(n * 256, 256), 256)
        angles = jnp.broadcast_to(pos_ref[pl.ds(n, 1), :], (PAIR, 256)).T * inv_ref[...]
        cos_part, sine_part = jnp.cos(angles), jnp.sin(angles)
        keep_ref[at, :] = jnp.where(lane < ROT, cos_part, 1.0)
        above_ref[at, :] = jnp.where(lane < ROT // 2, -sine_part, 0.0)
        below_ref[at, :] = jnp.where((lane >= ROT // 2) & (lane < ROT), sine_part, 0.0)

    def out(buf, row):
        return pltpu.make_async_copy(stage.at[buf], h_ref.at[pl.ds(row, half)], out_sem.at[buf])

    def body_step(i, carry):
        await_slot(i, copies)
        row = pl.multiple_of(arrival_slot(i) * half, half)
        buf = i % 2

        @pl.when(i >= 2)
        def _():
            out(buf, row).wait()

        @pl.loop(0, half // step)
        def _(r):
            at = pl.ds(pl.multiple_of(r * step, step), step)
            x = all_s[pl.ds(pl.multiple_of(row + r * step, step), step), :].astype(jnp.float32)
            c = x - jnp.mean(x, axis=-1, keepdims=True)
            s = lax.rsqrt(jnp.mean(c * c, axis=-1, keepdims=True) + norm_eps)
            stage[buf, at, :] = (c * s * full_ref[0:1, :] + full_ref[2:3, :]).astype(low_type)

        out(buf, row).start()

        @pl.when((i >= 2) & (i < 6))
        def _():
            turns(2 * i - 4)
            turns(2 * i - 3)

        return carry

    lax.fori_loop(0, 8, body_step, 0)
    for buf in (0, 1):
        out(buf, 0).wait()
    for c in copies:
        c.wait_send()
    for c in small:
        c.wait_send()


def gather_norm(x, small, pos, inverse, out_grad, live, w):
    nd = lax.axis_size("dp")
    rows, model = x.shape
    total = 4 * rows
    count, width = small.shape
    vmem = pl.BlockSpec(memory_space=pltpu.VMEM)
    table = jax.ShapeDtypeStruct((total, PAIR), jnp.float32)
    return pl.pallas_call(
        functools.partial(gather_norm_kernel, nd),
        in_specs=[ANY, vmem, vmem, vmem, vmem, vmem, ANY],
        out_specs=[ANY, vmem, vmem, vmem, vmem, vmem, vmem, ANY],
        out_shape=[
            jax.ShapeDtypeStruct((total, model), low_type),
            jax.ShapeDtypeStruct((count, width * nd), jnp.float32),
            table,
            table,
            table,
            jax.ShapeDtypeStruct((rows // 2, model), low_type),
            jax.ShapeDtypeStruct((rows // 2, model), low_type),
            jax.ShapeDtypeStruct(w.shape, low_type),
        ],
        scratch_shapes=[
            pltpu.VMEM((total, model), low_type),
            pltpu.VMEM((nd, count, width), jnp.float32),
            pltpu.VMEM((2, rows // 2, model), low_type),
            pltpu.VMEM((2, 64, w.shape[2]), jnp.float32),
            pltpu.VMEM((2, 64, w.shape[2]), low_type),
            pltpu.SemaphoreType.DMA((6,)),
            pltpu.SemaphoreType.DMA((6,)),
            pltpu.SemaphoreType.DMA,
            pltpu.SemaphoreType.DMA((nd,)),
            pltpu.SemaphoreType.DMA((nd,)),
            pltpu.SemaphoreType.DMA((2,)),
            pltpu.SemaphoreType.DMA((2,)),
            pltpu.SemaphoreType.DMA((2,)),
        ],
        cost_estimate=cost(20 * total * model, 4 * total * model),
        compiler_params=pltpu.CompilerParams(vmem_limit_bytes=62 * MIB, collective_id=3, has_side_effects=True),
        name="gather_norm",
    )(x, small, pos, inverse, out_grad, live, w)


def gather_do_kernel(d_ref, act_ref, h_hbm, dup_hbm, o_a_ref, o_b_ref, wo_hbm, wd_hbm, do_ref, grad_ref, mlp_ref, top_ref, end_ref, up_ref,
                     all_s, wo_s, wd_s, dup_s, acc, act_s, h_s, stage, up_s, send, recv, local, act_sem, h_sem, out_sem, up_sem):
    near_x, near_y = neighbours()
    half = d_ref.shape[0] // 2
    model = d_ref.shape[1]
    part = o_a_ref.shape[1]
    tile = 512
    own = pltpu.make_async_copy(d_ref, all_s.at[pl.ds(0, 2 * half)], local.at[0])
    own.start()
    weights = pltpu.make_async_copy(wd_hbm, wd_s, local.at[1])
    weights.start()
    cotangent = pltpu.make_async_copy(dup_hbm, dup_s, local.at[2])
    cotangent.start()
    turned = pltpu.make_async_copy(wo_hbm.at[3], wo_s, local.at[3])
    turned.start()
    greet(near_x, near_y)
    own.wait()
    copies = square_copies(all_s, half, send, recv)
    for c in copies[:4]:
        c.start()
    acc[...] = jnp.zeros_like(acc)
    weights.wait()
    cotangent.wait()
    turned.wait()
    strip = model // 8

    def loads(i):
        at = pl.ds(pl.multiple_of(i * half, half), half)
        cols = pl.ds(pl.multiple_of(i * strip, strip), strip)
        return [
            pltpu.make_async_copy(act_ref.at[at], act_s.at[i % 2], act_sem.at[i % 2]),
            pltpu.make_async_copy(h_hbm.at[:, cols], h_s.at[i % 2], h_sem.at[i % 2]),
        ]

    def outs(i, target=top_ref):
        side = pl.ds(pl.multiple_of(i * strip, strip), strip)
        return [
            pltpu.make_async_copy(stage.at[i % 2], target, out_sem.at[i % 2]),
            pltpu.make_async_copy(up_s.at[i % 2], up_ref.at[side], up_sem.at[i % 2]),
        ]

    for c in loads(0):
        c.start()

    def beside(p):
        @pl.when(p < 7)
        def _():
            for c in loads(p + 1):
                c.start()

        for c in loads(p):
            c.wait()

        @pl.when(p >= 2)
        def _():
            for c in outs(p - 2):
                c.wait()

        stage[p % 2] = dot32(act_s[p % 2], wd_s[...]).astype(low_type)
        up_s[p % 2] = dot32(h_s[p % 2], dup_s[...], contract_first).astype(low_type)

        @pl.when(p < 6)
        def _():
            for c in outs(p, mlp_ref.at[pl.ds(pl.multiple_of(p * half, half), half)]):
                c.start()

        for n, ref in ((6, top_ref), (7, end_ref)):

            @pl.when(p == n)
            def _(ref=ref):
                for c in outs(p, ref):
                    c.start()

    def step(i, carry):
        @pl.when(i < 6)
        def _():
            beside(jnp.where(i == 5, 6, i))

        @pl.when((i == 4) | (i == 5))
        def _():
            beside(2 * i - 3)

        await_slot(i, copies)
        at = pl.ds(pl.multiple_of(arrival_slot(i) * half, half), half)
        dattn = all_s[at, :]
        do_ref[at, :] = dot32(dattn, wo_s[...]).astype(low_type)
        acc[:part, :] += dot32(o_a_ref[at, :], dattn, contract_first)
        acc[part:, :] += dot32(o_b_ref[at, :], dattn, contract_first)
        return carry

    lax.fori_loop(0, 8, step, 0)

    @pl.loop(0, model // tile)
    def _(n):
        cols = pl.ds(pl.multiple_of(n * tile, tile), tile)
        grad_ref[cols, :] = acc[:, cols].T.astype(low_type)

    for i in (6, 7):
        for c in outs(i):
            c.wait()
    for c in copies:
        c.wait_send()


def gather_do(dattn, act, h, dup, o_a, o_b, wo, wd):
    rows, model = dattn.shape
    total = 4 * rows
    depth = act.shape[1]
    width = wo.shape[2]
    vmem = pl.BlockSpec(memory_space=pltpu.VMEM)
    return pl.pallas_call(
        gather_do_kernel,
        in_specs=[ANY, ANY, ANY, ANY, vmem, vmem, ANY, ANY],
        out_specs=[vmem, vmem, ANY, ANY, ANY, ANY],
        out_shape=[
            jax.ShapeDtypeStruct((total, width), low_type),
            jax.ShapeDtypeStruct((model, width), low_type),
            jax.ShapeDtypeStruct((3 * rows, model), low_type),
            jax.ShapeDtypeStruct((rows // 2, model), low_type),
            jax.ShapeDtypeStruct((rows // 2, model), low_type),
            jax.ShapeDtypeStruct((model, depth), low_type),
        ],
        scratch_shapes=[
            pltpu.VMEM((total, model), low_type),
            pltpu.VMEM(wo.shape[1:], low_type),
            pltpu.VMEM(wd.shape, low_type),
            pltpu.VMEM(dup.shape, low_type),
            pltpu.VMEM((width, model), jnp.float32),
            pltpu.VMEM((2, rows // 2, depth), low_type),
            pltpu.VMEM((2, total, model // 8), low_type),
            pltpu.VMEM((2, rows // 2, model), low_type),
            pltpu.VMEM((2, model // 8, depth), low_type),
            pltpu.SemaphoreType.DMA((6,)),
            pltpu.SemaphoreType.DMA((6,)),
            pltpu.SemaphoreType.DMA((4,)),
            pltpu.SemaphoreType.DMA((2,)),
            pltpu.SemaphoreType.DMA((2,)),
            pltpu.SemaphoreType.DMA((2,)),
            pltpu.SemaphoreType.DMA((2,)),
        ],
        cost_estimate=cost(2 * total * model * (depth + 2 * width), 6 * total * model),
        compiler_params=pltpu.CompilerParams(vmem_limit_bytes=62 * MIB, collective_id=4, has_side_effects=True),
        name="gather_do",
    )(dattn, act, h, dup, o_a, o_b, wo, wd)


def exchange(rows, partial, bufs, send, recv, fill_one, fill_two):
    far_s, for_x, for_y, top_s, end_s, from_x, from_y = bufs
    near_x, near_y = neighbours()
    half = rows // 2
    t, e = pl.ds(0, half), pl.ds(half, half)
    copies = [
        remote(0, far_s.at[t], top_s, near_x, send, recv),
        remote(1, far_s.at[e], end_s, near_y, send, recv),
        remote(2, for_x.at[t], from_x.at[t], near_x, send, recv),
        remote(3, for_y.at[e], from_y.at[e], near_y, send, recv),
    ]
    quarter = half // 2
    for n in range(2):
        at = pl.ds(half + n * quarter, quarter)
        copies.append(remote(4 + n, for_x.at[at], from_x.at[at], near_x, send, recv))
    for n in range(2):
        at = pl.ds(n * quarter, quarter)
        copies.append(remote(6 + n, for_y.at[at], from_y.at[at], near_y, send, recv))

    def into(ref, which):
        def store(cols, value):
            ref[pl.ds(which * half, half), cols] = value.astype(low_type)

        return store

    def added(ref, which, other):
        def store(cols, value):
            ref[pl.ds(which * half, half), cols] = (value + other[:, cols].astype(jnp.float32)).astype(low_type)

        return store

    partial(3, 0, into(far_s, 0))
    copies[0].start()
    partial(3, 1, into(far_s, 1))
    copies[1].start()
    partial(1, 0, into(for_x, 0))
    copies[2].start()
    partial(2, 1, into(for_y, 1))
    copies[3].start()
    fill_one()
    copies[0].wait_recv()
    partial(2, 0, added(for_y, 0, top_s))
    copies[6].start()
    copies[7].start()
    copies[1].wait_recv()
    partial(1, 1, added(for_x, 1, end_s))
    copies[4].start()
    copies[5].start()
    fill_two()
    return copies


def finish_quarters(copies, finish, sent=0):
    copies[2].wait_recv()
    copies[6].wait_recv()
    finish(0)
    copies[3].wait_recv()
    copies[4].wait_recv()
    finish(2)
    copies[7].wait_recv()
    finish(1)
    copies[5].wait_recv()
    finish(3)
    for c in copies[sent:]:
        c.wait_send()


def finish_back(copies, rows, gain_row, v_ref, base_ref, own_ref, live_ref, norm_ref, from_x, from_y, dx_ref, low_ref, gain_ref, shift_ref, gain_s, shift_s, sent=0):
    quarter = rows // 4
    step = 16
    gain_s[...] = jnp.zeros_like(gain_s)
    shift_s[...] = jnp.zeros_like(shift_s)

    def finish(which):
        @pl.loop(0, quarter // step)
        def _(r):
            at = pl.ds(pl.multiple_of(which * quarter + r * step, step), step)
            e = own_ref[at, :].astype(jnp.float32) + from_x[at, :].astype(jnp.float32) + from_y[at, :].astype(jnp.float32)
            v = v_ref[at, :].astype(jnp.float32)
            c = v - jnp.mean(v, axis=-1, keepdims=True)
            s = lax.rsqrt(jnp.mean(c * c, axis=-1, keepdims=True) + norm_eps)
            xh = c * s
            w = e * norm_ref[gain_row : gain_row + 1, :]
            back = s * (w - jnp.mean(w, axis=-1, keepdims=True) - xh * jnp.mean(w * xh, axis=-1, keepdims=True))
            dx = base_ref[at, :].astype(jnp.float32) + back
            dx_ref[at, :] = dx.astype(dx_ref.dtype)
            if low_ref is not None:
                low_ref[at, :] = (dx * live_ref[at, :]).astype(low_type)
            ex = e * xh
            gain_s[...] += ex[:8] + ex[8:]
            shift_s[...] += e[:8] + e[8:]

    finish_quarters(copies, finish, sent)
    gain_ref[...] = jnp.sum(gain_s[...], axis=0, keepdims=True)
    shift_ref[...] = jnp.sum(shift_s[...], axis=0, keepdims=True)


def exchange_scratch(rows, model):
    big = pltpu.VMEM((rows, model), low_type)
    small = pltpu.VMEM((rows // 2, model), low_type)
    line = pltpu.VMEM((8, model), jnp.float32)
    sems = pltpu.SemaphoreType.DMA((8,))
    return [big, big, big, small, small, big, big, line, line, sems, sems]


def out_scatter_kernel(a_ref, b_ref, w_hbm, x_ref, live_ref, norm_ref, x1_ref, h_ref, *scratch):
    bufs, (send, recv, w_s, local) = scratch[:7], scratch[9:]
    weights = pltpu.make_async_copy(w_hbm.at[3], w_s, local)
    weights.start()
    near_x, near_y = neighbours()
    rows, model = x_ref.shape
    half = rows // 2
    part = a_ref.shape[1]
    tile = 512
    greet(near_x, near_y)
    weights.wait()

    def partial(slot, which, store):
        at = pl.ds(slot * rows + which * half, half)

        @pl.loop(0, model // tile)
        def _(n):
            cols = pl.ds(pl.multiple_of(n * tile, tile), tile)
            value = dot32(a_ref[at, :], w_s[cols, :part], contract_last)
            store(cols, value + dot32(b_ref[at, :], w_s[cols, part:], contract_last))

    def own(which):
        def store(cols, value):
            x1_ref[pl.ds(which * half, half), cols] = value

        return store

    def fill_one():
        partial(0, 0, own(0))
        partial(0, 1, own(1))

    copies = exchange(rows, partial, bufs, send, recv, fill_one, lambda: None)
    from_x, from_y = bufs[5:]
    quarter = rows // 4
    step = 32

    def finish(which):
        @pl.loop(0, quarter // step)
        def _(r):
            at = pl.ds(pl.multiple_of(which * quarter + r * step, step), step)
            attn = x1_ref[at, :] + from_x[at, :].astype(jnp.float32) + from_y[at, :].astype(jnp.float32)
            x1 = x_ref[at, :].astype(jnp.float32) + live_ref[at, :] * attn
            x1_ref[at, :] = x1
            c = x1 - jnp.mean(x1, axis=-1, keepdims=True)
            s = lax.rsqrt(jnp.mean(c * c, axis=-1, keepdims=True) + norm_eps)
            h_ref[at, :] = (c * s * norm_ref[1:2, :] + norm_ref[3:4, :]).astype(low_type)

    finish_quarters(copies, finish)


def out_scatter(a, b, w, x, live, norm):
    rows, model = x.shape
    vmem = pl.BlockSpec(memory_space=pltpu.VMEM)
    total = a.shape[0]
    return pl.pallas_call(
        out_scatter_kernel,
        in_specs=[vmem, vmem, ANY, vmem, vmem, vmem],
        out_specs=[vmem] * 2,
        out_shape=[jax.ShapeDtypeStruct((rows, model), jnp.float32), jax.ShapeDtypeStruct((rows, model), low_type)],
        scratch_shapes=exchange_scratch(rows, model) + [pltpu.VMEM(w.shape[1:], low_type), pltpu.SemaphoreType.DMA],
        cost_estimate=cost(2 * total * model * w.shape[2], 20 * rows * model),
        compiler_params=pltpu.CompilerParams(vmem_limit_bytes=62 * MIB, collective_id=0, has_side_effects=True),
        name="out_scatter",
    )(a, b, w, x, live, norm)


sending = (6, 7, 2, 5, 0, 1, 4, 3)


def sending_slot(j):
    slot = jnp.int32(sending[-1])
    for n in range(7):
        slot = jnp.where(j == n, sending[n], slot)
    return slot


def hidden_scatter_kernel(count, *refs):
    dm_refs, refs = refs[:count], refs[count:]
    one_hbm, two_hbm, wd_hbm, w_hbm, h_hbm, x1_hbm, og_hbm, live_ref, norm_ref = refs[:9]
    grad_ref, dup_ref, dx_ref, low_ref, gain_ref, shift_ref = refs[9:15]
    scratch = refs[15:]
    bufs, (gain_s, shift_s, send, recv) = scratch[:7], scratch[7:11]
    g_s, w_s, wd_s, dm_s, slope_s, h_s, stage, local, dm_sem, slope_sem, h_sem, out_sem = scratch[11:]
    rows, model = dx_ref.shape
    half = rows // 2
    near_x, near_y = neighbours()
    down_load = pltpu.make_async_copy(wd_hbm, wd_s, local.at[0])
    weight_load = pltpu.make_async_copy(w_hbm, w_s, local.at[1])
    x1_load = pltpu.make_async_copy(x1_hbm, dx_ref, local.at[2])
    og_load = pltpu.make_async_copy(og_hbm, bufs[0], local.at[3])
    dup_store = pltpu.make_async_copy(g_s.at[1], dup_ref, local.at[4])

    def slope_loads(j):
        at = pl.ds(pl.multiple_of(sending_slot(j) * half, half), half)
        return [
            pltpu.make_async_copy(ref.at[at], slope_s.at[j % 2, n], slope_sem.at[j % 2, n])
            for n, ref in enumerate((one_hbm, two_hbm))
        ]

    def dm_load(n):
        return pltpu.make_async_copy(dm_refs[sending[n]], dm_s.at[n % 2], dm_sem.at[n % 2])

    down_load.start()
    dm_load(0).start()
    for c in slope_loads(0):
        c.start()
    weight_load.start()
    x1_load.start()
    greet(near_x, near_y)
    down_load.wait()

    def back_step(j, carry):
        @pl.when(j < 7)
        def _():
            for c in slope_loads(j + 1):
                c.start()

        for n in range(1, 8):

            @pl.when(j == n - 1)
            def _(n=n):
                dm_load(n).start()

        b = j % 2
        pltpu.make_async_copy(dm_refs[0], dm_s.at[b], dm_sem.at[b]).wait()
        for c in slope_loads(j):
            c.wait()
        at = pl.ds(pl.multiple_of(sending_slot(j) * half, half), half)
        da = dot32(dm_s[b], wd_s[...], contract_last)
        g_s[0, at, :] = (da * slope_s[b, 0].astype(jnp.float32)).astype(low_type)
        g_s[1, at, :] = (da * slope_s[b, 1].astype(jnp.float32)).astype(low_type)
        return carry

    def back(first, last):
        lax.fori_loop(first, last, back_step, 0)

    tile = 512

    def partial(slot, which, store):
        if slot == 3:
            back(which, which + 1)
        if slot == 3 and which == 0:
            weight_load.wait()
        if slot == 1 and which == 0:
            back(2, 4)
        at = pl.ds(slot * rows + which * half, half)

        @pl.loop(0, model // tile)
        def _(n):
            cols = pl.ds(pl.multiple_of(n * tile, tile), tile)
            value = dot32(g_s[0, at, :], w_s[0, cols, :], contract_last)
            store(cols, value + dot32(g_s[1, at, :], w_s[1, cols, :], contract_last))

    def own(which):
        def store(cols, value):
            low_ref[pl.ds(which * half, half), cols] = value.astype(low_type)

        return store

    strip = 256

    def load(i):
        return pltpu.make_async_copy(h_hbm.at[:, pl.ds(pl.multiple_of(i * strip, strip), strip)], h_s.at[i % 2], h_sem.at[i % 2])

    def out(i):
        at = pl.ds(pl.multiple_of(i * strip, strip), strip)
        return pltpu.make_async_copy(stage.at[i % 2], grad_ref.at[at], out_sem.at[i % 2])

    strips = model // strip

    def strip_step(i, carry):
        @pl.when(i < strips - 1)
        def _():
            load(i + 1).start()

        load(i).wait()

        @pl.when(i >= 2)
        def _():
            out(i - 2).wait()

        stage[i % 2] = dot32(h_s[i % 2], g_s[0], contract_first).astype(low_type)
        out(i).start()
        return carry

    def fill_one():
        back(4, 8)
        dup_store.start()
        load(0).start()
        partial(0, 0, own(0))

    def fill_two():
        partial(0, 1, own(1))
        lax.fori_loop(0, strips, strip_step, 0)

    copies = exchange(rows, partial, bufs, send, recv, fill_one, fill_two)
    copies[0].wait_send()
    copies[1].wait_send()
    og_load.start()
    x1_load.wait()
    og_load.wait()
    finish_back(copies, rows, 1, dx_ref, bufs[0], low_ref, live_ref, norm_ref, bufs[5], bufs[6], dx_ref, low_ref, gain_ref, shift_ref, gain_s, shift_s, 2)
    out(strips - 2).wait()
    out(strips - 1).wait()
    dup_store.wait()


def hidden_scatter(dm_blocks, one, two, wd, w, h, x1, out_grad, live, norm):
    rows, model = x1.shape
    total, depth = one.shape
    half = rows // 2
    vmem = pl.BlockSpec(memory_space=pltpu.VMEM)
    line = jax.ShapeDtypeStruct((1, model), jnp.float32)
    return pl.pallas_call(
        functools.partial(hidden_scatter_kernel, len(dm_blocks)),
        in_specs=[ANY] * (len(dm_blocks) + 7) + [vmem, vmem],
        out_specs=[ANY, ANY, vmem, vmem, vmem, vmem],
        out_shape=[
            jax.ShapeDtypeStruct((model, depth), low_type),
            jax.ShapeDtypeStruct((total, depth), low_type),
            jax.ShapeDtypeStruct((rows, model), jnp.float32),
            jax.ShapeDtypeStruct((rows, model), low_type),
            line,
            line,
        ],
        scratch_shapes=exchange_scratch(rows, model)
        + [
            pltpu.VMEM((2, total, depth), low_type),
            pltpu.VMEM(w.shape, low_type),
            pltpu.VMEM(wd.shape, low_type),
            pltpu.VMEM((2, half, model), low_type),
            pltpu.VMEM((2, 2, half, depth), low_type),
            pltpu.VMEM((2, total, 256), low_type),
            pltpu.VMEM((2, 256, depth), low_type),
            pltpu.SemaphoreType.DMA((5,)),
            pltpu.SemaphoreType.DMA((2,)),
            pltpu.SemaphoreType.DMA((2, 2)),
            pltpu.SemaphoreType.DMA((2,)),
            pltpu.SemaphoreType.DMA((2,)),
        ],
        cost_estimate=cost(8 * total * model * depth, 16 * total * model),
        compiler_params=pltpu.CompilerParams(vmem_limit_bytes=62 * MIB, collective_id=5, has_side_effects=True),
        name="hidden_scatter",
    )(*dm_blocks, one, two, wd, w, h, x1, out_grad, live, norm)


def first_scatter_kernel(count, *refs):
    lefts_hbm = refs[:count]
    w_hbm, x_ref, base_ref, norm_ref, live_ref, small_ref = refs[count : count + 6]
    refs = refs[count + 6 :]
    x1_hbm, mlp_hbm = refs[0], refs[1:4]
    dx_ref, total_ref, layer_hbm = refs[4:7]
    scratch = refs[7:]
    bufs, (gain_s, shift_s, send, recv, own_s, left_s, w_s) = scratch[:7], scratch[7:14]
    x1_s, mlp_s, layer_s, left_sem, in_sem, layer_sem, gain_ref, shift_ref, small_s = scratch[14:23]
    nd, nt = lax.axis_size("dp"), lax.axis_size("tensor")
    rows, model = x_ref.shape
    half = rows // 2
    tile = 512
    far = pl.ds(3 * rows, rows)
    rest = pl.ds(0, 3 * rows)
    early = [pltpu.make_async_copy(left.at[far], left_s.at[n, far], left_sem.at[n]) for n, left in enumerate(lefts_hbm)]
    early.append(pltpu.make_async_copy(w_hbm.at[pl.ds(0, 3)], w_s, left_sem.at[2 * count]))
    late = [
        pltpu.make_async_copy(left.at[rest], left_s.at[n, rest], left_sem.at[count + n]) for n, left in enumerate(lefts_hbm)
    ]
    for c in early + late:
        c.start()
    greet_all(nd, nt)
    for c in early:
        c.wait()

    def partial(slot, which, store):
        if slot == 1 and which == 0:
            for c in late:
                c.wait()
        at = pl.ds(slot * rows + which * half, half)

        @pl.loop(0, model // tile)
        def _(n):
            cols = pl.ds(pl.multiple_of(n * tile, tile), tile)
            value = None
            for m in range(count):
                depth = left_s.shape[2]
                per = w_s.shape[2] // depth
                side = slice((m % per) * depth, (m % per + 1) * depth)
                term = dot32(left_s[m, at, :], w_s[m // per, cols, side], contract_last)
                value = term if value is None else value + term
            store(cols, value)

    def own(which):
        def store(cols, value):
            own_s[pl.ds(which * half, half), cols] = value

        return store

    def layer_moves():
        deep = x1_s.shape[1]
        at = lambda i: pl.ds(pl.multiple_of(i * deep, deep), deep)

        def loads(i):
            return [pltpu.make_async_copy(x1_hbm.at[at(i)], x1_s.at[i % 2], in_sem.at[i % 2, 0])] + [
                pltpu.make_async_copy(ref.at[at(i)], mlp_s.at[i % 2, n], in_sem.at[i % 2, 1 + n])
                for n, ref in enumerate(mlp_hbm)
            ]

        def stores(i):
            return [pltpu.make_async_copy(layer_s.at[i % 2], layer_hbm.at[at(i)], layer_sem.at[i % 2])]

        def work(i):
            b = i % 2
            total = mlp_s[b, 0].astype(jnp.float32) + mlp_s[b, 1].astype(jnp.float32) + mlp_s[b, 2].astype(jnp.float32)
            layer_s[b] = (x1_s[b] + live_ref[at(i), :] * total).astype(low_type)

        flow(0, rows // deep, loads, work, stores)

    def fill_one():
        partial(0, 0, own(0))
        partial(0, 1, own(1))

    def fill_two():
        layer_moves()

    copies = exchange(rows, partial, bufs, send, recv, fill_one, fill_two)
    finish_back(copies, rows, 0, x_ref, base_ref, own_s, None, norm_ref, bufs[5], bufs[6], dx_ref, None, gain_ref, shift_ref, gain_s, shift_s)
    small_s[...] = small_ref[...]
    small_s[0:1, :] = gain_ref[...]
    small_s[2:3, :] = shift_ref[...]
    share(nd, nt, small_s, total_ref, *scratch[23:])


def first_scatter(lefts, w, x, base, norm, live, small, x1, mlp_parts):
    rows, model = x.shape
    count = len(lefts)
    total, part = lefts[0].shape
    vmem = pl.BlockSpec(memory_space=pltpu.VMEM)
    nd, nt = lax.axis_size("dp"), lax.axis_size("tensor")
    deep = 64
    both = lambda block, n, t: pltpu.VMEM((2,) + ((n,) if n else ()) + block, t)
    return pl.pallas_call(
        functools.partial(first_scatter_kernel, count),
        in_specs=[ANY] * (count + 1) + [vmem] * 5 + [ANY] * 4,
        out_specs=[vmem, vmem, ANY],
        out_shape=[
            jax.ShapeDtypeStruct((rows, model), low_type),
            jax.ShapeDtypeStruct((small.shape[0], model // nd), jnp.float32),
            jax.ShapeDtypeStruct((rows, model), low_type),
        ],
        scratch_shapes=exchange_scratch(rows, model)
        + [
            pltpu.VMEM((rows, model), jnp.float32),
            pltpu.VMEM((count, total, part), low_type),
            pltpu.VMEM((3,) + w.shape[1:], low_type),
            both((deep, model), 0, jnp.float32),
            both((deep, model), 3, low_type),
            both((deep, model), 0, low_type),
            pltpu.SemaphoreType.DMA((2 * count + 1,)),
            pltpu.SemaphoreType.DMA((2, 4)),
            pltpu.SemaphoreType.DMA((2,)),
            pltpu.VMEM((1, model), jnp.float32),
            pltpu.VMEM((1, model), jnp.float32),
            pltpu.VMEM(small.shape, jnp.float32),
        ]
        + share_scratch(nd, nt, small.shape[0], model // nd),
        cost_estimate=cost(10**13, 30 * rows * model),
        compiler_params=pltpu.CompilerParams(vmem_limit_bytes=62 * MIB, collective_id=6, has_side_effects=True),
        name="first_scatter",
    )(*lefts, w, x, base, norm, live, small, x1, *mlp_parts)


def adam_rest_kernel(low_ref, turned_ref, *refs):
    qkv_in, out_in, qkv_out, out_out = refs[:3], refs[3:6], refs[6:10], refs[10:]
    step = pl.program_id(0)
    last = pl.num_programs(0) - 2

    @pl.when(step < last)
    def _():
        adam_blocks(low_ref, qkv_in, qkv_out)

    @pl.when(step >= last)
    def _():
        gradient = turned_ref[0].astype(jnp.float32).T
        out_out[0][...] = gradient
        results = adamw_update(out_in[0][...], gradient, out_in[1][...], out_in[2][...], weight_decay)
        for ref, value in zip(out_out[1:], results):
            ref[...] = value


def adam_rest(low, qkv, out):
    count, depth, width = low.shape
    half = depth // 2
    last = 2 * count - 2
    stack = lambda k: (jnp.minimum(k, last - 1) // 2, jnp.minimum(k, last - 1) % 2, 0)
    late = lambda k: jnp.maximum(k, last) - last
    three = pl.BlockSpec((1, half, width), stack)
    flat = pl.BlockSpec((width, half), lambda k: (0, late(k)))
    like = lambda value: jax.ShapeDtypeStruct(value.shape, jnp.float32)
    return pl.pallas_call(
        adam_rest_kernel,
        grid=(last + 2,),
        in_specs=[three, pl.BlockSpec((1, half, width), lambda k: (count - 1, late(k), 0))] + [three] * 3 + [flat] * 3,
        out_specs=[three] * 4 + [flat] * 4,
        out_shape=[like(qkv[0])] * 4 + [like(out[0])] * 4,
        cost_estimate=cost(30 * count * depth * width, 30 * count * depth * width),
        compiler_params=params(60),
        name="adam_rest",
    )(low, low, *qkv, *out)


def gather_gate_up_kernel(count, h_ref, w_hbm, *rest):
    blocks, (all_ref, act_ref, one_ref, two_ref, grad_ref) = rest[:count], rest[count : count + 5]
    w_s, all_s, stage, acc, turned, dm_s, send, recv, local, h_sem, out_sem, dm_sem = rest[count + 5 :]
    near_x, near_y = neighbours()
    half = h_ref.shape[0] // 2
    own = pltpu.make_async_copy(h_ref, all_s.at[pl.ds(0, 2 * half)], local.at[0])
    own.start()
    weights = pltpu.make_async_copy(w_hbm, w_s, local.at[1])
    weights.start()
    greet(near_x, near_y)
    own.wait()
    copies = square_copies(all_s, half, send, recv)
    for c in copies[:4]:
        c.start()
    acc[...] = jnp.zeros_like(acc)
    weights.wait()
    in_order = [blocks[n] for n in arrival]
    tile = 512

    def outs(buf, row):
        return [
            pltpu.make_async_copy(stage.at[buf, n], ref.at[pl.ds(row, half)], out_sem.at[buf, n])
            for n, ref in enumerate((act_ref, one_ref, two_ref))
        ]

    def keep(i, row):
        return pltpu.make_async_copy(all_s.at[pl.ds(row, half)], all_ref.at[pl.ds(row, half)], h_sem.at[i])

    def step(i, carry):
        await_slot(i, copies)
        row = pl.multiple_of(arrival_slot(i) * half, half)
        buf = i % 2
        keep(i, row).start()

        @pl.when(i >= 2)
        def _():
            for c in outs(buf, row):
                c.wait()

        h = all_s[pl.ds(row, half), :]
        gate = dot32(h, w_s[0])
        up = dot32(h, w_s[1])
        sig = 1.0 / (1.0 + jnp.exp(-gate))
        silu = gate * sig
        act = (silu * up).astype(low_type)
        stage[buf, 0] = act
        stage[buf, 1] = (up * sig * (1.0 + gate * (1.0 - sig))).astype(low_type)
        stage[buf, 2] = silu.astype(low_type)
        for c in outs(buf, row):
            c.start()
        turned[...] = act.T
        fetch_next(i, in_order, dm_s, dm_sem)

        @pl.loop(0, acc.shape[1] // tile)
        def _(n):
            cols = pl.ds(pl.multiple_of(n * tile, tile), tile)
            acc[:, cols] += dot32(turned[...], dm_s[buf, :, cols])

        return carry

    lax.fori_loop(0, 8, step, 0)
    for buf in (0, 1):
        for c in outs(buf, 0):
            c.wait()
    for i in range(8):
        keep(i, 0).wait()
    for c in copies:
        c.wait_send()
    depth = acc.shape[0]
    strip = depth // 8

    @pl.loop(0, 8)
    def _(n):
        at = pl.ds(pl.multiple_of(n * strip, strip), strip)
        all_s[at, :] = acc[at, :].astype(low_type)

    last = pltpu.make_async_copy(all_s.at[pl.ds(0, depth)], grad_ref, local.at[0])
    last.start()
    last.wait()


def gather_gate_up(h, w, dm_blocks):
    rows, model = h.shape
    depth = w.shape[2]
    total = 4 * rows
    half = rows // 2
    deep = jax.ShapeDtypeStruct((total, depth), low_type)
    return pl.pallas_call(
        functools.partial(gather_gate_up_kernel, len(dm_blocks)),
        in_specs=[ANY] * (2 + len(dm_blocks)),
        out_specs=[ANY] * 5,
        out_shape=[
            jax.ShapeDtypeStruct((total, model), low_type),
            deep,
            deep,
            deep,
            jax.ShapeDtypeStruct((depth, model), low_type),
        ],
        scratch_shapes=[
            pltpu.VMEM(w.shape, low_type),
            pltpu.VMEM((total, model), low_type),
            pltpu.VMEM((2, 3, half, depth), low_type),
            pltpu.VMEM((depth, model), jnp.float32),
            pltpu.VMEM((depth, half), low_type),
            pltpu.VMEM((2, half, model), low_type),
            pltpu.SemaphoreType.DMA((6,)),
            pltpu.SemaphoreType.DMA((6,)),
            pltpu.SemaphoreType.DMA((2,)),
            pltpu.SemaphoreType.DMA((8,)),
            pltpu.SemaphoreType.DMA((2, 3)),
            pltpu.SemaphoreType.DMA((2,)),
        ],
        cost_estimate=cost(6 * total * model * depth, 4 * model * depth + 4 * total * model + 6 * total * depth),
        compiler_params=pltpu.CompilerParams(vmem_limit_bytes=62 * MIB, collective_id=1, has_side_effects=True),
        name="gather_gate_up",
    )(h, w, *dm_blocks)


def greet_all(nd, nt):
    d, t = lax.axis_index("dp"), lax.axis_index("tensor")
    barrier = pltpu.get_barrier_semaphore()
    for k in range(1, nd):
        pl.semaphore_signal(barrier, inc=1, device_id={"dp": lax.rem(d + k, nd)}, device_id_type=MESH)
    for k in range(1, nt):
        pl.semaphore_signal(barrier, inc=1, device_id={"tensor": lax.rem(t + k, nt)}, device_id_type=MESH)
    pl.semaphore_wait(barrier, nd + nt - 2)


def share(nd, nt, x_ref, o_ref, groups, partial, shares, send, recv, send_t, recv_t):
    d, t = lax.axis_index("dp"), lax.axis_index("tensor")
    width = o_ref.shape[1]
    copies = []
    for k in range(1, nd):
        peer = lax.rem(d + k, nd)
        c = pltpu.make_async_remote_copy(
            src_ref=x_ref.at[:, pl.ds(pl.multiple_of(peer * width, width), width)],
            dst_ref=groups.at[k],
            send_sem=send.at[k],
            recv_sem=recv.at[k],
            device_id={"dp": peer},
            device_id_type=MESH,
        )
        c.start()
        copies.append(c)
    total = x_ref[:, pl.ds(pl.multiple_of(d * width, width), width)]
    for k in range(1, nd):
        copies[k - 1].wait_recv()
        total += groups[k]
    partial[...] = total
    shares[t] = total
    for k in range(1, nt):
        c = pltpu.make_async_remote_copy(
            src_ref=partial,
            dst_ref=shares.at[t],
            send_sem=send_t.at[k],
            recv_sem=recv_t.at[k],
            device_id={"tensor": lax.rem(t + k, nt)},
            device_id_type=MESH,
        )
        c.start()
        copies.append(c)
    for k in range(1, nt):
        copies[nd - 2 + k].wait_recv()
    total = shares[0]
    for k in range(1, nt):
        total += shares[k]
    o_ref[...] = total
    for c in copies:
        c.wait_send()


def share_scratch(nd, nt, rows, width):
    return [
        pltpu.VMEM((nd, rows, width), jnp.float32),
        pltpu.VMEM((rows, width), jnp.float32),
        pltpu.VMEM((nt, rows, width), jnp.float32),
        pltpu.SemaphoreType.DMA((nd,)),
        pltpu.SemaphoreType.DMA((nd,)),
        pltpu.SemaphoreType.DMA((nt,)),
        pltpu.SemaphoreType.DMA((nt,)),
    ]


def body(
    tokens,
    out_grad,
    lengths,
    norm_gain,
    norm_bias,
    qkv_weight,
    qkv_bias,
    out_weight,
    gate_up_weight,
    down_weight,
    first_norm_gain,
    first_norm_bias,
    first_qkv_weight,
    first_qkv_bias,
    first_out_weight,
    first_gate_up_weight,
    first_down_weight,
    second_norm_gain,
    second_norm_bias,
    second_qkv_weight,
    second_qkv_bias,
    second_out_weight,
    second_gate_up_weight,
    second_down_weight,
):
    slots = lax.axis_size("tensor")
    rank = lax.axis_index("tensor")
    own_rows = tokens.shape[0]
    group_rows = own_rows * slots
    width = out_weight.shape[0]
    order = rank if square(slots) else jnp.zeros_like(rank)

    chunk = jnp.bitwise_xor(jnp.arange(slots, dtype=jnp.int32), order)
    row_index = (chunk[:, None] * own_rows + jnp.arange(own_rows, dtype=jnp.int32)[None, :]).reshape(-1)
    seq_start, _ = layout(lengths[0], row_index)
    position = row_index - seq_start
    own_index = rank * own_rows + jnp.arange(own_rows, dtype=jnp.int32)
    live = layout(lengths[0], own_index)[1][:, None]
    block_start, _ = layout(lengths[0], jnp.arange(group_rows // BLOCK, dtype=jnp.int32) * BLOCK)
    table = jnp.concatenate([order.reshape(1).astype(jnp.int32), block_start // BLOCK])
    starts = seq_start[None, :]
    small_low = jnp.concatenate([norm_gain, norm_bias, qkv_bias, qkv_bias[:1]], axis=0).astype(low_type)
    own_bias = lambda full: lax.dynamic_slice_in_dim(full[4:7], rank * width, width, 1)[:, None, :]

    if square(slots):
        attn_low = jnp.concatenate([qkv_weight, out_weight.T[None]], axis=0).astype(low_type)
        attn_full = lax.all_gather(attn_low, "dp", axis=1, tiled=True)
        lane = jnp.arange(PAIR, dtype=jnp.int32) % (ROT // 2)
        inverse = jnp.power(rope_base, -lane.astype(jnp.float32) * (2.0 / ROT))[None, :]
        position = position.astype(jnp.float32).reshape(-1, 256)
        h1, small_full, *tables, dm_top, dm_end, gate_up_low = gather_norm(
            tokens, small_low.astype(jnp.float32), position, inverse, out_grad, live, gate_up_weight
        )
        norm = small_full[:4]
        gate_up_full = lax.all_gather(after(gate_up_low, attn_full), "dp", axis=1, tiled=True)
        dm_first, dm_rest = gather_rows(dm_top, dm_end)
        q, k, v, kt, vt = qkv_all(h1, attn_full, own_bias(small_full), tables)

        o_a, lse_a = attn_fwd(0, slots, table, q, k, vt, starts)
        dm_far = dm_rest(o_a)
        o_b, lse_b = attn_fwd(1, slots, table, after(q, o_a, *dm_first), k, vt, starts)
        o_b = after(o_b, *dm_far)
        dm_blocks = dm_first + dm_far

        x1, h2_own = out_scatter(o_a, o_b, attn_full, tokens, live, norm)
        down_low = after(down_weight.astype(low_type), gate_up_full, h2_own)
        down_full = lax.all_gather(down_low, "dp", axis=1, tiled=True)
        h2, act, slope_gate, slope_up, grad_down = gather_gate_up(h2_own, gate_up_full, dm_blocks)
        grad_down_own = lax.psum_scatter(after(grad_down, down_full), "dp", scatter_dimension=1, tiled=True)

        grad_gate, dup, dx1, dattn_own, gain_two, shift_two = hidden_scatter(
            dm_blocks, slope_gate, slope_up, down_full, gate_up_full, h2, x1, out_grad, live, norm
        )
        grad_gate = after(grad_gate, grad_down_own)
        grad_gate_own = lax.psum_scatter(grad_gate, "dp", scatter_dimension=0, tiled=True)

        do, grad_out, mlp, far_top, far_end, grad_up = gather_do(dattn_own, act, h2, dup, o_a, o_b, attn_full, down_full)
        grad_up = after(grad_up, grad_gate_own)
        grad_up_own = lax.psum_scatter(grad_up, "dp", scatter_dimension=0, tiled=True)
        mlp_first = [lax.ppermute(far_top, "tensor", swap_x), lax.ppermute(far_end, "tensor", swap_y)]
        *back_a, grad_down_full, down_one, down_two, down_three = attn_bwd(
            0, slots, table, q, do, o_a, k, v, kt, starts, lse_a, tables,
            grad_down_own, (down_weight, first_down_weight, second_down_weight),
        )
        down_step = (grad_down_full, down_one, down_two, down_three)
        hidden = (gate_up_weight, first_gate_up_weight, second_gate_up_weight)
        for_x, for_y = pass_on(mlp, *[after(part, back_a[0]) for part in mlp_first])
        mlp_parts = [mlp, lax.ppermute(for_x, "tensor", swap_x), lax.ppermute(for_y, "tensor", swap_y)]
        results = attn_bwd(
            1, slots, table, q, after(do, back_a[0], for_x), o_b, k, v, kt, starts, lse_b, tables, grad_gate_own, hidden
        )
        back_b, begun = results[:3], results[3:]
        dlin = [side for pair in zip(back_a, back_b) for side in pair]
        grad_rest, bias_local, *hidden_step = qkv_grad(h1, dlin, grad_out, grad_up_own, hidden, begun)
        late = [after(dlin[0], grad_rest, *mlp_parts[1:])] + dlin[1:]
        spread = lambda part: lax.dynamic_update_slice(
            jnp.zeros((3, small_full.shape[1]), jnp.float32), part, (jnp.int32(0), rank * width)
        )
        biases = spread(bias_local)
        small = jnp.concatenate([gain_two, gain_two, shift_two, shift_two, biases, biases[:1]], axis=0)
        input_grad, small_own, layer_out = first_scatter(
            late, attn_full, tokens, dx1, norm, live, small, x1, mlp_parts
        )
        grad_rest = after(grad_rest, grad_up_own)
        grad_rest_own = lax.psum_scatter(grad_rest, "dp", scatter_dimension=1, tiled=True)
        rest_step = adam_rest(
            grad_rest_own,
            (qkv_weight, first_qkv_weight, second_qkv_weight),
            (out_weight, first_out_weight, second_out_weight),
        )
        qkv_step, out_step = rest_step[:4], rest_step[4:]
    else:
        everyone = lambda value: lax.all_gather(value, "tensor", axis=0, tiled=True)
        scatter = lambda value, axis, at: lax.psum_scatter(value.astype(low_type), axis, scatter_dimension=at, tiled=True)
        small_full = lax.all_gather(small_low, "dp", axis=1, tiled=True).astype(jnp.float32)
        qkv_full, out_full, gate_up_full, down_full = (
            lax.all_gather(w.astype(low_type), "dp", axis=1, tiled=True)
            for w in (qkv_weight, out_weight, gate_up_weight, down_weight)
        )
        gain_rows, shift_rows = small_full[0:2], small_full[2:4]
        rows_in, cotangent = tokens.astype(jnp.float32), out_grad.astype(jnp.float32)
        tables = rotary_tables(position)
        h1 = everyone(layer_norm(rows_in, gain_rows[0], shift_rows[0]).astype(low_type))
        q, k, v, kt, vt = qkv_all(h1, qkv_full, own_bias(small_full), tables)
        o_a, lse_a = attn_fwd(0, slots, table, q, k, vt, starts)
        o_b, lse_b = attn_fwd(1, slots, table, q, k, vt, starts)
        o = jnp.concatenate([o_a, o_b], axis=1)
        x1 = rows_in + live * scatter(dot32(o, out_full), "tensor", 0).astype(jnp.float32)
        h2 = everyone(layer_norm(x1, gain_rows[1], shift_rows[1]).astype(low_type))
        gate, up = dot32(h2, gate_up_full[0]), dot32(h2, gate_up_full[1])
        sig = 1.0 / (1.0 + jnp.exp(-gate))
        act = (gate * sig * up).astype(low_type)
        mlp_rows = scatter(dot32(act, down_full), "tensor", 0).astype(jnp.float32)
        layer_out = (x1 + live * mlp_rows).astype(low_type)
        dm = everyone((cotangent * live).astype(low_type))
        da = dot32(dm, down_full, contract_last)
        dgate = (da * up * sig * (1.0 + gate * (1.0 - sig))).astype(low_type)
        dup = (da * gate * sig).astype(low_type)
        grad_down_own = scatter(dot32(act, dm, contract_first), "dp", 1)
        grad_gate_up = jnp.stack([dot32(h2, dgate, contract_first), dot32(h2, dup, contract_first)])
        grad_gate_up_own = scatter(grad_gate_up, "dp", 1)
        dh2 = dot32(dgate, gate_up_full[0], contract_last) + dot32(dup, gate_up_full[1], contract_last)
        dh2 = scatter(dh2, "tensor", 0).astype(jnp.float32)
        back, gain_two, shift_two = jax.vjp(layer_norm, x1, gain_rows[1], shift_rows[1])[1](dh2)
        dx1 = cotangent + back
        dattn = everyone((dx1 * live).astype(low_type))
        do = dot32(dattn, out_full, contract_last).astype(low_type)
        grad_out = dot32(dattn, o, contract_first).astype(low_type)
        back_a = attn_bwd(0, slots, table, q, do, o_a, k, v, kt, starts, lse_a, tables)
        back_b = attn_bwd(1, slots, table, q, do, o_b, k, v, kt, starts, lse_b, tables)
        dlin = [side for pair in zip(back_a, back_b) for side in pair]
        grad_rest, bias_local = qkv_grad(h1, dlin, grad_out)
        grad_rest_own = scatter(grad_rest, "dp", 1)
        grad_qkv_own, grad_out_own = grad_rest_own[:3], grad_rest_own[3].T
        dh1 = sum(
            dot32(jnp.concatenate(dlin[2 * n : 2 * n + 2], axis=1), qkv_full[n], contract_last) for n in range(3)
        )
        dh1 = scatter(dh1, "tensor", 0).astype(jnp.float32)
        back, gain_one, shift_one = jax.vjp(layer_norm, rows_in, gain_rows[0], shift_rows[0])[1](dh1)
        input_grad = (dx1 + back).astype(low_type)
        gain_one, gain_two, shift_one, shift_two = (
            value[None, :] for value in (gain_one, gain_two, shift_one, shift_two)
        )

        bias_placed = lax.dynamic_update_slice(
            jnp.zeros((3, small_full.shape[1]), jnp.float32), bias_local, (jnp.int32(0), rank * width)
        )
        small_local = jnp.concatenate([gain_one, gain_two, shift_one, shift_two, bias_placed], axis=0)
        small_own = lax.psum(lax.psum_scatter(small_local, "dp", scatter_dimension=1, tiled=True), "tensor")

        def whole_step(gradient, *held):
            gradient = gradient.astype(jnp.float32)
            return (gradient,) + adamw_update(held[0], gradient, held[1], held[2], weight_decay)

        qkv_step = whole_step(grad_qkv_own, qkv_weight, first_qkv_weight, second_qkv_weight)
        out_step = whole_step(grad_out_own, out_weight, first_out_weight, second_out_weight)
        hidden_step = whole_step(grad_gate_up_own, gate_up_weight, first_gate_up_weight, second_gate_up_weight)
        down_step = whole_step(grad_down_own, down_weight, first_down_weight, second_down_weight)

    def small_step(gradient, *held):
        return (gradient,) + adamw_update(held[0], gradient, held[1], held[2], 0.0)

    gain_step = small_step(small_own[0:2], norm_gain, first_norm_gain, second_norm_gain)
    shift_step = small_step(small_own[2:4], norm_bias, first_norm_bias, second_norm_bias)
    bias_step = small_step(small_own[4:7], qkv_bias, first_qkv_bias, second_qkv_bias)
    steps = (gain_step, shift_step, qkv_step, bias_step, out_step, hidden_step, down_step)
    return (layer_out, input_grad) + tuple(step[n] for n in range(4) for step in steps)


def solution(mesh):
    return jax.shard_map(
        body,
        mesh=mesh,
        in_specs=(
            P(("dp", "tensor"), None),
            P(("dp", "tensor"), None),
            P("dp", None),
            P(None, "dp"),
            P(None, "dp"),
            P(None, "dp", "tensor"),
            P(None, "dp"),
            P("tensor", "dp"),
            P(None, "dp", "tensor"),
            P("tensor", "dp"),
            P(None, "dp"),
            P(None, "dp"),
            P(None, "dp", "tensor"),
            P(None, "dp"),
            P("tensor", "dp"),
            P(None, "dp", "tensor"),
            P("tensor", "dp"),
            P(None, "dp"),
            P(None, "dp"),
            P(None, "dp", "tensor"),
            P(None, "dp"),
            P("tensor", "dp"),
            P(None, "dp", "tensor"),
            P("tensor", "dp"),
        ),
        out_specs=(
            P(("dp", "tensor"), None),
            P(("dp", "tensor"), None),
            P(None, "dp"),
            P(None, "dp"),
            P(None, "dp", "tensor"),
            P(None, "dp"),
            P("tensor", "dp"),
            P(None, "dp", "tensor"),
            P("tensor", "dp"),
            P(None, "dp"),
            P(None, "dp"),
            P(None, "dp", "tensor"),
            P(None, "dp"),
            P("tensor", "dp"),
            P(None, "dp", "tensor"),
            P("tensor", "dp"),
            P(None, "dp"),
            P(None, "dp"),
            P(None, "dp", "tensor"),
            P(None, "dp"),
            P("tensor", "dp"),
            P(None, "dp", "tensor"),
            P("tensor", "dp"),
            P(None, "dp"),
            P(None, "dp"),
            P(None, "dp", "tensor"),
            P(None, "dp"),
            P("tensor", "dp"),
            P(None, "dp", "tensor"),
            P("tensor", "dp"),
        ),
        check_vma=False,
    )
```

```python
import functools

import jax
import jax.numpy as jnp
from jax import lax
from jax.experimental import pallas as pl
from jax.experimental.pallas import tpu as pltpu
from jax.sharding import PartitionSpec as P

HEAD_DIM = 64
ROT = 16
PAIR = 2 * HEAD_DIM
BLOCK = 256

norm_eps = 1e-05
rope_base = 10000.0
beta_one = 0.9
beta_two = 0.95
adam_eps = 1e-08
learn_rate = 0.01
weight_decay = 0.1
step_count = 10.0
masked_score = -1e30
contract_last = (((1,), (1,)), ((), ()))
contract_first = (((0,), (0,)), ((), ()))
low_type = jnp.bfloat16
MIB = 2**20


def layout(seq_lengths, row_index):
    slot = jnp.arange(seq_lengths.shape[0])
    seq_ends = jnp.sum(
        jnp.where(slot[:, None] <= slot[None, :], seq_lengths[:, None], 0), axis=0
    )
    passed = row_index[:, None] >= seq_ends[None, :]
    seq_start = jnp.sum(jnp.where(passed, seq_lengths[None, :], 0), axis=1)
    live_rows = (row_index < jnp.sum(seq_lengths)).astype(jnp.float32)
    return (seq_start, live_rows)


def rotary_tables(position):
    half_rot = ROT // 2
    lane = jnp.arange(PAIR, dtype=jnp.int32) % HEAD_DIM
    powers = (lane % half_rot).astype(jnp.float32) * (2.0 / ROT)
    inverse = jnp.power(rope_base, -powers)
    angles = position.astype(jnp.float32)[:, None] * inverse[None, :]
    cos_part, sine_part = jnp.cos(angles), jnp.sin(angles)
    lane = lane[None, :]
    keep = jnp.where(lane < ROT, cos_part, 1.0)
    above = jnp.where(lane < half_rot, -sine_part, 0.0)
    below = jnp.where((lane >= half_rot) & (lane < ROT), sine_part, 0.0)
    return (keep, above, below)


def dot32(a, b, dims=None):
    if dims is None:
        return jnp.dot(a, b, preferred_element_type=jnp.float32)
    return lax.dot_general(a, b, dims, preferred_element_type=jnp.float32)


def turn(values, keep, above, below):
    up = pltpu.roll(values, PAIR - ROT // 2, 1)
    down = pltpu.roll(values, ROT // 2, 1)
    return values * keep + up * above + down * below


def turn_back(values, keep, above, below):
    up = pltpu.roll(values, PAIR - ROT // 2, 1)
    down = pltpu.roll(values, ROT // 2, 1)
    return values * keep - up * above - down * below


def adamw_update(weight_now, gradient, moment_one, moment_two, decay_rate):
    moment_one = beta_one * moment_one + (1.0 - beta_one) * gradient
    moment_two = beta_two * moment_two + (1.0 - beta_two) * gradient * gradient
    scaled_one = moment_one * (1.0 / (1.0 - beta_one**step_count))
    scaled_two = moment_two * (1.0 / (1.0 - beta_two**step_count))
    change = scaled_one / (jnp.sqrt(scaled_two) + adam_eps) + decay_rate * weight_now
    return (-learn_rate * change, moment_one, moment_two)


def cost(flops, moved, exps=0):
    return pl.CostEstimate(flops=int(flops) // 16, bytes_accessed=int(moved) // 16, transcendentals=int(exps) // 16)


def params(limit):
    return pltpu.CompilerParams(vmem_limit_bytes=limit * MIB)


ANY = pl.BlockSpec(memory_space=pl.ANY)


def layer_norm(values, gain_row, shift_row):
    center = values - jnp.mean(values, axis=-1, keepdims=True)
    spread = jnp.mean(center * center, axis=-1, keepdims=True)
    return center * lax.rsqrt(spread + norm_eps) * gain_row + shift_row


def qkv_kernel(scale, h_ref, w_ref, bias_ref, keep_ref, above_ref, below_ref, q_ref, k_ref, v_ref, kt_ref, vt_ref):
    h = h_ref[...]
    keep, above, below = keep_ref[...], above_ref[...], below_ref[...]
    width = q_ref.shape[1]
    lin = dot32(h, w_ref[0]) + bias_ref[0]
    for c in range(0, width, PAIR):
        u = turn(lin[:, c : c + PAIR], keep, above, below)
        q_ref[:, c : c + PAIR] = (u.astype(low_type) * scale).astype(low_type)
    lin = dot32(h, w_ref[1]) + bias_ref[1]
    for c in range(0, width, PAIR):
        u = turn(lin[:, c : c + PAIR], keep, above, below)
        k_ref[:, c : c + PAIR] = u.astype(low_type)
        kt_ref[c : c + PAIR, :] = u.T.astype(low_type)
    lin = dot32(h, w_ref[2]) + bias_ref[2]
    v_ref[...] = lin.astype(low_type)
    vt_ref[...] = lin.T.astype(low_type)


def qkv_all(h, w, bias, tables):
    total, model = h.shape
    rows = 256
    width = w.shape[2]
    row = lambda n: pl.BlockSpec((rows, n), lambda i: (i, 0))
    col = pl.BlockSpec((width, rows), lambda i: (0, i))
    flat = jax.ShapeDtypeStruct((total, width), low_type)
    turned = jax.ShapeDtypeStruct((width, total), low_type)
    return pl.pallas_call(
        functools.partial(qkv_kernel, HEAD_DIM ** (-0.5)),
        grid=(total // rows,),
        in_specs=[
            row(model),
            pl.BlockSpec((3,) + w.shape[1:], lambda i: (0, 0, 0), pipeline_mode=pl.Buffered(1)),
            pl.BlockSpec(bias.shape, lambda i: (0, 0, 0)),
            row(PAIR),
            row(PAIR),
            row(PAIR),
        ],
        out_specs=[row(width), row(width), row(width), col, col],
        out_shape=[flat, flat, flat, turned, turned],
        cost_estimate=cost(6 * total * model * width, 6 * model * width + 10 * total * model),
        compiler_params=params(60),
        name="qkv",
    )(h, w, bias, *tables)


def place(block, rank, per):
    return jnp.bitwise_xor(block // per, rank) * per + block % per


def attn_fwd_kernel(per, table_ref, q_ref, k_ref, vt_ref, start_ref, o_ref, lse_ref, m_s, l_s, acc_s):
    i = pl.program_id(0)
    rank = table_ref[0]
    heads = q_ref.shape[1] // HEAD_DIM
    first = lax.broadcasted_iota(jnp.int32, (BLOCK, PAIR), 1) < HEAD_DIM
    queries = []
    for h in range(heads):
        pair = q_ref[:, (h // 2) * PAIR : (h // 2 + 1) * PAIR]
        keep = first if h % 2 == 0 else jnp.logical_not(first)
        queries.append(jnp.where(keep, pair, jnp.zeros_like(pair)))
    m_s[...] = jnp.full_like(m_s, -jnp.inf)
    l_s[...] = jnp.zeros_like(l_s)
    acc_s[...] = jnp.zeros_like(acc_s)
    start = start_ref[...]
    row = i * BLOCK + lax.broadcasted_iota(jnp.int32, (BLOCK, BLOCK), 1)

    def step(kb, carry):
        col = kb * BLOCK + lax.broadcasted_iota(jnp.int32, (BLOCK, BLOCK), 0)
        bias = jnp.where((col >= start) & (col <= row), 0.0, masked_score)
        at = pl.ds(pl.multiple_of(place(kb, rank, per) * BLOCK, BLOCK), BLOCK)
        scores = [
            dot32(k_ref[at, (h // 2) * PAIR : (h // 2 + 1) * PAIR], queries[h], contract_last) for h in range(heads)
        ]
        probs, alphas = [], []
        for h in range(heads):
            s = scores[h] + bias
            m_old = m_s[h : h + 1, :]
            m_new = jnp.maximum(m_old, jnp.max(s, axis=0, keepdims=True))
            alpha = jnp.exp(m_old - m_new)
            p = jnp.exp(s - m_new)
            l_s[h : h + 1, :] = l_s[h : h + 1, :] * alpha + jnp.sum(p, axis=0, keepdims=True)
            m_s[h : h + 1, :] = m_new
            probs.append(p.astype(low_type))
            alphas.append(alpha)
        for h in range(heads):
            own = slice(h * HEAD_DIM, (h + 1) * HEAD_DIM)
            acc_s[own, :] = acc_s[own, :] * alphas[h] + dot32(vt_ref[own, at], probs[h])
        return carry

    lax.fori_loop(table_ref[1 + i], i + 1, step, 0)
    for h in range(heads):
        own = slice(h * HEAD_DIM, (h + 1) * HEAD_DIM)
        acc_s[own, :] = acc_s[own, :] / l_s[h : h + 1, :]
    o_ref[...] = acc_s[...].T.astype(low_type)
    lse_ref[0] = m_s[...] + jnp.log(l_s[...])


def attn_fwd(half, slots, table, q, k, vt, start):
    rows, width = q.shape
    part = width // 2
    heads = part // HEAD_DIM
    count = rows // BLOCK
    per = rows // slots // BLOCK
    at = lambda i, t: place(i, t[0], per)
    return pl.pallas_call(
        functools.partial(attn_fwd_kernel, per),
        grid_spec=pltpu.PrefetchScalarGridSpec(
            num_scalar_prefetch=1,
            grid=(count,),
            in_specs=[
                pl.BlockSpec((BLOCK, part), lambda i, t: (at(i, t), half)),
                pl.BlockSpec((rows, part), lambda i, t: (0, half)),
                pl.BlockSpec((part, rows), lambda i, t: (half, 0)),
                pl.BlockSpec((1, BLOCK), lambda i, t: (0, at(i, t))),
            ],
            out_specs=[
                pl.BlockSpec((BLOCK, part), lambda i, t: (at(i, t), 0)),
                pl.BlockSpec((1, heads, BLOCK), lambda i, t: (at(i, t), 0, 0)),
            ],
            scratch_shapes=[
                pltpu.VMEM((heads, BLOCK), jnp.float32),
                pltpu.VMEM((heads, BLOCK), jnp.float32),
                pltpu.VMEM((part, BLOCK), jnp.float32),
            ],
        ),
        out_shape=[
            jax.ShapeDtypeStruct((rows, part), low_type),
            jax.ShapeDtypeStruct((count, heads, BLOCK), jnp.float32),
        ],
        cost_estimate=cost(rows * rows, rows * part),
        compiler_params=params(60),
        name="attn_fwd",
    )(table, q, k, vt, start)


def adam_blocks(low_ref, in_refs, out_refs):
    gradient = low_ref[...].astype(jnp.float32).reshape(out_refs[0].shape)
    results = adamw_update(in_refs[0][...], gradient, in_refs[1][...], in_refs[2][...], weight_decay)
    out_refs[0][...] = gradient
    for ref, value in zip(out_refs[1:], results):
        ref[...] = value


def attn_bwd_kernel(per, adam, table_ref, q_ref, do_ref, o_ref, k_ref, v_ref, kt_ref, start_ref, lse_ref,
                    keep_ref, above_ref, below_ref, *rest):
    (dq_ref, dk_ref, dv_ref), (dq_s, dk_s, dv_s) = rest[4 * adam : 4 * adam + 3], rest[-3:]
    if adam:
        adam_blocks(rest[0], rest[1:4], rest[7:11])
    i = pl.program_id(0)
    rank = table_ref[0]
    width = q_ref.shape[1]
    heads = width // HEAD_DIM
    first = lax.broadcasted_iota(jnp.int32, (BLOCK, PAIR), 1) < HEAD_DIM

    @pl.when(i == 0)
    def _():
        dk_s[...] = jnp.zeros_like(dk_s)
        dv_s[...] = jnp.zeros_like(dv_s)

    dq_s[...] = jnp.zeros_like(dq_s)
    queries, cotangents, inner = [], [], []
    product = (do_ref[...].astype(jnp.float32) * o_ref[...].astype(jnp.float32)).T
    for h in range(heads):
        cols = slice((h // 2) * PAIR, (h // 2 + 1) * PAIR)
        keep = first if h % 2 == 0 else jnp.logical_not(first)
        pair = q_ref[:, cols]
        queries.append(jnp.where(keep, pair, jnp.zeros_like(pair)))
        pair = do_ref[:, cols]
        cotangents.append(jnp.where(keep, pair, jnp.zeros_like(pair)))
        inner.append(jnp.sum(product[h * HEAD_DIM : (h + 1) * HEAD_DIM, :], axis=0, keepdims=True))
    start = start_ref[...]
    row = i * BLOCK + lax.broadcasted_iota(jnp.int32, (BLOCK, BLOCK), 1)

    def step(kb, carry):
        col = kb * BLOCK + lax.broadcasted_iota(jnp.int32, (BLOCK, BLOCK), 0)
        bias = jnp.where((col >= start) & (col <= row), 0.0, masked_score)
        at = pl.ds(pl.multiple_of(place(kb, rank, per) * BLOCK, BLOCK), BLOCK)
        raw, grads = [], []
        for h in range(heads):
            cols = slice((h // 2) * PAIR, (h // 2 + 1) * PAIR)
            raw.append(dot32(k_ref[at, cols], queries[h], contract_last))
            grads.append(dot32(v_ref[at, cols], cotangents[h], contract_last))
        probs, scores = [], []
        for h in range(heads):
            p = jnp.exp(raw[h] + bias - lse_ref[0, h : h + 1, :])
            scores.append((p * (grads[h] - inner[h])).astype(low_type))
            probs.append(p.astype(low_type))
        for h in range(heads):
            own = slice(h * HEAD_DIM, (h + 1) * HEAD_DIM)
            dq_s[own, :] += dot32(kt_ref[own, at], scores[h])
        for one in range(0, heads, 2):
            cols = slice(one * HEAD_DIM, one * HEAD_DIM + PAIR)
            dv_s[at, cols] += dot32(probs[one], cotangents[one]) + dot32(probs[one + 1], cotangents[one + 1])
            dk_s[at, cols] += dot32(scores[one], queries[one]) + dot32(scores[one + 1], queries[one + 1])
        return carry

    lax.fori_loop(table_ref[1 + i], i + 1, step, 0)
    dq = dq_s[...].T * (HEAD_DIM ** (-0.5))
    here = pl.ds(pl.multiple_of(place(i, rank, per) * BLOCK, BLOCK), BLOCK)
    for c in range(0, width, PAIR):
        dq_ref[:, c : c + PAIR] = turn_back(
            dq[:, c : c + PAIR], keep_ref[here, :], above_ref[here, :], below_ref[here, :]
        ).astype(low_type)

    @pl.when(i == pl.num_programs(0) - 1)
    def _():
        @pl.loop(0, dk_s.shape[0] // BLOCK)
        def _(b):
            at = pl.ds(pl.multiple_of(b * BLOCK, BLOCK), BLOCK)
            for c in range(0, width, PAIR):
                cols = slice(c, c + PAIR)
                dk_ref[at, cols] = turn_back(
                    dk_s[at, cols], keep_ref[at, :], above_ref[at, :], below_ref[at, :]
                ).astype(low_type)
                dv_ref[at, cols] = dv_s[at, cols].astype(low_type)


def attn_bwd(half, slots, table, q, do, o, k, v, kt, start, lse, tables, low=None, held=()):
    rows, width = q.shape
    part = width // 2
    heads = part // HEAD_DIM
    count = rows // BLOCK
    per = rows // slots // BLOCK
    at = lambda i, t: place(i, t[0], per)
    whole = pl.BlockSpec((rows, part), lambda i, t: (0, half))
    turns = pl.BlockSpec((rows, PAIR), lambda i, t: (0, 0))
    result = pl.BlockSpec((rows, part), lambda i, t: (0, 0))
    adam = low is not None
    adam_in, adam_out, adam_like = [], [], []
    if adam:
        strip, depth = low.shape[0] // count, low.shape[1]
        flat = pl.BlockSpec((strip, depth), lambda i, t: (i, 0))
        one = flat if held[0].ndim == 2 else pl.BlockSpec((1, strip, depth), lambda i, t: (0, i, 0))
        adam_in, adam_out = [flat, one, one, one], [one] * 4
        adam_like = [jax.ShapeDtypeStruct(held[0].shape, jnp.float32)] * 4
    return pl.pallas_call(
        functools.partial(attn_bwd_kernel, per, int(adam)),
        grid_spec=pltpu.PrefetchScalarGridSpec(
            num_scalar_prefetch=1,
            grid=(count,),
            in_specs=[
                pl.BlockSpec((BLOCK, part), lambda i, t: (at(i, t), half)),
                pl.BlockSpec((BLOCK, part), lambda i, t: (at(i, t), half)),
                pl.BlockSpec((BLOCK, part), lambda i, t: (at(i, t), 0)),
                whole,
                whole,
                pl.BlockSpec((part, rows), lambda i, t: (half, 0)),
                pl.BlockSpec((1, BLOCK), lambda i, t: (0, at(i, t))),
                pl.BlockSpec((1, heads, BLOCK), lambda i, t: (at(i, t), 0, 0)),
                turns,
                turns,
                turns,
            ]
            + adam_in,
            out_specs=[pl.BlockSpec((BLOCK, part), lambda i, t: (at(i, t), 0)), result, result] + adam_out,
            scratch_shapes=[
                pltpu.VMEM((part, BLOCK), jnp.float32),
                pltpu.VMEM((rows, part), jnp.float32),
                pltpu.VMEM((rows, part), jnp.float32),
            ],
        ),
        out_shape=[jax.ShapeDtypeStruct((rows, part), low_type)] * 3 + adam_like,
        cost_estimate=cost(25 * rows * rows * part // 2, 16 * rows * part, 8 * rows * rows // 4),
        compiler_params=params(60),
        name="attn_bwd",
    )(table, q, do, o, k, v, kt, start, lse, *tables, *((low,) + tuple(held) if adam else ()))


def qkv_grad_kernel(count, adam, *refs):
    left_ref, other_ref, rights = refs[0], refs[1], refs[2 : 2 + count]
    out_ref, sum_ref = refs[2 + count + 8 * adam : 4 + count + 8 * adam]
    if adam:
        adam_blocks(refs[2 + count], refs[3 + count : 6 + count], refs[-4:])
    part = rights[0].shape[1]

    @pl.when(pl.program_id(0) == 0)
    def _():
        for n, right in enumerate(rights):
            sum_ref[n // 2 : n // 2 + 1, (n % 2) * part : (n % 2 + 1) * part] = jnp.sum(
                right[...].astype(jnp.float32), axis=0, keepdims=True
            )

    left = left_ref[...]
    for n, right in enumerate(rights):
        out_ref[n // 2, :, (n % 2) * part : (n % 2 + 1) * part] = dot32(left, right[...], contract_first).astype(low_type)
    out_ref[len(rights) // 2] = other_ref[...]


def qkv_grad(left, rights, other, low=None, held=(), begun=()):
    rows, model = left.shape
    part = rights[0].shape[1]
    count = len(rights) // 2
    tile = 512
    adam = low is not None
    adam_in, adam_out, adam_like, extra = [], [], [], ()
    if adam:
        strip, depth = low.shape[0] // (model // tile), low.shape[1]
        one = pl.BlockSpec((1, strip, depth), lambda n: (1, n, 0))
        adam_in = [pl.BlockSpec((strip, depth), lambda n: (n, 0)), one, one, one] + [ANY] * 4
        adam_out = [one] * 4
        adam_like = [jax.ShapeDtypeStruct(held[0].shape, jnp.float32)] * 4
        extra = (low,) + tuple(held) + tuple(begun)
    first = 2 + len(rights) + 4
    return pl.pallas_call(
        functools.partial(qkv_grad_kernel, len(rights), int(adam)),
        grid=(model // tile,),
        in_specs=[pl.BlockSpec((rows, tile), lambda n: (0, n)), pl.BlockSpec((tile, 2 * part), lambda n: (n, 0))]
        + [pl.BlockSpec((rows, part), lambda n: (0, 0), pipeline_mode=pl.Buffered(1))] * len(rights)
        + adam_in,
        input_output_aliases={first + n: 2 + n for n in range(4)} if adam else {},
        out_specs=[
            pl.BlockSpec((count + 1, tile, 2 * part), lambda n: (0, n, 0)),
            pl.BlockSpec((count, 2 * part), lambda n: (0, 0)),
        ]
        + adam_out,
        out_shape=[
            jax.ShapeDtypeStruct((count + 1, model, 2 * part), low_type),
            jax.ShapeDtypeStruct((count, 2 * part), jnp.float32),
        ]
        + adam_like,
        cost_estimate=cost(4 * count * rows * model * part, 4 * rows * model),
        compiler_params=params(60),
        name="qkv_grad",
    )(left, other, *rights, *extra)


swap_x = [(0, 1), (1, 0), (2, 3), (3, 2)]
swap_y = [(0, 2), (2, 0), (1, 3), (3, 1)]


def square(count):
    return count == 4


def gather_rows(top, end):
    x_top = lax.ppermute(top, "tensor", swap_x)
    y_end = lax.ppermute(end, "tensor", swap_y)
    x_end = lax.ppermute(end, "tensor", swap_x)
    y_top = lax.ppermute(top, "tensor", swap_y)
    first = [top, end, x_top, x_end, y_top, y_end]

    def rest(*between):
        far_top = lax.ppermute(after(x_top, *between), "tensor", swap_y)
        far_end = lax.ppermute(after(y_end, *between), "tensor", swap_x)
        return [far_top, far_end]

    return first, rest


def after(value, *others):
    return lax.optimization_barrier((value,) + others)[0]


def pass_on_kernel(one_ref, two_ref, top_ref, end_ref, for_x_ref, for_y_ref):
    i, half = pl.program_id(0), pl.num_programs(0) // 2
    add = lambda a, b: (a[...].astype(jnp.float32) + b[...].astype(jnp.float32)).astype(low_type)

    @pl.when(i < half)
    def _():
        for_x_ref[...] = one_ref[...]
        for_y_ref[...] = add(two_ref, top_ref)

    @pl.when(i >= half)
    def _():
        for_x_ref[...] = add(one_ref, end_ref)
        for_y_ref[...] = two_ref[...]


def pass_on(rows_in, top, end):
    half, model = top.shape
    block = half // 2
    per = 2 * half // block
    spec = lambda index: pl.BlockSpec((block, model), lambda i: (index(i), 0))
    return pl.pallas_call(
        pass_on_kernel,
        grid=(per,),
        in_specs=[
            spec(lambda i: per + i),
            spec(lambda i: 2 * per + i),
            spec(lambda i: jnp.minimum(i, per // 2 - 1)),
            spec(lambda i: jnp.maximum(i, per // 2) - per // 2),
        ],
        out_specs=[spec(lambda i: i)] * 2,
        out_shape=[jax.ShapeDtypeStruct((2 * half, model), low_type)] * 2,
        cost_estimate=cost(4 * half * model, 20 * half * model),
        compiler_params=params(60),
        name="pass_on",
    )(rows_in, rows_in, top, end)


MESH = pl.DeviceIdType.MESH


def greet(near_x, near_y):
    barrier = pltpu.get_barrier_semaphore()
    for near in (near_x, near_y):
        pl.semaphore_signal(barrier, inc=1, device_id={"tensor": near}, device_id_type=MESH)
    pl.semaphore_wait(barrier, 2)


def neighbours():
    rank = lax.axis_index("tensor")
    return jnp.bitwise_xor(rank, 1), jnp.bitwise_xor(rank, 2)


def remote(index, source, target, near, send, recv):
    return pltpu.make_async_remote_copy(
        src_ref=source,
        dst_ref=target,
        send_sem=send.at[index],
        recv_sem=recv.at[index],
        device_id={"tensor": near},
        device_id_type=MESH,
    )


arrival = (0, 1, 2, 5, 3, 4, 6, 7)


def arrival_slot(i):
    return jnp.where(i == 3, 5, jnp.where(i == 4, 3, jnp.where(i == 5, 4, i)))


def square_copies(all_s, half, send, recv):
    near_x, near_y = neighbours()
    at = lambda n: all_s.at[pl.ds(n * half, half)]
    return (
        remote(0, at(0), at(2), near_x, send, recv),
        remote(1, at(1), at(5), near_y, send, recv),
        remote(2, at(1), at(3), near_x, send, recv),
        remote(3, at(0), at(4), near_y, send, recv),
        remote(4, at(2), at(6), near_y, send, recv),
        remote(5, at(5), at(7), near_x, send, recv),
    )


def await_slot(i, copies):
    x_top, y_end, x_end, y_top, far_top, far_end = copies

    @pl.when(i == 2)
    def _():
        x_top.wait_recv()
        far_top.start()
        y_end.wait_recv()
        far_end.start()

    for n, c in ((4, x_end), (5, y_top), (6, far_top), (7, far_end)):

        @pl.when(i == n)
        def _(c=c):
            c.wait_recv()


def fetch_next(i, refs, buf, sem):
    def fetch(j):
        pltpu.make_async_copy(refs[j], buf.at[j % 2], sem.at[j % 2]).start()

    for j in range(len(refs)):

        @pl.when(i == max(j - 1, 0) if j else i == 0)
        def _(j=j):
            fetch(j)

    pltpu.make_async_copy(refs[0], buf.at[i % 2], sem.at[i % 2]).wait()


def flow(first, last, loads, work, stores):
    def all_of(copies, act):
        for c in copies:
            act(c)

    all_of(loads(first), lambda c: c.start())

    def step(i, carry):
        @pl.when(i < last - 1)
        def _():
            all_of(loads(i + 1), lambda c: c.start())

        all_of(loads(i), lambda c: c.wait())

        @pl.when(i >= first + 2)
        def _():
            all_of(stores(i - 2), lambda c: c.wait())

        work(i)
        all_of(stores(i), lambda c: c.start())
        return carry

    lax.fori_loop(first, last, step, 0)
    for i in range(max(first, last - 2), last):
        all_of(stores(i), lambda c: c.wait())


def gather_norm_kernel(nd, x_ref, small_ref, pos_ref, inv_ref, og_ref, live_ref, w_hbm,
                       h_ref, full_ref, keep_ref, above_ref, below_ref, top_ref, end_ref, low_hbm,
                       all_s, full_s, stage, w_s, low_s, send, recv, local, small_send, small_recv, out_sem, w_sem, low_sem):
    d = lax.axis_index("dp")
    near_x, near_y = neighbours()
    half = x_ref.shape[0] // 2
    width = small_ref.shape[1]
    own = pltpu.make_async_copy(x_ref, all_s.at[pl.ds(0, 2 * half)], local)
    own.start()
    barrier = pltpu.get_barrier_semaphore()
    for near in (near_x, near_y):
        pl.semaphore_signal(barrier, inc=1, device_id={"tensor": near}, device_id_type=MESH)
    for k in range(1, nd):
        pl.semaphore_signal(barrier, inc=1, device_id={"dp": lax.rem(d + k, nd)}, device_id_type=MESH)
    pl.semaphore_wait(barrier, nd + 1)
    own.wait()
    copies = square_copies(all_s, half, send, recv)
    for c in copies[:4]:
        c.start()
    small = []
    for k in range(1, nd):
        c = pltpu.make_async_remote_copy(
            src_ref=small_ref,
            dst_ref=full_s.at[d],
            send_sem=small_send.at[k],
            recv_sem=small_recv.at[k],
            device_id={"dp": lax.rem(d + k, nd)},
            device_id_type=MESH,
        )
        c.start()
        small.append(c)
    full_s[d] = small_ref[...]
    for n, ref in enumerate((top_ref, end_ref)):

        @pl.loop(0, half // 32)
        def _(r, n=n, ref=ref):
            to = pl.ds(pl.multiple_of(r * 32, 32), 32)
            at = pl.ds(pl.multiple_of(n * half + r * 32, 32), 32)
            ref[to, :] = (og_ref[at, :].astype(jnp.float32) * live_ref[at, :]).astype(low_type)

    strip = w_s.shape[1]
    per = w_hbm.shape[1] // strip

    def side(i):
        return i // per, pl.ds(pl.multiple_of((i % per) * strip, strip), strip)

    def cast(i):
        low_s[i % 2] = w_s[i % 2].astype(low_type)

    for c in small:
        c.wait_recv()
    for n in range(nd):
        full_ref[:, n * width : (n + 1) * width] = full_s[n]
    step = 32
    lane = lax.broadcasted_iota(jnp.int32, (256, PAIR), 1) % HEAD_DIM

    def turns(n):
        at = pl.ds(pl.multiple_of(n * 256, 256), 256)
        angles = jnp.broadcast_to(pos_ref[pl.ds(n, 1), :], (PAIR, 256)).T * inv_ref[...]
        cos_part, sine_part = jnp.cos(angles), jnp.sin(angles)
        keep_ref[at, :] = jnp.where(lane < ROT, cos_part, 1.0)
        above_ref[at, :] = jnp.where(lane < ROT // 2, -sine_part, 0.0)
        below_ref[at, :] = jnp.where((lane >= ROT // 2) & (lane < ROT), sine_part, 0.0)

    def out(buf, row):
        return pltpu.make_async_copy(stage.at[buf], h_ref.at[pl.ds(row, half)], out_sem.at[buf])

    def body_step(i, carry):
        await_slot(i, copies)
        row = pl.multiple_of(arrival_slot(i) * half, half)
        buf = i % 2

        @pl.when(i >= 2)
        def _():
            out(buf, row).wait()

        @pl.loop(0, half // step)
        def _(r):
            at = pl.ds(pl.multiple_of(r * step, step), step)
            x = all_s[pl.ds(pl.multiple_of(row + r * step, step), step), :].astype(jnp.float32)
            c = x - jnp.mean(x, axis=-1, keepdims=True)
            s = lax.rsqrt(jnp.mean(c * c, axis=-1, keepdims=True) + norm_eps)
            stage[buf, at, :] = (c * s * full_ref[0:1, :] + full_ref[2:3, :]).astype(low_type)

        out(buf, row).start()

        @pl.when((i >= 2) & (i < 6))
        def _():
            turns(2 * i - 4)
            turns(2 * i - 3)

        return carry

    lax.fori_loop(0, 3, body_step, 0)
    flow(
        0,
        w_hbm.shape[0] * per,
        lambda i: [pltpu.make_async_copy(w_hbm.at[side(i)], w_s.at[i % 2], w_sem.at[i % 2])],
        cast,
        lambda i: [pltpu.make_async_copy(low_s.at[i % 2], low_hbm.at[side(i)], low_sem.at[i % 2])],
    )
    lax.fori_loop(3, 8, body_step, 0)
    for buf in (0, 1):
        out(buf, 0).wait()
    for c in copies:
        c.wait_send()
    for c in small:
        c.wait_send()


def gather_norm(x, small, pos, inverse, out_grad, live, w):
    nd = lax.axis_size("dp")
    rows, model = x.shape
    total = 4 * rows
    count, width = small.shape
    vmem = pl.BlockSpec(memory_space=pltpu.VMEM)
    table = jax.ShapeDtypeStruct((total, PAIR), jnp.float32)
    return pl.pallas_call(
        functools.partial(gather_norm_kernel, nd),
        in_specs=[ANY, vmem, vmem, vmem, vmem, vmem, ANY],
        out_specs=[ANY, vmem, vmem, vmem, vmem, vmem, vmem, ANY],
        out_shape=[
            jax.ShapeDtypeStruct((total, model), low_type),
            jax.ShapeDtypeStruct((count, width * nd), jnp.float32),
            table,
            table,
            table,
            jax.ShapeDtypeStruct((rows // 2, model), low_type),
            jax.ShapeDtypeStruct((rows // 2, model), low_type),
            jax.ShapeDtypeStruct(w.shape, low_type),
        ],
        scratch_shapes=[
            pltpu.VMEM((total, model), low_type),
            pltpu.VMEM((nd, count, width), jnp.float32),
            pltpu.VMEM((2, rows // 2, model), low_type),
            pltpu.VMEM((2, 64, w.shape[2]), jnp.float32),
            pltpu.VMEM((2, 64, w.shape[2]), low_type),
            pltpu.SemaphoreType.DMA((6,)),
            pltpu.SemaphoreType.DMA((6,)),
            pltpu.SemaphoreType.DMA,
            pltpu.SemaphoreType.DMA((nd,)),
            pltpu.SemaphoreType.DMA((nd,)),
            pltpu.SemaphoreType.DMA((2,)),
            pltpu.SemaphoreType.DMA((2,)),
            pltpu.SemaphoreType.DMA((2,)),
        ],
        cost_estimate=cost(20 * total * model, 4 * total * model),
        compiler_params=pltpu.CompilerParams(vmem_limit_bytes=62 * MIB, collective_id=3, has_side_effects=True),
        name="gather_norm",
    )(x, small, pos, inverse, out_grad, live, w)


def gather_do_kernel(d_ref, act_ref, h_hbm, dup_hbm, o_a_ref, o_b_ref, wo_hbm, wd_hbm, do_ref, grad_ref, mlp_ref, top_ref, end_ref, up_ref,
                     all_s, wo_s, wd_s, dup_s, acc, act_s, h_s, stage, up_s, send, recv, local, act_sem, h_sem, out_sem, up_sem):
    near_x, near_y = neighbours()
    half = d_ref.shape[0] // 2
    model = d_ref.shape[1]
    part = o_a_ref.shape[1]
    tile = 512
    own = pltpu.make_async_copy(d_ref, all_s.at[pl.ds(0, 2 * half)], local.at[0])
    own.start()
    weights = pltpu.make_async_copy(wd_hbm, wd_s, local.at[1])
    weights.start()
    cotangent = pltpu.make_async_copy(dup_hbm, dup_s, local.at[2])
    cotangent.start()
    turned = pltpu.make_async_copy(wo_hbm.at[3], wo_s, local.at[3])
    turned.start()
    greet(near_x, near_y)
    own.wait()
    copies = square_copies(all_s, half, send, recv)
    for c in copies[:4]:
        c.start()
    acc[...] = jnp.zeros_like(acc)
    weights.wait()
    cotangent.wait()
    turned.wait()
    strip = model // 8

    def loads(i):
        at = pl.ds(pl.multiple_of(i * half, half), half)
        cols = pl.ds(pl.multiple_of(i * strip, strip), strip)
        return [
            pltpu.make_async_copy(act_ref.at[at], act_s.at[i % 2], act_sem.at[i % 2]),
            pltpu.make_async_copy(h_hbm.at[:, cols], h_s.at[i % 2], h_sem.at[i % 2]),
        ]

    def outs(i, target=top_ref):
        side = pl.ds(pl.multiple_of(i * strip, strip), strip)
        return [
            pltpu.make_async_copy(stage.at[i % 2], target, out_sem.at[i % 2]),
            pltpu.make_async_copy(up_s.at[i % 2], up_ref.at[side], up_sem.at[i % 2]),
        ]

    for c in loads(0):
        c.start()

    def beside(p):
        @pl.when(p < 7)
        def _():
            for c in loads(p + 1):
                c.start()

        for c in loads(p):
            c.wait()

        @pl.when(p >= 2)
        def _():
            for c in outs(p - 2):
                c.wait()

        stage[p % 2] = dot32(act_s[p % 2], wd_s[...]).astype(low_type)
        up_s[p % 2] = dot32(h_s[p % 2], dup_s[...], contract_first).astype(low_type)

        @pl.when(p < 6)
        def _():
            for c in outs(p, mlp_ref.at[pl.ds(pl.multiple_of(p * half, half), half)]):
                c.start()

        for n, ref in ((6, top_ref), (7, end_ref)):

            @pl.when(p == n)
            def _(ref=ref):
                for c in outs(p, ref):
                    c.start()

    def step(i, carry):
        @pl.when(i < 6)
        def _():
            beside(jnp.where(i == 5, 6, i))

        @pl.when((i == 4) | (i == 5))
        def _():
            beside(2 * i - 3)

        await_slot(i, copies)
        at = pl.ds(pl.multiple_of(arrival_slot(i) * half, half), half)
        dattn = all_s[at, :]
        do_ref[at, :] = dot32(dattn, wo_s[...]).astype(low_type)
        acc[:part, :] += dot32(o_a_ref[at, :], dattn, contract_first)
        acc[part:, :] += dot32(o_b_ref[at, :], dattn, contract_first)
        return carry

    lax.fori_loop(0, 8, step, 0)

    @pl.loop(0, model // tile)
    def _(n):
        cols = pl.ds(pl.multiple_of(n * tile, tile), tile)
        grad_ref[cols, :] = acc[:, cols].T.astype(low_type)

    for i in (6, 7):
        for c in outs(i):
            c.wait()
    for c in copies:
        c.wait_send()


def gather_do(dattn, act, h, dup, o_a, o_b, wo, wd):
    rows, model = dattn.shape
    total = 4 * rows
    depth = act.shape[1]
    width = wo.shape[2]
    vmem = pl.BlockSpec(memory_space=pltpu.VMEM)
    return pl.pallas_call(
        gather_do_kernel,
        in_specs=[ANY, ANY, ANY, ANY, vmem, vmem, ANY, ANY],
        out_specs=[vmem, vmem, ANY, ANY, ANY, ANY],
        out_shape=[
            jax.ShapeDtypeStruct((total, width), low_type),
            jax.ShapeDtypeStruct((model, width), low_type),
            jax.ShapeDtypeStruct((3 * rows, model), low_type),
            jax.ShapeDtypeStruct((rows // 2, model), low_type),
            jax.ShapeDtypeStruct((rows // 2, model), low_type),
            jax.ShapeDtypeStruct((model, depth), low_type),
        ],
        scratch_shapes=[
            pltpu.VMEM((total, model), low_type),
            pltpu.VMEM(wo.shape[1:], low_type),
            pltpu.VMEM(wd.shape, low_type),
            pltpu.VMEM(dup.shape, low_type),
            pltpu.VMEM((width, model), jnp.float32),
            pltpu.VMEM((2, rows // 2, depth), low_type),
            pltpu.VMEM((2, total, model // 8), low_type),
            pltpu.VMEM((2, rows // 2, model), low_type),
            pltpu.VMEM((2, model // 8, depth), low_type),
            pltpu.SemaphoreType.DMA((6,)),
            pltpu.SemaphoreType.DMA((6,)),
            pltpu.SemaphoreType.DMA((4,)),
            pltpu.SemaphoreType.DMA((2,)),
            pltpu.SemaphoreType.DMA((2,)),
            pltpu.SemaphoreType.DMA((2,)),
            pltpu.SemaphoreType.DMA((2,)),
        ],
        cost_estimate=cost(2 * total * model * (depth + 2 * width), 6 * total * model),
        compiler_params=pltpu.CompilerParams(vmem_limit_bytes=62 * MIB, collective_id=4, has_side_effects=True),
        name="gather_do",
    )(dattn, act, h, dup, o_a, o_b, wo, wd)


def exchange(rows, partial, bufs, send, recv, fill_one, fill_two):
    far_s, for_x, for_y, top_s, end_s, from_x, from_y = bufs
    near_x, near_y = neighbours()
    half = rows // 2
    t, e = pl.ds(0, half), pl.ds(half, half)
    copies = [
        remote(0, far_s.at[t], top_s, near_x, send, recv),
        remote(1, far_s.at[e], end_s, near_y, send, recv),
        remote(2, for_x.at[t], from_x.at[t], near_x, send, recv),
        remote(3, for_y.at[e], from_y.at[e], near_y, send, recv),
    ]
    quarter = half // 2
    for n in range(2):
        at = pl.ds(half + n * quarter, quarter)
        copies.append(remote(4 + n, for_x.at[at], from_x.at[at], near_x, send, recv))
    for n in range(2):
        at = pl.ds(n * quarter, quarter)
        copies.append(remote(6 + n, for_y.at[at], from_y.at[at], near_y, send, recv))

    def into(ref, which):
        def store(cols, value):
            ref[pl.ds(which * half, half), cols] = value.astype(low_type)

        return store

    def added(ref, which, other):
        def store(cols, value):
            ref[pl.ds(which * half, half), cols] = (value + other[:, cols].astype(jnp.float32)).astype(low_type)

        return store

    partial(3, 0, into(far_s, 0))
    copies[0].start()
    partial(3, 1, into(far_s, 1))
    copies[1].start()
    partial(1, 0, into(for_x, 0))
    copies[2].start()
    partial(2, 1, into(for_y, 1))
    copies[3].start()
    fill_one()
    copies[0].wait_recv()
    partial(2, 0, added(for_y, 0, top_s))
    copies[6].start()
    copies[7].start()
    copies[1].wait_recv()
    partial(1, 1, added(for_x, 1, end_s))
    copies[4].start()
    copies[5].start()
    fill_two()
    return copies


def finish_quarters(copies, finish, sent=0):
    copies[2].wait_recv()
    copies[6].wait_recv()
    finish(0)
    copies[3].wait_recv()
    copies[4].wait_recv()
    finish(2)
    copies[7].wait_recv()
    finish(1)
    copies[5].wait_recv()
    finish(3)
    for c in copies[sent:]:
        c.wait_send()


def finish_back(copies, rows, gain_row, v_ref, base_ref, own_ref, live_ref, norm_ref, from_x, from_y, dx_ref, low_ref, gain_ref, shift_ref, gain_s, shift_s, sent=0):
    quarter = rows // 4
    step = 16
    gain_s[...] = jnp.zeros_like(gain_s)
    shift_s[...] = jnp.zeros_like(shift_s)

    def finish(which):
        @pl.loop(0, quarter // step)
        def _(r):
            at = pl.ds(pl.multiple_of(which * quarter + r * step, step), step)
            e = own_ref[at, :].astype(jnp.float32) + from_x[at, :].astype(jnp.float32) + from_y[at, :].astype(jnp.float32)
            v = v_ref[at, :].astype(jnp.float32)
            c = v - jnp.mean(v, axis=-1, keepdims=True)
            s = lax.rsqrt(jnp.mean(c * c, axis=-1, keepdims=True) + norm_eps)
            xh = c * s
            w = e * norm_ref[gain_row : gain_row + 1, :]
            back = s * (w - jnp.mean(w, axis=-1, keepdims=True) - xh * jnp.mean(w * xh, axis=-1, keepdims=True))
            dx = base_ref[at, :].astype(jnp.float32) + back
            dx_ref[at, :] = dx.astype(dx_ref.dtype)
            if low_ref is not None:
                low_ref[at, :] = (dx * live_ref[at, :]).astype(low_type)
            ex = e * xh
            gain_s[...] += ex[:8] + ex[8:]
            shift_s[...] += e[:8] + e[8:]

    finish_quarters(copies, finish, sent)
    gain_ref[...] = jnp.sum(gain_s[...], axis=0, keepdims=True)
    shift_ref[...] = jnp.sum(shift_s[...], axis=0, keepdims=True)


def exchange_scratch(rows, model):
    big = pltpu.VMEM((rows, model), low_type)
    small = pltpu.VMEM((rows // 2, model), low_type)
    line = pltpu.VMEM((8, model), jnp.float32)
    sems = pltpu.SemaphoreType.DMA((8,))
    return [big, big, big, small, small, big, big, line, line, sems, sems]


def out_scatter_kernel(a_ref, b_ref, w_hbm, x_ref, live_ref, norm_ref, x1_ref, h_ref, *scratch):
    bufs, (send, recv, w_s, local) = scratch[:7], scratch[9:]
    weights = pltpu.make_async_copy(w_hbm.at[3], w_s, local)
    weights.start()
    near_x, near_y = neighbours()
    rows, model = x_ref.shape
    half = rows // 2
    part = a_ref.shape[1]
    tile = 512
    greet(near_x, near_y)
    weights.wait()

    def partial(slot, which, store):
        at = pl.ds(slot * rows + which * half, half)

        @pl.loop(0, model // tile)
        def _(n):
            cols = pl.ds(pl.multiple_of(n * tile, tile), tile)
            value = dot32(a_ref[at, :], w_s[cols, :part], contract_last)
            store(cols, value + dot32(b_ref[at, :], w_s[cols, part:], contract_last))

    def own(which):
        def store(cols, value):
            x1_ref[pl.ds(which * half, half), cols] = value

        return store

    def fill_one():
        partial(0, 0, own(0))
        partial(0, 1, own(1))

    copies = exchange(rows, partial, bufs, send, recv, fill_one, lambda: None)
    from_x, from_y = bufs[5:]
    quarter = rows // 4
    step = 32

    def finish(which):
        @pl.loop(0, quarter // step)
        def _(r):
            at = pl.ds(pl.multiple_of(which * quarter + r * step, step), step)
            attn = x1_ref[at, :] + from_x[at, :].astype(jnp.float32) + from_y[at, :].astype(jnp.float32)
            x1 = x_ref[at, :].astype(jnp.float32) + live_ref[at, :] * attn
            x1_ref[at, :] = x1
            c = x1 - jnp.mean(x1, axis=-1, keepdims=True)
            s = lax.rsqrt(jnp.mean(c * c, axis=-1, keepdims=True) + norm_eps)
            h_ref[at, :] = (c * s * norm_ref[1:2, :] + norm_ref[3:4, :]).astype(low_type)

    finish_quarters(copies, finish)


def out_scatter(a, b, w, x, live, norm):
    rows, model = x.shape
    vmem = pl.BlockSpec(memory_space=pltpu.VMEM)
    total = a.shape[0]
    return pl.pallas_call(
        out_scatter_kernel,
        in_specs=[vmem, vmem, ANY, vmem, vmem, vmem],
        out_specs=[vmem] * 2,
        out_shape=[jax.ShapeDtypeStruct((rows, model), jnp.float32), jax.ShapeDtypeStruct((rows, model), low_type)],
        scratch_shapes=exchange_scratch(rows, model) + [pltpu.VMEM(w.shape[1:], low_type), pltpu.SemaphoreType.DMA],
        cost_estimate=cost(2 * total * model * w.shape[2], 20 * rows * model),
        compiler_params=pltpu.CompilerParams(vmem_limit_bytes=62 * MIB, collective_id=0, has_side_effects=True),
        name="out_scatter",
    )(a, b, w, x, live, norm)


sending = (6, 7, 2, 5, 0, 1, 4, 3)


def sending_slot(j):
    slot = jnp.int32(sending[-1])
    for n in range(7):
        slot = jnp.where(j == n, sending[n], slot)
    return slot


def hidden_scatter_kernel(count, *refs):
    dm_refs, refs = refs[:count], refs[count:]
    one_hbm, two_hbm, wd_hbm, w_hbm, h_hbm, x1_hbm, og_hbm, live_ref, norm_ref = refs[:9]
    grad_ref, dup_ref, dx_ref, low_ref, gain_ref, shift_ref = refs[9:15]
    scratch = refs[15:]
    bufs, (gain_s, shift_s, send, recv) = scratch[:7], scratch[7:11]
    g_s, w_s, wd_s, dm_s, slope_s, h_s, stage, local, dm_sem, slope_sem, h_sem, out_sem = scratch[11:]
    rows, model = dx_ref.shape
    half = rows // 2
    near_x, near_y = neighbours()
    down_load = pltpu.make_async_copy(wd_hbm, wd_s, local.at[0])
    weight_load = pltpu.make_async_copy(w_hbm, w_s, local.at[1])
    x1_load = pltpu.make_async_copy(x1_hbm, dx_ref, local.at[2])
    og_load = pltpu.make_async_copy(og_hbm, bufs[0], local.at[3])
    dup_store = pltpu.make_async_copy(g_s.at[1], dup_ref, local.at[4])

    def slope_loads(j):
        at = pl.ds(pl.multiple_of(sending_slot(j) * half, half), half)
        return [
            pltpu.make_async_copy(ref.at[at], slope_s.at[j % 2, n], slope_sem.at[j % 2, n])
            for n, ref in enumerate((one_hbm, two_hbm))
        ]

    def dm_load(n):
        return pltpu.make_async_copy(dm_refs[sending[n]], dm_s.at[n % 2], dm_sem.at[n % 2])

    down_load.start()
    dm_load(0).start()
    for c in slope_loads(0):
        c.start()
    weight_load.start()
    x1_load.start()
    greet(near_x, near_y)
    down_load.wait()

    def back_step(j, carry):
        @pl.when(j < 7)
        def _():
            for c in slope_loads(j + 1):
                c.start()

        for n in range(1, 8):

            @pl.when(j == n - 1)
            def _(n=n):
                dm_load(n).start()

        b = j % 2
        pltpu.make_async_copy(dm_refs[0], dm_s.at[b], dm_sem.at[b]).wait()
        for c in slope_loads(j):
            c.wait()
        at = pl.ds(pl.multiple_of(sending_slot(j) * half, half), half)
        da = dot32(dm_s[b], wd_s[...], contract_last)
        g_s[0, at, :] = (da * slope_s[b, 0].astype(jnp.float32)).astype(low_type)
        g_s[1, at, :] = (da * slope_s[b, 1].astype(jnp.float32)).astype(low_type)
        return carry

    def back(first, last):
        lax.fori_loop(first, last, back_step, 0)

    tile = 512

    def partial(slot, which, store):
        if slot == 3:
            back(which, which + 1)
        if slot == 3 and which == 0:
            weight_load.wait()
        if slot == 1 and which == 0:
            back(2, 4)
        at = pl.ds(slot * rows + which * half, half)

        @pl.loop(0, model // tile)
        def _(n):
            cols = pl.ds(pl.multiple_of(n * tile, tile), tile)
            value = dot32(g_s[0, at, :], w_s[0, cols, :], contract_last)
            store(cols, value + dot32(g_s[1, at, :], w_s[1, cols, :], contract_last))

    def own(which):
        def store(cols, value):
            low_ref[pl.ds(which * half, half), cols] = value.astype(low_type)

        return store

    strip = 256

    def load(i):
        return pltpu.make_async_copy(h_hbm.at[:, pl.ds(pl.multiple_of(i * strip, strip), strip)], h_s.at[i % 2], h_sem.at[i % 2])

    def out(i):
        at = pl.ds(pl.multiple_of(i * strip, strip), strip)
        return pltpu.make_async_copy(stage.at[i % 2], grad_ref.at[at], out_sem.at[i % 2])

    strips = model // strip

    def strip_step(i, carry):
        @pl.when(i < strips - 1)
        def _():
            load(i + 1).start()

        load(i).wait()

        @pl.when(i >= 2)
        def _():
            out(i - 2).wait()

        stage[i % 2] = dot32(h_s[i % 2], g_s[0], contract_first).astype(low_type)
        out(i).start()
        return carry

    def fill_one():
        back(4, 8)
        dup_store.start()
        load(0).start()
        partial(0, 0, own(0))

    def fill_two():
        partial(0, 1, own(1))
        lax.fori_loop(0, strips, strip_step, 0)

    copies = exchange(rows, partial, bufs, send, recv, fill_one, fill_two)
    copies[0].wait_send()
    copies[1].wait_send()
    og_load.start()
    x1_load.wait()
    og_load.wait()
    finish_back(copies, rows, 1, dx_ref, bufs[0], low_ref, live_ref, norm_ref, bufs[5], bufs[6], dx_ref, low_ref, gain_ref, shift_ref, gain_s, shift_s, 2)
    out(strips - 2).wait()
    out(strips - 1).wait()
    dup_store.wait()


def hidden_scatter(dm_blocks, one, two, wd, w, h, x1, out_grad, live, norm):
    rows, model = x1.shape
    total, depth = one.shape
    half = rows // 2
    vmem = pl.BlockSpec(memory_space=pltpu.VMEM)
    line = jax.ShapeDtypeStruct((1, model), jnp.float32)
    return pl.pallas_call(
        functools.partial(hidden_scatter_kernel, len(dm_blocks)),
        in_specs=[ANY] * (len(dm_blocks) + 7) + [vmem, vmem],
        out_specs=[ANY, ANY, vmem, vmem, vmem, vmem],
        out_shape=[
            jax.ShapeDtypeStruct((model, depth), low_type),
            jax.ShapeDtypeStruct((total, depth), low_type),
            jax.ShapeDtypeStruct((rows, model), jnp.float32),
            jax.ShapeDtypeStruct((rows, model), low_type),
            line,
            line,
        ],
        scratch_shapes=exchange_scratch(rows, model)
        + [
            pltpu.VMEM((2, total, depth), low_type),
            pltpu.VMEM(w.shape, low_type),
            pltpu.VMEM(wd.shape, low_type),
            pltpu.VMEM((2, half, model), low_type),
            pltpu.VMEM((2, 2, half, depth), low_type),
            pltpu.VMEM((2, total, 256), low_type),
            pltpu.VMEM((2, 256, depth), low_type),
            pltpu.SemaphoreType.DMA((5,)),
            pltpu.SemaphoreType.DMA((2,)),
            pltpu.SemaphoreType.DMA((2, 2)),
            pltpu.SemaphoreType.DMA((2,)),
            pltpu.SemaphoreType.DMA((2,)),
        ],
        cost_estimate=cost(8 * total * model * depth, 16 * total * model),
        compiler_params=pltpu.CompilerParams(vmem_limit_bytes=62 * MIB, collective_id=5, has_side_effects=True),
        name="hidden_scatter",
    )(*dm_blocks, one, two, wd, w, h, x1, out_grad, live, norm)


def first_scatter_kernel(count, *refs):
    lefts_hbm = refs[:count]
    w_hbm, x_ref, base_ref, norm_ref, live_ref, small_ref = refs[count : count + 6]
    refs = refs[count + 6 :]
    x1_hbm, mlp_hbm = refs[0], refs[1:4]
    dx_ref, total_ref, layer_hbm = refs[4:7]
    scratch = refs[7:]
    bufs, (gain_s, shift_s, send, recv, own_s, left_s, w_s) = scratch[:7], scratch[7:14]
    x1_s, mlp_s, layer_s, left_sem, in_sem, layer_sem, gain_ref, shift_ref, small_s = scratch[14:23]
    nd, nt = lax.axis_size("dp"), lax.axis_size("tensor")
    rows, model = x_ref.shape
    half = rows // 2
    tile = 512
    far = pl.ds(3 * rows, rows)
    rest = pl.ds(0, 3 * rows)
    early = [pltpu.make_async_copy(left.at[far], left_s.at[n, far], left_sem.at[n]) for n, left in enumerate(lefts_hbm)]
    early.append(pltpu.make_async_copy(w_hbm.at[pl.ds(0, 3)], w_s, left_sem.at[2 * count]))
    late = [
        pltpu.make_async_copy(left.at[rest], left_s.at[n, rest], left_sem.at[count + n]) for n, left in enumerate(lefts_hbm)
    ]
    for c in early + late:
        c.start()
    greet_all(nd, nt)
    for c in early:
        c.wait()

    def partial(slot, which, store):
        if slot == 1 and which == 0:
            for c in late:
                c.wait()
        at = pl.ds(slot * rows + which * half, half)

        @pl.loop(0, model // tile)
        def _(n):
            cols = pl.ds(pl.multiple_of(n * tile, tile), tile)
            value = None
            for m in range(count):
                depth = left_s.shape[2]
                per = w_s.shape[2] // depth
                side = slice((m % per) * depth, (m % per + 1) * depth)
                term = dot32(left_s[m, at, :], w_s[m // per, cols, side], contract_last)
                value = term if value is None else value + term
            store(cols, value)

    def own(which):
        def store(cols, value):
            own_s[pl.ds(which * half, half), cols] = value

        return store

    def layer_moves():
        deep = x1_s.shape[1]
        at = lambda i: pl.ds(pl.multiple_of(i * deep, deep), deep)

        def loads(i):
            return [pltpu.make_async_copy(x1_hbm.at[at(i)], x1_s.at[i % 2], in_sem.at[i % 2, 0])] + [
                pltpu.make_async_copy(ref.at[at(i)], mlp_s.at[i % 2, n], in_sem.at[i % 2, 1 + n])
                for n, ref in enumerate(mlp_hbm)
            ]

        def stores(i):
            return [pltpu.make_async_copy(layer_s.at[i % 2], layer_hbm.at[at(i)], layer_sem.at[i % 2])]

        def work(i):
            b = i % 2
            total = mlp_s[b, 0].astype(jnp.float32) + mlp_s[b, 1].astype(jnp.float32) + mlp_s[b, 2].astype(jnp.float32)
            layer_s[b] = (x1_s[b] + live_ref[at(i), :] * total).astype(low_type)

        flow(0, rows // deep, loads, work, stores)

    def fill_one():
        partial(0, 0, own(0))
        partial(0, 1, own(1))

    def fill_two():
        layer_moves()

    copies = exchange(rows, partial, bufs, send, recv, fill_one, fill_two)
    finish_back(copies, rows, 0, x_ref, base_ref, own_s, None, norm_ref, bufs[5], bufs[6], dx_ref, None, gain_ref, shift_ref, gain_s, shift_s)
    small_s[...] = small_ref[...]
    small_s[0:1, :] = gain_ref[...]
    small_s[2:3, :] = shift_ref[...]
    share(nd, nt, small_s, total_ref, *scratch[23:])


def first_scatter(lefts, w, x, base, norm, live, small, x1, mlp_parts):
    rows, model = x.shape
    count = len(lefts)
    total, part = lefts[0].shape
    vmem = pl.BlockSpec(memory_space=pltpu.VMEM)
    nd, nt = lax.axis_size("dp"), lax.axis_size("tensor")
    deep = 64
    both = lambda block, n, t: pltpu.VMEM((2,) + ((n,) if n else ()) + block, t)
    return pl.pallas_call(
        functools.partial(first_scatter_kernel, count),
        in_specs=[ANY] * (count + 1) + [vmem] * 5 + [ANY] * 4,
        out_specs=[vmem, vmem, ANY],
        out_shape=[
            jax.ShapeDtypeStruct((rows, model), low_type),
            jax.ShapeDtypeStruct((small.shape[0], model // nd), jnp.float32),
            jax.ShapeDtypeStruct((rows, model), low_type),
        ],
        scratch_shapes=exchange_scratch(rows, model)
        + [
            pltpu.VMEM((rows, model), jnp.float32),
            pltpu.VMEM((count, total, part), low_type),
            pltpu.VMEM((3,) + w.shape[1:], low_type),
            both((deep, model), 0, jnp.float32),
            both((deep, model), 3, low_type),
            both((deep, model), 0, low_type),
            pltpu.SemaphoreType.DMA((2 * count + 1,)),
            pltpu.SemaphoreType.DMA((2, 4)),
            pltpu.SemaphoreType.DMA((2,)),
            pltpu.VMEM((1, model), jnp.float32),
            pltpu.VMEM((1, model), jnp.float32),
            pltpu.VMEM(small.shape, jnp.float32),
        ]
        + share_scratch(nd, nt, small.shape[0], model // nd),
        cost_estimate=cost(10**13, 30 * rows * model),
        compiler_params=pltpu.CompilerParams(vmem_limit_bytes=62 * MIB, collective_id=6, has_side_effects=True),
        name="first_scatter",
    )(*lefts, w, x, base, norm, live, small, x1, *mlp_parts)


def adam_rest_kernel(low_ref, turned_ref, *refs):
    qkv_in, out_in, qkv_out, out_out = refs[:3], refs[3:6], refs[6:10], refs[10:]
    step = pl.program_id(0)
    last = pl.num_programs(0) - 2

    @pl.when(step < last)
    def _():
        adam_blocks(low_ref, qkv_in, qkv_out)

    @pl.when(step >= last)
    def _():
        gradient = turned_ref[0].astype(jnp.float32).T
        out_out[0][...] = gradient
        results = adamw_update(out_in[0][...], gradient, out_in[1][...], out_in[2][...], weight_decay)
        for ref, value in zip(out_out[1:], results):
            ref[...] = value


def adam_rest(low, qkv, out):
    count, depth, width = low.shape
    half = depth // 2
    last = 2 * count - 2
    stack = lambda k: (jnp.minimum(k, last - 1) // 2, jnp.minimum(k, last - 1) % 2, 0)
    late = lambda k: jnp.maximum(k, last) - last
    three = pl.BlockSpec((1, half, width), stack)
    flat = pl.BlockSpec((width, half), lambda k: (0, late(k)))
    like = lambda value: jax.ShapeDtypeStruct(value.shape, jnp.float32)
    return pl.pallas_call(
        adam_rest_kernel,
        grid=(last + 2,),
        in_specs=[three, pl.BlockSpec((1, half, width), lambda k: (count - 1, late(k), 0))] + [three] * 3 + [flat] * 3,
        out_specs=[three] * 4 + [flat] * 4,
        out_shape=[like(qkv[0])] * 4 + [like(out[0])] * 4,
        cost_estimate=cost(30 * count * depth * width, 30 * count * depth * width),
        compiler_params=params(60),
        name="adam_rest",
    )(low, low, *qkv, *out)


def gather_gate_up_kernel(count, h_ref, w_hbm, *rest):
    blocks, (all_ref, act_ref, one_ref, two_ref, grad_ref) = rest[:count], rest[count : count + 5]
    w_s, all_s, stage, acc, turned, dm_s, send, recv, local, h_sem, out_sem, dm_sem = rest[count + 5 :]
    near_x, near_y = neighbours()
    half = h_ref.shape[0] // 2
    own = pltpu.make_async_copy(h_ref, all_s.at[pl.ds(0, 2 * half)], local.at[0])
    own.start()
    weights = pltpu.make_async_copy(w_hbm, w_s, local.at[1])
    weights.start()
    greet(near_x, near_y)
    own.wait()
    copies = square_copies(all_s, half, send, recv)
    for c in copies[:4]:
        c.start()
    acc[...] = jnp.zeros_like(acc)
    weights.wait()
    in_order = [blocks[n] for n in arrival]
    tile = 512

    def outs(buf, row):
        return [
            pltpu.make_async_copy(stage.at[buf, n], ref.at[pl.ds(row, half)], out_sem.at[buf, n])
            for n, ref in enumerate((act_ref, one_ref, two_ref))
        ]

    def keep(i, row):
        return pltpu.make_async_copy(all_s.at[pl.ds(row, half)], all_ref.at[pl.ds(row, half)], h_sem.at[i])

    def step(i, carry):
        await_slot(i, copies)
        row = pl.multiple_of(arrival_slot(i) * half, half)
        buf = i % 2
        keep(i, row).start()

        @pl.when(i >= 2)
        def _():
            for c in outs(buf, row):
                c.wait()

        h = all_s[pl.ds(row, half), :]
        gate = dot32(h, w_s[0])
        up = dot32(h, w_s[1])
        sig = 1.0 / (1.0 + jnp.exp(-gate))
        silu = gate * sig
        act = (silu * up).astype(low_type)
        stage[buf, 0] = act
        stage[buf, 1] = (up * sig * (1.0 + gate * (1.0 - sig))).astype(low_type)
        stage[buf, 2] = silu.astype(low_type)
        for c in outs(buf, row):
            c.start()
        turned[...] = act.T
        fetch_next(i, in_order, dm_s, dm_sem)

        @pl.loop(0, acc.shape[1] // tile)
        def _(n):
            cols = pl.ds(pl.multiple_of(n * tile, tile), tile)
            acc[:, cols] += dot32(turned[...], dm_s[buf, :, cols])

        return carry

    lax.fori_loop(0, 8, step, 0)
    for buf in (0, 1):
        for c in outs(buf, 0):
            c.wait()
    for i in range(8):
        keep(i, 0).wait()
    for c in copies:
        c.wait_send()
    depth = acc.shape[0]
    strip = depth // 8

    @pl.loop(0, 8)
    def _(n):
        at = pl.ds(pl.multiple_of(n * strip, strip), strip)
        all_s[at, :] = acc[at, :].astype(low_type)

    last = pltpu.make_async_copy(all_s.at[pl.ds(0, depth)], grad_ref, local.at[0])
    last.start()
    last.wait()


def gather_gate_up(h, w, dm_blocks):
    rows, model = h.shape
    depth = w.shape[2]
    total = 4 * rows
    half = rows // 2
    deep = jax.ShapeDtypeStruct((total, depth), low_type)
    return pl.pallas_call(
        functools.partial(gather_gate_up_kernel, len(dm_blocks)),
        in_specs=[ANY] * (2 + len(dm_blocks)),
        out_specs=[ANY] * 5,
        out_shape=[
            jax.ShapeDtypeStruct((total, model), low_type),
            deep,
            deep,
            deep,
            jax.ShapeDtypeStruct((depth, model), low_type),
        ],
        scratch_shapes=[
            pltpu.VMEM(w.shape, low_type),
            pltpu.VMEM((total, model), low_type),
            pltpu.VMEM((2, 3, half, depth), low_type),
            pltpu.VMEM((depth, model), jnp.float32),
            pltpu.VMEM((depth, half), low_type),
            pltpu.VMEM((2, half, model), low_type),
            pltpu.SemaphoreType.DMA((6,)),
            pltpu.SemaphoreType.DMA((6,)),
            pltpu.SemaphoreType.DMA((2,)),
            pltpu.SemaphoreType.DMA((8,)),
            pltpu.SemaphoreType.DMA((2, 3)),
            pltpu.SemaphoreType.DMA((2,)),
        ],
        cost_estimate=cost(6 * total * model * depth, 4 * model * depth + 4 * total * model + 6 * total * depth),
        compiler_params=pltpu.CompilerParams(vmem_limit_bytes=62 * MIB, collective_id=1, has_side_effects=True),
        name="gather_gate_up",
    )(h, w, *dm_blocks)


def greet_all(nd, nt):
    d, t = lax.axis_index("dp"), lax.axis_index("tensor")
    barrier = pltpu.get_barrier_semaphore()
    for k in range(1, nd):
        pl.semaphore_signal(barrier, inc=1, device_id={"dp": lax.rem(d + k, nd)}, device_id_type=MESH)
    for k in range(1, nt):
        pl.semaphore_signal(barrier, inc=1, device_id={"tensor": lax.rem(t + k, nt)}, device_id_type=MESH)
    pl.semaphore_wait(barrier, nd + nt - 2)


def share(nd, nt, x_ref, o_ref, groups, partial, shares, send, recv, send_t, recv_t):
    d, t = lax.axis_index("dp"), lax.axis_index("tensor")
    width = o_ref.shape[1]
    copies = []
    for k in range(1, nd):
        peer = lax.rem(d + k, nd)
        c = pltpu.make_async_remote_copy(
            src_ref=x_ref.at[:, pl.ds(pl.multiple_of(peer * width, width), width)],
            dst_ref=groups.at[k],
            send_sem=send.at[k],
            recv_sem=recv.at[k],
            device_id={"dp": peer},
            device_id_type=MESH,
        )
        c.start()
        copies.append(c)
    total = x_ref[:, pl.ds(pl.multiple_of(d * width, width), width)]
    for k in range(1, nd):
        copies[k - 1].wait_recv()
        total += groups[k]
    partial[...] = total
    shares[t] = total
    for k in range(1, nt):
        c = pltpu.make_async_remote_copy(
            src_ref=partial,
            dst_ref=shares.at[t],
            send_sem=send_t.at[k],
            recv_sem=recv_t.at[k],
            device_id={"tensor": lax.rem(t + k, nt)},
            device_id_type=MESH,
        )
        c.start()
        copies.append(c)
    for k in range(1, nt):
        copies[nd - 2 + k].wait_recv()
    total = shares[0]
    for k in range(1, nt):
        total += shares[k]
    o_ref[...] = total
    for c in copies:
        c.wait_send()


def share_scratch(nd, nt, rows, width):
    return [
        pltpu.VMEM((nd, rows, width), jnp.float32),
        pltpu.VMEM((rows, width), jnp.float32),
        pltpu.VMEM((nt, rows, width), jnp.float32),
        pltpu.SemaphoreType.DMA((nd,)),
        pltpu.SemaphoreType.DMA((nd,)),
        pltpu.SemaphoreType.DMA((nt,)),
        pltpu.SemaphoreType.DMA((nt,)),
    ]


def body(
    tokens,
    out_grad,
    lengths,
    norm_gain,
    norm_bias,
    qkv_weight,
    qkv_bias,
    out_weight,
    gate_up_weight,
    down_weight,
    first_norm_gain,
    first_norm_bias,
    first_qkv_weight,
    first_qkv_bias,
    first_out_weight,
    first_gate_up_weight,
    first_down_weight,
    second_norm_gain,
    second_norm_bias,
    second_qkv_weight,
    second_qkv_bias,
    second_out_weight,
    second_gate_up_weight,
    second_down_weight,
):
    slots = lax.axis_size("tensor")
    rank = lax.axis_index("tensor")
    own_rows = tokens.shape[0]
    group_rows = own_rows * slots
    width = out_weight.shape[0]
    order = rank if square(slots) else jnp.zeros_like(rank)

    chunk = jnp.bitwise_xor(jnp.arange(slots, dtype=jnp.int32), order)
    row_index = (chunk[:, None] * own_rows + jnp.arange(own_rows, dtype=jnp.int32)[None, :]).reshape(-1)
    seq_start, _ = layout(lengths[0], row_index)
    position = row_index - seq_start
    own_index = rank * own_rows + jnp.arange(own_rows, dtype=jnp.int32)
    live = layout(lengths[0], own_index)[1][:, None]
    block_start, _ = layout(lengths[0], jnp.arange(group_rows // BLOCK, dtype=jnp.int32) * BLOCK)
    table = jnp.concatenate([order.reshape(1).astype(jnp.int32), block_start // BLOCK])
    starts = seq_start[None, :]
    small_low = jnp.concatenate([norm_gain, norm_bias, qkv_bias, qkv_bias[:1]], axis=0).astype(low_type)
    own_bias = lambda full: lax.dynamic_slice_in_dim(full[4:7], rank * width, width, 1)[:, None, :]

    if square(slots):
        attn_low = jnp.concatenate([qkv_weight, out_weight.T[None]], axis=0).astype(low_type)
        attn_full = lax.all_gather(attn_low, "dp", axis=1, tiled=True)
        lane = jnp.arange(PAIR, dtype=jnp.int32) % (ROT // 2)
        inverse = jnp.power(rope_base, -lane.astype(jnp.float32) * (2.0 / ROT))[None, :]
        position = position.astype(jnp.float32).reshape(-1, 256)
        h1, small_full, *tables, dm_top, dm_end, gate_up_low = gather_norm(
            tokens, small_low.astype(jnp.float32), position, inverse, out_grad, live, gate_up_weight
        )
        norm = small_full[:4]
        gate_up_full = lax.all_gather(after(gate_up_low, attn_full), "dp", axis=1, tiled=True)
        dm_first, dm_rest = gather_rows(dm_top, dm_end)
        q, k, v, kt, vt = qkv_all(h1, attn_full, own_bias(small_full), tables)

        o_a, lse_a = attn_fwd(0, slots, table, q, k, vt, starts)
        dm_far = dm_rest(o_a)
        o_b, lse_b = attn_fwd(1, slots, table, after(q, o_a, *dm_first), k, vt, starts)
        o_b = after(o_b, *dm_far)
        dm_blocks = dm_first + dm_far

        x1, h2_own = out_scatter(o_a, o_b, attn_full, tokens, live, norm)
        down_low = after(down_weight.astype(low_type), gate_up_full, h2_own)
        down_full = lax.all_gather(down_low, "dp", axis=1, tiled=True)
        h2, act, slope_gate, slope_up, grad_down = gather_gate_up(h2_own, gate_up_full, dm_blocks)
        grad_down_own = lax.psum_scatter(after(grad_down, down_full), "dp", scatter_dimension=1, tiled=True)

        grad_gate, dup, dx1, dattn_own, gain_two, shift_two = hidden_scatter(
            dm_blocks, slope_gate, slope_up, down_full, gate_up_full, h2, x1, out_grad, live, norm
        )
        grad_gate = after(grad_gate, grad_down_own)
        grad_gate_own = lax.psum_scatter(grad_gate, "dp", scatter_dimension=0, tiled=True)

        do, grad_out, mlp, far_top, far_end, grad_up = gather_do(dattn_own, act, h2, dup, o_a, o_b, attn_full, down_full)
        grad_up = after(grad_up, grad_gate_own)
        grad_up_own = lax.psum_scatter(grad_up, "dp", scatter_dimension=0, tiled=True)
        mlp_first = [lax.ppermute(far_top, "tensor", swap_x), lax.ppermute(far_end, "tensor", swap_y)]
        *back_a, grad_down_full, down_one, down_two, down_three = attn_bwd(
            0, slots, table, q, do, o_a, k, v, kt, starts, lse_a, tables,
            grad_down_own, (down_weight, first_down_weight, second_down_weight),
        )
        down_step = (grad_down_full, down_one, down_two, down_three)
        hidden = (gate_up_weight, first_gate_up_weight, second_gate_up_weight)
        for_x, for_y = pass_on(mlp, *[after(part, back_a[0]) for part in mlp_first])
        mlp_parts = [mlp, lax.ppermute(for_x, "tensor", swap_x), lax.ppermute(for_y, "tensor", swap_y)]
        results = attn_bwd(
            1, slots, table, q, after(do, back_a[0], for_x), o_b, k, v, kt, starts, lse_b, tables, grad_gate_own, hidden
        )
        back_b, begun = results[:3], results[3:]
        dlin = [side for pair in zip(back_a, back_b) for side in pair]
        grad_rest, bias_local, *hidden_step = qkv_grad(h1, dlin, grad_out, grad_up_own, hidden, begun)
        late = [after(dlin[0], grad_rest, *mlp_parts[1:])] + dlin[1:]
        spread = lambda part: lax.dynamic_update_slice(
            jnp.zeros((3, small_full.shape[1]), jnp.float32), part, (jnp.int32(0), rank * width)
        )
        biases = spread(bias_local)
        small = jnp.concatenate([gain_two, gain_two, shift_two, shift_two, biases, biases[:1]], axis=0)
        input_grad, small_own, layer_out = first_scatter(
            late, attn_full, tokens, dx1, norm, live, small, x1, mlp_parts
        )
        grad_rest = after(grad_rest, grad_up_own)
        grad_rest_own = lax.psum_scatter(grad_rest, "dp", scatter_dimension=1, tiled=True)
        rest_step = adam_rest(
            grad_rest_own,
            (qkv_weight, first_qkv_weight, second_qkv_weight),
            (out_weight, first_out_weight, second_out_weight),
        )
        qkv_step, out_step = rest_step[:4], rest_step[4:]
    else:
        everyone = lambda value: lax.all_gather(value, "tensor", axis=0, tiled=True)
        scatter = lambda value, axis, at: lax.psum_scatter(value.astype(low_type), axis, scatter_dimension=at, tiled=True)
        small_full = lax.all_gather(small_low, "dp", axis=1, tiled=True).astype(jnp.float32)
        qkv_full, out_full, gate_up_full, down_full = (
            lax.all_gather(w.astype(low_type), "dp", axis=1, tiled=True)
            for w in (qkv_weight, out_weight, gate_up_weight, down_weight)
        )
        gain_rows, shift_rows = small_full[0:2], small_full[2:4]
        rows_in, cotangent = tokens.astype(jnp.float32), out_grad.astype(jnp.float32)
        tables = rotary_tables(position)
        h1 = everyone(layer_norm(rows_in, gain_rows[0], shift_rows[0]).astype(low_type))
        q, k, v, kt, vt = qkv_all(h1, qkv_full, own_bias(small_full), tables)
        o_a, lse_a = attn_fwd(0, slots, table, q, k, vt, starts)
        o_b, lse_b = attn_fwd(1, slots, table, q, k, vt, starts)
        o = jnp.concatenate([o_a, o_b], axis=1)
        x1 = rows_in + live * scatter(dot32(o, out_full), "tensor", 0).astype(jnp.float32)
        h2 = everyone(layer_norm(x1, gain_rows[1], shift_rows[1]).astype(low_type))
        gate, up = dot32(h2, gate_up_full[0]), dot32(h2, gate_up_full[1])
        sig = 1.0 / (1.0 + jnp.exp(-gate))
        act = (gate * sig * up).astype(low_type)
        mlp_rows = scatter(dot32(act, down_full), "tensor", 0).astype(jnp.float32)
        layer_out = (x1 + live * mlp_rows).astype(low_type)
        dm = everyone((cotangent * live).astype(low_type))
        da = dot32(dm, down_full, contract_last)
        dgate = (da * up * sig * (1.0 + gate * (1.0 - sig))).astype(low_type)
        dup = (da * gate * sig).astype(low_type)
        grad_down_own = scatter(dot32(act, dm, contract_first), "dp", 1)
        grad_gate_up = jnp.stack([dot32(h2, dgate, contract_first), dot32(h2, dup, contract_first)])
        grad_gate_up_own = scatter(grad_gate_up, "dp", 1)
        dh2 = dot32(dgate, gate_up_full[0], contract_last) + dot32(dup, gate_up_full[1], contract_last)
        dh2 = scatter(dh2, "tensor", 0).astype(jnp.float32)
        back, gain_two, shift_two = jax.vjp(layer_norm, x1, gain_rows[1], shift_rows[1])[1](dh2)
        dx1 = cotangent + back
        dattn = everyone((dx1 * live).astype(low_type))
        do = dot32(dattn, out_full, contract_last).astype(low_type)
        grad_out = dot32(dattn, o, contract_first).astype(low_type)
        back_a = attn_bwd(0, slots, table, q, do, o_a, k, v, kt, starts, lse_a, tables)
        back_b = attn_bwd(1, slots, table, q, do, o_b, k, v, kt, starts, lse_b, tables)
        dlin = [side for pair in zip(back_a, back_b) for side in pair]
        grad_rest, bias_local = qkv_grad(h1, dlin, grad_out)
        grad_rest_own = scatter(grad_rest, "dp", 1)
        grad_qkv_own, grad_out_own = grad_rest_own[:3], grad_rest_own[3].T
        dh1 = sum(
            dot32(jnp.concatenate(dlin[2 * n : 2 * n + 2], axis=1), qkv_full[n], contract_last) for n in range(3)
        )
        dh1 = scatter(dh1, "tensor", 0).astype(jnp.float32)
        back, gain_one, shift_one = jax.vjp(layer_norm, rows_in, gain_rows[0], shift_rows[0])[1](dh1)
        input_grad = (dx1 + back).astype(low_type)
        gain_one, gain_two, shift_one, shift_two = (
            value[None, :] for value in (gain_one, gain_two, shift_one, shift_two)
        )

        bias_placed = lax.dynamic_update_slice(
            jnp.zeros((3, small_full.shape[1]), jnp.float32), bias_local, (jnp.int32(0), rank * width)
        )
        small_local = jnp.concatenate([gain_one, gain_two, shift_one, shift_two, bias_placed], axis=0)
        small_own = lax.psum(lax.psum_scatter(small_local, "dp", scatter_dimension=1, tiled=True), "tensor")

        def whole_step(gradient, *held):
            gradient = gradient.astype(jnp.float32)
            return (gradient,) + adamw_update(held[0], gradient, held[1], held[2], weight_decay)

        qkv_step = whole_step(grad_qkv_own, qkv_weight, first_qkv_weight, second_qkv_weight)
        out_step = whole_step(grad_out_own, out_weight, first_out_weight, second_out_weight)
        hidden_step = whole_step(grad_gate_up_own, gate_up_weight, first_gate_up_weight, second_gate_up_weight)
        down_step = whole_step(grad_down_own, down_weight, first_down_weight, second_down_weight)

    def small_step(gradient, *held):
        return (gradient,) + adamw_update(held[0], gradient, held[1], held[2], 0.0)

    gain_step = small_step(small_own[0:2], norm_gain, first_norm_gain, second_norm_gain)
    shift_step = small_step(small_own[2:4], norm_bias, first_norm_bias, second_norm_bias)
    bias_step = small_step(small_own[4:7], qkv_bias, first_qkv_bias, second_qkv_bias)
    steps = (gain_step, shift_step, qkv_step, bias_step, out_step, hidden_step, down_step)
    return (layer_out, input_grad) + tuple(step[n] for n in range(4) for step in steps)


def solution(mesh):
    return jax.shard_map(
        body,
        mesh=mesh,
        in_specs=(
            P(("dp", "tensor"), None),
            P(("dp", "tensor"), None),
            P("dp", None),
            P(None, "dp"),
            P(None, "dp"),
            P(None, "dp", "tensor"),
            P(None, "dp"),
            P("tensor", "dp"),
            P(None, "dp", "tensor"),
            P("tensor", "dp"),
            P(None, "dp"),
            P(None, "dp"),
            P(None, "dp", "tensor"),
            P(None, "dp"),
            P("tensor", "dp"),
            P(None, "dp", "tensor"),
            P("tensor", "dp"),
            P(None, "dp"),
            P(None, "dp"),
            P(None, "dp", "tensor"),
            P(None, "dp"),
            P("tensor", "dp"),
            P(None, "dp", "tensor"),
            P("tensor", "dp"),
        ),
        out_specs=(
            P(("dp", "tensor"), None),
            P(("dp", "tensor"), None),
            P(None, "dp"),
            P(None, "dp"),
            P(None, "dp", "tensor"),
            P(None, "dp"),
            P("tensor", "dp"),
            P(None, "dp", "tensor"),
            P("tensor", "dp"),
            P(None, "dp"),
            P(None, "dp"),
            P(None, "dp", "tensor"),
            P(None, "dp"),
            P("tensor", "dp"),
            P(None, "dp", "tensor"),
            P("tensor", "dp"),
            P(None, "dp"),
            P(None, "dp"),
            P(None, "dp", "tensor"),
            P(None, "dp"),
            P("tensor", "dp"),
            P(None, "dp", "tensor"),
            P("tensor", "dp"),
            P(None, "dp"),
            P(None, "dp"),
            P(None, "dp", "tensor"),
            P(None, "dp"),
            P("tensor", "dp"),
            P(None, "dp", "tensor"),
            P("tensor", "dp"),
        ),
        check_vma=False,
    )
```
